32 devices in a mesh: grp: 4 (over y, core), dev: 8 (over z, x).
Axes of the slice: x: 2, y: 2, z: 4, core: 2. Of those that a mesh axis runs over, the one named last changes fastest.
Arguments:
- wave: bfloat16 [1024, 384], P(('grp', 'dev')), may hold values from -6 to 6
- lengths: int32 [1024], P('grp'), may hold values from 288 to 384, as said below
- order: int32 [32, 32], P('grp'), may hold values from 0 to 31, each once within a row
- w_first: bfloat16 [10, 512], replicated, may hold values from -2 to 2
- norm_gain: float32 [512], replicated, may hold values from 0.1 to 1.9
- norm_bias: float32 [512], replicated, may hold values from -3 to 3
- w_second: bfloat16 [3, 512, 512], replicated, may hold values from -0.15625 to 0.15625
- cot: bfloat16 [1024, 37, 512], P(('grp', 'dev')), may hold values from -0.0234375 to 0.0234375
Outputs:
- features: bfloat16 [1024, 37, 512], P(('grp', 'dev'))
- grad_second: float32 [3, 512, 512], P(None, None, 'dev')
- grad_first: float32 [10, 512], P(None, 'dev')
- grad_gain: float32 [512], P('dev')
- grad_bias: float32 [512], P('dev')
The draws below stay inside these ranges and needn't reach their ends.
Inputs may be any that keep to these rules, and one draw needn't show every extreme that they name: `lengths`: every aligned block of 32 rows (the rows of one device) holds a row of exactly 384 valid samples. Each row of order is a permutation of 0 .. 31.
All inputs are finite; a program needn't handle non-finite values.
Results may differ from the reference program's by a relative error of at most 0.0054.
Values may be sent and summed in bfloat16 or wider, within the bound.
No kernel may reach another device: no remote copies, remote signals or barrier semaphores. Data moves between devices by JAX's collectives and lax.ppermute only.
A program may use at most 64 MiB of HBM per device.

```python
import jax
import jax.numpy as jnp
from jax import lax

CH = 512
K0 = 10
K1 = 3
ROW_DEV = 32
SAMP = 384
MINLEN = 288
F1 = 37
ROWS = 1024
N_GRP = 4
N_DEV = 8
DEVICES = 32


def draw_lengths(key, part):
    first, second = jax.random.split(jax.random.fold_in(key, 17))
    blocks = ROWS // ROW_DEV
    values = jax.random.randint(first, (blocks, ROW_DEV), MINLEN, SAMP + 1, dtype=jnp.int32)
    where_full = jax.random.randint(second, (blocks, 1), 0, ROW_DEV, dtype=jnp.int32)
    column = jnp.arange(ROW_DEV, dtype=jnp.int32)[None, :]
    values = jnp.where(column == where_full, SAMP, values)
    return values.reshape(ROWS).astype(jnp.int32)


def levels(stream_key, extent, cuts, least, top_value):
    factor_of = 1.0
    for position, shards_of in cuts:
        steps = jax.random.uniform(jax.random.fold_in(jax.random.fold_in(stream_key, 6), position), (shards_of,), jnp.float32, least / len(cuts), top_value / len(cuts))
        factor_of = factor_of * jnp.repeat(jnp.exp(steps), extent[position] // shards_of).reshape((-1,) + (1,) * (len(extent) - 1 - position))
    return factor_of


def noise(own_key, shape, width, most, cuts=(), kind=jnp.bfloat16):
    loudness = levels(own_key, shape, cuts, -0.22, 0.18) if cuts else 1.0
    array = jax.random.normal(own_key, shape, jnp.float32) * width * loudness
    return jnp.minimum(jnp.maximum(array, -most), most).astype(kind)


def setup_inputs(seed: int = 0) -> dict:
    streams_of = jax.random.split(jax.random.key(seed), 9)
    wave = noise(streams_of[0], (ROWS, SAMP), 1.0, 6.0, ((0, 32),))
    lengths = draw_lengths(jax.random.fold_in(streams_of[8], 71), 0)
    order = jax.vmap(lambda own: jax.random.permutation(own, ROW_DEV))(jax.random.split(streams_of[2], DEVICES)).reshape((DEVICES, ROW_DEV)).astype(jnp.int32)
    w_first = noise(streams_of[3], (K0, CH), K0 ** -0.5, 2.0)
    norm_gain = jnp.clip(1.0 + 0.18 * jax.random.normal(streams_of[4], (CH,), jnp.float32), 0.1, 1.9)
    norm_bias = noise(streams_of[5], (CH,), 0.5, 3.0, (), jnp.float32)
    w_second = noise(streams_of[6], (K1, CH, CH), (K1 * CH) ** -0.5, 0.15625)
    cot = noise(streams_of[7], (ROWS, F1, CH), 0.004, 0.0234375, ((0, 32),))
    return dict(wave=wave, lengths=lengths, order=order, w_first=w_first, norm_gain=norm_gain, norm_bias=norm_bias, w_second=w_second, cot=cot)


def gelu_slope(value):
    return 0.5 * (1.0 + lax.erf(value * 0.7071067811865476)) + value * jnp.exp(-0.5 * value * value) * 0.3989422804014327

def local_pass(wave, lens, w_first, norm_gain, norm_bias, w_second, cot):
    rows, samp = wave.shape
    ker_first = w_first.shape[0]
    stride_first = ker_first // 2
    chans = w_first.shape[1]
    taps_second = w_second.shape[0]
    frames0 = (samp - ker_first) // stride_first + 1
    frames1 = (frames0 - taps_second) // 2 + 1
    blocks = wave[:, :stride_first * (frames0 + 1)].reshape(rows, frames0 + 1, stride_first)
    patches = jnp.concatenate([blocks[:, :-1], blocks[:, 1:]], axis=2).reshape(rows * frames0, ker_first)
    pre0 = jnp.dot(patches, w_first, preferred_element_type=jnp.float32).reshape(rows, frames0, chans)
    valid0 = (lens - ker_first) // stride_first + 1
    mask0 = (jnp.arange(frames0, dtype=jnp.int32)[None, :] < valid0[:, None]).astype(jnp.float32)[:, :, None]
    count0 = valid0.astype(jnp.float32)[:, None, None]
    mean0 = lax.optimization_barrier(jnp.sum(pre0 * mask0, axis=1, keepdims=True)) / count0
    centred = (pre0 - mean0) * mask0
    var0 = lax.optimization_barrier(jnp.sum(centred * centred, axis=1, keepdims=True)) / count0
    inv_std = lax.rsqrt(var0 + 1e-05)
    normed = centred * inv_std
    lifted = normed * norm_gain + norm_bias
    act0 = (jax.nn.gelu(lifted, approximate=False) * mask0).astype(jnp.bfloat16)
    span = 2 * frames1
    taps = jnp.concatenate([act0[:, 0:span:2], act0[:, 1:span:2], act0[:, 2:span + 1:2]], axis=2)
    taps = taps.reshape(rows * frames1, taps_second * chans)
    kernel = w_second.reshape(taps_second * chans, chans)
    pre1 = jnp.dot(taps, kernel, preferred_element_type=jnp.float32).reshape(rows, frames1, chans)
    valid1 = (valid0 - taps_second) // 2 + 1
    mask1 = (jnp.arange(frames1, dtype=jnp.int32)[None, :] < valid1[:, None]).astype(jnp.float32)[:, :, None]
    features = (jax.nn.gelu(pre1, approximate=False) * mask1).astype(jnp.bfloat16)
    grad1 = (cot.astype(jnp.float32) * gelu_slope(pre1) * mask1).astype(jnp.bfloat16).reshape(rows * frames1, chans)
    grad_kernel = lax.dot_general(taps, grad1, (((0,), (0,)), ((), ())), preferred_element_type=jnp.float32)
    back = lax.dot_general(grad1, kernel, (((1,), (1,)), ((), ())), preferred_element_type=jnp.float32)
    back = back.reshape(rows, frames1, taps_second, chans)
    zero_row = jnp.zeros((rows, 1, chans), jnp.float32)
    even = back[:, :, 0] + jnp.concatenate([zero_row, back[:, :-1, 2]], axis=1)
    odd = back[:, :, 1]
    pieces = [jnp.stack([even, odd], axis=2).reshape(rows, span, chans), back[:, -1:, 2]]
    if frames0 > span + 1:
        pieces.append(jnp.zeros((rows, frames0 - span - 1, chans), jnp.float32))
    dact0 = jnp.concatenate(pieces, axis=1)
    dlift = dact0 * gelu_slope(lifted) * mask0
    grad_gain = lax.optimization_barrier(jnp.sum(dlift * normed, axis=(0, 1)))
    grad_bias = lax.optimization_barrier(jnp.sum(dlift, axis=(0, 1)))
    dnorm = dlift * norm_gain
    first_mean = lax.optimization_barrier(jnp.sum(dnorm, axis=1, keepdims=True)) / count0
    second_mean = lax.optimization_barrier(jnp.sum(dnorm * normed, axis=1, keepdims=True)) / count0
    dpre0 = inv_std * (dnorm - first_mean - normed * second_mean) * mask0
    grad_filter = lax.dot_general(patches.astype(jnp.float32), dpre0.reshape(rows * frames0, chans), (((0,), (0,)), ((), ())), precision=lax.Precision.HIGHEST, preferred_element_type=jnp.float32)
    grads = jnp.concatenate([grad_kernel, grad_filter, grad_gain[None, :], grad_bias[None, :]], axis=0)
    return (features, grads)

def reference(wave, lengths, order, w_first, norm_gain, norm_bias, w_second, cot):
    groups = N_GRP
    members = N_DEV
    share = ROW_DEV // members
    samp = wave.shape[1]
    shaped = wave.reshape(groups, members, ROW_DEV, samp)
    picks = order.reshape(groups, members, ROW_DEV)
    picked = jnp.take_along_axis(shaped, picks[..., None], axis=2)
    moved = picked.reshape(groups, members, share, members, samp).transpose(0, 3, 1, 2, 4).reshape(groups * members, ROW_DEV, samp)
    lens = jnp.take_along_axis(lengths.reshape(groups, members, ROW_DEV), picks, axis=2)
    lens = lens.reshape(groups, members, share, members).transpose(0, 3, 1, 2).reshape(groups * members, ROW_DEV)
    cots = cot.reshape(groups * members, ROW_DEV, F1, CH)

    def step(total, block):
        feats, grads = local_pass(block[0], block[1], w_first, norm_gain, norm_bias, w_second, block[2])
        return (total + grads, feats)
    init = jnp.zeros((K1 * CH + K0 + 2, CH), jnp.float32)
    total, feats = lax.scan(step, init, (moved, lens, cots))
    features = feats.reshape(ROWS, F1, CH)
    grad_second = total[:K1 * CH].reshape(K1, CH, CH)
    grad_first = total[K1 * CH:K1 * CH + K0]
    grad_gain = total[K1 * CH + K0]
    grad_bias = total[K1 * CH + K0 + 1]
    return (features, grad_second, grad_first, grad_gain, grad_bias)
```

```python
import functools

import jax
import jax.numpy as jnp
from jax import lax
from jax.experimental import pallas as pl
from jax.experimental.pallas import tpu as pltpu
from jax.sharding import PartitionSpec as P

F32 = jnp.float32
BF16 = jnp.bfloat16
GROUP = 8
MIN_SAMPLES = 288
MIB = 1 << 20


def gelu_and_slope(value):
    size = jnp.abs(value)
    bell = jnp.exp(value * value * -0.5)
    base = 1.0 + size * (0.3275911 * 0.7071067811865476)
    frac = pl.reciprocal(base, approx=True)
    frac = frac * (2.0 - base * frac)
    poly = 0.5 * 1.061405429
    for coef in (-1.453152027, 1.421413741, -0.284496736, 0.254829592):
        poly = poly * frac + 0.5 * coef
    tail = poly * frac * bell
    gelu = jnp.maximum(value, 0.0) - size * tail
    phi = jnp.where(value < 0.0, tail, 1.0 - tail)
    return gelu, phi + value * bell * 0.3989422804014327


def rows_first(a, b):
    return lax.dot_general(a, b, (((0,), (0,)), ((), ())), preferred_element_type=F32)


def cols_both(a, b):
    return lax.dot_general(a, b, (((1,), (1,)), ((), ())), preferred_element_type=F32)


def dot(a, b):
    return jnp.dot(a, b, preferred_element_type=F32)


def iota(shape, dim):
    return lax.broadcasted_iota(jnp.int32, shape, dim)


def onehot(mask):
    return mask.astype(F32).astype(BF16)


def deal_kernel(members, order_ref, wave_ref, out_ref):
    rows = wave_ref.shape[0]
    share = rows // members
    own = order_ref[pl.ds(lax.axis_index("dev"), 1), :]
    picks = onehot(iota((rows, rows), 0) == own)
    row = iota((rows, rows), 0)
    column = iota((rows, rows), 1)
    swap = onehot(column == lax.rem(row, share) * members + row // share)
    choose = cols_both(swap, picks).astype(BF16)
    out_ref[...] = dot(choose, wave_ref[...]).astype(BF16)


def setup_kernel(members, frames0, order_ref, len_ref, w_ref, valid_ref, band_ref):
    rows = order_ref.shape[1]
    share = rows // members
    taps, chans = w_ref.shape
    stride = taps // 2
    dealt = iota((rows, members), 0)
    owner = onehot(dealt // share == iota((rows, members), 1))
    order_of = dot(owner, order_ref[...].astype(F32).astype(BF16))
    high = len_ref[...] // 16
    low = len_ref[...] - high * 16
    lens_of = dot(owner, high.astype(F32).astype(BF16)) * 16.0 + dot(owner, low.astype(F32).astype(BF16))
    row = iota((rows, rows), 0)
    column = iota((rows, rows), 1)
    mine = column == lax.rem(row, share) * members + lax.axis_index("dev")
    index = jnp.sum(jnp.where(mine, order_of, 0.0), axis=1, keepdims=True)
    picked = column == index.astype(jnp.int32)
    lens = jnp.sum(jnp.where(picked, lens_of, 0.0), axis=1, keepdims=True).astype(jnp.int32)
    valid = (lens - taps) // stride + 1
    valid_ref[...] = jnp.broadcast_to(valid, valid_ref.shape)
    depth = band_ref.shape[0]
    for f in range(GROUP):
        spread = onehot(iota((depth, taps), 0) == iota((depth, taps), 1) + stride * f)
        band_ref[:, f * chans : (f + 1) * chans] = dot(spread, w_ref[...]).astype(BF16)


def forward_kernel(
    frames0,
    frames1,
    taps,
    reverse,
    wave_ref,
    valid_ref,
    band_ref,
    gain_ref,
    bias_ref,
    w_ref,
    cot_ref,
    feat_ref,
    even_ref,
    odd_ref,
    normed_ref,
    slope_ref,
    inv_ref,
    patch_ref,
    grad_ref,
    grad_t_ref,
    pre0,
    pre1,
):
    rows, samp = wave_ref.shape
    chans = gain_ref.shape[1]
    stride = taps // 2
    depth = band_ref.shape[0]
    groups = pre0.shape[0]
    width = pre0.shape[2] // GROUP
    min_valid = (MIN_SAMPLES - taps) // stride + 1
    free_groups = min(min_valid // GROUP, frames0 // GROUP)
    full_groups = frames0 // GROUP
    wave = wave_ref[...]
    for g in range(groups):
        pick = onehot(iota((samp, depth), 0) == iota((samp, depth), 1) + GROUP * stride * g)
        patch_ref[g] = dot(wave, pick).astype(BF16)
    patches = patch_ref[...].reshape(groups * rows, depth)

    for block in range(chans // width):
        lanes = slice(block * width, (block + 1) * width)
        for f in range(GROUP):
            cols = slice(f * chans + block * width, f * chans + (block + 1) * width)
            pre0[:, :, f * width : (f + 1) * width] = dot(patches, band_ref[:, cols]).reshape(groups, rows, width)
        valid = jnp.broadcast_to(valid_ref[:, :1], (rows, width))
        count = valid.astype(F32)

        def frame(g, f):
            return pre0[g, :, f * width : (f + 1) * width]

        def over_frames(body, init):
            def step(masked, g, carry):
                for f in range(GROUP):
                    carry = body(carry, g, f, masked)
                return carry

            carry = lax.fori_loop(0, free_groups, functools.partial(step, False), init)
            carry = lax.fori_loop(free_groups, full_groups, functools.partial(step, True), carry)
            for f in range(frames0 - full_groups * GROUP):
                carry = body(carry, full_groups, f, True)
            return carry

        def masked_to(value, g, f, masked):
            return jnp.where(valid > g * GROUP + f, value, 0.0) if masked else value

        def add_mean(total, g, f, masked):
            return total + masked_to(frame(g, f), g, f, masked)

        mean = over_frames(add_mean, jnp.zeros((rows, width), F32)) / count

        def add_var(total, g, f, masked):
            centred = masked_to(frame(g, f) - mean, g, f, masked)
            return total + centred * centred

        var = over_frames(add_var, jnp.zeros((rows, width), F32)) / count
        inv = lax.rsqrt(var + 1e-05)
        inv_ref[:, lanes] = inv
        gain = jnp.broadcast_to(gain_ref[:, lanes], (rows, width))
        bias = jnp.broadcast_to(bias_ref[:, lanes], (rows, width))

        def finish(carry, g, f, masked):
            normed = (frame(g, f) - mean) * inv
            gelu, slope = gelu_and_slope(normed * gain + bias)
            t = g * GROUP + f
            normed_ref[t, :, lanes] = masked_to(normed, g, f, masked)
            slope_ref[t, :, lanes] = masked_to(slope, g, f, masked)
            act_ref = odd_ref if f % 2 else even_ref
            act_ref[g * (GROUP // 2) + f // 2, :, lanes] = masked_to(gelu, g, f, masked).astype(BF16)
            return carry

        over_frames(finish, 0)
    for ref, used in ((even_ref, (frames0 + 1) // 2), (odd_ref, frames0 // 2)):
        ref[used:] = jnp.zeros((ref.shape[0] - used,) + ref.shape[1:], BF16)

    grad_ref[0] = jnp.zeros(grad_ref.shape[1:], BF16)
    grad_ref[frames1 + 1] = jnp.zeros(grad_ref.shape[1:], BF16)
    padded = grad_t_ref.shape[1]
    used = frames1 * rows
    grad_t_ref[:, (used // 128) * 128 :] = jnp.zeros((chans, padded - (used // 128) * 128), BF16)
    valid = jnp.broadcast_to(valid_ref[:, :1], (rows, chans))
    valid1 = lax.shift_right_arithmetic(valid - 3, 1) + 1
    chunk = 12
    for first in range(0, frames1 - chunk + 1, chunk):
        count = chunk if first + 2 * chunk <= frames1 else frames1 - first
        size = count * rows
        total = dot(even_ref[first : first + count].reshape(size, chans), w_ref[0])
        total += dot(odd_ref[first : first + count].reshape(size, chans), w_ref[1])
        total += dot(even_ref[first + 1 : first + count + 1].reshape(size, chans), w_ref[2])
        pre1[:count] = total.reshape(count, rows, chans)

        def activate(u, carry):
            gelu, slope = gelu_and_slope(pre1[u])
            keep = valid1 > u + first
            feat_ref[u + first] = jnp.where(keep, gelu, 0.0).astype(BF16)
            grad = cot_ref[u + first].astype(F32) * slope
            grad_ref[u + first + 1] = jnp.where(keep, grad, 0.0).astype(BF16)
            return carry

        lax.fori_loop(0, count, activate, 0)
        turned = grad_ref[first + 1 : first + 1 + count].reshape(size, chans).T
        slab = chans // len(reverse)
        for place, source in enumerate(reverse):
            grad_t_ref[place * slab : (place + 1) * slab, first * rows : first * rows + size] = turned[
                source * slab : (source + 1) * slab
            ]


def outer_kernel(even_ref, odd_ref, grad_t_ref, keep_ref, send_ref):
    frames = grad_t_ref.shape[1] // even_ref.shape[1]
    rows, chans = even_ref.shape[1:]
    half = chans // 2
    core = lax.rem(lax.axis_index("grp"), 2)
    turned = grad_t_ref[...]
    for tap, (ref, skip) in enumerate(((even_ref, 0), (odd_ref, 0), (even_ref, 1))):
        for side, out_ref in ((core, keep_ref), (1 - core, send_ref)):
            lanes = pl.ds(pl.multiple_of(side * half, half), half)
            acts = ref[skip : skip + frames, :, lanes].reshape(frames * rows, half)
            out_ref[:, tap * half : (tap + 1) * half] = dot(turned, acts).astype(out_ref.dtype)


def backward_kernel(
    frames0,
    frames1,
    taps,
    valid_ref,
    normed_ref,
    slope_ref,
    inv_ref,
    patch_ref,
    grad_ref,
    gain_ref,
    w_ref,
    out_ref,
    lift,
    dpre0,
    spread,
):
    groups, rows, depth = patch_ref.shape
    chans = gain_ref.shape[1]
    stride = taps // 2
    width = dpre0.shape[2] // GROUP
    full_groups = frames0 // GROUP
    patches = patch_ref[...].reshape(groups * rows, depth)
    evens = (frames0 + 1) // 2
    odds = frames0 // 2
    first = grad_ref[1 : evens + 1].reshape(evens * rows, chans)
    second = grad_ref[1 : odds + 1].reshape(odds * rows, chans)
    third = grad_ref[0:evens].reshape(evens * rows, chans)
    for block in range(chans // width):
        lanes = slice(block * width, (block + 1) * width)
        lift[0, :evens] = (cols_both(first, w_ref[0, lanes]) + cols_both(third, w_ref[2, lanes])).reshape(
            evens, rows, width
        )
        lift[1, :odds] = cols_both(second, w_ref[1, lanes]).reshape(odds, rows, width)

        def slopes(parity, e, carry):
            bias_sum, gain_sum = carry
            t = 2 * e + parity
            dlift = lift[parity, e] * slope_ref[t, :, lanes]
            lift[parity, e] = dlift
            return bias_sum + dlift, gain_sum + dlift * normed_ref[t, :, lanes]

        def both(e, carry):
            return slopes(1, e, slopes(0, e, carry))

        zero = jnp.zeros((rows, width), F32)
        carry = lax.fori_loop(0, odds, both, (zero, zero))
        if evens > odds:
            carry = slopes(0, odds, carry)
        bias_sum, gain_sum = carry
        out_ref[taps : taps + 1, lanes] = jnp.sum(gain_sum, axis=0, keepdims=True)
        out_ref[taps + 1 : taps + 2, lanes] = jnp.sum(bias_sum, axis=0, keepdims=True)
        valid = jnp.broadcast_to(valid_ref[:, :1], (rows, width))
        count = valid.astype(F32)
        scale = inv_ref[:, lanes] * gain_ref[:, lanes]
        bias_sum = bias_sum / count
        gain_sum = gain_sum / count

        def finish(g, f):
            t = g * GROUP + f
            dlift = lift[f % 2, g * (GROUP // 2) + f // 2]
            value = scale * (dlift - bias_sum - normed_ref[t, :, lanes] * gain_sum)
            dpre0[g, :, f * width : (f + 1) * width] = jnp.where(valid > t, value, 0.0).astype(BF16)

        def whole(g, carry):
            for f in range(GROUP):
                finish(g, f)
            return carry

        lax.fori_loop(0, full_groups, whole, 0)
        rest = frames0 - full_groups * GROUP
        for f in range(rest):
            finish(full_groups, f)
        if full_groups < groups:
            dpre0[full_groups, :, rest * width :] = jnp.zeros((rows, (GROUP - rest) * width), BF16)
        spread[...] = rows_first(patches, dpre0[...].reshape(groups * rows, GROUP * width))
        total = jnp.zeros((taps, width), F32)
        for f in range(GROUP):
            total += spread[stride * f : stride * f + taps, f * width : (f + 1) * width]
        out_ref[:taps, lanes] = total


def fold_kernel(axis, bit, keep_ref, got_ref, next_ref, send_ref):
    half = keep_ref.shape[0] // 2
    side = lax.rem(lax.shift_right_logical(lax.axis_index(axis), bit), 2)
    mine = pl.ds(pl.multiple_of(side * half, half), half)
    other = pl.ds(pl.multiple_of((1 - side) * half, half), half)
    next_ref[...] = keep_ref[mine, :] + got_ref[mine, :].astype(F32)
    send_ref[...] = (keep_ref[other, :] + got_ref[other, :].astype(F32)).astype(BF16)


def last_fold_kernel(keep_ref, got_ref, send_ref):
    send_ref[...] = (keep_ref[...] + got_ref[...].astype(F32)).astype(BF16)


def join_kernel(own_ref, other_ref, out_ref):
    half = out_ref.shape[2] // 2
    core = lax.rem(lax.axis_index("grp"), 2)
    for tap in range(out_ref.shape[0]):
        lanes = slice(tap * half, (tap + 1) * half)
        out_ref[tap, :, pl.ds(pl.multiple_of(core * half, half), half)] = own_ref[:, lanes]
        out_ref[tap, :, pl.ds(pl.multiple_of((1 - core) * half, half), half)] = other_ref[:, lanes]


def call(kernel, outs, args, scratch=(), limit=32, flops=0, touched=0):
    vmem = pl.BlockSpec(memory_space=pltpu.VMEM)
    return pl.pallas_call(
        kernel,
        out_shape=[jax.ShapeDtypeStruct(shape, kind) for shape, kind in outs],
        in_specs=[vmem] * len(args),
        out_specs=[vmem] * len(outs),
        scratch_shapes=[pltpu.VMEM(shape, kind) for shape, kind in scratch],
        compiler_params=pltpu.CompilerParams(vmem_limit_bytes=limit * MIB),
        cost_estimate=pl.CostEstimate(flops=flops, bytes_accessed=touched, transcendentals=0),
    )(*args)


def swap(value, axis, bit):
    size = lax.axis_size(axis)
    return lax.ppermute(value, axis, [(i, i ^ (1 << bit)) for i in range(size)])


def shards(wave, lengths, order, w_first, norm_gain, norm_bias, w_second, cot):
    members = lax.axis_size("dev")
    groups_of = lax.axis_size("grp")
    rows, samp = wave.shape
    taps, chans = w_first.shape
    taps_second = w_second.shape[0]
    stride = taps // 2
    frames0 = (samp - taps) // stride + 1
    frames1 = (frames0 - taps_second) // 2 + 1
    groups = -(-frames0 // GROUP)
    depth = 128
    width = 256
    dev_bits = members.bit_length() - 1
    grp_bits = groups_of.bit_length() - 1

    outgoing = call(functools.partial(deal_kernel, members), [((rows, samp), BF16)], [order, wave])[0]
    arrived = lax.all_to_all(outgoing, "dev", split_axis=0, concat_axis=0, tiled=True)
    valid, band = call(
        functools.partial(setup_kernel, members, frames0),
        [((rows, 128), jnp.int32), ((depth, GROUP * chans), BF16)],
        [order, lengths.reshape(members, rows), w_first],
    )
    gain = norm_gain.reshape(1, chans)
    bias = norm_bias.reshape(1, chans)
    cot_t = cot.transpose(1, 0, 2)
    pad_frames = -(-frames1 // 4) * 4
    reverse = [int(format(i, "b").zfill(dev_bits)[::-1], 2) for i in range(members)]
    feat, even, odd, normed, slope, inv, patch, grad, grad_t = call(
        functools.partial(forward_kernel, frames0, frames1, taps, reverse),
        [
            ((frames1, rows, chans), BF16),
            ((pad_frames + 1, rows, chans), BF16),
            ((pad_frames, rows, chans), BF16),
            ((frames0, rows, chans), F32),
            ((frames0, rows, chans), F32),
            ((rows, chans), F32),
            ((groups, rows, depth), BF16),
            ((frames1 + 2, rows, chans), BF16),
            ((chans, pad_frames * rows), BF16),
        ],
        [arrived, valid, band, gain, bias, w_second, cot_t],
        scratch=[((groups, rows, GROUP * width), F32), ((16, rows, chans), F32)],
        limit=48,
    )
    keep, send = call(
        outer_kernel,
        [((chans, taps_second * chans // 2), F32), ((chans, taps_second * chans // 2), BF16)],
        [even, odd, grad_t],
    )
    small = call(
        functools.partial(backward_kernel, frames0, frames1, taps),
        [((16, chans), F32)],
        [valid, normed, slope, inv, patch, grad, gain, w_second],
        scratch=[
            ((2, (frames0 + 1) // 2, rows, width), F32),
            ((groups, rows, GROUP * width), BF16),
            ((depth, GROUP * width), F32),
        ],
        limit=48,
    )[0]

    got = swap(send, "grp", 0)
    for bit in range(dev_bits):
        half = (keep.shape[0] // 2, keep.shape[1])
        keep, send = call(functools.partial(fold_kernel, "dev", bit), [(half, F32), (half, BF16)], [keep, got])
        got = swap(send, "dev", bit)
    total = call(last_fold_kernel, [(keep.shape, BF16)], [keep, got])[0]
    for bit in range(1, grp_bits):
        got = swap(total, "grp", bit)
        total = total.astype(F32) + got.astype(F32)
        if bit < grp_bits - 1:
            total = total.astype(BF16)
    total = total.astype(F32)
    other = swap(total, "grp", 0)
    grad_second = call(join_kernel, [((taps_second, chans // members, chans), F32)], [total, other])[0]

    for axis, bits in (("dev", dev_bits), ("grp", grp_bits)):
        for bit in range(bits):
            small = small + swap(small, axis, bit)
    member = lax.axis_index("dev")
    share = chans // members
    owned = lax.dynamic_slice_in_dim(small, member * share, share, 1)
    return (
        feat.transpose(1, 0, 2),
        grad_second.transpose(0, 2, 1),
        owned[:taps],
        owned[taps],
        owned[taps + 1],
    )


def solution(mesh):
    placed = (
        P(("grp", "dev"), None),
        P("grp"),
        P("grp", None),
        P(),
        P(),
        P(),
        P(),
        P(("grp", "dev"), None, None),
    )
    return jax.shard_map(
        shards,
        mesh=mesh,
        in_specs=placed,
        out_specs=(
            P(("grp", "dev"), None, None),
            P(None, None, "dev"),
            P(None, "dev"),
            P("dev"),
            P("dev"),
        ),
        check_vma=False,
    )
```

```python
import functools

import jax
import jax.numpy as jnp
from jax import lax
from jax.experimental import pallas as pl
from jax.experimental.pallas import tpu as pltpu
from jax.sharding import PartitionSpec as P

F32 = jnp.float32
BF16 = jnp.bfloat16
GROUP = 8
MIN_SAMPLES = 288
MIB = 1 << 20


def gelu_and_slope(value):
    size = jnp.abs(value)
    bell = jnp.exp(value * value * -0.5)
    base = 1.0 + size * (0.3275911 * 0.7071067811865476)
    frac = pl.reciprocal(base, approx=True)
    frac = frac * (2.0 - base * frac)
    poly = 0.5 * 1.061405429
    for coef in (-1.453152027, 1.421413741, -0.284496736, 0.254829592):
        poly = poly * frac + 0.5 * coef
    tail = poly * frac * bell
    gelu = jnp.maximum(value, 0.0) - size * tail
    phi = jnp.where(value < 0.0, tail, 1.0 - tail)
    return gelu, phi + value * bell * 0.3989422804014327


def rows_first(a, b):
    return lax.dot_general(a, b, (((0,), (0,)), ((), ())), preferred_element_type=F32)


def cols_both(a, b):
    return lax.dot_general(a, b, (((1,), (1,)), ((), ())), preferred_element_type=F32)


def dot(a, b):
    return jnp.dot(a, b, preferred_element_type=F32)


def iota(shape, dim):
    return lax.broadcasted_iota(jnp.int32, shape, dim)


def onehot(mask):
    return mask.astype(F32).astype(BF16)


def copies(sources, targets, sems):
    started = [pltpu.make_async_copy(source, target, sems.at[i]) for i, (source, target) in enumerate(zip(sources, targets))]
    for copy in started:
        copy.start()
    return started


def deal_kernel(members, order_hbm, wave_hbm, out_ref, order_ref, wave_ref, sems):
    for copy in copies((order_hbm, wave_hbm), (order_ref, wave_ref), sems):
        copy.wait()
    rows = wave_ref.shape[0]
    share = rows // members
    own = order_ref[pl.ds(lax.axis_index("dev"), 1), :]
    picks = onehot(iota((rows, rows), 0) == own)
    row = iota((rows, rows), 0)
    column = iota((rows, rows), 1)
    swap = onehot(column == lax.rem(row, share) * members + row // share)
    choose = cols_both(swap, picks).astype(BF16)
    out_ref[...] = dot(choose, wave_ref[...]).astype(BF16).reshape(out_ref.shape)


def setup_kernel(members, frames0, order_ref, len_ref, w_ref, valid_ref, band_ref):
    rows = order_ref.shape[1]
    share = rows // members
    taps, chans = w_ref.shape
    stride = taps // 2
    dealt = iota((rows, members), 0)
    owner = onehot(dealt // share == iota((rows, members), 1))
    order_of = dot(owner, order_ref[...].astype(F32).astype(BF16))
    high = len_ref[...] // 16
    low = len_ref[...] - high * 16
    lens_of = dot(owner, high.astype(F32).astype(BF16)) * 16.0 + dot(owner, low.astype(F32).astype(BF16))
    row = iota((rows, rows), 0)
    column = iota((rows, rows), 1)
    mine = column == lax.rem(row, share) * members + lax.axis_index("dev")
    index = jnp.sum(jnp.where(mine, order_of, 0.0), axis=1, keepdims=True)
    picked = column == index.astype(jnp.int32)
    lens = jnp.sum(jnp.where(picked, lens_of, 0.0), axis=1, keepdims=True).astype(jnp.int32)
    valid = (lens - taps) // stride + 1
    valid_ref[...] = jnp.broadcast_to(valid, valid_ref.shape)
    depth = band_ref.shape[0]
    for f in range(GROUP):
        spread = onehot(iota((depth, taps), 0) == iota((depth, taps), 1) + stride * f)
        band_ref[:, f * chans : (f + 1) * chans] = dot(spread, w_ref[...]).astype(BF16)


def forward_kernel(
    frames0,
    frames1,
    taps,
    reverse,
    wave_ref,
    valid_ref,
    band_ref,
    gain_hbm,
    bias_hbm,
    w_hbm,
    cot_hbm,
    feat_ref,
    even_ref,
    odd_ref,
    normed_ref,
    slope_ref,
    inv_ref,
    patch_ref,
    grad_ref,
    grad_t_ref,
    pre0,
    pre1,
    gain_ref,
    bias_ref,
    w_ref,
    cot_ref,
    sems,
):
    waiting = copies((gain_hbm, bias_hbm, w_hbm, cot_hbm), (gain_ref, bias_ref, w_ref, cot_ref), sems)
    rows, samp = wave_ref.shape
    chans = gain_ref.shape[1]
    stride = taps // 2
    depth = band_ref.shape[0]
    groups = pre0.shape[0]
    width = pre0.shape[2] // GROUP
    min_valid = (MIN_SAMPLES - taps) // stride + 1
    free_groups = min(min_valid // GROUP, frames0 // GROUP)
    full_groups = frames0 // GROUP
    wave = wave_ref[...]
    for g in range(groups):
        pick = onehot(iota((samp, depth), 0) == iota((samp, depth), 1) + GROUP * stride * g)
        patch_ref[g] = dot(wave, pick).astype(BF16)
    patches = patch_ref[...].reshape(groups * rows, depth)

    for block in range(chans // width):
        lanes = slice(block * width, (block + 1) * width)
        for f in range(GROUP):
            cols = slice(f * chans + block * width, f * chans + (block + 1) * width)
            pre0[:, :, f * width : (f + 1) * width] = dot(patches, band_ref[:, cols]).reshape(groups, rows, width)
        valid = jnp.broadcast_to(valid_ref[:, :1], (rows, width))
        count = valid.astype(F32)

        def frame(g, f):
            return pre0[g, :, f * width : (f + 1) * width]

        def over_frames(body, init):
            def step(masked, g, carry):
                for f in range(GROUP):
                    carry = body(carry, g, f, masked)
                return carry

            carry = lax.fori_loop(0, free_groups, functools.partial(step, False), init)
            carry = lax.fori_loop(free_groups, full_groups, functools.partial(step, True), carry)
            for f in range(frames0 - full_groups * GROUP):
                carry = body(carry, full_groups, f, True)
            return carry

        def masked_to(value, g, f, masked):
            return jnp.where(valid > g * GROUP + f, value, 0.0) if masked else value

        def add_mean(total, g, f, masked):
            return total + masked_to(frame(g, f), g, f, masked)

        mean = over_frames(add_mean, jnp.zeros((rows, width), F32)) / count

        def add_var(total, g, f, masked):
            centred = masked_to(frame(g, f) - mean, g, f, masked)
            return total + centred * centred

        var = over_frames(add_var, jnp.zeros((rows, width), F32)) / count
        inv = lax.rsqrt(var + 1e-05)
        inv_ref[:, lanes] = inv
        if block == 0:
            waiting[0].wait()
            waiting[1].wait()
        gain = jnp.broadcast_to(gain_ref[:, lanes], (rows, width))
        bias = jnp.broadcast_to(bias_ref[:, lanes], (rows, width))

        def finish(carry, g, f, masked):
            normed = (frame(g, f) - mean) * inv
            gelu, slope = gelu_and_slope(normed * gain + bias)
            t = g * GROUP + f
            normed_ref[t, :, lanes] = masked_to(normed, g, f, masked)
            slope_ref[t, :, lanes] = masked_to(slope, g, f, masked)
            act_ref = odd_ref if f % 2 else even_ref
            act_ref[g * (GROUP // 2) + f // 2, :, lanes] = masked_to(gelu, g, f, masked).astype(BF16)
            return carry

        over_frames(finish, 0)
    for ref, used in ((even_ref, (frames0 + 1) // 2), (odd_ref, frames0 // 2)):
        ref[used:] = jnp.zeros((ref.shape[0] - used,) + ref.shape[1:], BF16)

    waiting[2].wait()
    waiting[3].wait()
    grad_ref[0] = jnp.zeros(grad_ref.shape[1:], BF16)
    grad_ref[frames1 + 1] = jnp.zeros(grad_ref.shape[1:], BF16)
    padded = grad_t_ref.shape[1]
    used = frames1 * rows
    grad_t_ref[:, (used // 128) * 128 :] = jnp.zeros((chans, padded - (used // 128) * 128), BF16)
    valid = jnp.broadcast_to(valid_ref[:, :1], (rows, chans))
    valid1 = lax.shift_right_arithmetic(valid - 3, 1) + 1
    chunk = 12
    for first in range(0, frames1 - chunk + 1, chunk):
        count = chunk if first + 2 * chunk <= frames1 else frames1 - first
        size = count * rows
        total = dot(even_ref[first : first + count].reshape(size, chans), w_ref[0])
        total += dot(odd_ref[first : first + count].reshape(size, chans), w_ref[1])
        total += dot(even_ref[first + 1 : first + count + 1].reshape(size, chans), w_ref[2])
        pre1[:count] = total.reshape(count, rows, chans)

        def activate(u, carry):
            gelu, slope = gelu_and_slope(pre1[u])
            keep = valid1 > u + first
            feat_ref[u + first] = jnp.where(keep, gelu, 0.0).astype(BF16)
            grad = cot_ref[u + first].astype(F32) * slope
            grad_ref[u + first + 1] = jnp.where(keep, grad, 0.0).astype(BF16)
            return carry

        lax.fori_loop(0, count, activate, 0)
        turned = grad_ref[first + 1 : first + 1 + count].reshape(size, chans).T
        slab = chans // len(reverse)
        for place, source in enumerate(reverse):
            grad_t_ref[place * slab : (place + 1) * slab, first * rows : first * rows + size] = turned[
                source * slab : (source + 1) * slab
            ]


def outer_kernel(even_ref, odd_ref, grad_t_ref, keep_ref, send_ref):
    frames = grad_t_ref.shape[1] // even_ref.shape[1]
    rows, chans = even_ref.shape[1:]
    half = chans // 2
    core = lax.rem(lax.axis_index("grp"), 2)
    turned = grad_t_ref[...]
    for tap, (ref, skip) in enumerate(((even_ref, 0), (odd_ref, 0), (even_ref, 1))):
        for side, out_ref in ((core, keep_ref), (1 - core, send_ref)):
            lanes = pl.ds(pl.multiple_of(side * half, half), half)
            acts = ref[skip : skip + frames, :, lanes].reshape(frames * rows, half)
            out_ref[:, tap * half : (tap + 1) * half] = dot(turned, acts).astype(out_ref.dtype)


def backward_kernel(
    frames0,
    frames1,
    taps,
    valid_ref,
    normed_ref,
    slope_ref,
    inv_ref,
    patch_ref,
    grad_ref,
    gain_ref,
    w_ref,
    out_ref,
    lift,
    dpre0,
    spread,
):
    groups, rows, depth = patch_ref.shape
    chans = gain_ref.shape[1]
    stride = taps // 2
    width = dpre0.shape[2] // GROUP
    full_groups = frames0 // GROUP
    patches = patch_ref[...].reshape(groups * rows, depth)
    evens = (frames0 + 1) // 2
    odds = frames0 // 2
    first = grad_ref[1 : evens + 1].reshape(evens * rows, chans)
    second = grad_ref[1 : odds + 1].reshape(odds * rows, chans)
    third = grad_ref[0:evens].reshape(evens * rows, chans)
    for block in range(chans // width):
        lanes = slice(block * width, (block + 1) * width)
        lift[0, :evens] = (cols_both(first, w_ref[0, lanes]) + cols_both(third, w_ref[2, lanes])).reshape(
            evens, rows, width
        )
        lift[1, :odds] = cols_both(second, w_ref[1, lanes]).reshape(odds, rows, width)

        def slopes(parity, e, carry):
            bias_sum, gain_sum = carry
            t = 2 * e + parity
            dlift = lift[parity, e] * slope_ref[t, :, lanes]
            lift[parity, e] = dlift
            return bias_sum + dlift, gain_sum + dlift * normed_ref[t, :, lanes]

        def both(e, carry):
            return slopes(1, e, slopes(0, e, carry))

        zero = jnp.zeros((rows, width), F32)
        carry = lax.fori_loop(0, odds, both, (zero, zero))
        if evens > odds:
            carry = slopes(0, odds, carry)
        bias_sum, gain_sum = carry
        out_ref[taps : taps + 1, lanes] = jnp.sum(gain_sum, axis=0, keepdims=True)
        out_ref[taps + 1 : taps + 2, lanes] = jnp.sum(bias_sum, axis=0, keepdims=True)
        valid = jnp.broadcast_to(valid_ref[:, :1], (rows, width))
        count = valid.astype(F32)
        scale = inv_ref[:, lanes] * gain_ref[:, lanes]
        bias_sum = bias_sum / count
        gain_sum = gain_sum / count

        def finish(g, f):
            t = g * GROUP + f
            dlift = lift[f % 2, g * (GROUP // 2) + f // 2]
            value = scale * (dlift - bias_sum - normed_ref[t, :, lanes] * gain_sum)
            dpre0[g, :, f * width : (f + 1) * width] = jnp.where(valid > t, value, 0.0).astype(BF16)

        def whole(g, carry):
            for f in range(GROUP):
                finish(g, f)
            return carry

        lax.fori_loop(0, full_groups, whole, 0)
        rest = frames0 - full_groups * GROUP
        for f in range(rest):
            finish(full_groups, f)
        if full_groups < groups:
            dpre0[full_groups, :, rest * width :] = jnp.zeros((rows, (GROUP - rest) * width), BF16)
        spread[...] = rows_first(patches, dpre0[...].reshape(groups * rows, GROUP * width))
        total = jnp.zeros((taps, width), F32)
        for f in range(GROUP):
            total += spread[stride * f : stride * f + taps, f * width : (f + 1) * width]
        out_ref[:taps, lanes] = total


def pack(value):
    high = value.astype(BF16)
    return high, (value - high.astype(F32)).astype(BF16)


def plane_kernel(keep_ref, got_ref, own_ref, *send_refs):
    size = own_ref.shape[0]
    place = lax.rem(lax.axis_index("dev"), 4)

    def quarter(index):
        lines = pl.ds(pl.multiple_of(index * size, size), size)
        return keep_ref[lines, :] + got_ref[lines, :].astype(F32)

    own_ref[...] = quarter(place)
    for offset, send_ref in enumerate(send_refs, 1):
        send_ref[...] = quarter(jnp.bitwise_xor(place, offset)).astype(BF16)


def gather_kernel(
    bit, own_ref, got1, got2, got3, small_ref, small1, small2, small3, next_ref, send_ref, total_ref
):
    half = next_ref.shape[0]
    side = lax.rem(lax.shift_right_logical(lax.axis_index("dev"), bit), 2)

    def part(index):
        lines = pl.ds(pl.multiple_of(index * half, half), half)
        return own_ref[lines, :] + (
            got1[lines, :].astype(F32) + got2[lines, :].astype(F32) + got3[lines, :].astype(F32)
        )

    next_ref[...] = part(side)
    send_ref[:half] = part(1 - side).astype(BF16)
    total = (small_ref[...] + small1[...]) + (small2[...] + small3[...])
    total_ref[...] = total
    write_small(send_ref, half, total)


def write_small(send_ref, first, total):
    lines, chans = total.shape
    send_ref[first:, chans:] = jnp.zeros((2 * lines, send_ref.shape[1] - chans), BF16)
    for place, term in enumerate(pack(total)):
        send_ref[first + place * lines : first + (place + 1) * lines, :chans] = term


def read_small(got_ref, first, lines, chans):
    return (
        got_ref[first : first + lines, :chans].astype(F32)
        + got_ref[first + lines : first + 2 * lines, :chans].astype(F32)
    )


def fold_kernel(bit, last, keep_ref, got_ref, small_ref, *out_refs):
    lines, chans = small_ref.shape
    half = keep_ref.shape[0]
    total = small_ref[...] + read_small(got_ref, half, lines, chans)
    total_ref, send_ref = out_refs[0], out_refs[1]
    total_ref[...] = total
    if last:
        send_ref[:half] = (keep_ref[...] + got_ref[:half].astype(F32)).astype(BF16)
        write_small(send_ref, half, total)
        return
    next_ref = out_refs[2]
    size = next_ref.shape[0]
    side = lax.rem(lax.shift_right_logical(lax.axis_index("dev"), bit), 2)

    def part(index):
        here = pl.ds(pl.multiple_of(index * size, size), size)
        return keep_ref[here, :] + got_ref[here, :].astype(F32)

    next_ref[...] = part(side)
    send_ref[:size] = part(1 - side).astype(BF16)
    write_small(send_ref, size, total)


def across_kernel(last, mine_ref, got_ref, small_ref, total_ref, out_ref):
    lines, chans = small_ref.shape
    half = mine_ref.shape[0] - 2 * lines
    total = read_small(mine_ref, half, lines, chans) + read_small(got_ref, half, lines, chans)
    value = mine_ref[:half].astype(F32) + got_ref[:half].astype(F32)
    total_ref[...] = total
    out_ref[:half] = value.astype(out_ref.dtype)
    if last:
        out_ref[half:, chans:] = jnp.zeros((lines, out_ref.shape[1] - chans), F32)
        out_ref[half:, :chans] = total
    else:
        write_small(out_ref, half, total)


def join_kernel(members, taps, own_ref, other_ref, out_ref, first_ref, gain_ref, bias_ref):
    second, size, chans = out_ref.shape
    half = chans // 2
    core = lax.rem(lax.axis_index("grp"), 2)
    for tap in range(second):
        lanes = slice(tap * half, (tap + 1) * half)
        out_ref[tap, :, pl.ds(pl.multiple_of(core * half, half), half)] = own_ref[:size, lanes]
        out_ref[tap, :, pl.ds(pl.multiple_of((1 - core) * half, half), half)] = other_ref[:size, lanes]
    wide = max(size, 128)
    member = lax.axis_index("dev")
    block = pl.ds(pl.multiple_of(member // (wide // size) * wide, wide), wide)
    total = own_ref[size:, block] + other_ref[size:, block]
    value = total[:, :size]
    for place in range(1, wide // size):
        value = jnp.where(lax.rem(member, wide // size) == place, total[:, place * size : (place + 1) * size], value)
    first_ref[...] = value[:taps]
    gain_ref[...] = value[taps : taps + 1]
    bias_ref[...] = value[taps + 1 : taps + 2]


def call(kernel, outs, args, scratch=(), limit=24, flops=0, touched=0, outside=()):
    vmem = pl.BlockSpec(memory_space=pltpu.VMEM)
    args = [pltpu.with_memory_space_constraint(arg, pltpu.HBM) if i in outside else arg for i, arg in enumerate(args)]
    return pl.pallas_call(
        kernel,
        out_shape=[
            jax.ShapeDtypeStruct(out[0], out[1]) if len(out) > 2 else pltpu.VMEM(out[0], out[1]) for out in outs
        ],
        in_specs=[pl.BlockSpec(memory_space=pltpu.HBM) if i in outside else vmem for i in range(len(args))],
        out_specs=[vmem] * len(outs),
        scratch_shapes=[pltpu.VMEM(*entry) if isinstance(entry, tuple) else entry for entry in scratch],
        compiler_params=pltpu.CompilerParams(vmem_limit_bytes=limit * MIB),
        cost_estimate=pl.CostEstimate(flops=flops, bytes_accessed=touched, transcendentals=0),
    )(*args)


def swap(value, axis, offset):
    size = lax.axis_size(axis)
    return lax.ppermute(value, axis, [(i, i ^ offset) for i in range(size)])


def shards(wave, lengths, order, w_first, norm_gain, norm_bias, w_second, cot):
    members = lax.axis_size("dev")
    groups_of = lax.axis_size("grp")
    rows, samp = wave.shape
    taps, chans = w_first.shape
    taps_second = w_second.shape[0]
    stride = taps // 2
    frames0 = (samp - taps) // stride + 1
    frames1 = (frames0 - taps_second) // 2 + 1
    groups = -(-frames0 // GROUP)
    depth = 128
    width = 256
    dev_bits = members.bit_length() - 1
    grp_bits = groups_of.bit_length() - 1

    outgoing = call(
        functools.partial(deal_kernel, members),
        [((members, rows // members, samp), BF16)],
        [order, wave],
        scratch=[(order.shape, order.dtype), (wave.shape, wave.dtype), pltpu.SemaphoreType.DMA((2,))],
        outside=(0, 1),
    )[0]
    arrived = lax.all_to_all(outgoing, "dev", split_axis=0, concat_axis=0, tiled=True).reshape(rows, samp)
    valid, band = call(
        functools.partial(setup_kernel, members, frames0),
        [((rows, 128), jnp.int32), ((depth, GROUP * chans), BF16)],
        [order, lengths.reshape(members, rows), w_first],
    )
    gain = norm_gain.reshape(1, chans)
    bias = norm_bias.reshape(1, chans)
    cot_t = cot.transpose(1, 0, 2)
    pad_frames = -(-frames1 // 4) * 4
    places = [0] * members
    for dev in range(members):
        places[dev % 4 * (members // 4) + dev // 4] = dev
    feat, even, odd, normed, slope, inv, patch, grad, grad_t = call(
        functools.partial(forward_kernel, frames0, frames1, taps, places),
        [
            ((frames1, rows, chans), BF16, "out"),
            ((pad_frames + 1, rows, chans), BF16),
            ((pad_frames, rows, chans), BF16),
            ((frames0, rows, chans), F32),
            ((frames0, rows, chans), F32),
            ((rows, chans), F32),
            ((groups, rows, depth), BF16),
            ((frames1 + 2, rows, chans), BF16),
            ((chans, pad_frames * rows), BF16),
        ],
        [arrived, valid, band, gain, bias, w_second, cot_t],
        scratch=[
            ((groups, rows, GROUP * width), F32),
            ((16, rows, chans), F32),
            (gain.shape, F32),
            (bias.shape, F32),
            (w_second.shape, BF16),
            (cot_t.shape, BF16),
            pltpu.SemaphoreType.DMA((4,)),
        ],
        outside=(3, 4, 5, 6),
    )
    wide = taps_second * chans // 2
    keep, send = call(outer_kernel, [((chans, wide), F32), ((chans, wide), BF16)], [even, odd, grad_t], flops=1 << 30)
    got = swap(send, "grp", 1)
    quarter = chans // 4
    own, *sends = call(plane_kernel, [((quarter, wide), F32)] + [((quarter, wide), BF16)] * 3, [keep, got])
    gots = [swap(part, "dev", offset) for offset, part in enumerate(sends, 1)]
    small = call(
        functools.partial(backward_kernel, frames0, frames1, taps),
        [((16, chans), F32)],
        [valid, normed, slope, inv, patch, grad, gain, w_second],
        scratch=[
            ((2, (frames0 + 1) // 2, rows, width), F32),
            ((groups, rows, GROUP * width), BF16),
            ((depth, GROUP * width), F32),
        ],
        flops=1 << 32,
    )[0]
    smalls = [swap(small, "dev", offset) for offset in (1, 2, 3)]
    size = quarter // 2
    extra = 2 * small.shape[0]
    keep, send, small = call(
        functools.partial(gather_kernel, dev_bits - 1),
        [((size, wide), F32), ((size + extra, wide), BF16), (small.shape, F32)],
        [own, *gots, small, *smalls],
    )
    for bit in range(dev_bits - 1, 1, -1):
        got = swap(send, "dev", 1 << bit)
        last = bit == 2
        outs = [(small.shape, F32), ((size + extra, wide), BF16)]
        if not last:
            size //= 2
            outs = [(small.shape, F32), ((size + extra, wide), BF16), ((size, wide), F32)]
        small, send, *rest = call(functools.partial(fold_kernel, bit - 1, last), outs, [keep, got, small])
        keep = rest[0] if rest else None
    for bit in range(1, grp_bits):
        got = swap(send, "grp", 1 << bit)
        last = bit == grp_bits - 1
        shape = ((size + small.shape[0], wide), F32) if last else (send.shape, BF16)
        small, send = call(functools.partial(across_kernel, last), [(small.shape, F32), shape], [send, got, small])
    other = swap(send, "grp", 1)
    grad_second, grad_first, grad_gain, grad_bias = call(
        functools.partial(join_kernel, members, taps),
        [
            ((taps_second, size, chans), F32, "out"),
            ((taps, size), F32, "out"),
            ((1, size), F32, "out"),
            ((1, size), F32, "out"),
        ],
        [send, other],
    )
    return (
        feat.transpose(1, 0, 2),
        grad_second.transpose(0, 2, 1),
        grad_first,
        grad_gain.reshape(size),
        grad_bias.reshape(size),
    )


def solution(mesh):
    placed = (
        P(("grp", "dev"), None),
        P("grp"),
        P("grp", None),
        P(),
        P(),
        P(),
        P(),
        P(("grp", "dev"), None, None),
    )
    return jax.shard_map(
        shards,
        mesh=mesh,
        in_specs=placed,
        out_specs=(
            P(("grp", "dev"), None, None),
            P(None, None, "dev"),
            P(None, "dev"),
            P("dev"),
            P("dev"),
        ),
        check_vma=False,
    )
```

```python
import functools

import jax
import jax.numpy as jnp
from jax import lax
from jax.experimental import pallas as pl
from jax.experimental.pallas import tpu as pltpu
from jax.sharding import PartitionSpec as P

F32 = jnp.float32
BF16 = jnp.bfloat16
GROUP = 8
MIN_SAMPLES = 288
MIB = 1 << 20


def gelu_and_slope(value):
    size = jnp.abs(value)
    bell = jnp.exp(value * value * -0.5)
    base = 1.0 + size * (0.3275911 * 0.7071067811865476)
    frac = pl.reciprocal(base, approx=True)
    frac = frac * (2.0 - base * frac)
    poly = 0.5 * 1.061405429
    for coef in (-1.453152027, 1.421413741, -0.284496736, 0.254829592):
        poly = poly * frac + 0.5 * coef
    tail = poly * frac * bell
    gelu = jnp.maximum(value, 0.0) - size * tail
    phi = jnp.where(value < 0.0, tail, 1.0 - tail)
    return gelu, phi + value * bell * 0.3989422804014327


def rows_first(a, b):
    return lax.dot_general(a, b, (((0,), (0,)), ((), ())), preferred_element_type=F32)


def cols_both(a, b):
    return lax.dot_general(a, b, (((1,), (1,)), ((), ())), preferred_element_type=F32)


def dot(a, b):
    return jnp.dot(a, b, preferred_element_type=F32)


def iota(shape, dim):
    return lax.broadcasted_iota(jnp.int32, shape, dim)


def onehot(mask):
    return mask.astype(F32).astype(BF16)


def copies(sources, targets, sems):
    started = [pltpu.make_async_copy(source, target, sems.at[i]) for i, (source, target) in enumerate(zip(sources, targets))]
    for copy in started:
        copy.start()
    return started


def setup_kernel(
    members,
    order_hbm,
    len_hbm,
    w_hbm,
    wave_hbm,
    valid_ref,
    band_ref,
    near_ref,
    far_ref,
    own_ref,
    order_ref,
    len_ref,
    w_ref,
    sems,
):
    for copy in copies((order_hbm, len_hbm, w_hbm, wave_hbm), (order_ref, len_ref, w_ref, own_ref), sems):
        copy.wait()
    rows = order_ref.shape[1]
    share = rows // members
    taps, chans = w_ref.shape
    stride = taps // 2
    owner = onehot(iota((rows, members), 0) // share == iota((rows, members), 1))
    order_of = dot(owner, order_ref[...].astype(F32).astype(BF16))
    slot = iota((rows, rows), 1) - lax.rem(iota((rows, rows), 0), share) * members
    owner_first = iota((rows, 1), 0) // share * rows
    column = iota((rows, members * rows), 1)
    member = lax.axis_index("dev")
    for target, out_ref in ((member, near_ref), (jnp.bitwise_xor(member, members // 2), far_ref)):
        local = jnp.sum(jnp.where(slot == target, order_of, 0.0), axis=1, keepdims=True).astype(jnp.int32)
        picked = column == owner_first + local
        out_ref[...] = onehot(picked)
        if out_ref is near_ref:
            lens = jnp.sum(jnp.where(picked, len_ref[...], 0), axis=1, keepdims=True)
    valid = (lens - taps) // stride + 1
    valid_ref[...] = jnp.broadcast_to(valid, valid_ref.shape)
    depth = band_ref.shape[0]
    for f in range(GROUP):
        spread = onehot(iota((depth, taps), 0) == iota((depth, taps), 1) + stride * f)
        band_ref[:, f * chans : (f + 1) * chans] = dot(spread, w_ref[...]).astype(BF16)


def pick_kernel(offsets, near_ref, far_ref, *refs):
    waves, (mine_ref, send_ref, all_ref) = refs[:-3], refs[-3:]
    rows = mine_ref.shape[0]
    all_ref[...] = jnp.zeros(all_ref.shape, BF16)
    for offset, wave_ref in zip(offsets, waves):
        first = pl.multiple_of(jnp.bitwise_xor(lax.axis_index("dev"), offset) * rows, rows)
        all_ref[pl.ds(first, rows), :] = wave_ref[...]
    mine_ref[...] = dot(near_ref[...], all_ref[...]).astype(BF16)
    send_ref[...] = dot(far_ref[...], all_ref[...]).astype(BF16)


def forward_kernel(
    frames0,
    frames1,
    taps,
    reverse,
    near_ref,
    far_ref,
    valid_ref,
    band_ref,
    gain_hbm,
    bias_hbm,
    w_hbm,
    cot_hbm,
    feat_ref,
    even_ref,
    odd_ref,
    normed_ref,
    slope_ref,
    inv_ref,
    patch_ref,
    grad_ref,
    grad_t_ref,
    gain_ref,
    w_ref,
    pre0,
    pre1,
    bias_ref,
    cot_ref,
    sems,
):
    waiting = copies((gain_hbm, bias_hbm, w_hbm, cot_hbm), (gain_ref, bias_ref, w_ref, cot_ref), sems)
    rows, samp = near_ref.shape
    chans = gain_ref.shape[1]
    stride = taps // 2
    depth = band_ref.shape[0]
    groups = pre0.shape[0]
    width = pre0.shape[2] // GROUP
    min_valid = (MIN_SAMPLES - taps) // stride + 1
    free_groups = min(min_valid // GROUP, frames0 // GROUP)
    full_groups = frames0 // GROUP
    wave = near_ref[...] + far_ref[...]
    for g in range(groups):
        pick = onehot(iota((samp, depth), 0) == iota((samp, depth), 1) + GROUP * stride * g)
        patch_ref[g] = dot(wave, pick).astype(BF16)
    patches = patch_ref[...].reshape(groups * rows, depth)

    for block in range(chans // width):
        lanes = slice(block * width, (block + 1) * width)
        for f in range(GROUP):
            cols = slice(f * chans + block * width, f * chans + (block + 1) * width)
            pre0[:, :, f * width : (f + 1) * width] = dot(patches, band_ref[:, cols]).reshape(groups, rows, width)
        valid = jnp.broadcast_to(valid_ref[:, :1], (rows, width))
        count = valid.astype(F32)

        def frame(g, f):
            return pre0[g, :, f * width : (f + 1) * width]

        def over_frames(body, init):
            def step(masked, g, carry):
                for f in range(GROUP):
                    carry = body(carry, g, f, masked)
                return carry

            carry = lax.fori_loop(0, free_groups, functools.partial(step, False), init)
            carry = lax.fori_loop(free_groups, full_groups, functools.partial(step, True), carry)
            for f in range(frames0 - full_groups * GROUP):
                carry = body(carry, full_groups, f, True)
            return carry

        def masked_to(value, g, f, masked):
            return jnp.where(valid > g * GROUP + f, value, 0.0) if masked else value

        def add_mean(total, g, f, masked):
            return total + masked_to(frame(g, f), g, f, masked)

        mean = over_frames(add_mean, jnp.zeros((rows, width), F32)) / count

        def add_var(total, g, f, masked):
            centred = masked_to(frame(g, f) - mean, g, f, masked)
            return total + centred * centred

        var = over_frames(add_var, jnp.zeros((rows, width), F32)) / count
        inv = lax.rsqrt(var + 1e-05)
        inv_ref[:, lanes] = inv
        if block == 0:
            waiting[0].wait()
            waiting[1].wait()
        gain = jnp.broadcast_to(gain_ref[:, lanes], (rows, width))
        bias = jnp.broadcast_to(bias_ref[:, lanes], (rows, width))

        def finish(carry, g, f, masked):
            normed = (frame(g, f) - mean) * inv
            gelu, slope = gelu_and_slope(normed * gain + bias)
            t = g * GROUP + f
            normed_ref[t, :, lanes] = masked_to(normed, g, f, masked)
            slope_ref[t, :, lanes] = masked_to(slope, g, f, masked)
            act_ref = odd_ref if f % 2 else even_ref
            act_ref[g * (GROUP // 2) + f // 2, :, lanes] = masked_to(gelu, g, f, masked).astype(BF16)
            return carry

        over_frames(finish, 0)
    for ref, used in ((even_ref, (frames0 + 1) // 2), (odd_ref, frames0 // 2)):
        ref[used:] = jnp.zeros((ref.shape[0] - used,) + ref.shape[1:], BF16)

    waiting[2].wait()
    waiting[3].wait()
    grad_ref[0] = jnp.zeros(grad_ref.shape[1:], BF16)
    grad_ref[frames1 + 1] = jnp.zeros(grad_ref.shape[1:], BF16)
    padded = grad_t_ref.shape[1]
    used = frames1 * rows
    grad_t_ref[:, (used // 128) * 128 :] = jnp.zeros((chans, padded - (used // 128) * 128), BF16)
    valid = jnp.broadcast_to(valid_ref[:, :1], (rows, chans))
    valid1 = lax.shift_right_arithmetic(valid - 3, 1) + 1
    chunk = 12
    for first in range(0, frames1 - chunk + 1, chunk):
        count = chunk if first + 2 * chunk <= frames1 else frames1 - first
        size = count * rows
        total = dot(even_ref[first : first + count].reshape(size, chans), w_ref[0])
        total += dot(odd_ref[first : first + count].reshape(size, chans), w_ref[1])
        total += dot(even_ref[first + 1 : first + count + 1].reshape(size, chans), w_ref[2])
        pre1[:count] = total.reshape(count, rows, chans)

        def activate(u, carry):
            gelu, slope = gelu_and_slope(pre1[u])
            keep = valid1 > u + first
            feat_ref[u + first] = jnp.where(keep, gelu, 0.0).astype(BF16)
            grad = cot_ref[u + first].astype(F32) * slope
            grad_ref[u + first + 1] = jnp.where(keep, grad, 0.0).astype(BF16)
            return carry

        lax.fori_loop(0, count, activate, 0)
        turned = grad_ref[first + 1 : first + 1 + count].reshape(size, chans).T
        slab = chans // len(reverse)
        for place, source in enumerate(reverse):
            grad_t_ref[place * slab : (place + 1) * slab, first * rows : first * rows + size] = turned[
                source * slab : (source + 1) * slab
            ]


def outer_kernel(even_ref, odd_ref, grad_t_ref, keep_ref, send_ref):
    frames = grad_t_ref.shape[1] // even_ref.shape[1]
    rows, chans = even_ref.shape[1:]
    half = chans // 2
    core = lax.rem(lax.axis_index("grp"), 2)
    turned = grad_t_ref[...]
    for tap, (ref, skip) in enumerate(((even_ref, 0), (odd_ref, 0), (even_ref, 1))):
        for side, out_ref in ((core, keep_ref), (1 - core, send_ref)):
            lanes = pl.ds(pl.multiple_of(side * half, half), half)
            acts = ref[skip : skip + frames, :, lanes].reshape(frames * rows, half)
            out_ref[:, tap * half : (tap + 1) * half] = dot(turned, acts).astype(out_ref.dtype)


def input_kernel(grad_ref, w_ref, even_ref, odd_ref):
    evens, rows, chans = even_ref.shape
    odds = odd_ref.shape[0]
    first = grad_ref[1 : evens + 1].reshape(evens * rows, chans)
    third = grad_ref[0:evens].reshape(evens * rows, chans)
    even_ref[...] = (cols_both(first, w_ref[0]) + cols_both(third, w_ref[2])).reshape(even_ref.shape)
    second = grad_ref[1 : odds + 1].reshape(odds * rows, chans)
    odd_ref[...] = cols_both(second, w_ref[1]).reshape(odd_ref.shape)


def backward_kernel(
    frames0,
    taps,
    valid_ref,
    normed_ref,
    slope_ref,
    inv_ref,
    patch_ref,
    even_ref,
    odd_ref,
    gain_ref,
    out_ref,
    lift,
    dpre0,
    spread,
):
    groups, rows, depth = patch_ref.shape
    chans = gain_ref.shape[1]
    stride = taps // 2
    width = dpre0.shape[2] // GROUP
    full_groups = frames0 // GROUP
    rest = frames0 - full_groups * GROUP
    patches = patch_ref[...].reshape(groups * rows, depth)
    for block in range(chans // width):
        lanes = slice(block * width, (block + 1) * width)

        def slopes(g, f, carry):
            bias_sum, gain_sum = carry
            t = g * GROUP + f
            dact = (odd_ref if f % 2 else even_ref)[g * (GROUP // 2) + f // 2, :, lanes]
            dlift = dact * slope_ref[t, :, lanes]
            lift[t] = dlift
            return bias_sum + dlift, gain_sum + dlift * normed_ref[t, :, lanes]

        def add(g, carry):
            for f in range(GROUP):
                carry = slopes(g, f, carry)
            return carry

        zero = jnp.zeros((rows, width), F32)
        carry = lax.fori_loop(0, full_groups, add, (zero, zero))
        for f in range(rest):
            carry = slopes(full_groups, f, carry)
        bias_sum, gain_sum = carry
        out_ref[taps : taps + 1, lanes] = jnp.sum(gain_sum, axis=0, keepdims=True)
        out_ref[taps + 1 : taps + 2, lanes] = jnp.sum(bias_sum, axis=0, keepdims=True)
        valid = jnp.broadcast_to(valid_ref[:, :1], (rows, width))
        count = valid.astype(F32)
        scale = inv_ref[:, lanes] * gain_ref[:, lanes]
        bias_sum = bias_sum / count
        gain_sum = gain_sum / count

        def finish(g, f):
            t = g * GROUP + f
            value = scale * (lift[t] - bias_sum - normed_ref[t, :, lanes] * gain_sum)
            dpre0[g, :, f * width : (f + 1) * width] = jnp.where(valid > t, value, 0.0).astype(BF16)

        def whole(g, carry):
            for f in range(GROUP):
                finish(g, f)
            return carry

        lax.fori_loop(0, full_groups, whole, 0)
        for f in range(rest):
            finish(full_groups, f)
        if full_groups < groups:
            dpre0[full_groups, :, rest * width :] = jnp.zeros((rows, (GROUP - rest) * width), BF16)
        spread[...] = rows_first(patches, dpre0[...].reshape(groups * rows, GROUP * width))
        total = jnp.zeros((taps, width), F32)
        for f in range(GROUP):
            total += spread[stride * f : stride * f + taps, f * width : (f + 1) * width]
        out_ref[:taps, lanes] = total


def plane_kernel(keep_ref, got_ref, later_ref, own_ref, *send_refs):
    size = own_ref.shape[0]
    place = lax.rem(lax.axis_index("dev"), 4)

    def quarter(index):
        lines = pl.ds(pl.multiple_of(index * size, size), size)
        return keep_ref[lines, :] + got_ref[lines, :].astype(F32)

    own_ref[...] = quarter(place)
    for offset, send_ref in enumerate(send_refs, 1):
        send_ref[...] = quarter(jnp.bitwise_xor(place, offset)).astype(BF16)


def gather_kernel(bit, own_ref, got1, got2, got3, small_ref, small_got, next_ref, send_ref, total_ref):
    half = next_ref.shape[0]
    side = lax.rem(lax.shift_right_logical(lax.axis_index("dev"), bit), 2)

    def part(index):
        lines = pl.ds(pl.multiple_of(index * half, half), half)
        return own_ref[lines, :] + (
            got1[lines, :].astype(F32) + got2[lines, :].astype(F32) + got3[lines, :].astype(F32)
        )

    next_ref[...] = part(side)
    send_ref[...] = part(1 - side).astype(BF16)
    total_ref[...] = small_ref[...] + small_got[...]


def fold_kernel(bit, keep_ref, got_ref, send_ref, next_ref):
    size = next_ref.shape[0]
    side = lax.rem(lax.shift_right_logical(lax.axis_index("dev"), bit), 2)

    def part(index):
        here = pl.ds(pl.multiple_of(index * size, size), size)
        return keep_ref[here, :] + got_ref[here, :].astype(F32)

    next_ref[...] = part(side)
    send_ref[...] = part(1 - side).astype(BF16)


def round_kernel(keep_ref, got_ref, small0, small1, small2, small3, send_ref, total_ref):
    send_ref[...] = (keep_ref[...] + got_ref[...].astype(F32)).astype(BF16)
    total_ref[...] = (small0[...] + small1[...]) + (small2[...] + small3[...])


def across_kernel(mine_ref, got_ref, *refs):
    out_ref = refs[2] if len(refs) > 2 else refs[0]
    out_ref[...] = (mine_ref[...].astype(F32) + got_ref[...].astype(F32)).astype(out_ref.dtype)
    if len(refs) > 2:
        refs[3][...] = refs[0][...] + refs[1][...]


def join_kernel(members, taps, own_ref, other_ref, small_ref, out_ref, first_ref, gain_ref, bias_ref):
    second, size, chans = out_ref.shape
    half = chans // 2
    core = lax.rem(lax.axis_index("grp"), 2)
    for tap in range(second):
        lanes = slice(tap * half, (tap + 1) * half)
        out_ref[tap, :, pl.ds(pl.multiple_of(core * half, half), half)] = own_ref[:, lanes]
        out_ref[tap, :, pl.ds(pl.multiple_of((1 - core) * half, half), half)] = other_ref[:, lanes]
    wide = max(size, 128)
    member = lax.axis_index("dev")
    block = pl.ds(pl.multiple_of(member // (wide // size) * wide, wide), wide)
    total = small_ref[:, block]
    value = total[:, :size]
    for place in range(1, wide // size):
        value = jnp.where(lax.rem(member, wide // size) == place, total[:, place * size : (place + 1) * size], value)
    first_ref[...] = value[:taps]
    gain_ref[...] = value[taps : taps + 1]
    bias_ref[...] = value[taps + 1 : taps + 2]


def call(kernel, outs, args, scratch=(), limit=24, flops=0, touched=0, outside=()):
    vmem = pl.BlockSpec(memory_space=pltpu.VMEM)
    args = [pltpu.with_memory_space_constraint(arg, pltpu.HBM) if i in outside else arg for i, arg in enumerate(args)]
    return pl.pallas_call(
        kernel,
        out_shape=[
            jax.ShapeDtypeStruct(out[0], out[1]) if len(out) > 2 else pltpu.VMEM(out[0], out[1]) for out in outs
        ],
        in_specs=[pl.BlockSpec(memory_space=pltpu.HBM) if i in outside else vmem for i in range(len(args))],
        out_specs=[vmem] * len(outs),
        scratch_shapes=[pltpu.VMEM(*entry) if isinstance(entry, tuple) else entry for entry in scratch],
        compiler_params=pltpu.CompilerParams(vmem_limit_bytes=limit * MIB),
        cost_estimate=pl.CostEstimate(flops=flops, bytes_accessed=touched, transcendentals=0),
    )(*args)


def swap(value, axis, offset):
    size = lax.axis_size(axis)
    return lax.ppermute(value, axis, [(i, i ^ offset) for i in range(size)])


def shards(wave, lengths, order, w_first, norm_gain, norm_bias, w_second, cot):
    members = lax.axis_size("dev")
    groups_of = lax.axis_size("grp")
    rows, samp = wave.shape
    taps, chans = w_first.shape
    taps_second = w_second.shape[0]
    stride = taps // 2
    frames0 = (samp - taps) // stride + 1
    frames1 = (frames0 - taps_second) // 2 + 1
    groups = -(-frames0 // GROUP)
    depth = 128
    width = 256
    dev_bits = members.bit_length() - 1
    grp_bits = groups_of.bit_length() - 1

    offsets = [0, 1, 2, 3]
    waves = [wave] + [swap(wave, "dev", offset) for offset in offsets[1:]]
    for bit in range(2, dev_bits - 1):
        offsets += [offset | (1 << bit) for offset in offsets]
        waves += [swap(held, "dev", 1 << bit) for held in waves]
    lens = lengths.reshape(1, members * rows)
    every = members * rows
    valid, band, near_sel, far_sel, own_wave = call(
        functools.partial(setup_kernel, members),
        [
            ((rows, 128), jnp.int32),
            ((depth, GROUP * chans), BF16),
            ((rows, every), BF16),
            ((rows, every), BF16),
            ((rows, samp), BF16),
        ],
        [order, lens, w_first, wave],
        scratch=[
            (order.shape, order.dtype),
            (lens.shape, lens.dtype),
            (w_first.shape, BF16),
            pltpu.SemaphoreType.DMA((4,)),
        ],
        outside=(0, 1, 2, 3),
    )
    near, send = call(
        functools.partial(pick_kernel, offsets),
        [((rows, samp), BF16), ((rows, samp), BF16)],
        [near_sel, far_sel, own_wave, *waves[1:]],
        scratch=[((every, samp), BF16)],
    )
    far = swap(send, "dev", members // 2)
    gain = norm_gain.reshape(1, chans)
    bias = norm_bias.reshape(1, chans)
    cot_t = cot.transpose(1, 0, 2)
    pad_frames = -(-frames1 // 4) * 4
    places = [0] * members
    for dev in range(members):
        places[dev % 4 * (members // 4) + dev // 4] = dev
    feat, even, odd, normed, slope, inv, patch, grad, grad_t, gain_in, w_in = call(
        functools.partial(forward_kernel, frames0, frames1, taps, places),
        [
            ((frames1, rows, chans), BF16, "out"),
            ((pad_frames + 1, rows, chans), BF16),
            ((pad_frames, rows, chans), BF16),
            ((frames0, rows, chans), F32),
            ((frames0, rows, chans), F32),
            ((rows, chans), F32),
            ((groups, rows, depth), BF16),
            ((frames1 + 2, rows, chans), BF16),
            ((chans, pad_frames * rows), BF16),
            ((1, chans), F32),
            (w_second.shape, BF16),
        ],
        [near, far, valid, band, gain, bias, w_second, cot_t],
        scratch=[
            ((groups, rows, GROUP * width), F32),
            ((16, rows, chans), F32),
            (bias.shape, F32),
            (cot_t.shape, BF16),
            pltpu.SemaphoreType.DMA((4,)),
        ],
        outside=(4, 5, 6, 7),
    )
    wide = taps_second * chans // 2
    keep, send = call(outer_kernel, [((chans, wide), F32), ((chans, wide), BF16)], [even, odd, grad_t], flops=1 << 30)
    got = swap(send, "grp", 1)
    evens, odds = (frames0 + 1) // 2, frames0 // 2
    dact_even, dact_odd = call(
        input_kernel,
        [((evens, rows, chans), F32), ((odds, rows, chans), F32)],
        [grad, w_in],
        flops=1 << 30,
    )
    quarter = chans // 4
    own, *sends = call(
        plane_kernel, [((quarter, wide), F32)] + [((quarter, wide), BF16)] * 3, [keep, got, dact_odd]
    )
    gots = [swap(part, "dev", offset) for offset, part in enumerate(sends, 1)]
    small = call(
        functools.partial(backward_kernel, frames0, taps),
        [((16, chans), F32)],
        [valid, normed, slope, inv, patch, dact_even, dact_odd, gain_in],
        scratch=[
            ((frames0, rows, width), F32),
            ((groups, rows, GROUP * width), BF16),
            ((depth, GROUP * width), F32),
        ],
        flops=1 << 32,
    )[0]
    small = small + swap(small, "grp", 1)
    for bit in range(1, grp_bits - 1):
        small = small + swap(small, "grp", 1 << bit)
    size = quarter // 2
    keep, send, small = call(
        functools.partial(gather_kernel, dev_bits - 1),
        [((size, wide), F32), ((size, wide), BF16), (small.shape, F32)],
        [own, *gots, small, swap(small, "grp", groups_of // 2)],
    )
    got = swap(send, "dev", members // 2)
    smalls = [small] + [swap(small, "dev", offset) for offset in (1, 2, 3)]
    for bit in range(dev_bits - 1, 2, -1):
        size //= 2
        send, keep = call(
            functools.partial(fold_kernel, bit - 1), [((size, wide), BF16), ((size, wide), F32)], [keep, got]
        )
        got = swap(send, "dev", 1 << (bit - 1))
    send, small = call(round_kernel, [((size, wide), BF16), (small.shape, F32)], [keep, got, *smalls])
    for bit in range(3, dev_bits):
        small = small + swap(small, "dev", 1 << bit)
    small_got = swap(small, "dev", 4)
    for bit in range(1, grp_bits - 1):
        got = swap(send, "grp", 1 << bit)
        send = call(across_kernel, [((size, wide), BF16)], [send, got])[0]
    got = swap(send, "grp", groups_of // 2)
    send, small = call(across_kernel, [((size, wide), F32), (small.shape, F32)], [send, got, small, small_got])
    other = swap(send, "grp", 1)
    grad_second, grad_first, grad_gain, grad_bias = call(
        functools.partial(join_kernel, members, taps),
        [
            ((taps_second, size, chans), F32, "out"),
            ((taps, size), F32, "out"),
            ((1, size), F32, "out"),
            ((1, size), F32, "out"),
        ],
        [send, other, small],
    )
    return (
        feat.transpose(1, 0, 2),
        grad_second.transpose(0, 2, 1),
        grad_first,
        grad_gain.reshape(size),
        grad_bias.reshape(size),
    )


def solution(mesh):
    placed = (
        P(("grp", "dev"), None),
        P("grp"),
        P("grp", None),
        P(),
        P(),
        P(),
        P(),
        P(("grp", "dev"), None, None),
    )
    return jax.shard_map(
        shards,
        mesh=mesh,
        in_specs=placed,
        out_specs=(
            P(("grp", "dev"), None, None),
            P(None, None, "dev"),
            P(None, "dev"),
            P("dev"),
            P("dev"),
        ),
        check_vma=False,
    )
```

```python
import functools

import jax
import jax.numpy as jnp
from jax import lax
from jax.experimental import pallas as pl
from jax.experimental.pallas import tpu as pltpu
from jax.sharding import PartitionSpec as P

F32 = jnp.float32
BF16 = jnp.bfloat16
GROUP = 8
LANES = 256
MIN_SAMPLES = 288
MIB = 1 << 20


def gelu_and_slope(value):
    bell = jnp.exp2(value * value * (-0.5 * 1.4426950408889634))
    base = 1.0 + jnp.abs(value) * (0.3275911 * 0.7071067811865476)
    frac = pltpu.reciprocal(base, approx=True)
    poly = 0.5 * 1.061405429
    for coef in (-1.453152027, 1.421413741, -0.284496736, 0.254829592):
        poly = poly * frac + 0.5 * coef
    tail = poly * frac * bell
    phi = jnp.where(value < 0.0, tail, 1.0 - tail)
    return value * phi, phi + value * bell * 0.3989422804014327


def rows_first(a, b):
    return lax.dot_general(a, b, (((0,), (0,)), ((), ())), preferred_element_type=F32)


def cols_both(a, b):
    return lax.dot_general(a, b, (((1,), (1,)), ((), ())), preferred_element_type=F32)


def dot(a, b):
    return jnp.dot(a, b, preferred_element_type=F32)


def iota(shape, dim):
    return lax.broadcasted_iota(jnp.int32, shape, dim)


def onehot(mask):
    return mask.astype(F32).astype(BF16)


def copies(sources, targets, sems):
    started = [pltpu.make_async_copy(source, target, sems.at[i]) for i, (source, target) in enumerate(zip(sources, targets))]
    for copy in started:
        copy.start()
    return started


def setup_kernel(
    members,
    order_hbm,
    len_hbm,
    w_hbm,
    wave_hbm,
    valid_ref,
    band_ref,
    near_ref,
    far_ref,
    own_ref,
    order_ref,
    len_ref,
    w_ref,
    sems,
):
    for copy in copies((order_hbm, len_hbm, w_hbm, wave_hbm), (order_ref, len_ref, w_ref, own_ref), sems):
        copy.wait()
    rows = order_ref.shape[1]
    share = rows // members
    taps, chans = w_ref.shape
    stride = taps // 2
    owner = onehot(iota((rows, members), 0) // share == iota((rows, members), 1))
    order_of = dot(owner, order_ref[...].astype(F32).astype(BF16))
    slot = iota((rows, rows), 1) - lax.rem(iota((rows, rows), 0), share) * members
    owner_first = iota((rows, 1), 0) // share * rows
    column = iota((rows, members * rows), 1)
    member = lax.axis_index("dev")
    for target, out_ref in ((member, near_ref), (jnp.bitwise_xor(member, members // 2), far_ref)):
        local = jnp.sum(jnp.where(slot == target, order_of, 0.0), axis=1, keepdims=True).astype(jnp.int32)
        picked = column == owner_first + local
        out_ref[...] = onehot(picked)
        if out_ref is near_ref:
            lens = jnp.sum(jnp.where(picked, len_ref[...], 0), axis=1, keepdims=True)
    valid = (lens - taps) // stride + 1
    valid_ref[...] = jnp.broadcast_to(valid, valid_ref.shape)
    depth = band_ref.shape[0]
    for f in range(GROUP):
        spread = onehot(iota((depth, taps), 0) == iota((depth, taps), 1) + stride * f)
        band_ref[:, f * chans : (f + 1) * chans] = dot(spread, w_ref[...]).astype(BF16)


def pick_kernel(offsets, near_ref, far_ref, *refs):
    waves, (mine_ref, send_ref, all_ref) = refs[:-3], refs[-3:]
    rows = mine_ref.shape[0]
    all_ref[...] = jnp.zeros(all_ref.shape, BF16)
    for offset, wave_ref in zip(offsets, waves):
        first = pl.multiple_of(jnp.bitwise_xor(lax.axis_index("dev"), offset) * rows, rows)
        all_ref[pl.ds(first, rows), :] = wave_ref[...]
    mine_ref[...] = dot(near_ref[...], all_ref[...]).astype(BF16)
    send_ref[...] = dot(far_ref[...], all_ref[...]).astype(BF16)


def forward_kernel(
    frames0,
    frames1,
    taps,
    places,
    near_ref,
    far_ref,
    valid_ref,
    band_ref,
    gain_hbm,
    bias_hbm,
    w_hbm,
    cot_hbm,
    feat_out,
    even_ref,
    odd_ref,
    pre0,
    slope_ref,
    mean_ref,
    inv_ref,
    patch_ref,
    grad_ref,
    grad_t_ref,
    gain_ref,
    w_ref,
    stage,
    fresh,
    pre1,
    scale_ref,
    shift_ref,
    bias_ref,
    cot_ref,
    feat_ref,
    sems,
    out_sem,
):
    waiting = copies((gain_hbm, bias_hbm, w_hbm, cot_hbm), (gain_ref, bias_ref, w_ref, cot_ref), sems)
    rows, samp = near_ref.shape
    chans = gain_ref.shape[1]
    stride = taps // 2
    depth = band_ref.shape[0]
    groups = pre0.shape[0]
    width = LANES
    parts = [slice(first, first + width) for first in range(0, chans, width)]
    min_valid = (MIN_SAMPLES - taps) // stride + 1
    full_groups = frames0 // GROUP
    free_groups = min(min_valid // GROUP, full_groups)
    wave = near_ref[...] + far_ref[...]
    for g in range(groups):
        pick = onehot(iota((samp, depth), 0) == iota((samp, depth), 1) + GROUP * stride * g)
        patch_ref[g] = dot(wave, pick).astype(BF16)
    patches = patch_ref[...].reshape(groups * rows, depth)
    for f in range(GROUP):
        cols = slice(f * chans, (f + 1) * chans)
        pre0[:, :, cols] = dot(patches, band_ref[:, cols]).reshape(groups, rows, chans)

    valid = jnp.broadcast_to(valid_ref[:, :1], (rows, width))
    count = valid.astype(F32)

    def frame(g, f, lanes):
        return pre0[g, :, f * chans + lanes.start : f * chans + lanes.stop]

    def masked_to(value, t, masked):
        return jnp.where(valid > t, value, 0.0) if masked else value

    for lanes in parts:

        def over_frames(body):
            def step(masked, g, total):
                for f in range(GROUP):
                    total = total + body(g, f, masked)
                return total

            total = lax.fori_loop(0, free_groups, functools.partial(step, False), jnp.zeros((rows, width), F32))
            total = lax.fori_loop(free_groups, full_groups, functools.partial(step, True), total)
            for f in range(frames0 - full_groups * GROUP):
                total = total + body(full_groups, f, True)
            return total

        mean = over_frames(lambda g, f, masked: masked_to(frame(g, f, lanes), g * GROUP + f, masked)) / count

        def square(g, f, masked):
            centred = masked_to(frame(g, f, lanes) - mean, g * GROUP + f, masked)
            return centred * centred

        inv = lax.rsqrt(over_frames(square) / count + 1e-05)
        mean_ref[:, lanes] = mean
        inv_ref[:, lanes] = inv
        if lanes.start == 0:
            waiting[0].wait()
            waiting[1].wait()
        scale = inv * gain_ref[:, lanes]
        scale_ref[:, lanes] = scale
        shift_ref[:, lanes] = bias_ref[:, lanes] - mean * scale

    half = GROUP // 2
    span = half * rows
    frames_of = even_ref.shape[0] - 1
    even_ref[frames_of:] = jnp.zeros((1,) + even_ref.shape[1:], BF16)
    grad_ref[0] = jnp.zeros(grad_ref.shape[1:], BF16)
    grad_ref[frames1 + 1] = jnp.zeros(grad_ref.shape[1:], BF16)
    grad_t_ref[:, frames1 // half * span :] = jnp.zeros((chans, grad_t_ref.shape[1] - frames1 // half * span), BF16)
    min_valid1 = (min_valid - 3) // 2 + 1
    valid1 = lax.shift_right_arithmetic(valid - 3, 1) + 1
    slab = chans // len(places)

    def unstage(g):
        for f in range(GROUP):
            (odd_ref if f % 2 else even_ref)[g * half + f // 2] = stage[f]

    def activate0(g, masked, used=GROUP):
        for f in range(used):
            for lanes in parts:
                gelu, slope = gelu_and_slope(frame(g, f, lanes) * scale_ref[:, lanes] + shift_ref[:, lanes])
                t = g * GROUP + f
                slope_ref[t, :, lanes] = masked_to(slope, t, masked)
                stage[f, :, lanes] = masked_to(gelu, t, masked).astype(BF16)

    def convolve(h, used):
        first = h * half
        for lanes in parts:
            total = dot(even_ref[pl.ds(first, used)].reshape(used * rows, chans), w_ref[0, :, lanes])
            total += dot(odd_ref[pl.ds(first, used)].reshape(used * rows, chans), w_ref[1, :, lanes])
            total += dot(even_ref[pl.ds(first + 1, used)].reshape(used * rows, chans), w_ref[2, :, lanes])
            fresh[:used, :, lanes] = total.reshape(used, rows, width)

    def activate1(h, used, masked):
        for j in range(used):
            u = h * half + j
            for lanes in parts:
                gelu, slope = gelu_and_slope(pre1[j, :, lanes])
                grad = cot_ref[u, :, lanes].astype(F32) * slope
                if masked:
                    gelu, grad = jnp.where(valid1 > u, gelu, 0.0), jnp.where(valid1 > u, grad, 0.0)
                feat_ref[u, :, lanes] = gelu.astype(BF16)
                grad_ref[u + 1, :, lanes] = grad.astype(BF16)

    def leave(h, used):
        frames = pl.ds(h * half, used)
        pltpu.make_async_copy(feat_ref.at[frames], feat_out.at[frames], out_sem).start()

    def turn(h, used):
        leave(h, used)
        turned = grad_ref[pl.ds(h * half + 1, used)].reshape(used * rows, chans).T
        start = h * span
        cols = pl.ds(start if isinstance(start, int) else pl.multiple_of(start, span), used * rows)
        for place, source in enumerate(places):
            grad_t_ref[place * slab : (place + 1) * slab, cols] = turned[source * slab : (source + 1) * slab]

    def fill(g, carry):
        unstage(jnp.maximum(g - 1, 0))
        activate0(g, False)
        return carry

    def steady(masked, g, carry, used=GROUP):
        unstage(g - 1)
        pre1[...] = fresh[...]
        convolve(g - 2, half)
        activate1(g - 3, half, masked)
        activate0(g, masked, used)
        turn(g - 3, half)
        return carry

    stage[...] = jnp.zeros(stage.shape, BF16)
    lax.fori_loop(0, 3, fill, 0)
    waiting[2].wait()
    waiting[3].wait()
    convolve(0, half)
    lax.fori_loop(3, free_groups, functools.partial(steady, False), 0)
    lax.fori_loop(free_groups, full_groups, functools.partial(steady, True), 0)
    rest = frames0 - full_groups * GROUP
    if rest:
        steady(True, full_groups, 0, rest)
        stage[rest:] = jnp.zeros((GROUP - rest,) + stage.shape[1:], BF16)
    unstage(groups - 1)
    last = frames1 // half
    for h in range(groups - 2, last + 1):
        pre1[...] = fresh[...]
        convolve(h, min(half, frames1 - h * half))
        activate1(h - 1, half, True)
        turn(h - 1, half)
    pre1[...] = fresh[...]
    activate1(last, frames1 - last * half, True)
    turn(last, frames1 - last * half)
    pltpu.make_async_copy(feat_ref, feat_out, out_sem).wait()


def outer_kernel(even_ref, odd_ref, grad_t_ref, keep_ref, send_ref):
    frames = grad_t_ref.shape[1] // even_ref.shape[1]
    rows, chans = even_ref.shape[1:]
    half = chans // 2
    core = lax.rem(lax.axis_index("grp"), 2)
    turned = grad_t_ref[...]
    for tap, (ref, skip) in enumerate(((even_ref, 0), (odd_ref, 0), (even_ref, 1))):
        for side, out_ref in ((core, keep_ref), (1 - core, send_ref)):
            lanes = pl.ds(pl.multiple_of(side * half, half), half)
            acts = ref[skip : skip + frames, :, lanes].reshape(frames * rows, half)
            out_ref[:, tap * half : (tap + 1) * half] = dot(turned, acts).astype(out_ref.dtype)


def input_kernel(grad_ref, w_ref, even_ref, odd_ref):
    evens, rows, chans = even_ref.shape
    odds = odd_ref.shape[0]
    first = grad_ref[1 : evens + 1].reshape(evens * rows, chans)
    third = grad_ref[0:evens].reshape(evens * rows, chans)
    even_ref[...] = (cols_both(first, w_ref[0]) + cols_both(third, w_ref[2])).reshape(even_ref.shape)
    second = grad_ref[1 : odds + 1].reshape(odds * rows, chans)
    odd_ref[...] = cols_both(second, w_ref[1]).reshape(odd_ref.shape)


def backward_kernel(
    frames0,
    taps,
    valid_ref,
    pre0,
    slope_ref,
    mean_ref,
    inv_ref,
    patch_ref,
    even_ref,
    odd_ref,
    gain_ref,
    out_ref,
    lift,
    dpre0,
    spread,
):
    groups, rows, depth = patch_ref.shape
    chans = gain_ref.shape[1]
    stride = taps // 2
    width = dpre0.shape[2] // GROUP
    full_groups = frames0 // GROUP
    rest = frames0 - full_groups * GROUP
    patches = patch_ref[...].reshape(groups * rows, depth)
    for block in range(chans // width):
        lanes = slice(block * width, (block + 1) * width)

        def frame(g, f):
            return pre0[g, :, f * chans + block * width : f * chans + (block + 1) * width]

        def slopes(g, f, carry):
            bias_sum, gain_sum = carry
            t = g * GROUP + f
            dact = (odd_ref if f % 2 else even_ref)[g * (GROUP // 2) + f // 2, :, lanes]
            dlift = dact * slope_ref[t, :, lanes]
            lift[t] = dlift
            return bias_sum + dlift, gain_sum + dlift * frame(g, f)

        def add(g, carry):
            for f in range(GROUP):
                carry = slopes(g, f, carry)
            return carry

        zero = jnp.zeros((rows, width), F32)
        carry = lax.fori_loop(0, full_groups, add, (zero, zero))
        for f in range(rest):
            carry = slopes(full_groups, f, carry)
        bias_sum, gain_sum = carry
        mean, inv = mean_ref[:, lanes], inv_ref[:, lanes]
        gain_sum = (gain_sum - mean * bias_sum) * inv
        out_ref[taps : taps + 1, lanes] = jnp.sum(gain_sum, axis=0, keepdims=True)
        out_ref[taps + 1 : taps + 2, lanes] = jnp.sum(bias_sum, axis=0, keepdims=True)
        valid = jnp.broadcast_to(valid_ref[:, :1], (rows, width))
        count = valid.astype(F32)
        scale = inv * gain_ref[:, lanes]
        slant = scale * inv * gain_sum / count
        level = scale * bias_sum / count - mean * slant

        def finish(g, f):
            t = g * GROUP + f
            value = scale * lift[t] - frame(g, f) * slant - level
            dpre0[g, :, f * width : (f + 1) * width] = jnp.where(valid > t, value, 0.0).astype(BF16)

        def whole(g, carry):
            for f in range(GROUP):
                finish(g, f)
            return carry

        lax.fori_loop(0, full_groups, whole, 0)
        for f in range(rest):
            finish(full_groups, f)
        if full_groups < groups:
            dpre0[full_groups, :, rest * width :] = jnp.zeros((rows, (GROUP - rest) * width), BF16)
        spread[...] = rows_first(patches, dpre0[...].reshape(groups * rows, GROUP * width))
        total = jnp.zeros((taps, width), F32)
        for f in range(GROUP):
            total += spread[stride * f : stride * f + taps, f * width : (f + 1) * width]
        out_ref[:taps, lanes] = total


def plane_kernel(keep_ref, got_ref, later_ref, own_ref, *send_refs):
    size = own_ref.shape[0]
    place = lax.rem(lax.axis_index("dev"), 4)

    def quarter(index):
        lines = pl.ds(pl.multiple_of(index * size, size), size)
        return keep_ref[lines, :] + got_ref[lines, :].astype(F32)

    own_ref[...] = quarter(place)
    for offset, send_ref in enumerate(send_refs, 1):
        send_ref[...] = quarter(jnp.bitwise_xor(place, offset)).astype(BF16)


def part_kernel(own_ref, got1, got2, small_ref, sum_ref, total_ref):
    sum_ref[...] = own_ref[...] + (got1[...].astype(F32) + got2[...].astype(F32))
    total_ref[...] = small_ref[...]


def write_small(send_ref, first, total):
    lines, chans = total.shape
    send_ref[first:, :chans] = total.astype(send_ref.dtype)
    send_ref[first:, chans:] = jnp.zeros((lines, send_ref.shape[1] - chans), send_ref.dtype)


def read_small(got_ref, first, chans):
    return got_ref[first:, :chans].astype(F32)


def gather_kernel(bit, own_ref, got3, small0, small1, small2, small3, next_ref, send_ref, total_ref):
    half = next_ref.shape[0]
    side = lax.rem(lax.shift_right_logical(lax.axis_index("dev"), bit), 2)

    def part(index):
        lines = pl.ds(pl.multiple_of(index * half, half), half)
        return own_ref[lines, :] + got3[lines, :].astype(F32)

    next_ref[...] = part(side)
    send_ref[:half] = part(1 - side).astype(BF16)
    total = (small0[...] + small1[...]) + (small2[...] + small3[...])
    total_ref[...] = total
    write_small(send_ref, half, total)


def fold_kernel(bit, keep_ref, got_ref, small_ref, total_ref, send_ref, *rest):
    half = keep_ref.shape[0]
    total = small_ref[...] + read_small(got_ref, half, small_ref.shape[1])
    total_ref[...] = total
    if not rest:
        send_ref[:half] = (keep_ref[...] + got_ref[:half].astype(F32)).astype(BF16)
        write_small(send_ref, half, total)
        return
    next_ref = rest[0]
    size = next_ref.shape[0]
    side = lax.rem(lax.shift_right_logical(lax.axis_index("dev"), bit), 2)

    def part(index):
        here = pl.ds(pl.multiple_of(index * size, size), size)
        return keep_ref[here, :] + got_ref[here, :].astype(F32)

    next_ref[...] = part(side)
    send_ref[:size] = part(1 - side).astype(BF16)
    write_small(send_ref, size, total)


def across_kernel(mine_ref, got_ref, out_ref):
    out_ref[...] = (mine_ref[...].astype(F32) + got_ref[...].astype(F32)).astype(out_ref.dtype)


def join_kernel(members, taps, own_ref, other_ref, out_ref, first_ref, gain_ref, bias_ref):
    second, size, chans = out_ref.shape
    half = chans // 2
    core = lax.rem(lax.axis_index("grp"), 2)
    for tap in range(second):
        lanes = slice(tap * half, (tap + 1) * half)
        out_ref[tap, :, pl.ds(pl.multiple_of(core * half, half), half)] = own_ref[:size, lanes]
        out_ref[tap, :, pl.ds(pl.multiple_of((1 - core) * half, half), half)] = other_ref[:size, lanes]
    wide = max(size, 128)
    member = lax.axis_index("dev")
    block = pl.ds(pl.multiple_of(member // (wide // size) * wide, wide), wide)
    total = own_ref[size:, block] + other_ref[size:, block]
    value = total[:, :size]
    for place in range(1, wide // size):
        value = jnp.where(lax.rem(member, wide // size) == place, total[:, place * size : (place + 1) * size], value)
    first_ref[...] = value[:taps]
    gain_ref[...] = value[taps : taps + 1]
    bias_ref[...] = value[taps + 1 : taps + 2]


def call(kernel, outs, args, scratch=(), limit=24, flops=0, touched=0, outside=()):
    vmem = pl.BlockSpec(memory_space=pltpu.VMEM)
    args = [pltpu.with_memory_space_constraint(arg, pltpu.HBM) if i in outside else arg for i, arg in enumerate(args)]
    return pl.pallas_call(
        kernel,
        out_shape=[
            jax.ShapeDtypeStruct(out[0], out[1]) if len(out) > 2 else pltpu.VMEM(out[0], out[1]) for out in outs
        ],
        in_specs=[pl.BlockSpec(memory_space=pltpu.HBM) if i in outside else vmem for i in range(len(args))],
        out_specs=[pl.BlockSpec(memory_space=pl.ANY) if out[-1] == "hbm" else vmem for out in outs],
        scratch_shapes=[pltpu.VMEM(*entry) if isinstance(entry, tuple) else entry for entry in scratch],
        compiler_params=pltpu.CompilerParams(vmem_limit_bytes=limit * MIB),
        cost_estimate=pl.CostEstimate(flops=flops, bytes_accessed=touched, transcendentals=0),
    )(*args)


def swap(value, axis, offset):
    size = lax.axis_size(axis)
    return lax.ppermute(value, axis, [(i, i ^ offset) for i in range(size)])


def shards(wave, lengths, order, w_first, norm_gain, norm_bias, w_second, cot):
    members = lax.axis_size("dev")
    groups_of = lax.axis_size("grp")
    rows, samp = wave.shape
    taps, chans = w_first.shape
    taps_second = w_second.shape[0]
    stride = taps // 2
    frames0 = (samp - taps) // stride + 1
    frames1 = (frames0 - taps_second) // 2 + 1
    groups = -(-frames0 // GROUP)
    depth = 128
    width = LANES
    dev_bits = members.bit_length() - 1
    grp_bits = groups_of.bit_length() - 1

    offsets = [0, 1, 2, 3]
    waves = [wave] + [swap(wave, "dev", offset) for offset in offsets[1:]]
    for bit in range(2, dev_bits - 1):
        offsets += [offset | (1 << bit) for offset in offsets]
        waves += [swap(held, "dev", 1 << bit) for held in waves]
    lens = lengths.reshape(1, members * rows)
    every = members * rows
    valid, band, near_sel, far_sel, own_wave = call(
        functools.partial(setup_kernel, members),
        [
            ((rows, 128), jnp.int32),
            ((depth, GROUP * chans), BF16),
            ((rows, every), BF16),
            ((rows, every), BF16),
            ((rows, samp), BF16),
        ],
        [order, lens, w_first, wave],
        scratch=[
            (order.shape, order.dtype),
            (lens.shape, lens.dtype),
            (w_first.shape, BF16),
            pltpu.SemaphoreType.DMA((4,)),
        ],
        outside=(0, 1, 2, 3),
    )
    near, send = call(
        functools.partial(pick_kernel, offsets),
        [((rows, samp), BF16), ((rows, samp), BF16)],
        [near_sel, far_sel, own_wave, *waves[1:]],
        scratch=[((every, samp), BF16)],
    )
    far = swap(send, "dev", members // 2)
    gain = norm_gain.reshape(1, chans)
    bias = norm_bias.reshape(1, chans)
    cot_t = cot.transpose(1, 0, 2)
    pad_frames = -(-frames1 // 4) * 4
    places = [0] * members
    for dev in range(members):
        places[dev % 4 * (members // 4) + dev // 4] = dev
    feat, even, odd, pre0, slope, mean, inv, patch, grad, grad_t, gain_in, w_in = call(
        functools.partial(forward_kernel, frames0, frames1, taps, places),
        [
            ((frames1, rows, chans), BF16, "hbm"),
            ((pad_frames + 1, rows, chans), BF16),
            ((pad_frames, rows, chans), BF16),
            ((groups, rows, GROUP * chans), F32),
            ((groups * GROUP, rows, chans), F32),
            ((rows, chans), F32),
            ((rows, chans), F32),
            ((groups, rows, depth), BF16),
            ((frames1 + 2, rows, chans), BF16),
            ((chans, pad_frames * rows), BF16),
            ((1, chans), F32),
            (w_second.shape, BF16),
        ],
        [near, far, valid, band, gain, bias, w_second, cot_t],
        scratch=[
            ((GROUP, rows, chans), BF16),
            ((GROUP // 2, rows, chans), F32),
            ((GROUP // 2, rows, chans), F32),
            ((rows, chans), F32),
            ((rows, chans), F32),
            (bias.shape, F32),
            (cot_t.shape, BF16),
            (cot_t.shape, BF16),
            pltpu.SemaphoreType.DMA((4,)),
            pltpu.SemaphoreType.DMA,
        ],
        outside=(4, 5, 6, 7),
    )
    wide = taps_second * chans // 2
    keep, send = call(outer_kernel, [((chans, wide), F32), ((chans, wide), BF16)], [even, odd, grad_t], flops=1 << 30)
    got = swap(send, "grp", 1)
    evens, odds = (frames0 + 1) // 2, frames0 // 2
    dact_even, dact_odd = call(
        input_kernel,
        [((evens, rows, chans), F32), ((odds, rows, chans), F32)],
        [grad, w_in],
        flops=1 << 30,
    )
    quarter = chans // 4
    own, *sends = call(
        plane_kernel, [((quarter, wide), F32)] + [((quarter, wide), BF16)] * 3, [keep, got, dact_odd]
    )
    gots = [swap(part, "dev", offset) for offset, part in enumerate(sends, 1)]
    small = call(
        functools.partial(backward_kernel, frames0, taps),
        [((16, chans), F32)],
        [valid, pre0, slope, mean, inv, patch, dact_even, dact_odd, gain_in],
        scratch=[
            ((frames0, rows, width), F32),
            ((groups, rows, GROUP * width), BF16),
            ((depth, GROUP * width), F32),
        ],
        flops=1 << 32,
    )[0]
    size = quarter // 2
    lines = small.shape[0]
    near_smalls = [swap(small, "dev", 1), swap(small, "dev", 2)]
    own, small_again = call(
        part_kernel, [((quarter, wide), F32), (small.shape, F32)], [own, gots[0], gots[1], small]
    )
    keep, send, small = call(
        functools.partial(gather_kernel, dev_bits - 1),
        [((size, wide), F32), ((size + lines, wide), BF16), (small.shape, F32)],
        [own, gots[2], small, *near_smalls, swap(small_again, "dev", 3)],
    )
    for bit in range(dev_bits - 1, 1, -1):
        got = swap(send, "dev", 1 << bit)
        outs = [(small.shape, F32), ((size + lines, wide), BF16)]
        if bit > 2:
            size //= 2
            outs = [(small.shape, F32), ((size + lines, wide), BF16), ((size, wide), F32)]
        small, send, *rest = call(functools.partial(fold_kernel, bit - 1), outs, [keep, got, small])
        keep = rest[0] if rest else None
    for bit in range(1, grp_bits):
        got = swap(send, "grp", 1 << bit)
        send = call(across_kernel, [((size + lines, wide), F32 if bit == grp_bits - 1 else BF16)], [send, got])[0]
    other = swap(send, "grp", 1)
    grad_second, grad_first, grad_gain, grad_bias = call(
        functools.partial(join_kernel, members, taps),
        [
            ((taps_second, size, chans), F32, "out"),
            ((taps, size), F32, "out"),
            ((1, size), F32, "out"),
            ((1, size), F32, "out"),
        ],
        [send, other],
    )
    return (
        feat.transpose(1, 0, 2),
        grad_second.transpose(0, 2, 1),
        grad_first,
        grad_gain.reshape(size),
        grad_bias.reshape(size),
    )


def solution(mesh):
    placed = (
        P(("grp", "dev"), None),
        P("grp"),
        P("grp", None),
        P(),
        P(),
        P(),
        P(),
        P(("grp", "dev"), None, None),
    )
    return jax.shard_map(
        shards,
        mesh=mesh,
        in_specs=placed,
        out_specs=(
            P(("grp", "dev"), None, None),
            P(None, None, "dev"),
            P(None, "dev"),
            P("dev"),
            P("dev"),
        ),
        check_vma=False,
    )
```

```python
import functools

import jax
import jax.numpy as jnp
from jax import lax
from jax.experimental import pallas as pl
from jax.experimental.pallas import tpu as pltpu
from jax.sharding import PartitionSpec as P

F32 = jnp.float32
BF16 = jnp.bfloat16
GROUP = 8
LANES = 256
MIN_SAMPLES = 288
MIB = 1 << 20


def gelu_and_slope(value):
    bell = jnp.exp2(value * value * (-0.5 * 1.4426950408889634))
    phi = 0.5 + 0.5 * lax.erf(value * 0.7071067811865476)
    return value * phi, phi + value * bell * 0.3989422804014327


def rows_first(a, b):
    return lax.dot_general(a, b, (((0,), (0,)), ((), ())), preferred_element_type=F32)


def cols_both(a, b):
    return lax.dot_general(a, b, (((1,), (1,)), ((), ())), preferred_element_type=F32)


def dot(a, b):
    return jnp.dot(a, b, preferred_element_type=F32)


def iota(shape, dim):
    return lax.broadcasted_iota(jnp.int32, shape, dim)


def onehot(mask):
    return mask.astype(F32).astype(BF16)


def copies(sources, targets, sems):
    started = [pltpu.make_async_copy(source, target, sems.at[i]) for i, (source, target) in enumerate(zip(sources, targets))]
    for copy in started:
        copy.start()
    return started


def setup_kernel(
    members,
    order_hbm,
    len_hbm,
    w_hbm,
    wave_hbm,
    valid_ref,
    band_ref,
    near_ref,
    far_ref,
    own_ref,
    order_ref,
    len_ref,
    w_ref,
    sems,
):
    for copy in copies((order_hbm, len_hbm, w_hbm, wave_hbm), (order_ref, len_ref, w_ref, own_ref), sems):
        copy.wait()
    rows = order_ref.shape[1]
    share = rows // members
    taps, chans = w_ref.shape
    stride = taps // 2
    owner = onehot(iota((rows, members), 0) // share == iota((rows, members), 1))
    order_of = dot(owner, order_ref[...].astype(F32).astype(BF16))
    slot = iota((rows, rows), 1) - lax.rem(iota((rows, rows), 0), share) * members
    owner_first = iota((rows, 1), 0) // share * rows
    column = iota((rows, members * rows), 1)
    member = lax.axis_index("dev")
    for target, out_ref in ((member, near_ref), (jnp.bitwise_xor(member, members // 2), far_ref)):
        local = jnp.sum(jnp.where(slot == target, order_of, 0.0), axis=1, keepdims=True).astype(jnp.int32)
        picked = column == owner_first + local
        out_ref[...] = onehot(picked)
        if out_ref is near_ref:
            lens = jnp.sum(jnp.where(picked, len_ref[...], 0), axis=1, keepdims=True)
    valid = (lens - taps) // stride + 1
    valid_ref[...] = jnp.broadcast_to(valid, valid_ref.shape)
    depth = band_ref.shape[0]
    for f in range(GROUP):
        spread = onehot(iota((depth, taps), 0) == iota((depth, taps), 1) + stride * f)
        band_ref[:, f * chans : (f + 1) * chans] = dot(spread, w_ref[...]).astype(BF16)


def pick_kernel(offsets, near_ref, far_ref, *refs):
    waves, (mine_ref, send_ref, all_ref) = refs[:-3], refs[-3:]
    rows = mine_ref.shape[0]
    all_ref[...] = jnp.zeros(all_ref.shape, BF16)
    for offset, wave_ref in zip(offsets, waves):
        first = pl.multiple_of(jnp.bitwise_xor(lax.axis_index("dev"), offset) * rows, rows)
        all_ref[pl.ds(first, rows), :] = wave_ref[...]
    mine_ref[...] = dot(near_ref[...], all_ref[...]).astype(BF16)
    send_ref[...] = dot(far_ref[...], all_ref[...]).astype(BF16)


def forward_kernel(
    frames0,
    frames1,
    taps,
    places,
    near_ref,
    far_ref,
    valid_ref,
    band_ref,
    gain_hbm,
    bias_hbm,
    w_hbm,
    cot_hbm,
    feat_out,
    even_ref,
    odd_ref,
    pre0,
    slope_ref,
    mean_ref,
    inv_ref,
    patch_ref,
    grad_ref,
    grad_t_ref,
    gain_ref,
    w_ref,
    stage,
    fresh,
    pre1,
    scale_ref,
    shift_ref,
    bias_ref,
    cot_ref,
    feat_ref,
    sems,
    out_sem,
):
    waiting = copies((gain_hbm, bias_hbm, w_hbm, cot_hbm), (gain_ref, bias_ref, w_ref, cot_ref), sems)
    rows, samp = near_ref.shape
    chans = gain_ref.shape[1]
    stride = taps // 2
    depth = band_ref.shape[0]
    groups = pre0.shape[0]
    width = LANES
    parts = [slice(first, first + width) for first in range(0, chans, width)]
    min_valid = (MIN_SAMPLES - taps) // stride + 1
    full_groups = frames0 // GROUP
    free_groups = min(min_valid // GROUP, full_groups)
    wave = near_ref[...] + far_ref[...]
    for g in range(groups):
        pick = onehot(iota((samp, depth), 0) == iota((samp, depth), 1) + GROUP * stride * g)
        patch_ref[g] = dot(wave, pick).astype(BF16)
    patches = patch_ref[...].reshape(groups * rows, depth)
    for f in range(GROUP):
        cols = slice(f * chans, (f + 1) * chans)
        pre0[:, :, cols] = dot(patches, band_ref[:, cols]).reshape(groups, rows, chans)

    valid = jnp.broadcast_to(valid_ref[:, :1], (rows, width))
    count = valid.astype(F32)

    def frame(g, f, lanes):
        return pre0[g, :, f * chans + lanes.start : f * chans + lanes.stop]

    def masked_to(value, t, masked):
        return jnp.where(valid > t, value, 0.0) if masked else value

    for lanes in parts:

        def over_frames(body):
            def step(masked, g, total):
                for f in range(GROUP):
                    total = total + body(g, f, masked)
                return total

            total = lax.fori_loop(0, free_groups, functools.partial(step, False), jnp.zeros((rows, width), F32))
            total = lax.fori_loop(free_groups, full_groups, functools.partial(step, True), total)
            for f in range(frames0 - full_groups * GROUP):
                total = total + body(full_groups, f, True)
            return total

        mean = over_frames(lambda g, f, masked: masked_to(frame(g, f, lanes), g * GROUP + f, masked)) / count

        def square(g, f, masked):
            centred = masked_to(frame(g, f, lanes) - mean, g * GROUP + f, masked)
            return centred * centred

        inv = lax.rsqrt(over_frames(square) / count + 1e-05)
        mean_ref[:, lanes] = mean
        inv_ref[:, lanes] = inv
        if lanes.start == 0:
            waiting[0].wait()
            waiting[1].wait()
        scale = inv * gain_ref[:, lanes]
        scale_ref[:, lanes] = scale
        shift_ref[:, lanes] = bias_ref[:, lanes] - mean * scale

    half = GROUP // 2
    span = half * rows
    frames_of = even_ref.shape[0] - 1
    even_ref[frames_of:] = jnp.zeros((1,) + even_ref.shape[1:], BF16)
    grad_ref[0] = jnp.zeros(grad_ref.shape[1:], BF16)
    grad_ref[frames1 + 1] = jnp.zeros(grad_ref.shape[1:], BF16)
    grad_t_ref[:, frames1 // half * span :] = jnp.zeros((chans, grad_t_ref.shape[1] - frames1 // half * span), BF16)
    min_valid1 = (min_valid - 3) // 2 + 1
    valid1 = lax.shift_right_arithmetic(valid - 3, 1) + 1
    slab = chans // len(places)

    def unstage(g):
        for f in range(GROUP):
            (odd_ref if f % 2 else even_ref)[g * half + f // 2] = stage[f]

    def activate0(g, masked, used=GROUP):
        for f in range(used):
            for lanes in parts:
                gelu, slope = gelu_and_slope(frame(g, f, lanes) * scale_ref[:, lanes] + shift_ref[:, lanes])
                t = g * GROUP + f
                slope_ref[t, :, lanes] = masked_to(slope, t, masked)
                stage[f, :, lanes] = masked_to(gelu, t, masked).astype(BF16)

    def convolve(h, used):
        first = h * half
        for lanes in parts:
            total = dot(even_ref[pl.ds(first, used)].reshape(used * rows, chans), w_ref[0, :, lanes])
            total += dot(odd_ref[pl.ds(first, used)].reshape(used * rows, chans), w_ref[1, :, lanes])
            total += dot(even_ref[pl.ds(first + 1, used)].reshape(used * rows, chans), w_ref[2, :, lanes])
            fresh[:used, :, lanes] = total.reshape(used, rows, width)

    def activate1(h, used, masked):
        for j in range(used):
            u = h * half + j
            for lanes in parts:
                gelu, slope = gelu_and_slope(pre1[j, :, lanes])
                grad = cot_ref[u, :, lanes].astype(F32) * slope
                if masked:
                    gelu, grad = jnp.where(valid1 > u, gelu, 0.0), jnp.where(valid1 > u, grad, 0.0)
                feat_ref[u, :, lanes] = gelu.astype(BF16)
                grad_ref[u + 1, :, lanes] = grad.astype(BF16)

    def leave(h, used):
        frames = pl.ds(h * half, used)
        pltpu.make_async_copy(feat_ref.at[frames], feat_out.at[frames], out_sem).start()

    def turn(h, used):
        leave(h, used)
        turned = grad_ref[pl.ds(h * half + 1, used)].reshape(used * rows, chans).T
        start = h * span
        cols = pl.ds(start if isinstance(start, int) else pl.multiple_of(start, span), used * rows)
        for place, source in enumerate(places):
            grad_t_ref[place * slab : (place + 1) * slab, cols] = turned[source * slab : (source + 1) * slab]

    def fill(g, carry):
        unstage(jnp.maximum(g - 1, 0))
        activate0(g, False)
        return carry

    def steady(masked, g, carry, used=GROUP):
        unstage(g - 1)
        pre1[...] = fresh[...]
        convolve(g - 2, half)
        activate1(g - 3, half, masked)
        activate0(g, masked, used)
        turn(g - 3, half)
        return carry

    stage[...] = jnp.zeros(stage.shape, BF16)
    lax.fori_loop(0, 3, fill, 0)
    waiting[2].wait()
    waiting[3].wait()
    convolve(0, half)
    lax.fori_loop(3, free_groups, functools.partial(steady, False), 0)
    lax.fori_loop(free_groups, full_groups, functools.partial(steady, True), 0)
    rest = frames0 - full_groups * GROUP
    if rest:
        steady(True, full_groups, 0, rest)
        stage[rest:] = jnp.zeros((GROUP - rest,) + stage.shape[1:], BF16)
    unstage(groups - 1)
    last = frames1 // half
    for h in range(groups - 2, last + 1):
        pre1[...] = fresh[...]
        convolve(h, min(half, frames1 - h * half))
        activate1(h - 1, half, True)
        turn(h - 1, half)
    pre1[...] = fresh[...]
    activate1(last, frames1 - last * half, True)
    turn(last, frames1 - last * half)
    pltpu.make_async_copy(feat_ref, feat_out, out_sem).wait()


def outer_kernel(skips, *refs):
    acts, (grad_t_ref, keep_ref, send_ref) = refs[:-3], refs[-3:]
    frames = grad_t_ref.shape[1] // acts[0].shape[1]
    rows, chans = acts[0].shape[1:]
    half = chans // 2
    core = lax.rem(lax.axis_index("grp"), 2)
    turned = grad_t_ref[...]
    for tap, (ref, skip) in enumerate(zip(acts, skips)):
        for side, out_ref in ((1 - core, send_ref), (core, keep_ref)):
            lanes = pl.ds(pl.multiple_of(side * half, half), half)
            value = dot(turned, ref[skip : skip + frames, :, lanes].reshape(frames * rows, half))
            out_ref[:, tap * half : (tap + 1) * half] = value.astype(out_ref.dtype)


def input_kernel(grad_ref, w_ref, even_ref, odd_ref):
    evens, rows, chans = even_ref.shape
    odds = odd_ref.shape[0]
    first = grad_ref[1 : evens + 1].reshape(evens * rows, chans)
    third = grad_ref[0:evens].reshape(evens * rows, chans)
    even_ref[...] = (cols_both(first, w_ref[0]) + cols_both(third, w_ref[2])).reshape(even_ref.shape)
    second = grad_ref[1 : odds + 1].reshape(odds * rows, chans)
    odd_ref[...] = cols_both(second, w_ref[1]).reshape(odd_ref.shape)


def backward_kernel(
    frames0,
    taps,
    valid_ref,
    pre0,
    slope_ref,
    mean_ref,
    inv_ref,
    patch_ref,
    even_ref,
    odd_ref,
    gain_ref,
    mine_ref,
    send1,
    send2,
    send3,
    lift,
    dpre0,
    spread,
    out_ref,
    quarters,
):
    groups, rows, depth = patch_ref.shape
    chans = gain_ref.shape[1]
    stride = taps // 2
    width = dpre0.shape[2] // GROUP
    full_groups = frames0 // GROUP
    rest = frames0 - full_groups * GROUP
    patches = patch_ref[...].reshape(groups * rows, depth)
    for block in range(chans // width):
        lanes = slice(block * width, (block + 1) * width)

        def frame(g, f):
            return pre0[g, :, f * chans + block * width : f * chans + (block + 1) * width]

        def slopes(g, f, carry):
            bias_sum, gain_sum = carry
            t = g * GROUP + f
            dact = (odd_ref if f % 2 else even_ref)[g * (GROUP // 2) + f // 2, :, lanes]
            dlift = dact * slope_ref[t, :, lanes]
            lift[t] = dlift
            return bias_sum + dlift, gain_sum + dlift * frame(g, f)

        def add(g, carry):
            for f in range(GROUP):
                carry = slopes(g, f, carry)
            return carry

        zero = jnp.zeros((rows, width), F32)
        carry = lax.fori_loop(0, full_groups, add, (zero, zero))
        for f in range(rest):
            carry = slopes(full_groups, f, carry)
        bias_sum, gain_sum = carry
        mean, inv = mean_ref[:, lanes], inv_ref[:, lanes]
        gain_sum = (gain_sum - mean * bias_sum) * inv
        out_ref[taps : taps + 1, lanes] = jnp.sum(gain_sum, axis=0, keepdims=True)
        out_ref[taps + 1 : taps + 2, lanes] = jnp.sum(bias_sum, axis=0, keepdims=True)
        valid = jnp.broadcast_to(valid_ref[:, :1], (rows, width))
        count = valid.astype(F32)
        scale = inv * gain_ref[:, lanes]
        slant = scale * inv * gain_sum / count
        level = scale * bias_sum / count - mean * slant

        def finish(g, f):
            t = g * GROUP + f
            value = scale * lift[t] - frame(g, f) * slant - level
            dpre0[g, :, f * width : (f + 1) * width] = jnp.where(valid > t, value, 0.0).astype(BF16)

        def whole(g, carry):
            for f in range(GROUP):
                finish(g, f)
            return carry

        lax.fori_loop(0, full_groups, whole, 0)
        for f in range(rest):
            finish(full_groups, f)
        if full_groups < groups:
            dpre0[full_groups, :, rest * width :] = jnp.zeros((rows, (GROUP - rest) * width), BF16)
        spread[...] = rows_first(patches, dpre0[...].reshape(groups * rows, GROUP * width))
        total = jnp.zeros((taps, width), F32)
        for f in range(GROUP):
            total += spread[stride * f : stride * f + taps, f * width : (f + 1) * width]
        out_ref[:taps, lanes] = total
    size = chans // lax.axis_size("dev")
    for place in range(4):
        columns = [slice(first, first + size) for first in range(place * size, chans, 4 * size)]
        quarters[place] = jnp.concatenate([out_ref[:, part] for part in columns], axis=1)
    place = lax.rem(lax.axis_index("dev"), 4)
    for offset, ref in enumerate((mine_ref, send1, send2, send3)):
        ref[...] = quarters[jnp.bitwise_xor(place, offset)]


def plane_kernel(keep0, got0, keep1, got1, later_ref, own_ref, *send_refs):
    size = own_ref.shape[0]
    edge = keep0.shape[1]
    place = lax.rem(lax.axis_index("dev"), 4)
    for offset, out_ref in enumerate((own_ref, *send_refs)):
        lines = pl.ds(pl.multiple_of(jnp.bitwise_xor(place, offset) * size, size), size)
        out_ref[:, :edge] = (keep0[lines, :] + got0[lines, :].astype(F32)).astype(out_ref.dtype)
        out_ref[:, edge:] = (keep1[lines, :] + got1[lines, :].astype(F32)).astype(out_ref.dtype)


def part_kernel(own_ref, got1, got2, small_ref, sum_ref, total_ref):
    sum_ref[...] = own_ref[...] + (got1[...].astype(F32) + got2[...].astype(F32))
    total_ref[...] = small_ref[...]


def packed(size, wide):
    return size + 16, wide - 128


def write_packed(ref, value, small):
    size, lanes = ref.shape[0] - 16, ref.shape[1]
    ref[:size] = value[:, :lanes].astype(ref.dtype)
    used = size // 16
    for block in range(used):
        piece = value[block * 16 : (block + 1) * 16, lanes:]
        ref[size:, block * 128 : (block + 1) * 128] = piece.astype(ref.dtype)
    for first in range(used * 128, lanes - 128, 128):
        ref[size:, first : first + 128] = jnp.zeros((16, 128), ref.dtype)
    ref[size:, lanes - 128 :] = small.astype(ref.dtype)


def read_packed(ref, first, count):
    size = ref.shape[0] - 16
    whole = ref[pl.ds(pl.multiple_of(first, 16), count), :].astype(F32)
    pieces = [
        ref[size:, pl.ds(pl.multiple_of(first * 8 + block * 128, 128), 128)].astype(F32) for block in range(count // 16)
    ]
    return jnp.concatenate([whole, jnp.concatenate(pieces, axis=0)], axis=1)


def gather_kernel(bit, own_ref, got3, small0, small1, small2, small3, keep_ref, send_ref):
    half = own_ref.shape[0] // 2
    side = lax.rem(lax.shift_right_logical(lax.axis_index("dev"), bit), 2)
    total = (small0[...] + small1[...]) + (small2[...] + small3[...])
    for index, ref in ((1 - side, send_ref), (side, keep_ref)):
        lines = pl.ds(pl.multiple_of(index * half, half), half)
        write_packed(ref, own_ref[lines, :] + got3[lines, :].astype(F32), total)


def halve_kernel(bit, keep_ref, got_ref, next_ref, send_ref):
    half = (keep_ref.shape[0] - 16) // 2
    side = lax.rem(lax.shift_right_logical(lax.axis_index("dev"), bit), 2)
    small = keep_ref[2 * half :, -128:] + got_ref[2 * half :, -128:].astype(F32)
    for index, ref in ((1 - side, send_ref), (side, next_ref)):
        first = index * half
        write_packed(ref, read_packed(keep_ref, first, half) + read_packed(got_ref, first, half), small)


def add_kernel(mine_ref, got_ref, out_ref):
    out_ref[...] = (mine_ref[...].astype(F32) + got_ref[...].astype(F32)).astype(out_ref.dtype)


def join_kernel(taps, own_ref, other_ref, out_ref, first_ref, gain_ref, bias_ref):
    second, size, chans = out_ref.shape
    half = chans // 2
    core = lax.rem(lax.axis_index("grp"), 2)
    for ref, side in ((own_ref, core), (other_ref, 1 - core)):
        value = read_packed(ref, 0, size)
        for tap in range(second):
            lanes = pl.ds(pl.multiple_of(side * half, half), half)
            out_ref[tap, :, lanes] = value[:, tap * half : (tap + 1) * half]
    total = own_ref[size:, -128:] + other_ref[size:, -128:]
    value = total[:, :size]
    for place in range(1, 128 // size):
        mine = lax.axis_index("dev") // 4 == place
        value = jnp.where(mine, total[:, place * size : (place + 1) * size], value)
    first_ref[...] = value[:taps]
    gain_ref[...] = value[taps : taps + 1]
    bias_ref[...] = value[taps + 1 : taps + 2]


def call(kernel, outs, args, scratch=(), limit=24, flops=0, touched=0, outside=()):
    vmem = pl.BlockSpec(memory_space=pltpu.VMEM)
    args = [pltpu.with_memory_space_constraint(arg, pltpu.HBM) if i in outside else arg for i, arg in enumerate(args)]
    return pl.pallas_call(
        kernel,
        out_shape=[
            jax.ShapeDtypeStruct(out[0], out[1]) if len(out) > 2 else pltpu.VMEM(out[0], out[1]) for out in outs
        ],
        in_specs=[pl.BlockSpec(memory_space=pltpu.HBM) if i in outside else vmem for i in range(len(args))],
        out_specs=[pl.BlockSpec(memory_space=pl.ANY) if out[-1] == "hbm" else vmem for out in outs],
        scratch_shapes=[pltpu.VMEM(*entry) if isinstance(entry, tuple) else entry for entry in scratch],
        compiler_params=pltpu.CompilerParams(vmem_limit_bytes=limit * MIB),
        cost_estimate=pl.CostEstimate(flops=flops, bytes_accessed=touched, transcendentals=0),
    )(*args)


def swap(value, axis, offset):
    size = lax.axis_size(axis)
    return lax.ppermute(value, axis, [(i, i ^ offset) for i in range(size)])


def shards(wave, lengths, order, w_first, norm_gain, norm_bias, w_second, cot):
    members = lax.axis_size("dev")
    groups_of = lax.axis_size("grp")
    rows, samp = wave.shape
    taps, chans = w_first.shape
    taps_second = w_second.shape[0]
    stride = taps // 2
    frames0 = (samp - taps) // stride + 1
    frames1 = (frames0 - taps_second) // 2 + 1
    groups = -(-frames0 // GROUP)
    depth = 128
    width = LANES
    dev_bits = members.bit_length() - 1
    grp_bits = groups_of.bit_length() - 1

    offsets = [0, 1, 2, 3]
    waves = [wave] + [swap(wave, "dev", offset) for offset in offsets[1:]]
    for bit in range(2, dev_bits - 1):
        offsets += [offset | (1 << bit) for offset in offsets]
        waves += [swap(held, "dev", 1 << bit) for held in waves]
    lens = lengths.reshape(1, members * rows)
    every = members * rows
    valid, band, near_sel, far_sel, own_wave = call(
        functools.partial(setup_kernel, members),
        [
            ((rows, 128), jnp.int32),
            ((depth, GROUP * chans), BF16),
            ((rows, every), BF16),
            ((rows, every), BF16),
            ((rows, samp), BF16),
        ],
        [order, lens, w_first, wave],
        scratch=[
            (order.shape, order.dtype),
            (lens.shape, lens.dtype),
            (w_first.shape, BF16),
            pltpu.SemaphoreType.DMA((4,)),
        ],
        outside=(0, 1, 2, 3),
    )
    near, send = call(
        functools.partial(pick_kernel, offsets),
        [((rows, samp), BF16), ((rows, samp), BF16)],
        [near_sel, far_sel, own_wave, *waves[1:]],
        scratch=[((every, samp), BF16)],
    )
    far = swap(send, "dev", members // 2)
    gain = norm_gain.reshape(1, chans)
    bias = norm_bias.reshape(1, chans)
    cot_t = cot.transpose(1, 0, 2)
    pad_frames = -(-frames1 // 4) * 4
    places = [0] * members
    for dev in range(members):
        places[dev % 4 * (members // 4) + dev // 4] = dev
    feat, even, odd, pre0, slope, mean, inv, patch, grad, grad_t, gain_in, w_in = call(
        functools.partial(forward_kernel, frames0, frames1, taps, places),
        [
            ((frames1, rows, chans), BF16, "hbm"),
            ((pad_frames + 1, rows, chans), BF16),
            ((pad_frames, rows, chans), BF16),
            ((groups, rows, GROUP * chans), F32),
            ((groups * GROUP, rows, chans), F32),
            ((rows, chans), F32),
            ((rows, chans), F32),
            ((groups, rows, depth), BF16),
            ((frames1 + 2, rows, chans), BF16),
            ((chans, pad_frames * rows), BF16),
            ((1, chans), F32),
            (w_second.shape, BF16),
        ],
        [near, far, valid, band, gain, bias, w_second, cot_t],
        scratch=[
            ((GROUP, rows, chans), BF16),
            ((GROUP // 2, rows, chans), F32),
            ((GROUP // 2, rows, chans), F32),
            ((rows, chans), F32),
            ((rows, chans), F32),
            (bias.shape, F32),
            (cot_t.shape, BF16),
            (cot_t.shape, BF16),
            pltpu.SemaphoreType.DMA((4,)),
            pltpu.SemaphoreType.DMA,
        ],
        outside=(4, 5, 6, 7),
    )
    half = chans // 2
    wide = taps_second * half
    keep0, send0 = call(
        functools.partial(outer_kernel, (0, 0)),
        [((chans, 2 * half), F32), ((chans, 2 * half), BF16)],
        [even, odd, grad_t],
        flops=1 << 30,
    )
    got0 = swap(send0, "grp", 1)
    keep1, send1 = call(
        functools.partial(outer_kernel, (1,)),
        [((chans, half), F32), ((chans, half), BF16)],
        [even, grad_t],
        flops=1 << 29,
    )
    got1 = swap(send1, "grp", 1)
    evens, odds = (frames0 + 1) // 2, frames0 // 2
    dact_even, dact_odd = call(
        input_kernel,
        [((evens, rows, chans), F32), ((odds, rows, chans), F32)],
        [grad, w_in],
        flops=1 << 30,
    )
    quarter = chans // 4
    own, *sends = call(
        plane_kernel,
        [((quarter, wide), F32)] + [((quarter, wide), BF16)] * 3,
        [keep0, got0, keep1, got1, dact_odd],
    )
    gots = [swap(part, "dev", offset) for offset, part in enumerate(sends, 1)]
    small, *smalls = call(
        functools.partial(backward_kernel, frames0, taps),
        [((16, quarter), F32)] * 4,
        [valid, pre0, slope, mean, inv, patch, dact_even, dact_odd, gain_in],
        scratch=[
            ((frames0, rows, width), F32),
            ((groups, rows, GROUP * width), BF16),
            ((depth, GROUP * width), F32),
            ((16, chans), F32),
            ((4, 16, quarter), F32),
        ],
        flops=1 << 32,
    )
    small1, small2 = swap(smalls[0], "dev", 1), swap(smalls[1], "dev", 2)
    own, third = call(
        part_kernel, [((quarter, wide), F32), (small.shape, F32)], [own, gots[0], gots[1], smalls[2]]
    )
    small3 = swap(third, "dev", 3)
    size = quarter // 2
    keep, send = call(
        functools.partial(gather_kernel, dev_bits - 1),
        [(packed(size, wide), F32), (packed(size, wide), BF16)],
        [own, gots[2], small, small1, small2, small3],
    )
    for bit in range(dev_bits - 1, 2, -1):
        size //= 2
        keep, send = call(
            functools.partial(halve_kernel, bit - 1),
            [(packed(size, wide), F32), (packed(size, wide), BF16)],
            [keep, swap(send, "dev", 1 << bit)],
        )
    send = call(add_kernel, [(packed(size, wide), BF16)], [keep, swap(send, "dev", 4)])[0]
    for bit in range(1, grp_bits):
        kind = F32 if bit == grp_bits - 1 else BF16
        send = call(add_kernel, [(packed(size, wide), kind)], [send, swap(send, "grp", 1 << bit)])[0]
    grad_second, grad_first, grad_gain, grad_bias = call(
        functools.partial(join_kernel, taps),
        [
            ((taps_second, size, chans), F32, "out"),
            ((taps, size), F32, "out"),
            ((1, size), F32, "out"),
            ((1, size), F32, "out"),
        ],
        [send, swap(send, "grp", 1)],
    )
    return (
        feat.transpose(1, 0, 2),
        grad_second.transpose(0, 2, 1),
        grad_first,
        grad_gain.reshape(size),
        grad_bias.reshape(size),
    )


def solution(mesh):
    placed = (
        P(("grp", "dev"), None),
        P("grp"),
        P("grp", None),
        P(),
        P(),
        P(),
        P(),
        P(("grp", "dev"), None, None),
    )
    return jax.shard_map(
        shards,
        mesh=mesh,
        in_specs=placed,
        out_specs=(
            P(("grp", "dev"), None, None),
            P(None, None, "dev"),
            P(None, "dev"),
            P("dev"),
            P("dev"),
        ),
        check_vma=False,
    )
```

```python
import functools

import jax
import jax.numpy as jnp
from jax import lax
from jax.experimental import pallas as pl
from jax.experimental.pallas import tpu as pltpu
from jax.sharding import PartitionSpec as P

F32 = jnp.float32
BF16 = jnp.bfloat16
GROUP = 8
LANES = 256
MIN_SAMPLES = 288
MIB = 1 << 20


def gelu_and_slope(value):
    bell = jnp.exp2(value * value * (-0.5 * 1.4426950408889634))
    phi = 0.5 + 0.5 * lax.erf(value * 0.7071067811865476)
    return value * phi, phi + value * bell * 0.3989422804014327


def rows_first(a, b):
    return lax.dot_general(a, b, (((0,), (0,)), ((), ())), preferred_element_type=F32)


def cols_both(a, b):
    return lax.dot_general(a, b, (((1,), (1,)), ((), ())), preferred_element_type=F32)


def dot(a, b):
    return jnp.dot(a, b, preferred_element_type=F32)


def iota(shape, dim):
    return lax.broadcasted_iota(jnp.int32, shape, dim)


def onehot(mask):
    return mask.astype(F32).astype(BF16)


def copies(sources, targets, sems):
    started = [pltpu.make_async_copy(source, target, sems.at[i]) for i, (source, target) in enumerate(zip(sources, targets))]
    for copy in started:
        copy.start()
    return started


def setup_kernel(
    members,
    order_hbm,
    len_hbm,
    w_hbm,
    wave_hbm,
    valid_ref,
    band_ref,
    near_ref,
    far_ref,
    own_ref,
    order_ref,
    len_ref,
    w_ref,
    sems,
):
    for copy in copies((order_hbm, len_hbm, w_hbm, wave_hbm), (order_ref, len_ref, w_ref, own_ref), sems):
        copy.wait()
    rows = order_ref.shape[1]
    share = rows // members
    taps, chans = w_ref.shape
    stride = taps // 2
    owner = onehot(iota((rows, members), 0) // share == iota((rows, members), 1))
    order_of = dot(owner, order_ref[...].astype(F32).astype(BF16))
    slot = iota((rows, rows), 1) - lax.rem(iota((rows, rows), 0), share) * members
    owner_first = iota((rows, 1), 0) // share * rows
    column = iota((rows, members * rows), 1)
    member = lax.axis_index("dev")
    low_half = member < members // 2
    for target, out_ref in ((member, near_ref), (jnp.bitwise_xor(member, members // 2), far_ref)):
        local = jnp.sum(jnp.where(slot == target, order_of, 0.0), axis=1, keepdims=True).astype(jnp.int32)
        picked = column == owner_first + local
        picks = picked.astype(F32)
        out_ref[...] = jnp.where(low_half, picks[: rows // 2], picks[rows // 2 :]).astype(BF16)
        if out_ref is near_ref:
            lens = jnp.sum(jnp.where(picked, len_ref[...], 0), axis=1, keepdims=True)
    valid = (lens - taps) // stride + 1
    valid_ref[...] = jnp.broadcast_to(valid, valid_ref.shape)
    depth = band_ref.shape[0]
    for f in range(GROUP):
        spread = onehot(iota((depth, taps), 0) == iota((depth, taps), 1) + stride * f)
        band_ref[:, f * chans : (f + 1) * chans] = dot(spread, w_ref[...]).astype(BF16)


def pick_kernel(offsets, near_ref, far_ref, *refs):
    waves, (mine_ref, send_ref, all_ref) = refs[:-3], refs[-3:]
    rows = waves[0].shape[0]
    all_ref[...] = jnp.zeros(all_ref.shape, BF16)
    for offset, wave_ref in zip(offsets, waves):
        first = pl.multiple_of(jnp.bitwise_xor(lax.axis_index("dev"), offset) * rows, rows)
        all_ref[pl.ds(first, rows), :] = wave_ref[...]
    mine_ref[...] = dot(near_ref[...], all_ref[...]).astype(BF16)
    send_ref[...] = dot(far_ref[...], all_ref[...]).astype(BF16)


def forward_kernel(
    frames0,
    frames1,
    taps,
    places,
    near_ref,
    far_ref,
    valid_ref,
    band_ref,
    gain_hbm,
    bias_hbm,
    w_hbm,
    cot_hbm,
    feat_out,
    even_ref,
    odd_ref,
    pre0,
    even_slope,
    odd_slope,
    mean_ref,
    inv_ref,
    patch_ref,
    grad_ref,
    grad_t_ref,
    gain_ref,
    w_ref,
    stage,
    fresh,
    pre1,
    scale_ref,
    shift_ref,
    bias_ref,
    cot_ref,
    feat_ref,
    sems,
    out_sem,
):
    waiting = copies((gain_hbm, bias_hbm, w_hbm, cot_hbm), (gain_ref, bias_ref, w_ref, cot_ref), sems)
    rows, samp = valid_ref.shape[0], near_ref.shape[1]
    chans = gain_ref.shape[1]
    stride = taps // 2
    depth = band_ref.shape[0]
    groups = pre0.shape[0]
    width = LANES
    parts = [slice(first, first + width) for first in range(0, chans, width)]
    min_valid = (MIN_SAMPLES - taps) // stride + 1
    full_groups = frames0 // GROUP
    free_groups = min(min_valid // GROUP, full_groups)
    low_half = lax.axis_index("dev") < lax.axis_size("dev") // 2
    near, far = near_ref[...].astype(F32), far_ref[...].astype(F32)
    wave = jnp.concatenate([jnp.where(low_half, near, far), jnp.where(low_half, far, near)], axis=0).astype(BF16)
    for g in range(groups):
        pick = onehot(iota((samp, depth), 0) == iota((samp, depth), 1) + GROUP * stride * g)
        patch_ref[g] = dot(wave, pick).astype(BF16)
    patches = patch_ref[...].reshape(groups * rows, depth)
    for f in range(GROUP):
        cols = slice(f * chans, (f + 1) * chans)
        pre0[:, :, cols] = dot(patches, band_ref[:, cols]).reshape(groups, rows, chans)

    valid = jnp.broadcast_to(valid_ref[:, :1], (rows, width))
    count = valid.astype(F32)

    def frame(g, f, lanes):
        return pre0[g, :, f * chans + lanes.start : f * chans + lanes.stop]

    def masked_to(value, t, masked):
        return jnp.where(valid > t, value, 0.0) if masked else value

    for lanes in parts:

        def over_frames(body):
            def step(masked, g, total):
                for f in range(GROUP):
                    total = total + body(g, f, masked)
                return total

            total = lax.fori_loop(0, free_groups, functools.partial(step, False), jnp.zeros((rows, width), F32))
            total = lax.fori_loop(free_groups, full_groups, functools.partial(step, True), total)
            for f in range(frames0 - full_groups * GROUP):
                total = total + body(full_groups, f, True)
            return total

        mean = over_frames(lambda g, f, masked: masked_to(frame(g, f, lanes), g * GROUP + f, masked)) / count

        def square(g, f, masked):
            centred = masked_to(frame(g, f, lanes) - mean, g * GROUP + f, masked)
            return centred * centred

        inv = lax.rsqrt(over_frames(square) / count + 1e-05)
        mean_ref[:, lanes] = mean
        inv_ref[:, lanes] = inv
        if lanes.start == 0:
            waiting[0].wait()
            waiting[1].wait()
        scale = inv * gain_ref[:, lanes]
        scale_ref[:, lanes] = scale
        shift_ref[:, lanes] = bias_ref[:, lanes] - mean * scale

    half = GROUP // 2
    span = half * rows
    frames_of = even_ref.shape[0] - 1
    even_ref[frames_of:] = jnp.zeros((1,) + even_ref.shape[1:], BF16)
    grad_ref[0] = jnp.zeros(grad_ref.shape[1:], BF16)
    grad_ref[frames1 + 1] = jnp.zeros(grad_ref.shape[1:], BF16)
    grad_t_ref[:, frames1 // half * span :] = jnp.zeros((chans, grad_t_ref.shape[1] - frames1 // half * span), BF16)
    min_valid1 = (min_valid - 3) // 2 + 1
    valid1 = lax.shift_right_arithmetic(valid - 3, 1) + 1
    slab = chans // len(places)

    def unstage(g):
        for f in range(GROUP):
            (odd_ref if f % 2 else even_ref)[g * half + f // 2] = stage[f]

    def activate0(g, masked, used=GROUP):
        for f in range(used):
            for lanes in parts:
                gelu, slope = gelu_and_slope(frame(g, f, lanes) * scale_ref[:, lanes] + shift_ref[:, lanes])
                t = g * GROUP + f
                slope_ref = odd_slope if f % 2 else even_slope
                slope_ref[g * half + f // 2, :, lanes] = masked_to(slope, t, masked)
                stage[f, :, lanes] = masked_to(gelu, t, masked).astype(BF16)

    def convolve(h, used):
        first = h * half
        for lanes in parts:
            total = dot(even_ref[pl.ds(first, used)].reshape(used * rows, chans), w_ref[0, :, lanes])
            total += dot(odd_ref[pl.ds(first, used)].reshape(used * rows, chans), w_ref[1, :, lanes])
            total += dot(even_ref[pl.ds(first + 1, used)].reshape(used * rows, chans), w_ref[2, :, lanes])
            fresh[:used, :, lanes] = total.reshape(used, rows, width)

    def activate1(h, used, masked):
        for j in range(used):
            u = h * half + j
            for lanes in parts:
                gelu, slope = gelu_and_slope(pre1[j, :, lanes])
                grad = cot_ref[u, :, lanes].astype(F32) * slope
                if masked:
                    gelu, grad = jnp.where(valid1 > u, gelu, 0.0), jnp.where(valid1 > u, grad, 0.0)
                feat_ref[u, :, lanes] = gelu.astype(BF16)
                grad_ref[u + 1, :, lanes] = grad.astype(BF16)

    def leave(h, used):
        frames = pl.ds(h * half, used)
        pltpu.make_async_copy(feat_ref.at[frames], feat_out.at[frames], out_sem).start()

    def turn(h, used):
        leave(h, used)
        turned = grad_ref[pl.ds(h * half + 1, used)].reshape(used * rows, chans).T
        start = h * span
        cols = pl.ds(start if isinstance(start, int) else pl.multiple_of(start, span), used * rows)
        for place, source in enumerate(places):
            grad_t_ref[place * slab : (place + 1) * slab, cols] = turned[source * slab : (source + 1) * slab]

    def fill(g, carry):
        unstage(jnp.maximum(g - 1, 0))
        activate0(g, False)
        return carry

    def steady(masked, g, carry, used=GROUP):
        unstage(g - 1)
        pre1[...] = fresh[...]
        convolve(g - 2, half)
        activate1(g - 3, half, masked)
        activate0(g, masked, used)
        turn(g - 3, half)
        return carry

    stage[...] = jnp.zeros(stage.shape, BF16)
    lax.fori_loop(0, 3, fill, 0)
    waiting[2].wait()
    waiting[3].wait()
    convolve(0, half)
    lax.fori_loop(3, free_groups, functools.partial(steady, False), 0)
    lax.fori_loop(free_groups, full_groups, functools.partial(steady, True), 0)
    rest = frames0 - full_groups * GROUP
    if rest:
        steady(True, full_groups, 0, rest)
        stage[rest:] = jnp.zeros((GROUP - rest,) + stage.shape[1:], BF16)
    unstage(groups - 1)
    last = frames1 // half
    for h in range(groups - 2, last + 1):
        pre1[...] = fresh[...]
        convolve(h, min(half, frames1 - h * half))
        activate1(h - 1, half, True)
        turn(h - 1, half)
    pre1[...] = fresh[...]
    activate1(last, frames1 - last * half, True)
    turn(last, frames1 - last * half)
    pltpu.make_async_copy(feat_ref, feat_out, out_sem).wait()


def outer_kernel(skips, *refs):
    acts, (grad_t_ref, keep_ref, send_ref) = refs[:-3], refs[-3:]
    frames = grad_t_ref.shape[1] // acts[0].shape[1]
    rows, chans = acts[0].shape[1:]
    half = chans // 2
    core = lax.rem(lax.axis_index("grp"), 2)
    turned = grad_t_ref[...]
    for tap, (ref, skip) in enumerate(zip(acts, skips)):
        for side, out_ref in ((1 - core, send_ref), (core, keep_ref)):
            lanes = pl.ds(pl.multiple_of(side * half, half), half)
            value = dot(turned, ref[skip : skip + frames, :, lanes].reshape(frames * rows, half))
            out_ref[:, tap * half : (tap + 1) * half] = value.astype(out_ref.dtype)


def input_kernel(grad_ref, w_ref, even_slope, odd_slope, after_ref, even_ref, odd_ref):
    evens, rows, chans = even_ref.shape
    odds = odd_ref.shape[0]
    first = grad_ref[1 : evens + 1].reshape(evens * rows, chans)
    third = grad_ref[0:evens].reshape(evens * rows, chans)
    total = cols_both(first, w_ref[0]) + cols_both(third, w_ref[2])
    even_ref[...] = total.reshape(even_ref.shape) * even_slope[:evens]
    second = grad_ref[1 : odds + 1].reshape(odds * rows, chans)
    odd_ref[...] = cols_both(second, w_ref[1]).reshape(odd_ref.shape) * odd_slope[:odds]


def backward_kernel(
    frames0,
    taps,
    valid_ref,
    pre0,
    mean_ref,
    inv_ref,
    patch_ref,
    even_ref,
    odd_ref,
    gain_ref,
    mine_ref,
    send1,
    send2,
    send3,
    dpre0,
    spread,
    out_ref,
    quarters,
):
    groups, rows, depth = patch_ref.shape
    chans = gain_ref.shape[1]
    stride = taps // 2
    width = dpre0.shape[2] // GROUP
    full_groups = frames0 // GROUP
    free_groups = min(((MIN_SAMPLES - taps) // stride + 1) // GROUP, full_groups)
    rest = frames0 - full_groups * GROUP
    patches = patch_ref[...].reshape(groups * rows, depth)
    for block in range(chans // width):
        lanes = slice(block * width, (block + 1) * width)

        def frame(g, f):
            return pre0[g, :, f * chans + block * width : f * chans + (block + 1) * width]

        def lift(g, f):
            return (odd_ref if f % 2 else even_ref)[g * (GROUP // 2) + f // 2, :, lanes]

        def sums(g, f, carry):
            bias_sum, gain_sum = carry
            return bias_sum + lift(g, f), gain_sum + lift(g, f) * frame(g, f)

        def add(g, carry):
            for f in range(GROUP):
                carry = sums(g, f, carry)
            return carry

        zero = jnp.zeros((rows, width), F32)
        carry = lax.fori_loop(0, full_groups, add, (zero, zero))
        for f in range(rest):
            carry = sums(full_groups, f, carry)
        bias_sum, gain_sum = carry
        mean, inv = mean_ref[:, lanes], inv_ref[:, lanes]
        gain_sum = (gain_sum - mean * bias_sum) * inv
        out_ref[taps : taps + 1, lanes] = jnp.sum(gain_sum, axis=0, keepdims=True)
        out_ref[taps + 1 : taps + 2, lanes] = jnp.sum(bias_sum, axis=0, keepdims=True)
        valid = jnp.broadcast_to(valid_ref[:, :1], (rows, width))
        count = valid.astype(F32)
        scale = inv * gain_ref[:, lanes]
        slant = scale * inv * gain_sum / count
        level = scale * bias_sum / count - mean * slant

        def finish(g, f, masked):
            value = scale * lift(g, f) - frame(g, f) * slant - level
            if masked:
                value = jnp.where(valid > g * GROUP + f, value, 0.0)
            dpre0[g, :, f * width : (f + 1) * width] = value.astype(BF16)

        def whole(masked, g, carry):
            for f in range(GROUP):
                finish(g, f, masked)
            return carry

        lax.fori_loop(0, free_groups, functools.partial(whole, False), 0)
        lax.fori_loop(free_groups, full_groups, functools.partial(whole, True), 0)
        for f in range(rest):
            finish(full_groups, f, True)
        if full_groups < groups:
            dpre0[full_groups, :, rest * width :] = jnp.zeros((rows, (GROUP - rest) * width), BF16)
        spread[...] = rows_first(patches, dpre0[...].reshape(groups * rows, GROUP * width))
        total = jnp.zeros((taps, width), F32)
        for f in range(GROUP):
            total += spread[stride * f : stride * f + taps, f * width : (f + 1) * width]
        out_ref[:taps, lanes] = total
    size = chans // lax.axis_size("dev")
    for place in range(4):
        columns = [slice(first, first + size) for first in range(place * size, chans, 4 * size)]
        quarters[place] = jnp.concatenate([out_ref[:, part] for part in columns], axis=1)
    place = lax.rem(lax.axis_index("dev"), 4)
    for offset, ref in enumerate((mine_ref, send1, send2, send3)):
        ref[...] = quarters[jnp.bitwise_xor(place, offset)]


def plane_kernel(keep0, got0, keep1, got1, own_ref, *send_refs):
    size = own_ref.shape[0]
    edge = keep0.shape[1]
    place = lax.rem(lax.axis_index("dev"), 4)
    for offset, out_ref in enumerate((own_ref, *send_refs)):
        lines = pl.ds(pl.multiple_of(jnp.bitwise_xor(place, offset) * size, size), size)
        out_ref[:, :edge] = (keep0[lines, :] + got0[lines, :].astype(F32)).astype(out_ref.dtype)
        out_ref[:, edge:] = (keep1[lines, :] + got1[lines, :].astype(F32)).astype(out_ref.dtype)


def part_kernel(own_ref, got1, got2, small_ref, sum_ref, total_ref):
    sum_ref[...] = own_ref[...] + (got1[...].astype(F32) + got2[...].astype(F32))
    total_ref[...] = small_ref[...]


def packed(size, wide):
    return size + 16, wide - 128


def write_packed(ref, value, small):
    size, lanes = ref.shape[0] - 16, ref.shape[1]
    ref[:size] = value[:, :lanes].astype(ref.dtype)
    used = size // 16
    for block in range(used):
        piece = value[block * 16 : (block + 1) * 16, lanes:]
        ref[size:, block * 128 : (block + 1) * 128] = piece.astype(ref.dtype)
    for first in range(used * 128, lanes - 128, 128):
        ref[size:, first : first + 128] = jnp.zeros((16, 128), ref.dtype)
    ref[size:, lanes - 128 :] = small.astype(ref.dtype)


def read_packed(ref, first, count):
    size = ref.shape[0] - 16
    whole = ref[pl.ds(pl.multiple_of(first, 16), count), :].astype(F32)
    pieces = [
        ref[size:, pl.ds(pl.multiple_of(first * 8 + block * 128, 128), 128)].astype(F32) for block in range(count // 16)
    ]
    return jnp.concatenate([whole, jnp.concatenate(pieces, axis=0)], axis=1)


def gather_kernel(bit, own_ref, got3, small0, small1, small2, small3, keep_ref, send_ref):
    half = own_ref.shape[0] // 2
    side = lax.rem(lax.shift_right_logical(lax.axis_index("dev"), bit), 2)
    total = (small0[...] + small1[...]) + (small2[...] + small3[...])
    for index, ref in ((1 - side, send_ref), (side, keep_ref)):
        lines = pl.ds(pl.multiple_of(index * half, half), half)
        write_packed(ref, own_ref[lines, :] + got3[lines, :].astype(F32), total)


def halve_kernel(bit, keep_ref, got_ref, next_ref, send_ref):
    half = (keep_ref.shape[0] - 16) // 2
    side = lax.rem(lax.shift_right_logical(lax.axis_index("dev"), bit), 2)
    small = keep_ref[2 * half :, -128:] + got_ref[2 * half :, -128:].astype(F32)
    for index, ref in ((1 - side, send_ref), (side, next_ref)):
        first = index * half
        write_packed(ref, read_packed(keep_ref, first, half) + read_packed(got_ref, first, half), small)


def add_kernel(mine_ref, got_ref, out_ref):
    out_ref[...] = (mine_ref[...].astype(F32) + got_ref[...].astype(F32)).astype(out_ref.dtype)


def join_kernel(taps, own_ref, other_ref, out_ref, first_ref, gain_ref, bias_ref):
    second, size, chans = out_ref.shape
    half = chans // 2
    core = lax.rem(lax.axis_index("grp"), 2)
    for ref, side in ((own_ref, core), (other_ref, 1 - core)):
        value = read_packed(ref, 0, size)
        for tap in range(second):
            lanes = pl.ds(pl.multiple_of(side * half, half), half)
            out_ref[tap, :, lanes] = value[:, tap * half : (tap + 1) * half]
    total = own_ref[size:, -128:] + other_ref[size:, -128:]
    value = total[:, :size]
    for place in range(1, 128 // size):
        mine = lax.axis_index("dev") // 4 == place
        value = jnp.where(mine, total[:, place * size : (place + 1) * size], value)
    first_ref[...] = value[:taps]
    gain_ref[...] = value[taps : taps + 1]
    bias_ref[...] = value[taps + 1 : taps + 2]


def call(kernel, outs, args, scratch=(), limit=24, flops=0, touched=0, outside=()):
    vmem = pl.BlockSpec(memory_space=pltpu.VMEM)
    args = [pltpu.with_memory_space_constraint(arg, pltpu.HBM) if i in outside else arg for i, arg in enumerate(args)]
    return pl.pallas_call(
        kernel,
        out_shape=[
            jax.ShapeDtypeStruct(out[0], out[1]) if len(out) > 2 else pltpu.VMEM(out[0], out[1]) for out in outs
        ],
        in_specs=[pl.BlockSpec(memory_space=pltpu.HBM) if i in outside else vmem for i in range(len(args))],
        out_specs=[pl.BlockSpec(memory_space=pl.ANY) if out[-1] == "hbm" else vmem for out in outs],
        scratch_shapes=[pltpu.VMEM(*entry) if isinstance(entry, tuple) else entry for entry in scratch],
        compiler_params=pltpu.CompilerParams(vmem_limit_bytes=limit * MIB),
        cost_estimate=pl.CostEstimate(flops=flops, bytes_accessed=touched, transcendentals=0),
    )(*args)


def swap(value, axis, offset):
    size = lax.axis_size(axis)
    return lax.ppermute(value, axis, [(i, i ^ offset) for i in range(size)])


def shards(wave, lengths, order, w_first, norm_gain, norm_bias, w_second, cot):
    members = lax.axis_size("dev")
    groups_of = lax.axis_size("grp")
    rows, samp = wave.shape
    taps, chans = w_first.shape
    taps_second = w_second.shape[0]
    stride = taps // 2
    frames0 = (samp - taps) // stride + 1
    frames1 = (frames0 - taps_second) // 2 + 1
    groups = -(-frames0 // GROUP)
    depth = 128
    width = LANES
    dev_bits = members.bit_length() - 1
    grp_bits = groups_of.bit_length() - 1

    offsets, waves = [0], [wave]
    for bit in range(dev_bits - 1):
        offsets += [offset | (1 << bit) for offset in offsets]
        waves += [swap(held, "dev", 1 << bit) for held in waves]
    lens = lengths.reshape(1, members * rows)
    every = members * rows
    valid, band, near_sel, far_sel, own_wave = call(
        functools.partial(setup_kernel, members),
        [
            ((rows, 128), jnp.int32),
            ((depth, GROUP * chans), BF16),
            ((rows // 2, every), BF16),
            ((rows // 2, every), BF16),
            ((rows, samp), BF16),
        ],
        [order, lens, w_first, wave],
        scratch=[
            (order.shape, order.dtype),
            (lens.shape, lens.dtype),
            (w_first.shape, BF16),
            pltpu.SemaphoreType.DMA((4,)),
        ],
        outside=(0, 1, 2, 3),
    )
    near, send = call(
        functools.partial(pick_kernel, offsets),
        [((rows // 2, samp), BF16), ((rows // 2, samp), BF16)],
        [near_sel, far_sel, own_wave, *waves[1:]],
        scratch=[((every, samp), BF16)],
    )
    far = swap(send, "dev", members // 2)
    gain = norm_gain.reshape(1, chans)
    bias = norm_bias.reshape(1, chans)
    cot_t = cot.transpose(1, 0, 2)
    pad_frames = -(-frames1 // 4) * 4
    places = [0] * members
    for dev in range(members):
        places[dev % 4 * (members // 4) + dev // 4] = dev
    feat, even, odd, pre0, even_slope, odd_slope, mean, inv, patch, grad, grad_t, gain_in, w_in = call(
        functools.partial(forward_kernel, frames0, frames1, taps, places),
        [
            ((frames1, rows, chans), BF16, "hbm"),
            ((pad_frames + 1, rows, chans), BF16),
            ((pad_frames, rows, chans), BF16),
            ((groups, rows, GROUP * chans), F32),
            ((pad_frames, rows, chans), F32),
            ((pad_frames, rows, chans), F32),
            ((rows, chans), F32),
            ((rows, chans), F32),
            ((groups, rows, depth), BF16),
            ((frames1 + 2, rows, chans), BF16),
            ((chans, pad_frames * rows), BF16),
            ((1, chans), F32),
            (w_second.shape, BF16),
        ],
        [near, far, valid, band, gain, bias, w_second, cot_t],
        scratch=[
            ((GROUP, rows, chans), BF16),
            ((GROUP // 2, rows, chans), F32),
            ((GROUP // 2, rows, chans), F32),
            ((rows, chans), F32),
            ((rows, chans), F32),
            (bias.shape, F32),
            (cot_t.shape, BF16),
            (cot_t.shape, BF16),
            pltpu.SemaphoreType.DMA((4,)),
            pltpu.SemaphoreType.DMA,
        ],
        outside=(4, 5, 6, 7),
    )
    half = chans // 2
    wide = taps_second * half
    keep0, send0 = call(
        functools.partial(outer_kernel, (0, 0)),
        [((chans, 2 * half), F32), ((chans, 2 * half), BF16)],
        [even, odd, grad_t],
        flops=1 << 30,
    )
    got0 = swap(send0, "grp", 1)
    keep1, send1 = call(
        functools.partial(outer_kernel, (1,)),
        [((chans, half), F32), ((chans, half), BF16)],
        [even, grad_t],
        flops=1 << 29,
    )
    got1 = swap(send1, "grp", 1)
    quarter = chans // 4
    own, *sends = call(
        plane_kernel,
        [((quarter, wide), F32)] + [((quarter, wide), BF16)] * 3,
        [keep0, got0, keep1, got1],
    )
    gots = [swap(part, "dev", offset) for offset, part in enumerate(sends, 1)]
    evens, odds = (frames0 + 1) // 2, frames0 // 2
    lift_even, lift_odd = call(
        input_kernel,
        [((evens, rows, chans), F32), ((odds, rows, chans), F32)],
        [grad, w_in, even_slope, odd_slope, own],
        flops=1 << 30,
    )
    small, *smalls = call(
        functools.partial(backward_kernel, frames0, taps),
        [((16, quarter), F32)] * 4,
        [valid, pre0, mean, inv, patch, lift_even, lift_odd, gain_in],
        scratch=[
            ((groups, rows, GROUP * width), BF16),
            ((depth, GROUP * width), F32),
            ((16, chans), F32),
            ((4, 16, quarter), F32),
        ],
        flops=1 << 32,
    )
    small3, small2 = swap(smalls[2], "dev", 3), swap(smalls[1], "dev", 2)
    own, first = call(
        part_kernel, [((quarter, wide), F32), (small.shape, F32)], [own, gots[0], gots[1], smalls[0]]
    )
    small1 = swap(first, "dev", 1)
    size = quarter // 2
    keep, send = call(
        functools.partial(gather_kernel, dev_bits - 1),
        [(packed(size, wide), F32), (packed(size, wide), BF16)],
        [own, gots[2], small, small1, small2, small3],
    )
    for bit in range(dev_bits - 1, 2, -1):
        size //= 2
        keep, send = call(
            functools.partial(halve_kernel, bit - 1),
            [(packed(size, wide), F32), (packed(size, wide), BF16)],
            [keep, swap(send, "dev", 1 << bit)],
        )
    send = call(add_kernel, [(packed(size, wide), BF16)], [keep, swap(send, "dev", 4)])[0]
    for bit in range(1, grp_bits):
        kind = F32 if bit == grp_bits - 1 else BF16
        send = call(add_kernel, [(packed(size, wide), kind)], [send, swap(send, "grp", 1 << bit)])[0]
    grad_second, grad_first, grad_gain, grad_bias = call(
        functools.partial(join_kernel, taps),
        [
            ((taps_second, size, chans), F32, "out"),
            ((taps, size), F32, "out"),
            ((1, size), F32, "out"),
            ((1, size), F32, "out"),
        ],
        [send, swap(send, "grp", 1)],
    )
    return (
        feat.transpose(1, 0, 2),
        grad_second.transpose(0, 2, 1),
        grad_first,
        grad_gain.reshape(size),
        grad_bias.reshape(size),
    )


def solution(mesh):
    placed = (
        P(("grp", "dev"), None),
        P("grp"),
        P("grp", None),
        P(),
        P(),
        P(),
        P(),
        P(("grp", "dev"), None, None),
    )
    return jax.shard_map(
        shards,
        mesh=mesh,
        in_specs=placed,
        out_specs=(
            P(("grp", "dev"), None, None),
            P(None, None, "dev"),
            P(None, "dev"),
            P("dev"),
            P("dev"),
        ),
        check_vma=False,
    )
```

```python
import functools

import jax
import jax.numpy as jnp
from jax import lax
from jax.experimental import pallas as pl
from jax.experimental.pallas import tpu as pltpu
from jax.sharding import PartitionSpec as P

F32 = jnp.float32
BF16 = jnp.bfloat16
GROUP = 8
LANES = 256
MIN_SAMPLES = 288
MIB = 1 << 20


def gelu_and_slope(value):
    bell = jnp.exp2(value * value * (-0.5 * 1.4426950408889634))
    phi = 0.5 + 0.5 * lax.erf(value * 0.7071067811865476)
    return value * phi, phi + value * bell * 0.3989422804014327


def rows_first(a, b):
    return lax.dot_general(a, b, (((0,), (0,)), ((), ())), preferred_element_type=F32)


def cols_both(a, b):
    return lax.dot_general(a, b, (((1,), (1,)), ((), ())), preferred_element_type=F32)


def dot(a, b):
    return jnp.dot(a, b, preferred_element_type=F32)


def iota(shape, dim):
    return lax.broadcasted_iota(jnp.int32, shape, dim)


def onehot(mask):
    return mask.astype(F32).astype(BF16)


def copies(sources, targets, sems):
    started = [pltpu.make_async_copy(source, target, sems.at[i]) for i, (source, target) in enumerate(zip(sources, targets))]
    for copy in started:
        copy.start()
    return started


def setup_kernel(
    members,
    order_hbm,
    len_hbm,
    w_hbm,
    wave_hbm,
    valid_ref,
    band_ref,
    near_ref,
    far_ref,
    own_ref,
    order_ref,
    len_ref,
    w_ref,
    sems,
):
    for copy in copies((order_hbm, len_hbm, w_hbm, wave_hbm), (order_ref, len_ref, w_ref, own_ref), sems):
        copy.wait()
    rows = order_ref.shape[1]
    share = rows // members
    taps, chans = w_ref.shape
    stride = taps // 2
    owner = onehot(iota((rows, members), 0) // share == iota((rows, members), 1))
    order_of = dot(owner, order_ref[...].astype(F32).astype(BF16))
    slot = iota((rows, rows), 1) - lax.rem(iota((rows, rows), 0), share) * members
    owner_first = iota((rows, 1), 0) // share * rows
    column = iota((rows, members * rows), 1)
    member = lax.axis_index("dev")
    low_half = member < members // 2
    for target, out_ref in ((member, near_ref), (jnp.bitwise_xor(member, members // 2), far_ref)):
        local = jnp.sum(jnp.where(slot == target, order_of, 0.0), axis=1, keepdims=True).astype(jnp.int32)
        picked = column == owner_first + local
        picks = picked.astype(F32)
        out_ref[...] = jnp.where(low_half, picks[: rows // 2], picks[rows // 2 :]).astype(BF16)
        if out_ref is near_ref:
            lens = jnp.sum(jnp.where(picked, len_ref[...], 0), axis=1, keepdims=True)
    valid = (lens - taps) // stride + 1
    valid_ref[...] = jnp.broadcast_to(valid, valid_ref.shape)
    depth = band_ref.shape[0]
    for f in range(GROUP):
        spread = onehot(iota((depth, taps), 0) == iota((depth, taps), 1) + stride * f)
        band_ref[:, f * chans : (f + 1) * chans] = dot(spread, w_ref[...]).astype(BF16)


def pick_kernel(offsets, near_ref, far_ref, *refs):
    waves, (mine_ref, send_ref, all_ref) = refs[:-3], refs[-3:]
    rows = waves[0].shape[0]
    all_ref[...] = jnp.zeros(all_ref.shape, BF16)
    for offset, wave_ref in zip(offsets, waves):
        first = pl.multiple_of(jnp.bitwise_xor(lax.axis_index("dev"), offset) * rows, rows)
        all_ref[pl.ds(first, rows), :] = wave_ref[...]
    mine_ref[...] = dot(near_ref[...], all_ref[...]).astype(BF16)
    send_ref[...] = dot(far_ref[...], all_ref[...]).astype(BF16)


def forward_kernel(
    frames0,
    frames1,
    taps,
    places,
    near_ref,
    far_ref,
    valid_ref,
    band_ref,
    gain_hbm,
    bias_hbm,
    w_hbm,
    cot_hbm,
    feat_ref,
    even_ref,
    odd_ref,
    pre0,
    even_slope,
    odd_slope,
    mean_ref,
    inv_ref,
    patch_ref,
    grad_ref,
    grad_t_ref,
    gain_ref,
    w_ref,
    stage,
    fresh,
    pre1,
    scale_ref,
    shift_ref,
    bias_ref,
    cot_ref,
    sems,
):
    waiting = copies((gain_hbm, bias_hbm, w_hbm, cot_hbm), (gain_ref, bias_ref, w_ref, cot_ref), sems)
    rows, samp = valid_ref.shape[0], near_ref.shape[1]
    chans = gain_ref.shape[1]
    stride = taps // 2
    depth = band_ref.shape[0]
    groups = pre0.shape[0]
    width = LANES
    parts = [slice(first, first + width) for first in range(0, chans, width)]
    min_valid = (MIN_SAMPLES - taps) // stride + 1
    full_groups = frames0 // GROUP
    free_groups = min(min_valid // GROUP, full_groups)
    low_half = lax.axis_index("dev") < lax.axis_size("dev") // 2
    near, far = near_ref[...].astype(F32), far_ref[...].astype(F32)
    wave = jnp.concatenate([jnp.where(low_half, near, far), jnp.where(low_half, far, near)], axis=0).astype(BF16)
    for g in range(groups):
        pick = onehot(iota((samp, depth), 0) == iota((samp, depth), 1) + GROUP * stride * g)
        patch_ref[g] = dot(wave, pick).astype(BF16)
    patches = patch_ref[...].reshape(groups * rows, depth)
    for f in range(GROUP):
        cols = slice(f * chans, (f + 1) * chans)
        pre0[:, :, cols] = dot(patches, band_ref[:, cols]).reshape(groups, rows, chans)

    valid = jnp.broadcast_to(valid_ref[:, :1], (rows, width))
    count = valid.astype(F32)

    def frame(g, f, lanes):
        return pre0[g, :, f * chans + lanes.start : f * chans + lanes.stop]

    def masked_to(value, t, masked):
        return jnp.where(valid > t, value, 0.0) if masked else value

    for lanes in parts:

        def over_frames(body):
            def step(masked, g, total):
                for f in range(GROUP):
                    total = total + body(g, f, masked)
                return total

            total = lax.fori_loop(0, free_groups, functools.partial(step, False), jnp.zeros((rows, width), F32))
            total = lax.fori_loop(free_groups, full_groups, functools.partial(step, True), total)
            for f in range(frames0 - full_groups * GROUP):
                total = total + body(full_groups, f, True)
            return total

        mean = over_frames(lambda g, f, masked: masked_to(frame(g, f, lanes), g * GROUP + f, masked)) / count

        def square(g, f, masked):
            centred = masked_to(frame(g, f, lanes) - mean, g * GROUP + f, masked)
            return centred * centred

        inv = lax.rsqrt(over_frames(square) / count + 1e-05)
        mean_ref[:, lanes] = mean
        inv_ref[:, lanes] = inv
        if lanes.start == 0:
            waiting[0].wait()
            waiting[1].wait()
        scale = inv * gain_ref[:, lanes]
        scale_ref[:, lanes] = scale
        shift_ref[:, lanes] = bias_ref[:, lanes] - mean * scale

    half = GROUP // 2
    span = half * rows
    frames_of = even_ref.shape[0] - 1
    even_ref[frames_of:] = jnp.zeros((1,) + even_ref.shape[1:], BF16)
    grad_ref[0] = jnp.zeros(grad_ref.shape[1:], BF16)
    grad_ref[frames1 + 1] = jnp.zeros(grad_ref.shape[1:], BF16)
    grad_t_ref[:, frames1 // half * span :] = jnp.zeros((chans, grad_t_ref.shape[1] - frames1 // half * span), BF16)
    min_valid1 = (min_valid - 3) // 2 + 1
    valid1 = lax.shift_right_arithmetic(valid - 3, 1) + 1
    slab = chans // len(places)

    def unstage(g):
        for f in range(GROUP):
            (odd_ref if f % 2 else even_ref)[g * half + f // 2] = stage[f]

    def activate0(g, masked, used=GROUP):
        for f in range(used):
            for lanes in parts:
                gelu, slope = gelu_and_slope(frame(g, f, lanes) * scale_ref[:, lanes] + shift_ref[:, lanes])
                t = g * GROUP + f
                slope_ref = odd_slope if f % 2 else even_slope
                slope_ref[g * half + f // 2, :, lanes] = masked_to(slope, t, masked)
                stage[f, :, lanes] = masked_to(gelu, t, masked).astype(BF16)

    def convolve(h, used):
        first = h * half
        for lanes in parts:
            total = dot(even_ref[pl.ds(first, used)].reshape(used * rows, chans), w_ref[0, :, lanes])
            total += dot(odd_ref[pl.ds(first, used)].reshape(used * rows, chans), w_ref[1, :, lanes])
            total += dot(even_ref[pl.ds(first + 1, used)].reshape(used * rows, chans), w_ref[2, :, lanes])
            fresh[:used, :, lanes] = total.reshape(used, rows, width)

    def activate1(h, used, masked):
        for j in range(used):
            u = h * half + j
            for lanes in parts:
                gelu, slope = gelu_and_slope(pre1[j, :, lanes])
                grad = cot_ref[u, :, lanes].astype(F32) * slope
                if masked:
                    gelu, grad = jnp.where(valid1 > u, gelu, 0.0), jnp.where(valid1 > u, grad, 0.0)
                feat_ref[u, :, lanes] = gelu.astype(BF16)
                grad_ref[u + 1, :, lanes] = grad.astype(BF16)

    def turn(h, used):
        turned = grad_ref[pl.ds(h * half + 1, used)].reshape(used * rows, chans).T
        start = h * span
        cols = pl.ds(start if isinstance(start, int) else pl.multiple_of(start, span), used * rows)
        for place, source in enumerate(places):
            grad_t_ref[place * slab : (place + 1) * slab, cols] = turned[source * slab : (source + 1) * slab]

    def fill(g, carry):
        unstage(jnp.maximum(g - 1, 0))
        activate0(g, False)
        return carry

    def steady(masked, g, carry, used=GROUP):
        unstage(g - 1)
        pre1[...] = fresh[...]
        convolve(g - 2, half)
        activate1(g - 3, half, masked)
        activate0(g, masked, used)
        turn(g - 3, half)
        return carry

    stage[...] = jnp.zeros(stage.shape, BF16)
    lax.fori_loop(0, 3, fill, 0)
    waiting[2].wait()
    waiting[3].wait()
    convolve(0, half)
    lax.fori_loop(3, free_groups, functools.partial(steady, False), 0)
    lax.fori_loop(free_groups, full_groups, functools.partial(steady, True), 0)
    rest = frames0 - full_groups * GROUP
    if rest:
        steady(True, full_groups, 0, rest)
        stage[rest:] = jnp.zeros((GROUP - rest,) + stage.shape[1:], BF16)
    unstage(groups - 1)
    last = frames1 // half
    for h in range(groups - 2, last + 1):
        pre1[...] = fresh[...]
        convolve(h, min(half, frames1 - h * half))
        activate1(h - 1, half, True)
        turn(h - 1, half)
    pre1[...] = fresh[...]
    activate1(last, frames1 - last * half, True)
    turn(last, frames1 - last * half)


def outer_kernel(skip, act_ref, grad_t_ref, keep_ref, send_ref):
    rows, chans = act_ref.shape[1:]
    frames = grad_t_ref.shape[1] // rows
    half = chans // 2
    core = lax.rem(lax.axis_index("grp"), 2)
    for side, out_ref in ((1 - core, send_ref), (core, keep_ref)):
        lanes = pl.ds(pl.multiple_of(side * half, half), half)
        acts = act_ref[skip : skip + frames, :, lanes].reshape(frames * rows, half)
        out_ref[...] = dot(grad_t_ref[...], acts).astype(out_ref.dtype)


def input_kernel(grad_ref, w_ref, even_slope, odd_slope, after_ref, feat_ref, even_ref, odd_ref, feat_out, sem):
    leaving = pltpu.make_async_copy(feat_ref, feat_out, sem)
    leaving.start()
    evens, rows, chans = even_ref.shape
    odds = odd_ref.shape[0]
    first = grad_ref[1 : evens + 1].reshape(evens * rows, chans)
    third = grad_ref[0:evens].reshape(evens * rows, chans)
    total = cols_both(first, w_ref[0]) + cols_both(third, w_ref[2])
    even_ref[...] = total.reshape(even_ref.shape) * even_slope[:evens]
    second = grad_ref[1 : odds + 1].reshape(odds * rows, chans)
    odd_ref[...] = cols_both(second, w_ref[1]).reshape(odd_ref.shape) * odd_slope[:odds]
    leaving.wait()


def backward_kernel(
    frames0,
    taps,
    valid_ref,
    pre0,
    mean_ref,
    inv_ref,
    patch_ref,
    even_ref,
    odd_ref,
    gain_ref,
    mine_ref,
    send1,
    send2,
    send3,
    dpre0,
    spread,
    out_ref,
    quarters,
):
    groups, rows, depth = patch_ref.shape
    chans = gain_ref.shape[1]
    stride = taps // 2
    width = dpre0.shape[2] // GROUP
    full_groups = frames0 // GROUP
    free_groups = min(((MIN_SAMPLES - taps) // stride + 1) // GROUP, full_groups)
    rest = frames0 - full_groups * GROUP
    patches = patch_ref[...].reshape(groups * rows, depth)
    for block in range(chans // width):
        lanes = slice(block * width, (block + 1) * width)

        def frame(g, f):
            return pre0[g, :, f * chans + block * width : f * chans + (block + 1) * width]

        def lift(g, f):
            return (odd_ref if f % 2 else even_ref)[g * (GROUP // 2) + f // 2, :, lanes]

        def sums(g, f, carry):
            bias_sum, gain_sum = carry
            return bias_sum + lift(g, f), gain_sum + lift(g, f) * frame(g, f)

        def add(g, carry):
            for f in range(GROUP):
                carry = sums(g, f, carry)
            return carry

        zero = jnp.zeros((rows, width), F32)
        carry = lax.fori_loop(0, full_groups, add, (zero, zero))
        for f in range(rest):
            carry = sums(full_groups, f, carry)
        bias_sum, gain_sum = carry
        mean, inv = mean_ref[:, lanes], inv_ref[:, lanes]
        gain_sum = (gain_sum - mean * bias_sum) * inv
        out_ref[taps : taps + 1, lanes] = jnp.sum(gain_sum, axis=0, keepdims=True)
        out_ref[taps + 1 : taps + 2, lanes] = jnp.sum(bias_sum, axis=0, keepdims=True)
        valid = jnp.broadcast_to(valid_ref[:, :1], (rows, width))
        count = valid.astype(F32)
        scale = inv * gain_ref[:, lanes]
        slant = scale * inv * gain_sum / count
        level = scale * bias_sum / count - mean * slant

        def finish(g, f, masked):
            value = scale * lift(g, f) - frame(g, f) * slant - level
            if masked:
                value = jnp.where(valid > g * GROUP + f, value, 0.0)
            dpre0[g, :, f * width : (f + 1) * width] = value.astype(BF16)

        def whole(masked, g, carry):
            for f in range(GROUP):
                finish(g, f, masked)
            return carry

        lax.fori_loop(0, free_groups, functools.partial(whole, False), 0)
        lax.fori_loop(free_groups, full_groups, functools.partial(whole, True), 0)
        for f in range(rest):
            finish(full_groups, f, True)
        if full_groups < groups:
            dpre0[full_groups, :, rest * width :] = jnp.zeros((rows, (GROUP - rest) * width), BF16)
        spread[...] = rows_first(patches, dpre0[...].reshape(groups * rows, GROUP * width))
        total = jnp.zeros((taps, width), F32)
        for f in range(GROUP):
            total += spread[stride * f : stride * f + taps, f * width : (f + 1) * width]
        out_ref[:taps, lanes] = total
    size = chans // lax.axis_size("dev")
    for place in range(4):
        columns = [slice(first, first + size) for first in range(place * size, chans, 4 * size)]
        quarters[place] = jnp.concatenate([out_ref[:, part] for part in columns], axis=1)
    place = lax.rem(lax.axis_index("dev"), 4)
    for offset, ref in enumerate((mine_ref, send1, send2, send3)):
        ref[...] = quarters[jnp.bitwise_xor(place, offset)]


def plane_kernel(second, *refs):
    keeps, others, outs = refs[:second], refs[second : 2 * second], refs[2 * second :]
    size = outs[0].shape[0]
    half = keeps[0].shape[1]
    place = lax.rem(lax.axis_index("dev"), 4)
    for offset, out_ref in enumerate(outs):
        lines = pl.ds(pl.multiple_of(jnp.bitwise_xor(place, offset) * size, size), size)
        for tap, (keep_ref, got_ref) in enumerate(zip(keeps, others)):
            value = keep_ref[lines, :] + got_ref[lines, :].astype(F32)
            out_ref[:, tap * half : (tap + 1) * half] = value.astype(out_ref.dtype)


def part_kernel(own_ref, got1, got2, small_ref, sum_ref, total_ref):
    sum_ref[...] = own_ref[...] + (got1[...].astype(F32) + got2[...].astype(F32))
    total_ref[...] = small_ref[...]


def packed(size, wide):
    return size + 16, wide - 128


def write_packed(ref, value, small):
    size, lanes = ref.shape[0] - 16, ref.shape[1]
    ref[:size] = value[:, :lanes].astype(ref.dtype)
    used = size // 16
    for block in range(used):
        piece = value[block * 16 : (block + 1) * 16, lanes:]
        ref[size:, block * 128 : (block + 1) * 128] = piece.astype(ref.dtype)
    for first in range(used * 128, lanes - 128, 128):
        ref[size:, first : first + 128] = jnp.zeros((16, 128), ref.dtype)
    ref[size:, lanes - 128 :] = small.astype(ref.dtype)


def read_packed(ref, first, count):
    size = ref.shape[0] - 16
    whole = ref[pl.ds(pl.multiple_of(first, 16), count), :].astype(F32)
    pieces = [
        ref[size:, pl.ds(pl.multiple_of(first * 8 + block * 128, 128), 128)].astype(F32) for block in range(count // 16)
    ]
    return jnp.concatenate([whole, jnp.concatenate(pieces, axis=0)], axis=1)


def gather_kernel(bit, own_ref, got3, small0, small1, small2, small3, keep_ref, send_ref):
    half = own_ref.shape[0] // 2
    side = lax.rem(lax.shift_right_logical(lax.axis_index("dev"), bit), 2)
    total = (small0[...] + small1[...]) + (small2[...] + small3[...])
    for index, ref in ((1 - side, send_ref), (side, keep_ref)):
        lines = pl.ds(pl.multiple_of(index * half, half), half)
        write_packed(ref, own_ref[lines, :] + got3[lines, :].astype(F32), total)


def halve_kernel(bit, keep_ref, got_ref, next_ref, send_ref):
    half = (keep_ref.shape[0] - 16) // 2
    side = lax.rem(lax.shift_right_logical(lax.axis_index("dev"), bit), 2)
    small = keep_ref[2 * half :, -128:] + got_ref[2 * half :, -128:].astype(F32)
    for index, ref in ((1 - side, send_ref), (side, next_ref)):
        first = index * half
        write_packed(ref, read_packed(keep_ref, first, half) + read_packed(got_ref, first, half), small)


def add_kernel(mine_ref, got_ref, out_ref):
    out_ref[...] = (mine_ref[...].astype(F32) + got_ref[...].astype(F32)).astype(out_ref.dtype)


def join_kernel(taps, own_ref, other_ref, out_ref, first_ref, gain_ref, bias_ref):
    second, size, chans = out_ref.shape
    half = chans // 2
    core = lax.rem(lax.axis_index("grp"), 2)
    for ref, side in ((own_ref, core), (other_ref, 1 - core)):
        value = read_packed(ref, 0, size)
        for tap in range(second):
            lanes = pl.ds(pl.multiple_of(side * half, half), half)
            out_ref[tap, :, lanes] = value[:, tap * half : (tap + 1) * half]
    total = own_ref[size:, -128:] + other_ref[size:, -128:]
    value = total[:, :size]
    for place in range(1, 128 // size):
        mine = lax.axis_index("dev") // 4 == place
        value = jnp.where(mine, total[:, place * size : (place + 1) * size], value)
    first_ref[...] = value[:taps]
    gain_ref[...] = value[taps : taps + 1]
    bias_ref[...] = value[taps + 1 : taps + 2]


def call(kernel, outs, args, scratch=(), limit=24, flops=0, touched=0, outside=()):
    vmem = pl.BlockSpec(memory_space=pltpu.VMEM)
    args = [pltpu.with_memory_space_constraint(arg, pltpu.HBM) if i in outside else arg for i, arg in enumerate(args)]
    return pl.pallas_call(
        kernel,
        out_shape=[
            jax.ShapeDtypeStruct(out[0], out[1]) if len(out) > 2 else pltpu.VMEM(out[0], out[1]) for out in outs
        ],
        in_specs=[pl.BlockSpec(memory_space=pltpu.HBM) if i in outside else vmem for i in range(len(args))],
        out_specs=[pl.BlockSpec(memory_space=pl.ANY) if out[-1] == "hbm" else vmem for out in outs],
        scratch_shapes=[pltpu.VMEM(*entry) if isinstance(entry, tuple) else entry for entry in scratch],
        compiler_params=pltpu.CompilerParams(vmem_limit_bytes=limit * MIB),
        cost_estimate=pl.CostEstimate(flops=flops, bytes_accessed=touched, transcendentals=0),
    )(*args)


def swap(value, axis, offset):
    size = lax.axis_size(axis)
    return lax.ppermute(value, axis, [(i, i ^ offset) for i in range(size)])


def shards(wave, lengths, order, w_first, norm_gain, norm_bias, w_second, cot):
    members = lax.axis_size("dev")
    groups_of = lax.axis_size("grp")
    rows, samp = wave.shape
    taps, chans = w_first.shape
    taps_second = w_second.shape[0]
    stride = taps // 2
    frames0 = (samp - taps) // stride + 1
    frames1 = (frames0 - taps_second) // 2 + 1
    groups = -(-frames0 // GROUP)
    depth = 128
    width = LANES
    dev_bits = members.bit_length() - 1
    grp_bits = groups_of.bit_length() - 1

    offsets = [0, 1, 2, 3]
    waves = [wave] + [swap(wave, "dev", offset) for offset in offsets[1:]]
    for bit in range(2, dev_bits - 1):
        offsets += [offset | (1 << bit) for offset in offsets]
        waves += [swap(held, "dev", 1 << bit) for held in waves]
    lens = lengths.reshape(1, members * rows)
    every = members * rows
    valid, band, near_sel, far_sel, own_wave = call(
        functools.partial(setup_kernel, members),
        [
            ((rows, 128), jnp.int32),
            ((depth, GROUP * chans), BF16),
            ((rows // 2, every), BF16),
            ((rows // 2, every), BF16),
            ((rows, samp), BF16),
        ],
        [order, lens, w_first, wave],
        scratch=[
            (order.shape, order.dtype),
            (lens.shape, lens.dtype),
            (w_first.shape, BF16),
            pltpu.SemaphoreType.DMA((4,)),
        ],
        outside=(0, 1, 2, 3),
    )
    near, send = call(
        functools.partial(pick_kernel, offsets),
        [((rows // 2, samp), BF16), ((rows // 2, samp), BF16)],
        [near_sel, far_sel, own_wave, *waves[1:]],
        scratch=[((every, samp), BF16)],
    )
    far = swap(send, "dev", members // 2)
    gain = norm_gain.reshape(1, chans)
    bias = norm_bias.reshape(1, chans)
    cot_t = cot.transpose(1, 0, 2)
    pad_frames = -(-frames1 // 4) * 4
    places = [0] * members
    for dev in range(members):
        places[dev % 4 * (members // 4) + dev // 4] = dev
    feat, even, odd, pre0, even_slope, odd_slope, mean, inv, patch, grad, grad_t, gain_in, w_in = call(
        functools.partial(forward_kernel, frames0, frames1, taps, places),
        [
            ((frames1, rows, chans), BF16),
            ((pad_frames + 1, rows, chans), BF16),
            ((pad_frames, rows, chans), BF16),
            ((groups, rows, GROUP * chans), F32),
            ((pad_frames, rows, chans), F32),
            ((pad_frames, rows, chans), F32),
            ((rows, chans), F32),
            ((rows, chans), F32),
            ((groups, rows, depth), BF16),
            ((frames1 + 2, rows, chans), BF16),
            ((chans, pad_frames * rows), BF16),
            ((1, chans), F32),
            (w_second.shape, BF16),
        ],
        [near, far, valid, band, gain, bias, w_second, cot_t],
        scratch=[
            ((GROUP, rows, chans), BF16),
            ((GROUP // 2, rows, chans), F32),
            ((GROUP // 2, rows, chans), F32),
            ((rows, chans), F32),
            ((rows, chans), F32),
            (bias.shape, F32),
            (cot_t.shape, BF16),
            pltpu.SemaphoreType.DMA((4,)),
        ],
        outside=(4, 5, 6, 7),
    )
    half = chans // 2
    wide = taps_second * half
    keeps, others = [], []
    for acts, skip in ((even, 0), (odd, 0), (even, 1)):
        keep, send = call(
            functools.partial(outer_kernel, skip),
            [((chans, half), F32), ((chans, half), BF16)],
            [acts, grad_t],
            flops=1 << 29,
        )
        keeps.append(keep)
        others.append(swap(send, "grp", 1))
    quarter = chans // 4
    own, *sends = call(
        functools.partial(plane_kernel, taps_second),
        [((quarter, wide), F32)] + [((quarter, wide), BF16)] * 3,
        [*keeps, *others],
    )
    gots = [swap(part, "dev", offset) for offset, part in enumerate(sends, 1)]
    evens, odds = (frames0 + 1) // 2, frames0 // 2
    lift_even, lift_odd, features = call(
        input_kernel,
        [((evens, rows, chans), F32), ((odds, rows, chans), F32), ((frames1, rows, chans), BF16, "hbm")],
        [grad, w_in, even_slope, odd_slope, own, feat],
        scratch=[pltpu.SemaphoreType.DMA],
        flops=1 << 30,
    )
    small, *smalls = call(
        functools.partial(backward_kernel, frames0, taps),
        [((16, quarter), F32)] * 4,
        [valid, pre0, mean, inv, patch, lift_even, lift_odd, gain_in],
        scratch=[
            ((groups, rows, GROUP * width), BF16),
            ((depth, GROUP * width), F32),
            ((16, chans), F32),
            ((4, 16, quarter), F32),
        ],
        flops=1 << 32,
    )
    small3, small2 = swap(smalls[2], "dev", 3), swap(smalls[1], "dev", 2)
    own, first = call(
        part_kernel, [((quarter, wide), F32), (small.shape, F32)], [own, gots[0], gots[1], smalls[0]]
    )
    small1 = swap(first, "dev", 1)
    size = quarter // 2
    keep, send = call(
        functools.partial(gather_kernel, dev_bits - 1),
        [(packed(size, wide), F32), (packed(size, wide), BF16)],
        [own, gots[2], small, small1, small2, small3],
    )
    for bit in range(dev_bits - 1, 2, -1):
        size //= 2
        keep, send = call(
            functools.partial(halve_kernel, bit - 1),
            [(packed(size, wide), F32), (packed(size, wide), BF16)],
            [keep, swap(send, "dev", 1 << bit)],
        )
    send = call(add_kernel, [(packed(size, wide), BF16)], [keep, swap(send, "dev", 4)])[0]
    for bit in range(1, grp_bits):
        kind = F32 if bit == grp_bits - 1 else BF16
        send = call(add_kernel, [(packed(size, wide), kind)], [send, swap(send, "grp", 1 << bit)])[0]
    grad_second, grad_first, grad_gain, grad_bias = call(
        functools.partial(join_kernel, taps),
        [
            ((taps_second, size, chans), F32, "out"),
            ((taps, size), F32, "out"),
            ((1, size), F32, "out"),
            ((1, size), F32, "out"),
        ],
        [send, swap(send, "grp", 1)],
    )
    return (
        features.transpose(1, 0, 2),
        grad_second.transpose(0, 2, 1),
        grad_first,
        grad_gain.reshape(size),
        grad_bias.reshape(size),
    )


def solution(mesh):
    placed = (
        P(("grp", "dev"), None),
        P("grp"),
        P("grp", None),
        P(),
        P(),
        P(),
        P(),
        P(("grp", "dev"), None, None),
    )
    return jax.shard_map(
        shards,
        mesh=mesh,
        in_specs=placed,
        out_specs=(
            P(("grp", "dev"), None, None),
            P(None, None, "dev"),
            P(None, "dev"),
            P("dev"),
            P("dev"),
        ),
        check_vma=False,
    )
```

```python
import functools

import jax
import jax.numpy as jnp
from jax import lax
from jax.experimental import pallas as pl
from jax.experimental.pallas import tpu as pltpu
from jax.sharding import PartitionSpec as P

F32 = jnp.float32
BF16 = jnp.bfloat16
GROUP = 8
LANES = 256
MIN_SAMPLES = 288
MIB = 1 << 20


def gelu_and_slope(value):
    bell = jnp.exp2(value * value * (-0.5 * 1.4426950408889634))
    phi = 0.5 + 0.5 * lax.erf(value * 0.7071067811865476)
    return value * phi, phi + value * bell * 0.3989422804014327


def rows_first(a, b):
    return lax.dot_general(a, b, (((0,), (0,)), ((), ())), preferred_element_type=F32)


def cols_both(a, b):
    return lax.dot_general(a, b, (((1,), (1,)), ((), ())), preferred_element_type=F32)


def dot(a, b):
    return jnp.dot(a, b, preferred_element_type=F32)


def iota(shape, dim):
    return lax.broadcasted_iota(jnp.int32, shape, dim)


def onehot(mask):
    return mask.astype(F32).astype(BF16)


def copies(sources, targets, sems):
    started = [pltpu.make_async_copy(source, target, sems.at[i]) for i, (source, target) in enumerate(zip(sources, targets))]
    for copy in started:
        copy.start()
    return started


def setup_kernel(
    members,
    order_hbm,
    len_hbm,
    w_hbm,
    wave_hbm,
    valid_ref,
    band_ref,
    near_ref,
    far_ref,
    own_ref,
    order_ref,
    len_ref,
    w_ref,
    sems,
):
    for copy in copies((order_hbm, len_hbm, w_hbm, wave_hbm), (order_ref, len_ref, w_ref, own_ref), sems):
        copy.wait()
    rows = order_ref.shape[1]
    share = rows // members
    taps, chans = w_ref.shape
    stride = taps // 2
    owner = onehot(iota((rows, members), 0) // share == iota((rows, members), 1))
    order_of = dot(owner, order_ref[...].astype(F32).astype(BF16))
    slot = iota((rows, rows), 1) - lax.rem(iota((rows, rows), 0), share) * members
    owner_first = iota((rows, 1), 0) // share * rows
    column = iota((rows, members * rows), 1)
    member = lax.axis_index("dev")
    low_half = member < members // 2
    for target, out_ref in ((member, near_ref), (jnp.bitwise_xor(member, members // 2), far_ref)):
        local = jnp.sum(jnp.where(slot == target, order_of, 0.0), axis=1, keepdims=True).astype(jnp.int32)
        picked = column == owner_first + local
        picks = picked.astype(F32)
        out_ref[...] = jnp.where(low_half, picks[: rows // 2], picks[rows // 2 :]).astype(BF16)
        if out_ref is near_ref:
            lens = jnp.sum(jnp.where(picked, len_ref[...], 0), axis=1, keepdims=True)
    valid = (lens - taps) // stride + 1
    valid_ref[...] = jnp.broadcast_to(valid, valid_ref.shape)
    depth = band_ref.shape[0]
    for f in range(GROUP):
        spread = onehot(iota((depth, taps), 0) == iota((depth, taps), 1) + stride * f)
        band_ref[:, f * chans : (f + 1) * chans] = dot(spread, w_ref[...]).astype(BF16)


def pick_kernel(offsets, near_ref, far_ref, *refs):
    waves, (mine_ref, send_ref, all_ref) = refs[:-3], refs[-3:]
    rows = waves[0].shape[0]
    all_ref[...] = jnp.zeros(all_ref.shape, BF16)
    for offset, wave_ref in zip(offsets, waves):
        first = pl.multiple_of(jnp.bitwise_xor(lax.axis_index("dev"), offset) * rows, rows)
        all_ref[pl.ds(first, rows), :] = wave_ref[...]
    mine_ref[...] = dot(near_ref[...], all_ref[...]).astype(BF16)
    send_ref[...] = dot(far_ref[...], all_ref[...]).astype(BF16)


def forward_kernel(
    frames0,
    frames1,
    taps,
    places,
    near_ref,
    far_ref,
    valid_ref,
    band_ref,
    gain_hbm,
    bias_hbm,
    w_hbm,
    cot_hbm,
    feat_ref,
    even_ref,
    odd_ref,
    pre0,
    even_slope,
    odd_slope,
    mean_ref,
    inv_ref,
    patch_ref,
    grad_ref,
    grad_t_ref,
    gain_ref,
    w_ref,
    stage,
    fresh,
    pre1,
    scale_ref,
    shift_ref,
    bias_ref,
    cot_ref,
    sems,
):
    waiting = copies((gain_hbm, bias_hbm, w_hbm, cot_hbm), (gain_ref, bias_ref, w_ref, cot_ref), sems)
    rows, samp = valid_ref.shape[0], near_ref.shape[1]
    chans = gain_ref.shape[1]
    stride = taps // 2
    depth = band_ref.shape[0]
    groups = pre0.shape[0]
    width = LANES
    parts = [slice(first, first + width) for first in range(0, chans, width)]
    min_valid = (MIN_SAMPLES - taps) // stride + 1
    full_groups = frames0 // GROUP
    free_groups = min(min_valid // GROUP, full_groups)
    low_half = lax.axis_index("dev") < lax.axis_size("dev") // 2
    near, far = near_ref[...].astype(F32), far_ref[...].astype(F32)
    wave = jnp.concatenate([jnp.where(low_half, near, far), jnp.where(low_half, far, near)], axis=0).astype(BF16)
    for g in range(groups):
        pick = onehot(iota((samp, depth), 0) == iota((samp, depth), 1) + GROUP * stride * g)
        patch_ref[g] = dot(wave, pick).astype(BF16)
    patches = patch_ref[...].reshape(groups * rows, depth)
    for f in range(GROUP):
        cols = slice(f * chans, (f + 1) * chans)
        pre0[:, :, cols] = dot(patches, band_ref[:, cols]).reshape(groups, rows, chans)

    valid = jnp.broadcast_to(valid_ref[:, :1], (rows, width))
    count = valid.astype(F32)

    def frame(g, f, lanes):
        return pre0[g, :, f * chans + lanes.start : f * chans + lanes.stop]

    def masked_to(value, t, masked):
        return jnp.where(valid > t, value, 0.0) if masked else value

    for lanes in parts:

        def over_frames(body):
            def step(masked, g, total):
                for f in range(GROUP):
                    total = total + body(g, f, masked)
                return total

            total = lax.fori_loop(0, free_groups, functools.partial(step, False), jnp.zeros((rows, width), F32))
            total = lax.fori_loop(free_groups, full_groups, functools.partial(step, True), total)
            for f in range(frames0 - full_groups * GROUP):
                total = total + body(full_groups, f, True)
            return total

        mean = over_frames(lambda g, f, masked: masked_to(frame(g, f, lanes), g * GROUP + f, masked)) / count

        def square(g, f, masked):
            centred = masked_to(frame(g, f, lanes) - mean, g * GROUP + f, masked)
            return centred * centred

        inv = lax.rsqrt(over_frames(square) / count + 1e-05)
        mean_ref[:, lanes] = mean
        inv_ref[:, lanes] = inv
        if lanes.start == 0:
            waiting[0].wait()
            waiting[1].wait()
        scale = inv * gain_ref[:, lanes]
        scale_ref[:, lanes] = scale
        shift_ref[:, lanes] = bias_ref[:, lanes] - mean * scale

    half = GROUP // 2
    span = half * rows
    frames_of = even_ref.shape[0] - 1
    even_ref[frames_of:] = jnp.zeros((1,) + even_ref.shape[1:], BF16)
    grad_ref[0] = jnp.zeros(grad_ref.shape[1:], BF16)
    grad_ref[frames1 + 1] = jnp.zeros(grad_ref.shape[1:], BF16)
    grad_t_ref[:, frames1 // half * span :] = jnp.zeros((chans, grad_t_ref.shape[1] - frames1 // half * span), BF16)
    min_valid1 = (min_valid - 3) // 2 + 1
    valid1 = lax.shift_right_arithmetic(valid - 3, 1) + 1
    slab = chans // len(places)

    def unstage(g):
        for f in range(GROUP):
            (odd_ref if f % 2 else even_ref)[g * half + f // 2] = stage[f]

    def activate0(g, masked, used=GROUP):
        for f in range(used):
            for lanes in parts:
                gelu, slope = gelu_and_slope(frame(g, f, lanes) * scale_ref[:, lanes] + shift_ref[:, lanes])
                t = g * GROUP + f
                slope_ref = odd_slope if f % 2 else even_slope
                slope_ref[g * half + f // 2, :, lanes] = masked_to(slope, t, masked)
                stage[f, :, lanes] = masked_to(gelu, t, masked).astype(BF16)

    def convolve(h, used):
        first = h * half
        for lanes in parts:
            total = dot(even_ref[pl.ds(first, used)].reshape(used * rows, chans), w_ref[0, :, lanes])
            total += dot(odd_ref[pl.ds(first, used)].reshape(used * rows, chans), w_ref[1, :, lanes])
            total += dot(even_ref[pl.ds(first + 1, used)].reshape(used * rows, chans), w_ref[2, :, lanes])
            fresh[:used, :, lanes] = total.reshape(used, rows, width)

    def activate1(h, used, masked):
        for j in range(used):
            u = h * half + j
            for lanes in parts:
                gelu, slope = gelu_and_slope(pre1[j, :, lanes])
                grad = cot_ref[u, :, lanes].astype(F32) * slope
                if masked:
                    gelu, grad = jnp.where(valid1 > u, gelu, 0.0), jnp.where(valid1 > u, grad, 0.0)
                feat_ref[u, :, lanes] = gelu.astype(BF16)
                grad_ref[u + 1, :, lanes] = grad.astype(BF16)

    def turn(h, used):
        turned = grad_ref[pl.ds(h * half + 1, used)].reshape(used * rows, chans).T
        start = h * span
        cols = pl.ds(start if isinstance(start, int) else pl.multiple_of(start, span), used * rows)
        for place, source in enumerate(places):
            grad_t_ref[place * slab : (place + 1) * slab, cols] = turned[source * slab : (source + 1) * slab]

    def fill(g, carry):
        unstage(jnp.maximum(g - 1, 0))
        activate0(g, False)
        return carry

    def steady(masked, g, carry, used=GROUP):
        unstage(g - 1)
        pre1[...] = fresh[...]
        convolve(g - 2, half)
        activate1(g - 3, half, masked)
        activate0(g, masked, used)
        turn(g - 3, half)
        return carry

    stage[...] = jnp.zeros(stage.shape, BF16)
    lax.fori_loop(0, 3, fill, 0)
    waiting[2].wait()
    waiting[3].wait()
    convolve(0, half)
    lax.fori_loop(3, free_groups, functools.partial(steady, False), 0)
    lax.fori_loop(free_groups, full_groups, functools.partial(steady, True), 0)
    rest = frames0 - full_groups * GROUP
    if rest:
        steady(True, full_groups, 0, rest)
        stage[rest:] = jnp.zeros((GROUP - rest,) + stage.shape[1:], BF16)
    unstage(groups - 1)
    last = frames1 // half
    for h in range(groups - 2, last + 1):
        pre1[...] = fresh[...]
        convolve(h, min(half, frames1 - h * half))
        activate1(h - 1, half, True)
        turn(h - 1, half)
    pre1[...] = fresh[...]
    activate1(last, frames1 - last * half, True)
    turn(last, frames1 - last * half)


def outer_kernel(skips, *refs):
    acts, (grad_t_ref, keep_ref, send_ref) = refs[:-3], refs[-3:]
    rows, chans = acts[0].shape[1:]
    frames = grad_t_ref.shape[1] // rows
    half = chans // 2
    core = lax.rem(lax.axis_index("grp"), 2)
    for tap, (act_ref, skip) in enumerate(zip(acts, skips)):
        for side, out_ref in ((1 - core, send_ref), (core, keep_ref)):
            lanes = pl.ds(pl.multiple_of(side * half, half), half)
            value = dot(grad_t_ref[...], act_ref[skip : skip + frames, :, lanes].reshape(frames * rows, half))
            out_ref[:, tap * half : (tap + 1) * half] = value.astype(out_ref.dtype)


def input_kernel(grad_ref, w_ref, even_slope, odd_slope, after_ref, feat_ref, even_ref, odd_ref, feat_out, sem):
    leaving = pltpu.make_async_copy(feat_ref, feat_out, sem)
    leaving.start()
    evens, rows, chans = even_ref.shape
    odds = odd_ref.shape[0]
    first = grad_ref[1 : evens + 1].reshape(evens * rows, chans)
    third = grad_ref[0:evens].reshape(evens * rows, chans)
    total = cols_both(first, w_ref[0]) + cols_both(third, w_ref[2])
    even_ref[...] = total.reshape(even_ref.shape) * even_slope[:evens]
    second = grad_ref[1 : odds + 1].reshape(odds * rows, chans)
    odd_ref[...] = cols_both(second, w_ref[1]).reshape(odd_ref.shape) * odd_slope[:odds]
    leaving.wait()


def backward_kernel(
    frames0,
    taps,
    valid_ref,
    pre0,
    mean_ref,
    inv_ref,
    patch_ref,
    even_ref,
    odd_ref,
    gain_ref,
    small_ref,
    dpre0,
    spread,
    out_ref,
    quarters,
):
    groups, rows, depth = patch_ref.shape
    chans = gain_ref.shape[1]
    stride = taps // 2
    width = dpre0.shape[2] // GROUP
    full_groups = frames0 // GROUP
    free_groups = min(((MIN_SAMPLES - taps) // stride + 1) // GROUP, full_groups)
    rest = frames0 - full_groups * GROUP
    patches = patch_ref[...].reshape(groups * rows, depth)
    for block in range(chans // width):
        lanes = slice(block * width, (block + 1) * width)

        def frame(g, f):
            return pre0[g, :, f * chans + block * width : f * chans + (block + 1) * width]

        def lift(g, f):
            return (odd_ref if f % 2 else even_ref)[g * (GROUP // 2) + f // 2, :, lanes]

        def sums(g, f, carry):
            bias_sum, gain_sum = carry
            return bias_sum + lift(g, f), gain_sum + lift(g, f) * frame(g, f)

        def add(g, carry):
            for f in range(GROUP):
                carry = sums(g, f, carry)
            return carry

        zero = jnp.zeros((rows, width), F32)
        carry = lax.fori_loop(0, full_groups, add, (zero, zero))
        for f in range(rest):
            carry = sums(full_groups, f, carry)
        bias_sum, gain_sum = carry
        mean, inv = mean_ref[:, lanes], inv_ref[:, lanes]
        gain_sum = (gain_sum - mean * bias_sum) * inv
        out_ref[taps : taps + 1, lanes] = jnp.sum(gain_sum, axis=0, keepdims=True)
        out_ref[taps + 1 : taps + 2, lanes] = jnp.sum(bias_sum, axis=0, keepdims=True)
        valid = jnp.broadcast_to(valid_ref[:, :1], (rows, width))
        count = valid.astype(F32)
        scale = inv * gain_ref[:, lanes]
        slant = scale * inv * gain_sum / count
        level = scale * bias_sum / count - mean * slant

        def finish(g, f, masked):
            value = scale * lift(g, f) - frame(g, f) * slant - level
            if masked:
                value = jnp.where(valid > g * GROUP + f, value, 0.0)
            dpre0[g, :, f * width : (f + 1) * width] = value.astype(BF16)

        def whole(masked, g, carry):
            for f in range(GROUP):
                finish(g, f, masked)
            return carry

        lax.fori_loop(0, free_groups, functools.partial(whole, False), 0)
        lax.fori_loop(free_groups, full_groups, functools.partial(whole, True), 0)
        for f in range(rest):
            finish(full_groups, f, True)
        if full_groups < groups:
            dpre0[full_groups, :, rest * width :] = jnp.zeros((rows, (GROUP - rest) * width), BF16)
        spread[...] = rows_first(patches, dpre0[...].reshape(groups * rows, GROUP * width))
        total = jnp.zeros((taps, width), F32)
        for f in range(GROUP):
            total += spread[stride * f : stride * f + taps, f * width : (f + 1) * width]
        out_ref[:taps, lanes] = total
    size = chans // lax.axis_size("dev")
    for place in range(4):
        columns = [slice(first, first + size) for first in range(place * size, chans, 4 * size)]
        quarters[place] = jnp.concatenate([out_ref[:, part] for part in columns], axis=1)
    place = lax.rem(lax.axis_index("dev"), 4)
    for offset in range(4):
        small_ref[offset * 16 : (offset + 1) * 16] = quarters[jnp.bitwise_xor(place, offset)]


def core_kernel(mine_ref, got_ref, *out_refs):
    for place, ref in enumerate(out_refs):
        lines = slice(place * 16, (place + 1) * 16)
        ref[...] = mine_ref[lines] + got_ref[lines]


def plane_kernel(*refs):
    keeps, others, outs = refs[:2], refs[2:4], refs[4:]
    size = outs[0].shape[0]
    edge = keeps[0].shape[1]
    place = lax.rem(lax.axis_index("dev"), 4)
    for offset, out_ref in enumerate(outs):
        lines = pl.ds(pl.multiple_of(jnp.bitwise_xor(place, offset) * size, size), size)
        for lanes, keep_ref, got_ref in zip((slice(0, edge), slice(edge, None)), keeps, others):
            out_ref[:, lanes] = (keep_ref[lines, :] + got_ref[lines, :].astype(F32)).astype(out_ref.dtype)


def part_kernel(own_ref, got1, got2, small_ref, sum_ref, total_ref):
    sum_ref[...] = own_ref[...] + (got1[...].astype(F32) + got2[...].astype(F32))
    total_ref[...] = small_ref[...]


def packed(size, wide):
    return size + 16, wide - 128


def write_packed(ref, value, small):
    size, lanes = ref.shape[0] - 16, ref.shape[1]
    ref[:size] = value[:, :lanes].astype(ref.dtype)
    used = size // 16
    for block in range(used):
        piece = value[block * 16 : (block + 1) * 16, lanes:]
        ref[size:, block * 128 : (block + 1) * 128] = piece.astype(ref.dtype)
    for first in range(used * 128, lanes - 128, 128):
        ref[size:, first : first + 128] = jnp.zeros((16, 128), ref.dtype)
    ref[size:, lanes - 128 :] = small.astype(ref.dtype)


def read_packed(ref, first, count):
    size = ref.shape[0] - 16
    whole = ref[pl.ds(pl.multiple_of(first, 16), count), :].astype(F32)
    pieces = [
        ref[size:, pl.ds(pl.multiple_of(first * 8 + block * 128, 128), 128)].astype(F32) for block in range(count // 16)
    ]
    return jnp.concatenate([whole, jnp.concatenate(pieces, axis=0)], axis=1)


def gather_kernel(bit, own_ref, got3, small0, small1, small2, small3, keep_ref, send_ref):
    half = own_ref.shape[0] // 2
    side = lax.rem(lax.shift_right_logical(lax.axis_index("dev"), bit), 2)
    total = (small0[...] + small1[...]) + (small2[...] + small3[...])
    for index, ref in ((1 - side, send_ref), (side, keep_ref)):
        lines = pl.ds(pl.multiple_of(index * half, half), half)
        write_packed(ref, own_ref[lines, :] + got3[lines, :].astype(F32), total)


def halve_kernel(bit, keep_ref, got_ref, next_ref, send_ref):
    half = (keep_ref.shape[0] - 16) // 2
    side = lax.rem(lax.shift_right_logical(lax.axis_index("dev"), bit), 2)
    small = keep_ref[2 * half :, -128:] + got_ref[2 * half :, -128:].astype(F32)
    for index, ref in ((1 - side, send_ref), (side, next_ref)):
        first = index * half
        write_packed(ref, read_packed(keep_ref, first, half) + read_packed(got_ref, first, half), small)


def add_kernel(mine_ref, got_ref, out_ref):
    out_ref[...] = (mine_ref[...].astype(F32) + got_ref[...].astype(F32)).astype(out_ref.dtype)


def join_kernel(taps, own_ref, other_ref, out_ref, first_ref, gain_ref, bias_ref):
    second, size, chans = out_ref.shape
    half = chans // 2
    core = lax.rem(lax.axis_index("grp"), 2)
    for ref, side in ((own_ref, core), (other_ref, 1 - core)):
        value = read_packed(ref, 0, size)
        for tap in range(second):
            lanes = pl.ds(pl.multiple_of(side * half, half), half)
            out_ref[tap, :, lanes] = value[:, tap * half : (tap + 1) * half]
    total = jnp.where(core == 1, own_ref[size:, -128:], other_ref[size:, -128:])
    value = total[:, :size]
    for place in range(1, 128 // size):
        mine = lax.axis_index("dev") // 4 == place
        value = jnp.where(mine, total[:, place * size : (place + 1) * size], value)
    first_ref[...] = value[:taps]
    gain_ref[...] = value[taps : taps + 1]
    bias_ref[...] = value[taps + 1 : taps + 2]


def call(kernel, outs, args, scratch=(), limit=24, flops=0, touched=0, outside=()):
    vmem = pl.BlockSpec(memory_space=pltpu.VMEM)
    args = [pltpu.with_memory_space_constraint(arg, pltpu.HBM) if i in outside else arg for i, arg in enumerate(args)]
    return pl.pallas_call(
        kernel,
        out_shape=[
            jax.ShapeDtypeStruct(out[0], out[1]) if len(out) > 2 else pltpu.VMEM(out[0], out[1]) for out in outs
        ],
        in_specs=[pl.BlockSpec(memory_space=pltpu.HBM) if i in outside else vmem for i in range(len(args))],
        out_specs=[pl.BlockSpec(memory_space=pl.ANY) if out[-1] == "hbm" else vmem for out in outs],
        scratch_shapes=[pltpu.VMEM(*entry) if isinstance(entry, tuple) else entry for entry in scratch],
        compiler_params=pltpu.CompilerParams(vmem_limit_bytes=limit * MIB),
        cost_estimate=pl.CostEstimate(flops=flops, bytes_accessed=touched, transcendentals=0),
    )(*args)


def swap(value, axis, offset):
    size = lax.axis_size(axis)
    return lax.ppermute(value, axis, [(i, i ^ offset) for i in range(size)])


def second_swap(value, offset):
    members = lax.axis_size("dev")
    pairs = [
        (grp * members + dev, grp * members + (dev ^ offset))
        for grp in range(1, lax.axis_size("grp"), 2)
        for dev in range(members)
    ]
    return lax.ppermute(value, ("grp", "dev"), pairs)


def shards(wave, lengths, order, w_first, norm_gain, norm_bias, w_second, cot):
    members = lax.axis_size("dev")
    groups_of = lax.axis_size("grp")
    rows, samp = wave.shape
    taps, chans = w_first.shape
    taps_second = w_second.shape[0]
    stride = taps // 2
    frames0 = (samp - taps) // stride + 1
    frames1 = (frames0 - taps_second) // 2 + 1
    groups = -(-frames0 // GROUP)
    depth = 128
    width = LANES
    dev_bits = members.bit_length() - 1
    grp_bits = groups_of.bit_length() - 1

    offsets = [0, 1, 2, 3]
    waves = [wave] + [swap(wave, "dev", offset) for offset in offsets[1:]]
    for bit in range(2, dev_bits - 1):
        offsets += [offset | (1 << bit) for offset in offsets]
        waves += [swap(held, "dev", 1 << bit) for held in waves]
    lens = lengths.reshape(1, members * rows)
    every = members * rows
    valid, band, near_sel, far_sel, own_wave = call(
        functools.partial(setup_kernel, members),
        [
            ((rows, 128), jnp.int32),
            ((depth, GROUP * chans), BF16),
            ((rows // 2, every), BF16),
            ((rows // 2, every), BF16),
            ((rows, samp), BF16),
        ],
        [order, lens, w_first, wave],
        scratch=[
            (order.shape, order.dtype),
            (lens.shape, lens.dtype),
            (w_first.shape, BF16),
            pltpu.SemaphoreType.DMA((4,)),
        ],
        outside=(0, 1, 2, 3),
    )
    near, send = call(
        functools.partial(pick_kernel, offsets),
        [((rows // 2, samp), BF16), ((rows // 2, samp), BF16)],
        [near_sel, far_sel, own_wave, *waves[1:]],
        scratch=[((every, samp), BF16)],
    )
    far = swap(send, "dev", members // 2)
    gain = norm_gain.reshape(1, chans)
    bias = norm_bias.reshape(1, chans)
    cot_t = cot.transpose(1, 0, 2)
    pad_frames = -(-frames1 // 4) * 4
    places = [0] * members
    for dev in range(members):
        places[dev % 4 * (members // 4) + dev // 4] = dev
    feat, even, odd, pre0, even_slope, odd_slope, mean, inv, patch, grad, grad_t, gain_in, w_in = call(
        functools.partial(forward_kernel, frames0, frames1, taps, places),
        [
            ((frames1, rows, chans), BF16),
            ((pad_frames + 1, rows, chans), BF16),
            ((pad_frames, rows, chans), BF16),
            ((groups, rows, GROUP * chans), F32),
            ((pad_frames, rows, chans), F32),
            ((pad_frames, rows, chans), F32),
            ((rows, chans), F32),
            ((rows, chans), F32),
            ((groups, rows, depth), BF16),
            ((frames1 + 2, rows, chans), BF16),
            ((chans, pad_frames * rows), BF16),
            ((1, chans), F32),
            (w_second.shape, BF16),
        ],
        [near, far, valid, band, gain, bias, w_second, cot_t],
        scratch=[
            ((GROUP, rows, chans), BF16),
            ((GROUP // 2, rows, chans), F32),
            ((GROUP // 2, rows, chans), F32),
            ((rows, chans), F32),
            ((rows, chans), F32),
            (bias.shape, F32),
            (cot_t.shape, BF16),
            pltpu.SemaphoreType.DMA((4,)),
        ],
        outside=(4, 5, 6, 7),
    )
    half = chans // 2
    wide = taps_second * half
    keeps, others = [], []
    for acts, skips in (((even, odd), (0, 0)), ((even,), (1,))):
        shape = (chans, len(acts) * half)
        keep, send = call(
            functools.partial(outer_kernel, skips), [(shape, F32), (shape, BF16)], [*acts, grad_t], flops=len(acts) << 29
        )
        keeps.append(keep)
        others.append(swap(send, "grp", 1))
    quarter = chans // 4
    own, *sends = call(
        plane_kernel,
        [((quarter, wide), F32)] + [((quarter, wide), BF16)] * 3,
        [*keeps, *others],
    )
    gots = [swap(part, "dev", offset) for offset, part in enumerate(sends, 1)]
    evens, odds = (frames0 + 1) // 2, frames0 // 2
    lift_even, lift_odd, features = call(
        input_kernel,
        [((evens, rows, chans), F32), ((odds, rows, chans), F32), ((frames1, rows, chans), BF16, "hbm")],
        [grad, w_in, even_slope, odd_slope, own, feat],
        scratch=[pltpu.SemaphoreType.DMA],
        flops=1 << 30,
    )
    parts = call(
        functools.partial(backward_kernel, frames0, taps),
        [((64, quarter), F32)],
        [valid, pre0, mean, inv, patch, lift_even, lift_odd, gain_in],
        scratch=[
            ((groups, rows, GROUP * width), BF16),
            ((depth, GROUP * width), F32),
            ((16, chans), F32),
            ((4, 16, quarter), F32),
        ],
        flops=1 << 32,
    )[0]
    small, *smalls = call(core_kernel, [((16, quarter), F32)] * 4, [parts, swap(parts, "grp", 1)])
    small3, small2 = second_swap(smalls[2], 3), second_swap(smalls[1], 2)
    own, first = call(
        part_kernel, [((quarter, wide), F32), (small.shape, F32)], [own, gots[0], gots[1], smalls[0]]
    )
    small1 = second_swap(first, 1)
    size = quarter // 2
    keep, send = call(
        functools.partial(gather_kernel, dev_bits - 1),
        [(packed(size, wide), F32), (packed(size, wide), BF16)],
        [own, gots[2], small, small1, small2, small3],
    )
    for bit in range(dev_bits - 1, 2, -1):
        size //= 2
        keep, send = call(
            functools.partial(halve_kernel, bit - 1),
            [(packed(size, wide), F32), (packed(size, wide), BF16)],
            [keep, swap(send, "dev", 1 << bit)],
        )
    send = call(add_kernel, [(packed(size, wide), BF16)], [keep, swap(send, "dev", 4)])[0]
    for bit in range(1, grp_bits):
        kind = F32 if bit == grp_bits - 1 else BF16
        send = call(add_kernel, [(packed(size, wide), kind)], [send, swap(send, "grp", 1 << bit)])[0]
    grad_second, grad_first, grad_gain, grad_bias = call(
        functools.partial(join_kernel, taps),
        [
            ((taps_second, size, chans), F32, "out"),
            ((taps, size), F32, "out"),
            ((1, size), F32, "out"),
            ((1, size), F32, "out"),
        ],
        [send, swap(send, "grp", 1)],
    )
    return (
        features.transpose(1, 0, 2),
        grad_second.transpose(0, 2, 1),
        grad_first,
        grad_gain.reshape(size),
        grad_bias.reshape(size),
    )


def solution(mesh):
    placed = (
        P(("grp", "dev"), None),
        P("grp"),
        P("grp", None),
        P(),
        P(),
        P(),
        P(),
        P(("grp", "dev"), None, None),
    )
    return jax.shard_map(
        shards,
        mesh=mesh,
        in_specs=placed,
        out_specs=(
            P(("grp", "dev"), None, None),
            P(None, None, "dev"),
            P(None, "dev"),
            P("dev"),
            P("dev"),
        ),
        check_vma=False,
    )
```

```python
import functools

import jax
import jax.numpy as jnp
from jax import lax
from jax.experimental import pallas as pl
from jax.experimental.pallas import tpu as pltpu
from jax.sharding import PartitionSpec as P

F32 = jnp.float32
BF16 = jnp.bfloat16
GROUP = 8
LANES = 256
MIN_SAMPLES = 288
MIB = 1 << 20


def gelu_and_slope(value):
    bell = jnp.exp2(value * value * (-0.5 * 1.4426950408889634))
    phi = 0.5 + 0.5 * lax.erf(value * 0.7071067811865476)
    return value * phi, phi + value * bell * 0.3989422804014327


def rows_first(a, b):
    return lax.dot_general(a, b, (((0,), (0,)), ((), ())), preferred_element_type=F32)


def cols_both(a, b):
    return lax.dot_general(a, b, (((1,), (1,)), ((), ())), preferred_element_type=F32)


def dot(a, b):
    return jnp.dot(a, b, preferred_element_type=F32)


def iota(shape, dim):
    return lax.broadcasted_iota(jnp.int32, shape, dim)


def onehot(mask):
    return mask.astype(F32).astype(BF16)


def copies(sources, targets, sems):
    started = [pltpu.make_async_copy(source, target, sems.at[i]) for i, (source, target) in enumerate(zip(sources, targets))]
    for copy in started:
        copy.start()
    return started


def setup_kernel(
    members,
    order_hbm,
    len_hbm,
    w_hbm,
    wave_hbm,
    valid_ref,
    band_ref,
    near_ref,
    far_ref,
    own_ref,
    order_ref,
    len_ref,
    w_ref,
    sems,
):
    for copy in copies((order_hbm, len_hbm, w_hbm, wave_hbm), (order_ref, len_ref, w_ref, own_ref), sems):
        copy.wait()
    rows = order_ref.shape[1]
    share = rows // members
    taps, chans = w_ref.shape
    stride = taps // 2
    owner = onehot(iota((rows, members), 0) // share == iota((rows, members), 1))
    order_of = dot(owner, order_ref[...].astype(F32).astype(BF16))
    slot = iota((rows, rows), 1) - lax.rem(iota((rows, rows), 0), share) * members
    owner_first = iota((rows, 1), 0) // share * rows
    column = iota((rows, members * rows), 1)
    member = lax.axis_index("dev")
    low_half = member < members // 2
    for target, out_ref in ((member, near_ref), (jnp.bitwise_xor(member, members // 2), far_ref)):
        local = jnp.sum(jnp.where(slot == target, order_of, 0.0), axis=1, keepdims=True).astype(jnp.int32)
        picked = column == owner_first + local
        picks = picked.astype(F32)
        out_ref[...] = jnp.where(low_half, picks[: rows // 2], picks[rows // 2 :]).astype(BF16)
        if out_ref is near_ref:
            lens = jnp.sum(jnp.where(picked, len_ref[...], 0), axis=1, keepdims=True)
    valid = (lens - taps) // stride + 1
    valid_ref[...] = jnp.broadcast_to(valid, valid_ref.shape)
    depth = band_ref.shape[0]
    for f in range(GROUP):
        spread = onehot(iota((depth, taps), 0) == iota((depth, taps), 1) + stride * f)
        band_ref[:, f * chans : (f + 1) * chans] = dot(spread, w_ref[...]).astype(BF16)


def pick_kernel(offsets, near_ref, far_ref, *refs):
    waves, (mine_ref, send_ref, all_ref) = refs[:-3], refs[-3:]
    rows = waves[0].shape[0]
    all_ref[...] = jnp.zeros(all_ref.shape, BF16)
    for offset, wave_ref in zip(offsets, waves):
        first = pl.multiple_of(jnp.bitwise_xor(lax.axis_index("dev"), offset) * rows, rows)
        all_ref[pl.ds(first, rows), :] = wave_ref[...]
    mine_ref[...] = dot(near_ref[...], all_ref[...]).astype(BF16)
    send_ref[...] = dot(far_ref[...], all_ref[...]).astype(BF16)


def forward_kernel(
    frames0,
    frames1,
    taps,
    places,
    near_ref,
    far_ref,
    valid_ref,
    band_ref,
    gain_hbm,
    bias_hbm,
    w_hbm,
    cot_hbm,
    feat_ref,
    even_ref,
    odd_ref,
    pre0,
    even_slope,
    odd_slope,
    mean_ref,
    inv_ref,
    patch_ref,
    grad_ref,
    grad_t_ref,
    gain_ref,
    w_ref,
    stage,
    fresh,
    pre1,
    scale_ref,
    shift_ref,
    bias_ref,
    cot_ref,
    sems,
):
    waiting = copies((gain_hbm, bias_hbm, w_hbm, cot_hbm), (gain_ref, bias_ref, w_ref, cot_ref), sems)
    rows, samp = valid_ref.shape[0], near_ref.shape[1]
    chans = gain_ref.shape[1]
    stride = taps // 2
    depth = band_ref.shape[0]
    groups = pre0.shape[0]
    width = LANES
    parts = [slice(first, first + width) for first in range(0, chans, width)]
    min_valid = (MIN_SAMPLES - taps) // stride + 1
    full_groups = frames0 // GROUP
    free_groups = min(min_valid // GROUP, full_groups)
    low_half = lax.axis_index("dev") < lax.axis_size("dev") // 2
    near, far = near_ref[...].astype(F32), far_ref[...].astype(F32)
    wave = jnp.concatenate([jnp.where(low_half, near, far), jnp.where(low_half, far, near)], axis=0).astype(BF16)
    for g in range(groups):
        pick = onehot(iota((samp, depth), 0) == iota((samp, depth), 1) + GROUP * stride * g)
        patch_ref[g] = dot(wave, pick).astype(BF16)
    patches = patch_ref[...].reshape(groups * rows, depth)
    for f in range(GROUP):
        cols = slice(f * chans, (f + 1) * chans)
        pre0[:, :, cols] = dot(patches, band_ref[:, cols]).reshape(groups, rows, chans)

    valid = jnp.broadcast_to(valid_ref[:, :1], (rows, width))
    count = valid.astype(F32)

    def frame(g, f, lanes):
        return pre0[g, :, f * chans + lanes.start : f * chans + lanes.stop]

    def masked_to(value, t, masked):
        return jnp.where(valid > t, value, 0.0) if masked else value

    for lanes in parts:

        def over_frames(body):
            def step(masked, g, total):
                for f in range(GROUP):
                    total = total + body(g, f, masked)
                return total

            total = lax.fori_loop(0, free_groups, functools.partial(step, False), jnp.zeros((rows, width), F32))
            total = lax.fori_loop(free_groups, full_groups, functools.partial(step, True), total)
            for f in range(frames0 - full_groups * GROUP):
                total = total + body(full_groups, f, True)
            return total

        mean = over_frames(lambda g, f, masked: masked_to(frame(g, f, lanes), g * GROUP + f, masked)) / count

        def square(g, f, masked):
            centred = masked_to(frame(g, f, lanes) - mean, g * GROUP + f, masked)
            return centred * centred

        inv = lax.rsqrt(over_frames(square) / count + 1e-05)
        mean_ref[:, lanes] = mean
        inv_ref[:, lanes] = inv
        if lanes.start == 0:
            waiting[0].wait()
            waiting[1].wait()
        scale = inv * gain_ref[:, lanes]
        scale_ref[:, lanes] = scale
        shift_ref[:, lanes] = bias_ref[:, lanes] - mean * scale

    half = GROUP // 2
    span = half * rows
    frames_of = even_ref.shape[0] - 1
    even_ref[frames_of:] = jnp.zeros((1,) + even_ref.shape[1:], BF16)
    grad_ref[0] = jnp.zeros(grad_ref.shape[1:], BF16)
    grad_ref[frames1 + 1] = jnp.zeros(grad_ref.shape[1:], BF16)
    grad_t_ref[:, frames1 // half * span :] = jnp.zeros((chans, grad_t_ref.shape[1] - frames1 // half * span), BF16)
    min_valid1 = (min_valid - 3) // 2 + 1
    valid1 = lax.shift_right_arithmetic(valid - 3, 1) + 1
    slab = chans // len(places)

    def unstage(g):
        for f in range(GROUP):
            (odd_ref if f % 2 else even_ref)[g * half + f // 2] = stage[f]

    def activate0(g, masked, used=GROUP):
        for f in range(used):
            for lanes in parts:
                gelu, slope = gelu_and_slope(frame(g, f, lanes) * scale_ref[:, lanes] + shift_ref[:, lanes])
                t = g * GROUP + f
                slope_ref = odd_slope if f % 2 else even_slope
                slope_ref[g * half + f // 2, :, lanes] = masked_to(slope, t, masked)
                stage[f, :, lanes] = masked_to(gelu, t, masked).astype(BF16)

    def convolve(h, used):
        first = h * half
        for lanes in parts:
            total = dot(even_ref[pl.ds(first, used)].reshape(used * rows, chans), w_ref[0, :, lanes])
            total += dot(odd_ref[pl.ds(first, used)].reshape(used * rows, chans), w_ref[1, :, lanes])
            total += dot(even_ref[pl.ds(first + 1, used)].reshape(used * rows, chans), w_ref[2, :, lanes])
            fresh[:used, :, lanes] = total.reshape(used, rows, width)

    def activate1(h, used, masked):
        for j in range(used):
            u = h * half + j
            for lanes in parts:
                gelu, slope = gelu_and_slope(pre1[j, :, lanes])
                grad = cot_ref[u, :, lanes].astype(F32) * slope
                if masked:
                    gelu, grad = jnp.where(valid1 > u, gelu, 0.0), jnp.where(valid1 > u, grad, 0.0)
                feat_ref[u, :, lanes] = gelu.astype(BF16)
                grad_ref[u + 1, :, lanes] = grad.astype(BF16)

    def turn(h, used):
        turned = grad_ref[pl.ds(h * half + 1, used)].reshape(used * rows, chans).T
        start = h * span
        cols = pl.ds(start if isinstance(start, int) else pl.multiple_of(start, span), used * rows)
        for place, source in enumerate(places):
            grad_t_ref[place * slab : (place + 1) * slab, cols] = turned[source * slab : (source + 1) * slab]

    def fill(g, carry):
        unstage(jnp.maximum(g - 1, 0))
        activate0(g, False)
        return carry

    def steady(masked, g, carry, used=GROUP):
        unstage(g - 1)
        pre1[...] = fresh[...]
        convolve(g - 2, half)
        activate1(g - 3, half, masked)
        activate0(g, masked, used)
        turn(g - 3, half)
        return carry

    stage[...] = jnp.zeros(stage.shape, BF16)
    lax.fori_loop(0, 3, fill, 0)
    waiting[2].wait()
    waiting[3].wait()
    convolve(0, half)
    lax.fori_loop(3, free_groups, functools.partial(steady, False), 0)
    lax.fori_loop(free_groups, full_groups, functools.partial(steady, True), 0)
    rest = frames0 - full_groups * GROUP
    if rest:
        steady(True, full_groups, 0, rest)
        stage[rest:] = jnp.zeros((GROUP - rest,) + stage.shape[1:], BF16)
    unstage(groups - 1)
    last = frames1 // half
    for h in range(groups - 2, last + 1):
        pre1[...] = fresh[...]
        convolve(h, min(half, frames1 - h * half))
        activate1(h - 1, half, True)
        turn(h - 1, half)
    pre1[...] = fresh[...]
    activate1(last, frames1 - last * half, True)
    turn(last, frames1 - last * half)


def outer_kernel(skips, *refs):
    acts, (grad_t_ref, keep_ref, send_ref) = refs[:-3], refs[-3:]
    rows, chans = acts[0].shape[1:]
    frames = grad_t_ref.shape[1] // rows
    half = chans // 2
    core = lax.rem(lax.axis_index("grp"), 2)
    for tap, (act_ref, skip) in enumerate(zip(acts, skips)):
        for side, out_ref in ((1 - core, send_ref), (core, keep_ref)):
            lanes = pl.ds(pl.multiple_of(side * half, half), half)
            value = dot(grad_t_ref[...], act_ref[skip : skip + frames, :, lanes].reshape(frames * rows, half))
            out_ref[:, tap * half : (tap + 1) * half] = value.astype(out_ref.dtype)


def input_kernel(grad_ref, w_ref, even_slope, odd_slope, after_ref, feat_ref, even_ref, odd_ref, feat_out, sem):
    leaving = pltpu.make_async_copy(feat_ref, feat_out, sem)
    leaving.start()
    evens, rows, chans = even_ref.shape
    odds = odd_ref.shape[0]
    first = grad_ref[1 : evens + 1].reshape(evens * rows, chans)
    third = grad_ref[0:evens].reshape(evens * rows, chans)
    total = cols_both(first, w_ref[0]) + cols_both(third, w_ref[2])
    even_ref[...] = total.reshape(even_ref.shape) * even_slope[:evens]
    second = grad_ref[1 : odds + 1].reshape(odds * rows, chans)
    odd_ref[...] = cols_both(second, w_ref[1]).reshape(odd_ref.shape) * odd_slope[:odds]
    leaving.wait()


def backward_kernel(
    frames0,
    taps,
    valid_ref,
    pre0,
    mean_ref,
    inv_ref,
    patch_ref,
    even_ref,
    odd_ref,
    gain_ref,
    small_ref,
    dpre0,
    spread,
    out_ref,
    quarters,
):
    groups, rows, depth = patch_ref.shape
    chans = gain_ref.shape[1]
    stride = taps // 2
    width = dpre0.shape[2] // GROUP
    full_groups = frames0 // GROUP
    free_groups = min(((MIN_SAMPLES - taps) // stride + 1) // GROUP, full_groups)
    rest = frames0 - full_groups * GROUP
    patches = patch_ref[...].reshape(groups * rows, depth)
    for block in range(chans // width):
        lanes = slice(block * width, (block + 1) * width)

        def frame(g, f):
            return pre0[g, :, f * chans + block * width : f * chans + (block + 1) * width]

        def lift(g, f):
            return (odd_ref if f % 2 else even_ref)[g * (GROUP // 2) + f // 2, :, lanes]

        def sums(g, f, carry):
            bias_sum, gain_sum = carry
            return bias_sum + lift(g, f), gain_sum + lift(g, f) * frame(g, f)

        def add(g, carry):
            for f in range(GROUP):
                carry = sums(g, f, carry)
            return carry

        zero = jnp.zeros((rows, width), F32)
        carry = lax.fori_loop(0, full_groups, add, (zero, zero))
        for f in range(rest):
            carry = sums(full_groups, f, carry)
        bias_sum, gain_sum = carry
        mean, inv = mean_ref[:, lanes], inv_ref[:, lanes]
        gain_sum = (gain_sum - mean * bias_sum) * inv
        out_ref[taps : taps + 1, lanes] = jnp.sum(gain_sum, axis=0, keepdims=True)
        out_ref[taps + 1 : taps + 2, lanes] = jnp.sum(bias_sum, axis=0, keepdims=True)
        valid = jnp.broadcast_to(valid_ref[:, :1], (rows, width))
        count = valid.astype(F32)
        scale = inv * gain_ref[:, lanes]
        slant = scale * inv * gain_sum / count
        level = scale * bias_sum / count - mean * slant

        def finish(g, f, masked):
            value = scale * lift(g, f) - frame(g, f) * slant - level
            if masked:
                value = jnp.where(valid > g * GROUP + f, value, 0.0)
            dpre0[g, :, f * width : (f + 1) * width] = value.astype(BF16)

        def whole(masked, g, carry):
            for f in range(GROUP):
                finish(g, f, masked)
            return carry

        lax.fori_loop(0, free_groups, functools.partial(whole, False), 0)
        lax.fori_loop(free_groups, full_groups, functools.partial(whole, True), 0)
        for f in range(rest):
            finish(full_groups, f, True)
        if full_groups < groups:
            dpre0[full_groups, :, rest * width :] = jnp.zeros((rows, (GROUP - rest) * width), BF16)
        spread[...] = rows_first(patches, dpre0[...].reshape(groups * rows, GROUP * width))
        total = jnp.zeros((taps, width), F32)
        for f in range(GROUP):
            total += spread[stride * f : stride * f + taps, f * width : (f + 1) * width]
        out_ref[:taps, lanes] = total
    size = chans // lax.axis_size("dev")
    for place in range(4):
        columns = [slice(first, first + size) for first in range(place * size, chans, 4 * size)]
        quarters[place] = jnp.concatenate([out_ref[:, part] for part in columns], axis=1)
    place = lax.rem(lax.axis_index("dev"), 4)
    for offset in range(4):
        small_ref[offset * 16 : (offset + 1) * 16] = quarters[jnp.bitwise_xor(place, offset)]


def core_kernel(mine_ref, got_ref, *out_refs):
    for place, ref in enumerate(out_refs):
        lines = slice(place * 16, (place + 1) * 16)
        ref[...] = mine_ref[lines] + got_ref[lines]


def plane_kernel(*refs):
    keeps, others, outs = refs[:2], refs[2:4], refs[4:]
    size = outs[0].shape[0]
    edge = keeps[0].shape[1]
    place = lax.rem(lax.axis_index("dev"), 4)
    for offset, out_ref in enumerate(outs):
        lines = pl.ds(pl.multiple_of(jnp.bitwise_xor(place, offset) * size, size), size)
        for lanes, keep_ref, got_ref in zip((slice(0, edge), slice(edge, None)), keeps, others):
            out_ref[:, lanes] = (keep_ref[lines, :] + got_ref[lines, :].astype(F32)).astype(out_ref.dtype)


def part_kernel(own_ref, got1, got2, small_ref, sum_ref, total_ref):
    sum_ref[...] = own_ref[...] + (got1[...].astype(F32) + got2[...].astype(F32))
    total_ref[...] = small_ref[...]


def packed(size, wide):
    return size + 16, wide - 128


def write_packed(ref, value, small):
    size, lanes = ref.shape[0] - 16, ref.shape[1]
    ref[:size] = value[:, :lanes].astype(ref.dtype)
    used = size // 16
    for block in range(used):
        piece = value[block * 16 : (block + 1) * 16, lanes:]
        ref[size:, block * 128 : (block + 1) * 128] = piece.astype(ref.dtype)
    for first in range(used * 128, lanes - 128, 128):
        ref[size:, first : first + 128] = jnp.zeros((16, 128), ref.dtype)
    ref[size:, lanes - 128 :] = small.astype(ref.dtype)


def read_packed(ref, first, count):
    size = ref.shape[0] - 16
    whole = ref[pl.ds(pl.multiple_of(first, 16), count), :].astype(F32)
    pieces = [
        ref[size:, pl.ds(pl.multiple_of(first * 8 + block * 128, 128), 128)].astype(F32) for block in range(count // 16)
    ]
    return jnp.concatenate([whole, jnp.concatenate(pieces, axis=0)], axis=1)


def gather_kernel(bit, own_ref, got3, small0, small1, small2, small3, keep_ref, send_ref):
    half = own_ref.shape[0] // 2
    side = lax.rem(lax.shift_right_logical(lax.axis_index("dev"), bit), 2)
    total = (small0[...] + small1[...]) + (small2[...] + small3[...])
    for index, ref in ((1 - side, send_ref), (side, keep_ref)):
        lines = pl.ds(pl.multiple_of(index * half, half), half)
        write_packed(ref, own_ref[lines, :] + got3[lines, :].astype(F32), total)


def halve_kernel(bit, keep_ref, got_ref, next_ref, send_ref):
    half = (keep_ref.shape[0] - 16) // 2
    side = lax.rem(lax.shift_right_logical(lax.axis_index("dev"), bit), 2)
    small = keep_ref[2 * half :, -128:] + got_ref[2 * half :, -128:].astype(F32)
    for index, ref in ((1 - side, send_ref), (side, next_ref)):
        first = index * half
        write_packed(ref, read_packed(keep_ref, first, half) + read_packed(got_ref, first, half), small)


def add_kernel(mine_ref, got_ref, out_ref):
    out_ref[...] = (mine_ref[...].astype(F32) + got_ref[...].astype(F32)).astype(out_ref.dtype)


def join_kernel(taps, own_ref, other_ref, out_ref, first_ref, gain_ref, bias_ref):
    second, size, chans = out_ref.shape
    half = chans // 2
    core = lax.rem(lax.axis_index("grp"), 2)
    for ref, side in ((own_ref, core), (other_ref, 1 - core)):
        value = read_packed(ref, 0, size)
        for tap in range(second):
            lanes = pl.ds(pl.multiple_of(side * half, half), half)
            out_ref[tap, :, lanes] = value[:, tap * half : (tap + 1) * half]
    total = jnp.where(core == 1, own_ref[size:, -128:], other_ref[size:, -128:])
    value = total[:, :size]
    for place in range(1, 128 // size):
        mine = lax.axis_index("dev") // 4 == place
        value = jnp.where(mine, total[:, place * size : (place + 1) * size], value)
    first_ref[...] = value[:taps]
    gain_ref[...] = value[taps : taps + 1]
    bias_ref[...] = value[taps + 1 : taps + 2]


def call(kernel, outs, args, scratch=(), limit=24, flops=0, touched=0, outside=()):
    vmem = pl.BlockSpec(memory_space=pltpu.VMEM)
    args = [pltpu.with_memory_space_constraint(arg, pltpu.HBM) if i in outside else arg for i, arg in enumerate(args)]
    return pl.pallas_call(
        kernel,
        out_shape=[
            jax.ShapeDtypeStruct(out[0], out[1]) if len(out) > 2 else pltpu.VMEM(out[0], out[1]) for out in outs
        ],
        in_specs=[pl.BlockSpec(memory_space=pltpu.HBM) if i in outside else vmem for i in range(len(args))],
        out_specs=[pl.BlockSpec(memory_space=pl.ANY) if out[-1] == "hbm" else vmem for out in outs],
        scratch_shapes=[pltpu.VMEM(*entry) if isinstance(entry, tuple) else entry for entry in scratch],
        compiler_params=pltpu.CompilerParams(vmem_limit_bytes=limit * MIB),
        cost_estimate=pl.CostEstimate(flops=flops, bytes_accessed=touched, transcendentals=0),
    )(*args)


def swap(value, axis, offset):
    size = lax.axis_size(axis)
    return lax.ppermute(value, axis, [(i, i ^ offset) for i in range(size)])


def second_swap(value, offset):
    members = lax.axis_size("dev")
    pairs = [
        (grp * members + dev, grp * members + (dev ^ (offset if grp % 2 else 0)))
        for grp in range(lax.axis_size("grp"))
        for dev in range(members)
    ]
    return lax.ppermute(value, ("grp", "dev"), pairs)


def shards(wave, lengths, order, w_first, norm_gain, norm_bias, w_second, cot):
    members = lax.axis_size("dev")
    groups_of = lax.axis_size("grp")
    rows, samp = wave.shape
    taps, chans = w_first.shape
    taps_second = w_second.shape[0]
    stride = taps // 2
    frames0 = (samp - taps) // stride + 1
    frames1 = (frames0 - taps_second) // 2 + 1
    groups = -(-frames0 // GROUP)
    depth = 128
    width = LANES
    dev_bits = members.bit_length() - 1
    grp_bits = groups_of.bit_length() - 1

    offsets = [0, 1, 2, 3]
    waves = [wave] + [swap(wave, "dev", offset) for offset in offsets[1:]]
    for bit in range(2, dev_bits - 1):
        offsets += [offset | (1 << bit) for offset in offsets]
        waves += [swap(held, "dev", 1 << bit) for held in waves]
    lens = lengths.reshape(1, members * rows)
    every = members * rows
    valid, band, near_sel, far_sel, own_wave = call(
        functools.partial(setup_kernel, members),
        [
            ((rows, 128), jnp.int32),
            ((depth, GROUP * chans), BF16),
            ((rows // 2, every), BF16),
            ((rows // 2, every), BF16),
            ((rows, samp), BF16),
        ],
        [order, lens, w_first, wave],
        scratch=[
            (order.shape, order.dtype),
            (lens.shape, lens.dtype),
            (w_first.shape, BF16),
            pltpu.SemaphoreType.DMA((4,)),
        ],
        outside=(0, 1, 2, 3),
    )
    near, send = call(
        functools.partial(pick_kernel, offsets),
        [((rows // 2, samp), BF16), ((rows // 2, samp), BF16)],
        [near_sel, far_sel, own_wave, *waves[1:]],
        scratch=[((every, samp), BF16)],
    )
    far = swap(send, "dev", members // 2)
    gain = norm_gain.reshape(1, chans)
    bias = norm_bias.reshape(1, chans)
    cot_t = cot.transpose(1, 0, 2)
    pad_frames = -(-frames1 // 4) * 4
    places = [0] * members
    for dev in range(members):
        places[dev % 4 * (members // 4) + dev // 4] = dev
    feat, even, odd, pre0, even_slope, odd_slope, mean, inv, patch, grad, grad_t, gain_in, w_in = call(
        functools.partial(forward_kernel, frames0, frames1, taps, places),
        [
            ((frames1, rows, chans), BF16),
            ((pad_frames + 1, rows, chans), BF16),
            ((pad_frames, rows, chans), BF16),
            ((groups, rows, GROUP * chans), F32),
            ((pad_frames, rows, chans), F32),
            ((pad_frames, rows, chans), F32),
            ((rows, chans), F32),
            ((rows, chans), F32),
            ((groups, rows, depth), BF16),
            ((frames1 + 2, rows, chans), BF16),
            ((chans, pad_frames * rows), BF16),
            ((1, chans), F32),
            (w_second.shape, BF16),
        ],
        [near, far, valid, band, gain, bias, w_second, cot_t],
        scratch=[
            ((GROUP, rows, chans), BF16),
            ((GROUP // 2, rows, chans), F32),
            ((GROUP // 2, rows, chans), F32),
            ((rows, chans), F32),
            ((rows, chans), F32),
            (bias.shape, F32),
            (cot_t.shape, BF16),
            pltpu.SemaphoreType.DMA((4,)),
        ],
        outside=(4, 5, 6, 7),
    )
    half = chans // 2
    wide = taps_second * half
    keeps, others = [], []
    for acts, skips in (((even, odd), (0, 0)), ((even,), (1,))):
        shape = (chans, len(acts) * half)
        keep, send = call(
            functools.partial(outer_kernel, skips), [(shape, F32), (shape, BF16)], [*acts, grad_t], flops=len(acts) << 29
        )
        keeps.append(keep)
        others.append(swap(send, "grp", 1))
    quarter = chans // 4
    own, *sends = call(
        plane_kernel,
        [((quarter, wide), F32)] + [((quarter, wide), BF16)] * 3,
        [*keeps, *others],
    )
    gots = [swap(part, "dev", offset) for offset, part in enumerate(sends, 1)]
    evens, odds = (frames0 + 1) // 2, frames0 // 2
    lift_even, lift_odd, features = call(
        input_kernel,
        [((evens, rows, chans), F32), ((odds, rows, chans), F32), ((frames1, rows, chans), BF16, "hbm")],
        [grad, w_in, even_slope, odd_slope, own, feat],
        scratch=[pltpu.SemaphoreType.DMA],
        flops=1 << 30,
    )
    parts = call(
        functools.partial(backward_kernel, frames0, taps),
        [((64, quarter), F32)],
        [valid, pre0, mean, inv, patch, lift_even, lift_odd, gain_in],
        scratch=[
            ((groups, rows, GROUP * width), BF16),
            ((depth, GROUP * width), F32),
            ((16, chans), F32),
            ((4, 16, quarter), F32),
        ],
        flops=1 << 32,
    )[0]
    small, *smalls = call(core_kernel, [((16, quarter), F32)] * 4, [parts, swap(parts, "grp", 1)])
    small3, small2 = second_swap(smalls[2], 3), second_swap(smalls[1], 2)
    own, first = call(
        part_kernel, [((quarter, wide), F32), (small.shape, F32)], [own, gots[0], gots[1], smalls[0]]
    )
    small1 = second_swap(first, 1)
    size = quarter // 2
    keep, send = call(
        functools.partial(gather_kernel, dev_bits - 1),
        [(packed(size, wide), F32), (packed(size, wide), BF16)],
        [own, gots[2], small, small1, small2, small3],
    )
    for bit in range(dev_bits - 1, 2, -1):
        size //= 2
        keep, send = call(
            functools.partial(halve_kernel, bit - 1),
            [(packed(size, wide), F32), (packed(size, wide), BF16)],
            [keep, swap(send, "dev", 1 << bit)],
        )
    send = call(add_kernel, [(packed(size, wide), BF16)], [keep, swap(send, "dev", 4)])[0]
    for bit in range(1, grp_bits):
        kind = F32 if bit == grp_bits - 1 else BF16
        send = call(add_kernel, [(packed(size, wide), kind)], [send, swap(send, "grp", 1 << bit)])[0]
    grad_second, grad_first, grad_gain, grad_bias = call(
        functools.partial(join_kernel, taps),
        [
            ((taps_second, size, chans), F32, "out"),
            ((taps, size), F32, "out"),
            ((1, size), F32, "out"),
            ((1, size), F32, "out"),
        ],
        [send, swap(send, "grp", 1)],
    )
    return (
        features.transpose(1, 0, 2),
        grad_second.transpose(0, 2, 1),
        grad_first,
        grad_gain.reshape(size),
        grad_bias.reshape(size),
    )


def solution(mesh):
    placed = (
        P(("grp", "dev"), None),
        P("grp"),
        P("grp", None),
        P(),
        P(),
        P(),
        P(),
        P(("grp", "dev"), None, None),
    )
    return jax.shard_map(
        shards,
        mesh=mesh,
        in_specs=placed,
        out_specs=(
            P(("grp", "dev"), None, None),
            P(None, None, "dev"),
            P(None, "dev"),
            P("dev"),
            P("dev"),
        ),
        check_vma=False,
    )
```

```python
import functools

import jax
import jax.numpy as jnp
from jax import lax
from jax.experimental import pallas as pl
from jax.experimental.pallas import tpu as pltpu
from jax.sharding import PartitionSpec as P

F32 = jnp.float32
BF16 = jnp.bfloat16
GROUP = 8
LANES = 256
MIN_SAMPLES = 288
MIB = 1 << 20


def gelu_and_slope(value):
    bell = jnp.exp2(value * value * (-0.5 * 1.4426950408889634))
    phi = 0.5 + 0.5 * lax.erf(value * 0.7071067811865476)
    return value * phi, phi + value * bell * 0.3989422804014327


def rows_first(a, b):
    return lax.dot_general(a, b, (((0,), (0,)), ((), ())), preferred_element_type=F32)


def cols_both(a, b):
    return lax.dot_general(a, b, (((1,), (1,)), ((), ())), preferred_element_type=F32)


def dot(a, b):
    return jnp.dot(a, b, preferred_element_type=F32)


def iota(shape, dim):
    return lax.broadcasted_iota(jnp.int32, shape, dim)


def onehot(mask):
    return mask.astype(F32).astype(BF16)


def copies(sources, targets, sems):
    started = [pltpu.make_async_copy(source, target, sems.at[i]) for i, (source, target) in enumerate(zip(sources, targets))]
    for copy in started:
        copy.start()
    return started


def setup_kernel(
    members,
    order_hbm,
    len_hbm,
    w_hbm,
    wave_hbm,
    valid_ref,
    band_ref,
    near_ref,
    far_ref,
    own_ref,
    order_ref,
    len_ref,
    w_ref,
    sems,
):
    for copy in copies((order_hbm, len_hbm, w_hbm, wave_hbm), (order_ref, len_ref, w_ref, own_ref), sems):
        copy.wait()
    rows = order_ref.shape[1]
    share = rows // members
    taps, chans = w_ref.shape
    stride = taps // 2
    owner = onehot(iota((rows, members), 0) // share == iota((rows, members), 1))
    order_of = dot(owner, order_ref[...].astype(F32).astype(BF16))
    slot = iota((rows, rows), 1) - lax.rem(iota((rows, rows), 0), share) * members
    owner_first = iota((rows, 1), 0) // share * rows
    column = iota((rows, members * rows), 1)
    member = lax.axis_index("dev")
    low_half = member < members // 2
    for target, out_ref in ((member, near_ref), (jnp.bitwise_xor(member, members // 2), far_ref)):
        local = jnp.sum(jnp.where(slot == target, order_of, 0.0), axis=1, keepdims=True).astype(jnp.int32)
        picked = column == owner_first + local
        picks = picked.astype(F32)
        out_ref[...] = jnp.where(low_half, picks[: rows // 2], picks[rows // 2 :]).astype(BF16)
        if out_ref is near_ref:
            lens = jnp.sum(jnp.where(picked, len_ref[...], 0), axis=1, keepdims=True)
    valid = (lens - taps) // stride + 1
    valid_ref[...] = jnp.broadcast_to(valid, valid_ref.shape)
    depth = band_ref.shape[0]
    for f in range(GROUP):
        spread = onehot(iota((depth, taps), 0) == iota((depth, taps), 1) + stride * f)
        band_ref[:, f * chans : (f + 1) * chans] = dot(spread, w_ref[...]).astype(BF16)


def pick_kernel(offsets, near_ref, far_ref, *refs):
    waves, (mine_ref, send_ref, all_ref) = refs[:-3], refs[-3:]
    rows = waves[0].shape[0]
    all_ref[...] = jnp.zeros(all_ref.shape, BF16)
    for offset, wave_ref in zip(offsets, waves):
        first = pl.multiple_of(jnp.bitwise_xor(lax.axis_index("dev"), offset) * rows, rows)
        all_ref[pl.ds(first, rows), :] = wave_ref[...]
    mine_ref[...] = dot(near_ref[...], all_ref[...]).astype(BF16)
    send_ref[...] = dot(far_ref[...], all_ref[...]).astype(BF16)


def forward_kernel(
    frames0,
    frames1,
    taps,
    places,
    near_ref,
    far_ref,
    valid_ref,
    band_ref,
    gain_hbm,
    bias_hbm,
    w_hbm,
    cot_hbm,
    feat_ref,
    even_ref,
    odd_ref,
    pre0,
    even_slope,
    odd_slope,
    mean_ref,
    inv_ref,
    patch_ref,
    grad_ref,
    grad_t_ref,
    gain_ref,
    w_ref,
    stage,
    fresh,
    pre1,
    scale_ref,
    shift_ref,
    bias_ref,
    cot_ref,
    sems,
):
    waiting = copies((gain_hbm, bias_hbm, w_hbm, cot_hbm), (gain_ref, bias_ref, w_ref, cot_ref), sems)
    rows, samp = valid_ref.shape[0], near_ref.shape[1]
    chans = gain_ref.shape[1]
    stride = taps // 2
    depth = band_ref.shape[0]
    groups = pre0.shape[0]
    width = LANES
    parts = [slice(first, first + width) for first in range(0, chans, width)]
    min_valid = (MIN_SAMPLES - taps) // stride + 1
    full_groups = frames0 // GROUP
    free_groups = min(min_valid // GROUP, full_groups)
    low_half = lax.axis_index("dev") < lax.axis_size("dev") // 2
    near, far = near_ref[...].astype(F32), far_ref[...].astype(F32)
    wave = jnp.concatenate([jnp.where(low_half, near, far), jnp.where(low_half, far, near)], axis=0).astype(BF16)
    for g in range(groups):
        pick = onehot(iota((samp, depth), 0) == iota((samp, depth), 1) + GROUP * stride * g)
        patch_ref[g] = dot(wave, pick).astype(BF16)
    patches = patch_ref[...].reshape(groups * rows, depth)
    for f in range(GROUP):
        cols = slice(f * chans, (f + 1) * chans)
        pre0[:, :, cols] = dot(patches, band_ref[:, cols]).reshape(groups, rows, chans)

    valid = jnp.broadcast_to(valid_ref[:, :1], (rows, width))
    count = valid.astype(F32)

    def frame(g, f, lanes):
        return pre0[g, :, f * chans + lanes.start : f * chans + lanes.stop]

    def masked_to(value, t, masked):
        return jnp.where(valid > t, value, 0.0) if masked else value

    for lanes in parts:

        def over_frames(body):
            def step(masked, g, total):
                for f in range(GROUP):
                    total = total + body(g, f, masked)
                return total

            total = lax.fori_loop(0, free_groups, functools.partial(step, False), jnp.zeros((rows, width), F32))
            total = lax.fori_loop(free_groups, full_groups, functools.partial(step, True), total)
            for f in range(frames0 - full_groups * GROUP):
                total = total + body(full_groups, f, True)
            return total

        mean = over_frames(lambda g, f, masked: masked_to(frame(g, f, lanes), g * GROUP + f, masked)) / count

        def square(g, f, masked):
            centred = masked_to(frame(g, f, lanes) - mean, g * GROUP + f, masked)
            return centred * centred

        inv = lax.rsqrt(over_frames(square) / count + 1e-05)
        mean_ref[:, lanes] = mean
        inv_ref[:, lanes] = inv
        if lanes.start == 0:
            waiting[0].wait()
            waiting[1].wait()
        scale = inv * gain_ref[:, lanes]
        scale_ref[:, lanes] = scale
        shift_ref[:, lanes] = bias_ref[:, lanes] - mean * scale

    half = GROUP // 2
    span = half * rows
    frames_of = even_ref.shape[0] - 1
    even_ref[frames_of:] = jnp.zeros((1,) + even_ref.shape[1:], BF16)
    grad_ref[0] = jnp.zeros(grad_ref.shape[1:], BF16)
    grad_ref[frames1 + 1] = jnp.zeros(grad_ref.shape[1:], BF16)
    grad_t_ref[:, frames1 // half * span :] = jnp.zeros((chans, grad_t_ref.shape[1] - frames1 // half * span), BF16)
    min_valid1 = (min_valid - 3) // 2 + 1
    valid1 = lax.shift_right_arithmetic(valid - 3, 1) + 1
    slab = chans // len(places)

    def unstage(g):
        for f in range(GROUP):
            (odd_ref if f % 2 else even_ref)[g * half + f // 2] = stage[f]

    def activate0(g, masked, used=GROUP):
        for f in range(used):
            for lanes in parts:
                gelu, slope = gelu_and_slope(frame(g, f, lanes) * scale_ref[:, lanes] + shift_ref[:, lanes])
                t = g * GROUP + f
                slope_ref = odd_slope if f % 2 else even_slope
                slope_ref[g * half + f // 2, :, lanes] = masked_to(slope, t, masked)
                stage[f, :, lanes] = masked_to(gelu, t, masked).astype(BF16)

    def convolve(h, used):
        first = h * half
        for lanes in parts:
            total = dot(even_ref[pl.ds(first, used)].reshape(used * rows, chans), w_ref[0, :, lanes])
            total += dot(odd_ref[pl.ds(first, used)].reshape(used * rows, chans), w_ref[1, :, lanes])
            total += dot(even_ref[pl.ds(first + 1, used)].reshape(used * rows, chans), w_ref[2, :, lanes])
            fresh[:used, :, lanes] = total.reshape(used, rows, width)

    def activate1(h, used, masked):
        for j in range(used):
            u = h * half + j
            for lanes in parts:
                gelu, slope = gelu_and_slope(pre1[j, :, lanes])
                grad = cot_ref[u, :, lanes].astype(F32) * slope
                if masked:
                    gelu, grad = jnp.where(valid1 > u, gelu, 0.0), jnp.where(valid1 > u, grad, 0.0)
                feat_ref[u, :, lanes] = gelu.astype(BF16)
                grad_ref[u + 1, :, lanes] = grad.astype(BF16)

    def turn(h, used):
        turned = grad_ref[pl.ds(h * half + 1, used)].reshape(used * rows, chans).T
        start = h * span
        cols = pl.ds(start if isinstance(start, int) else pl.multiple_of(start, span), used * rows)
        for place, source in enumerate(places):
            grad_t_ref[place * slab : (place + 1) * slab, cols] = turned[source * slab : (source + 1) * slab]

    def fill(g, carry):
        unstage(jnp.maximum(g - 1, 0))
        activate0(g, False)
        return carry

    def steady(masked, g, carry, used=GROUP):
        unstage(g - 1)
        pre1[...] = fresh[...]
        convolve(g - 2, half)
        activate1(g - 3, half, masked)
        activate0(g, masked, used)
        turn(g - 3, half)
        return carry

    stage[...] = jnp.zeros(stage.shape, BF16)
    lax.fori_loop(0, 3, fill, 0)
    waiting[2].wait()
    waiting[3].wait()
    convolve(0, half)
    lax.fori_loop(3, free_groups, functools.partial(steady, False), 0)
    lax.fori_loop(free_groups, full_groups, functools.partial(steady, True), 0)
    rest = frames0 - full_groups * GROUP
    if rest:
        steady(True, full_groups, 0, rest)
        stage[rest:] = jnp.zeros((GROUP - rest,) + stage.shape[1:], BF16)
    unstage(groups - 1)
    last = frames1 // half
    for h in range(groups - 2, last + 1):
        pre1[...] = fresh[...]
        convolve(h, min(half, frames1 - h * half))
        activate1(h - 1, half, True)
        turn(h - 1, half)
    pre1[...] = fresh[...]
    activate1(last, frames1 - last * half, True)
    turn(last, frames1 - last * half)


def outer_kernel(skips, *refs):
    acts, (grad_t_ref, keep_ref, send_ref) = refs[:-3], refs[-3:]
    rows, chans = acts[0].shape[1:]
    frames = grad_t_ref.shape[1] // rows
    half = chans // 2
    core = lax.rem(lax.axis_index("grp"), 2)
    for tap, (act_ref, skip) in enumerate(zip(acts, skips)):
        for side, out_ref in ((1 - core, send_ref), (core, keep_ref)):
            lanes = pl.ds(pl.multiple_of(side * half, half), half)
            value = dot(grad_t_ref[...], act_ref[skip : skip + frames, :, lanes].reshape(frames * rows, half))
            out_ref[:, tap * half : (tap + 1) * half] = value.astype(out_ref.dtype)


def input_kernel(grad_ref, w_ref, even_slope, odd_slope, after_ref, feat_ref, even_ref, odd_ref, feat_out, sem):
    leaving = pltpu.make_async_copy(feat_ref, feat_out, sem)
    leaving.start()
    evens, rows, chans = even_ref.shape
    odds = odd_ref.shape[0]
    first = grad_ref[1 : evens + 1].reshape(evens * rows, chans)
    third = grad_ref[0:evens].reshape(evens * rows, chans)
    total = cols_both(first, w_ref[0]) + cols_both(third, w_ref[2])
    even_ref[...] = total.reshape(even_ref.shape) * even_slope[:evens]
    second = grad_ref[1 : odds + 1].reshape(odds * rows, chans)
    odd_ref[...] = cols_both(second, w_ref[1]).reshape(odd_ref.shape) * odd_slope[:odds]
    leaving.wait()


def backward_kernel(
    frames0,
    taps,
    valid_ref,
    pre0,
    mean_ref,
    inv_ref,
    patch_ref,
    even_ref,
    odd_ref,
    gain_ref,
    small_ref,
    dpre0,
    spread,
    out_ref,
    quarters,
):
    groups, rows, depth = patch_ref.shape
    chans = gain_ref.shape[1]
    stride = taps // 2
    width = dpre0.shape[2] // GROUP
    full_groups = frames0 // GROUP
    free_groups = min(((MIN_SAMPLES - taps) // stride + 1) // GROUP, full_groups)
    rest = frames0 - full_groups * GROUP
    patches = patch_ref[...].reshape(groups * rows, depth)
    for block in range(chans // width):
        lanes = slice(block * width, (block + 1) * width)

        def frame(g, f):
            return pre0[g, :, f * chans + block * width : f * chans + (block + 1) * width]

        def lift(g, f):
            return (odd_ref if f % 2 else even_ref)[g * (GROUP // 2) + f // 2, :, lanes]

        def sums(g, f, carry):
            bias_sum, gain_sum = carry
            return bias_sum + lift(g, f), gain_sum + lift(g, f) * frame(g, f)

        def add(g, carry):
            for f in range(GROUP):
                carry = sums(g, f, carry)
            return carry

        zero = jnp.zeros((rows, width), F32)
        carry = lax.fori_loop(0, full_groups, add, (zero, zero))
        for f in range(rest):
            carry = sums(full_groups, f, carry)
        bias_sum, gain_sum = carry
        mean, inv = mean_ref[:, lanes], inv_ref[:, lanes]
        gain_sum = (gain_sum - mean * bias_sum) * inv
        out_ref[taps : taps + 1, lanes] = jnp.sum(gain_sum, axis=0, keepdims=True)
        out_ref[taps + 1 : taps + 2, lanes] = jnp.sum(bias_sum, axis=0, keepdims=True)
        valid = jnp.broadcast_to(valid_ref[:, :1], (rows, width))
        count = valid.astype(F32)
        scale = inv * gain_ref[:, lanes]
        slant = scale * inv * gain_sum / count
        level = scale * bias_sum / count - mean * slant

        def finish(g, f, masked):
            value = scale * lift(g, f) - frame(g, f) * slant - level
            if masked:
                value = jnp.where(valid > g * GROUP + f, value, 0.0)
            dpre0[g, :, f * width : (f + 1) * width] = value.astype(BF16)

        def whole(masked, g, carry):
            for f in range(GROUP):
                finish(g, f, masked)
            return carry

        lax.fori_loop(0, free_groups, functools.partial(whole, False), 0)
        lax.fori_loop(free_groups, full_groups, functools.partial(whole, True), 0)
        for f in range(rest):
            finish(full_groups, f, True)
        if full_groups < groups:
            dpre0[full_groups, :, rest * width :] = jnp.zeros((rows, (GROUP - rest) * width), BF16)
        spread[...] = rows_first(patches, dpre0[...].reshape(groups * rows, GROUP * width))
        total = jnp.zeros((taps, width), F32)
        for f in range(GROUP):
            total += spread[stride * f : stride * f + taps, f * width : (f + 1) * width]
        out_ref[:taps, lanes] = total
    size = chans // lax.axis_size("dev")
    for place in range(4):
        columns = [slice(first, first + size) for first in range(place * size, chans, 4 * size)]
        quarters[place] = jnp.concatenate([out_ref[:, part] for part in columns], axis=1)
    place = lax.rem(lax.axis_index("dev"), 4)
    for offset in range(4):
        small_ref[offset * 16 : (offset + 1) * 16] = quarters[jnp.bitwise_xor(place, offset)]


def plane_kernel(*refs):
    keeps, others, outs = refs[:2], refs[2:4], refs[4:]
    size = outs[0].shape[0]
    edge = keeps[0].shape[1]
    place = lax.rem(lax.axis_index("dev"), 4)
    for offset, out_ref in enumerate(outs):
        lines = pl.ds(pl.multiple_of(jnp.bitwise_xor(place, offset) * size, size), size)
        for lanes, keep_ref, got_ref in zip((slice(0, edge), slice(edge, None)), keeps, others):
            out_ref[:, lanes] = (keep_ref[lines, :] + got_ref[lines, :].astype(F32)).astype(out_ref.dtype)


def packed(size, wide):
    return size + 16, wide - 128


def write_packed(ref, value, small):
    size, lanes = ref.shape[0] - 16, ref.shape[1]
    ref[:size] = value[:, :lanes].astype(ref.dtype)
    used = size // 16
    for block in range(used):
        piece = value[block * 16 : (block + 1) * 16, lanes:]
        ref[size:, block * 128 : (block + 1) * 128] = piece.astype(ref.dtype)
    for first in range(used * 128, lanes - 128, 128):
        ref[size:, first : first + 128] = jnp.zeros((16, 128), ref.dtype)
    ref[size:, lanes - 128 :] = small.astype(ref.dtype)


def read_packed(ref, first, count):
    size = ref.shape[0] - 16
    whole = ref[pl.ds(pl.multiple_of(first, 16), count), :].astype(F32)
    pieces = [
        ref[size:, pl.ds(pl.multiple_of(first * 8 + block * 128, 128), 128)].astype(F32) for block in range(count // 16)
    ]
    return jnp.concatenate([whole, jnp.concatenate(pieces, axis=0)], axis=1)


def gather_kernel(bit, own_ref, got1, got2, got3, parts_ref, parts_got, keep_ref, send_ref, *small_refs):
    half = own_ref.shape[0] // 2
    side = lax.rem(lax.shift_right_logical(lax.axis_index("dev"), bit), 2)
    empty = jnp.zeros((16, 128), F32)
    for index, ref in ((1 - side, send_ref), (side, keep_ref)):
        lines = pl.ds(pl.multiple_of(index * half, half), half)
        terms = got1[lines, :].astype(F32) + got2[lines, :].astype(F32) + got3[lines, :].astype(F32)
        write_packed(ref, own_ref[lines, :] + terms, empty)
    for place, ref in enumerate(small_refs):
        lines = slice(place * 16, (place + 1) * 16)
        ref[...] = parts_ref[lines] + parts_got[lines]


def halve_kernel(bit, keep_ref, got_ref, next_ref, send_ref):
    half = (keep_ref.shape[0] - 16) // 2
    side = lax.rem(lax.shift_right_logical(lax.axis_index("dev"), bit), 2)
    small = keep_ref[2 * half :, -128:] + got_ref[2 * half :, -128:].astype(F32)
    for index, ref in ((1 - side, send_ref), (side, next_ref)):
        first = index * half
        write_packed(ref, read_packed(keep_ref, first, half) + read_packed(got_ref, first, half), small)


def round_kernel(keep_ref, got_ref, small0, small1, small2, small3, send_ref, total_ref):
    send_ref[...] = (keep_ref[...] + got_ref[...].astype(F32)).astype(BF16)
    total_ref[...] = (small0[...] + small1[...]) + (small2[...] + small3[...])


def add_kernel(mine_ref, got_ref, out_ref):
    out_ref[...] = (mine_ref[...].astype(F32) + got_ref[...].astype(F32)).astype(out_ref.dtype)


def last_add_kernel(mine_ref, got_ref, small_ref, small_got, out_ref):
    size, lanes = out_ref.shape[0] - 16, out_ref.shape[1] - 128
    out_ref[...] = mine_ref[...].astype(F32) + got_ref[...].astype(F32)
    out_ref[size:, lanes:] = small_ref[...] + small_got[...]


def join_kernel(taps, own_ref, other_ref, out_ref, first_ref, gain_ref, bias_ref):
    second, size, chans = out_ref.shape
    half = chans // 2
    core = lax.rem(lax.axis_index("grp"), 2)
    for ref, side in ((own_ref, core), (other_ref, 1 - core)):
        value = read_packed(ref, 0, size)
        for tap in range(second):
            lanes = pl.ds(pl.multiple_of(side * half, half), half)
            out_ref[tap, :, lanes] = value[:, tap * half : (tap + 1) * half]
    total = own_ref[size:, -128:] + other_ref[size:, -128:]
    value = total[:, :size]
    for place in range(1, 128 // size):
        mine = lax.axis_index("dev") // 4 == place
        value = jnp.where(mine, total[:, place * size : (place + 1) * size], value)
    first_ref[...] = value[:taps]
    gain_ref[...] = value[taps : taps + 1]
    bias_ref[...] = value[taps + 1 : taps + 2]


def call(kernel, outs, args, scratch=(), limit=24, flops=0, touched=0, outside=()):
    vmem = pl.BlockSpec(memory_space=pltpu.VMEM)
    args = [pltpu.with_memory_space_constraint(arg, pltpu.HBM) if i in outside else arg for i, arg in enumerate(args)]
    return pl.pallas_call(
        kernel,
        out_shape=[
            jax.ShapeDtypeStruct(out[0], out[1]) if len(out) > 2 else pltpu.VMEM(out[0], out[1]) for out in outs
        ],
        in_specs=[pl.BlockSpec(memory_space=pltpu.HBM) if i in outside else vmem for i in range(len(args))],
        out_specs=[pl.BlockSpec(memory_space=pl.ANY) if out[-1] == "hbm" else vmem for out in outs],
        scratch_shapes=[pltpu.VMEM(*entry) if isinstance(entry, tuple) else entry for entry in scratch],
        compiler_params=pltpu.CompilerParams(vmem_limit_bytes=limit * MIB),
        cost_estimate=pl.CostEstimate(flops=flops, bytes_accessed=touched, transcendentals=0),
    )(*args)


def swap(value, axis, offset):
    size = lax.axis_size(axis)
    return lax.ppermute(value, axis, [(i, i ^ offset) for i in range(size)])


def shards(wave, lengths, order, w_first, norm_gain, norm_bias, w_second, cot):
    members = lax.axis_size("dev")
    groups_of = lax.axis_size("grp")
    rows, samp = wave.shape
    taps, chans = w_first.shape
    taps_second = w_second.shape[0]
    stride = taps // 2
    frames0 = (samp - taps) // stride + 1
    frames1 = (frames0 - taps_second) // 2 + 1
    groups = -(-frames0 // GROUP)
    depth = 128
    width = LANES
    dev_bits = members.bit_length() - 1
    grp_bits = groups_of.bit_length() - 1

    offsets = [0, 1, 2, 3]
    waves = [wave] + [swap(wave, "dev", offset) for offset in offsets[1:]]
    for bit in range(2, dev_bits - 1):
        offsets += [offset | (1 << bit) for offset in offsets]
        waves += [swap(held, "dev", 1 << bit) for held in waves]
    lens = lengths.reshape(1, members * rows)
    every = members * rows
    valid, band, near_sel, far_sel, own_wave = call(
        functools.partial(setup_kernel, members),
        [
            ((rows, 128), jnp.int32),
            ((depth, GROUP * chans), BF16),
            ((rows // 2, every), BF16),
            ((rows // 2, every), BF16),
            ((rows, samp), BF16),
        ],
        [order, lens, w_first, wave],
        scratch=[
            (order.shape, order.dtype),
            (lens.shape, lens.dtype),
            (w_first.shape, BF16),
            pltpu.SemaphoreType.DMA((4,)),
        ],
        outside=(0, 1, 2, 3),
    )
    near, send = call(
        functools.partial(pick_kernel, offsets),
        [((rows // 2, samp), BF16), ((rows // 2, samp), BF16)],
        [near_sel, far_sel, own_wave, *waves[1:]],
        scratch=[((every, samp), BF16)],
    )
    far = swap(send, "dev", members // 2)
    gain = norm_gain.reshape(1, chans)
    bias = norm_bias.reshape(1, chans)
    cot_t = cot.transpose(1, 0, 2)
    pad_frames = -(-frames1 // 4) * 4
    places = [0] * members
    for dev in range(members):
        places[dev % 4 * (members // 4) + dev // 4] = dev
    feat, even, odd, pre0, even_slope, odd_slope, mean, inv, patch, grad, grad_t, gain_in, w_in = call(
        functools.partial(forward_kernel, frames0, frames1, taps, places),
        [
            ((frames1, rows, chans), BF16),
            ((pad_frames + 1, rows, chans), BF16),
            ((pad_frames, rows, chans), BF16),
            ((groups, rows, GROUP * chans), F32),
            ((pad_frames, rows, chans), F32),
            ((pad_frames, rows, chans), F32),
            ((rows, chans), F32),
            ((rows, chans), F32),
            ((groups, rows, depth), BF16),
            ((frames1 + 2, rows, chans), BF16),
            ((chans, pad_frames * rows), BF16),
            ((1, chans), F32),
            (w_second.shape, BF16),
        ],
        [near, far, valid, band, gain, bias, w_second, cot_t],
        scratch=[
            ((GROUP, rows, chans), BF16),
            ((GROUP // 2, rows, chans), F32),
            ((GROUP // 2, rows, chans), F32),
            ((rows, chans), F32),
            ((rows, chans), F32),
            (bias.shape, F32),
            (cot_t.shape, BF16),
            pltpu.SemaphoreType.DMA((4,)),
        ],
        outside=(4, 5, 6, 7),
    )
    half = chans // 2
    wide = taps_second * half
    keeps, others = [], []
    for acts, skips in (((even, odd), (0, 0)), ((even,), (1,))):
        shape = (chans, len(acts) * half)
        keep, send = call(
            functools.partial(outer_kernel, skips), [(shape, F32), (shape, BF16)], [*acts, grad_t], flops=len(acts) << 29
        )
        keeps.append(keep)
        others.append(swap(send, "grp", 1))
    quarter = chans // 4
    own, *sends = call(
        plane_kernel,
        [((quarter, wide), F32)] + [((quarter, wide), BF16)] * 3,
        [*keeps, *others],
    )
    gots = [swap(part, "dev", offset) for offset, part in enumerate(sends, 1)]
    evens, odds = (frames0 + 1) // 2, frames0 // 2
    lift_even, lift_odd, features = call(
        input_kernel,
        [((evens, rows, chans), F32), ((odds, rows, chans), F32), ((frames1, rows, chans), BF16, "hbm")],
        [grad, w_in, even_slope, odd_slope, own, feat],
        scratch=[pltpu.SemaphoreType.DMA],
        flops=1 << 30,
    )
    parts = call(
        functools.partial(backward_kernel, frames0, taps),
        [((64, quarter), F32)],
        [valid, pre0, mean, inv, patch, lift_even, lift_odd, gain_in],
        scratch=[
            ((groups, rows, GROUP * width), BF16),
            ((depth, GROUP * width), F32),
            ((16, chans), F32),
            ((4, 16, quarter), F32),
        ],
        flops=1 << 32,
    )[0]
    for bit in range(1, grp_bits - 1):
        parts = parts + swap(parts, "grp", 1 << bit)
    size = quarter // 2
    keep, send, small, *smalls = call(
        functools.partial(gather_kernel, dev_bits - 1),
        [(packed(size, wide), F32), (packed(size, wide), BF16)] + [((16, quarter), F32)] * 4,
        [own, *gots, parts, swap(parts, "grp", groups_of // 2)],
    )
    got = swap(send, "dev", members // 2)
    smalls = [swap(part, "dev", offset) for offset, part in enumerate(smalls, 1)]
    for bit in range(dev_bits - 1, 2, -1):
        size //= 2
        keep, send = call(
            functools.partial(halve_kernel, bit - 1),
            [(packed(size, wide), F32), (packed(size, wide), BF16)],
            [keep, got],
        )
        got = swap(send, "dev", 1 << (bit - 1))
    send, small = call(round_kernel, [(packed(size, wide), BF16), (small.shape, F32)], [keep, got, small, *smalls])
    for bit in range(3, dev_bits):
        small = small + swap(small, "dev", 1 << bit)
    small_got = swap(small, "dev", 4)
    for bit in range(1, grp_bits - 1):
        send = call(add_kernel, [(packed(size, wide), BF16)], [send, swap(send, "grp", 1 << bit)])[0]
    send = call(
        last_add_kernel, [(packed(size, wide), F32)], [send, swap(send, "grp", groups_of // 2), small, small_got]
    )[0]
    grad_second, grad_first, grad_gain, grad_bias = call(
        functools.partial(join_kernel, taps),
        [
            ((taps_second, size, chans), F32, "out"),
            ((taps, size), F32, "out"),
            ((1, size), F32, "out"),
            ((1, size), F32, "out"),
        ],
        [send, swap(send, "grp", 1)],
    )
    return (
        features.transpose(1, 0, 2),
        grad_second.transpose(0, 2, 1),
        grad_first,
        grad_gain.reshape(size),
        grad_bias.reshape(size),
    )


def solution(mesh):
    placed = (
        P(("grp", "dev"), None),
        P("grp"),
        P("grp", None),
        P(),
        P(),
        P(),
        P(),
        P(("grp", "dev"), None, None),
    )
    return jax.shard_map(
        shards,
        mesh=mesh,
        in_specs=placed,
        out_specs=(
            P(("grp", "dev"), None, None),
            P(None, None, "dev"),
            P(None, "dev"),
            P("dev"),
            P("dev"),
        ),
        check_vma=False,
    )
```

```python
import functools

import jax
import jax.numpy as jnp
from jax import lax
from jax.experimental import pallas as pl
from jax.experimental.pallas import tpu as pltpu
from jax.sharding import PartitionSpec as P

F32 = jnp.float32
BF16 = jnp.bfloat16
GROUP = 8
LANES = 256
MIN_SAMPLES = 288
MIB = 1 << 20


def gelu_and_slope(value):
    bell = jnp.exp2(value * value * (-0.5 * 1.4426950408889634))
    phi = 0.5 + 0.5 * lax.erf(value * 0.7071067811865476)
    return value * phi, phi + value * bell * 0.3989422804014327


def rows_first(a, b):
    return lax.dot_general(a, b, (((0,), (0,)), ((), ())), preferred_element_type=F32)


def cols_both(a, b):
    return lax.dot_general(a, b, (((1,), (1,)), ((), ())), preferred_element_type=F32)


def dot(a, b):
    return jnp.dot(a, b, preferred_element_type=F32)


def iota(shape, dim):
    return lax.broadcasted_iota(jnp.int32, shape, dim)


def onehot(mask):
    return mask.astype(F32).astype(BF16)


def copies(sources, targets, sems):
    started = [pltpu.make_async_copy(source, target, sems.at[i]) for i, (source, target) in enumerate(zip(sources, targets))]
    for copy in started:
        copy.start()
    return started


def setup_kernel(
    members,
    order_hbm,
    len_hbm,
    w_hbm,
    wave_hbm,
    valid_ref,
    band_ref,
    near_ref,
    far_ref,
    own_ref,
    order_ref,
    len_ref,
    w_ref,
    sems,
):
    for copy in copies((order_hbm, len_hbm, w_hbm, wave_hbm), (order_ref, len_ref, w_ref, own_ref), sems):
        copy.wait()
    rows = order_ref.shape[1]
    share = rows // members
    taps, chans = w_ref.shape
    stride = taps // 2
    owner = onehot(iota((rows, members), 0) // share == iota((rows, members), 1))
    order_of = dot(owner, order_ref[...].astype(F32).astype(BF16))
    slot = iota((rows, rows), 1) - lax.rem(iota((rows, rows), 0), share) * members
    owner_first = iota((rows, 1), 0) // share * rows
    column = iota((rows, members * rows), 1)
    member = lax.axis_index("dev")
    low_half = member < members // 2
    for target, out_ref in ((member, near_ref), (jnp.bitwise_xor(member, members // 2), far_ref)):
        local = jnp.sum(jnp.where(slot == target, order_of, 0.0), axis=1, keepdims=True).astype(jnp.int32)
        picked = column == owner_first + local
        picks = picked.astype(F32)
        out_ref[...] = jnp.where(low_half, picks[: rows // 2], picks[rows // 2 :]).astype(BF16)
        if out_ref is near_ref:
            lens = jnp.sum(jnp.where(picked, len_ref[...], 0), axis=1, keepdims=True)
    valid = (lens - taps) // stride + 1
    valid_ref[...] = jnp.broadcast_to(valid, valid_ref.shape)
    depth = band_ref.shape[0]
    for f in range(GROUP):
        spread = onehot(iota((depth, taps), 0) == iota((depth, taps), 1) + stride * f)
        band_ref[:, f * chans : (f + 1) * chans] = dot(spread, w_ref[...]).astype(BF16)


def pick_kernel(offsets, near_ref, far_ref, *refs):
    waves, (mine_ref, send_ref, all_ref) = refs[:-3], refs[-3:]
    rows = waves[0].shape[0]
    all_ref[...] = jnp.zeros(all_ref.shape, BF16)
    for offset, wave_ref in zip(offsets, waves):
        first = pl.multiple_of(jnp.bitwise_xor(lax.axis_index("dev"), offset) * rows, rows)
        all_ref[pl.ds(first, rows), :] = wave_ref[...]
    mine_ref[...] = dot(near_ref[...], all_ref[...]).astype(BF16)
    send_ref[...] = dot(far_ref[...], all_ref[...]).astype(BF16)


def forward_kernel(
    frames0,
    frames1,
    taps,
    places,
    near_ref,
    far_ref,
    valid_ref,
    band_ref,
    gain_hbm,
    bias_hbm,
    w_hbm,
    cot_hbm,
    feat_ref,
    even_ref,
    odd_ref,
    pre0,
    even_slope,
    odd_slope,
    mean_ref,
    inv_ref,
    patch_ref,
    grad_ref,
    grad_t_ref,
    gain_ref,
    w_ref,
    stage,
    fresh,
    pre1,
    scale_ref,
    shift_ref,
    bias_ref,
    cot_ref,
    sems,
):
    waiting = copies((gain_hbm, bias_hbm, w_hbm, cot_hbm), (gain_ref, bias_ref, w_ref, cot_ref), sems)
    rows, samp = valid_ref.shape[0], near_ref.shape[1]
    chans = gain_ref.shape[1]
    stride = taps // 2
    depth = band_ref.shape[0]
    groups = pre0.shape[0]
    width = LANES
    parts = [slice(first, first + width) for first in range(0, chans, width)]
    min_valid = (MIN_SAMPLES - taps) // stride + 1
    full_groups = frames0 // GROUP
    free_groups = min(min_valid // GROUP, full_groups)
    low_half = lax.axis_index("dev") < lax.axis_size("dev") // 2
    near, far = near_ref[...].astype(F32), far_ref[...].astype(F32)
    wave = jnp.concatenate([jnp.where(low_half, near, far), jnp.where(low_half, far, near)], axis=0).astype(BF16)
    for g in range(groups):
        pick = onehot(iota((samp, depth), 0) == iota((samp, depth), 1) + GROUP * stride * g)
        patch_ref[g] = dot(wave, pick).astype(BF16)
    patches = patch_ref[...].reshape(groups * rows, depth)
    for f in range(GROUP):
        cols = slice(f * chans, (f + 1) * chans)
        pre0[:, :, cols] = dot(patches, band_ref[:, cols]).reshape(groups, rows, chans)

    valid = jnp.broadcast_to(valid_ref[:, :1], (rows, width))
    count = valid.astype(F32)

    def frame(g, f, lanes):
        return pre0[g, :, f * chans + lanes.start : f * chans + lanes.stop]

    def masked_to(value, t, masked):
        return jnp.where(valid > t, value, 0.0) if masked else value

    for lanes in parts:

        def over_frames(body):
            def step(masked, g, total):
                for f in range(GROUP):
                    total = total + body(g, f, masked)
                return total

            total = lax.fori_loop(0, free_groups, functools.partial(step, False), jnp.zeros((rows, width), F32))
            total = lax.fori_loop(free_groups, full_groups, functools.partial(step, True), total)
            for f in range(frames0 - full_groups * GROUP):
                total = total + body(full_groups, f, True)
            return total

        mean = over_frames(lambda g, f, masked: masked_to(frame(g, f, lanes), g * GROUP + f, masked)) / count

        def square(g, f, masked):
            centred = masked_to(frame(g, f, lanes) - mean, g * GROUP + f, masked)
            return centred * centred

        inv = lax.rsqrt(over_frames(square) / count + 1e-05)
        mean_ref[:, lanes] = mean
        inv_ref[:, lanes] = inv
        if lanes.start == 0:
            waiting[0].wait()
            waiting[1].wait()
        scale = inv * gain_ref[:, lanes]
        scale_ref[:, lanes] = scale
        shift_ref[:, lanes] = bias_ref[:, lanes] - mean * scale

    half = GROUP // 2
    span = half * rows
    frames_of = even_ref.shape[0] - 1
    even_ref[frames_of:] = jnp.zeros((1,) + even_ref.shape[1:], BF16)
    grad_ref[0] = jnp.zeros(grad_ref.shape[1:], BF16)
    grad_ref[frames1 + 1] = jnp.zeros(grad_ref.shape[1:], BF16)
    grad_t_ref[:, frames1 // half * span :] = jnp.zeros((chans, grad_t_ref.shape[1] - frames1 // half * span), BF16)
    min_valid1 = (min_valid - 3) // 2 + 1
    valid1 = lax.shift_right_arithmetic(valid - 3, 1) + 1
    slab = chans // len(places)

    def unstage(g):
        for f in range(GROUP):
            (odd_ref if f % 2 else even_ref)[g * half + f // 2] = stage[f]

    def activate0(g, masked, used=GROUP):
        for f in range(used):
            for lanes in parts:
                gelu, slope = gelu_and_slope(frame(g, f, lanes) * scale_ref[:, lanes] + shift_ref[:, lanes])
                t = g * GROUP + f
                slope_ref = odd_slope if f % 2 else even_slope
                slope_ref[g * half + f // 2, :, lanes] = masked_to(slope, t, masked)
                stage[f, :, lanes] = masked_to(gelu, t, masked).astype(BF16)

    def convolve(h, used):
        first = h * half
        for lanes in parts:
            total = dot(even_ref[pl.ds(first, used)].reshape(used * rows, chans), w_ref[0, :, lanes])
            total += dot(odd_ref[pl.ds(first, used)].reshape(used * rows, chans), w_ref[1, :, lanes])
            total += dot(even_ref[pl.ds(first + 1, used)].reshape(used * rows, chans), w_ref[2, :, lanes])
            fresh[:used, :, lanes] = total.reshape(used, rows, width)

    def activate1(h, used, masked):
        for j in range(used):
            u = h * half + j
            for lanes in parts:
                gelu, slope = gelu_and_slope(pre1[j, :, lanes])
                grad = cot_ref[u, :, lanes].astype(F32) * slope
                if masked:
                    gelu, grad = jnp.where(valid1 > u, gelu, 0.0), jnp.where(valid1 > u, grad, 0.0)
                feat_ref[u, :, lanes] = gelu.astype(BF16)
                grad_ref[u + 1, :, lanes] = grad.astype(BF16)

    def turn(h, used):
        turned = grad_ref[pl.ds(h * half + 1, used)].reshape(used * rows, chans).T
        start = h * span
        cols = pl.ds(start if isinstance(start, int) else pl.multiple_of(start, span), used * rows)
        for place, source in enumerate(places):
            grad_t_ref[place * slab : (place + 1) * slab, cols] = turned[source * slab : (source + 1) * slab]

    def fill(g, carry):
        unstage(jnp.maximum(g - 1, 0))
        activate0(g, False)
        return carry

    def steady(masked, g, carry, used=GROUP):
        unstage(g - 1)
        pre1[...] = fresh[...]
        convolve(g - 2, half)
        activate1(g - 3, half, masked)
        activate0(g, masked, used)
        turn(g - 3, half)
        return carry

    stage[...] = jnp.zeros(stage.shape, BF16)
    lax.fori_loop(0, 3, fill, 0)
    waiting[2].wait()
    waiting[3].wait()
    convolve(0, half)
    lax.fori_loop(3, free_groups, functools.partial(steady, False), 0)
    lax.fori_loop(free_groups, full_groups, functools.partial(steady, True), 0)
    rest = frames0 - full_groups * GROUP
    if rest:
        steady(True, full_groups, 0, rest)
        stage[rest:] = jnp.zeros((GROUP - rest,) + stage.shape[1:], BF16)
    unstage(groups - 1)
    last = frames1 // half
    for h in range(groups - 2, last + 1):
        pre1[...] = fresh[...]
        convolve(h, min(half, frames1 - h * half))
        activate1(h - 1, half, True)
        turn(h - 1, half)
    pre1[...] = fresh[...]
    activate1(last, frames1 - last * half, True)
    turn(last, frames1 - last * half)


def outer_kernel(skips, *refs):
    acts, (grad_t_ref, keep_ref, send_ref) = refs[:-3], refs[-3:]
    rows, chans = acts[0].shape[1:]
    frames = grad_t_ref.shape[1] // rows
    half = chans // 2
    core = lax.rem(lax.axis_index("grp"), 2)
    for tap, (act_ref, skip) in enumerate(zip(acts, skips)):
        for side, out_ref in ((1 - core, send_ref), (core, keep_ref)):
            lanes = pl.ds(pl.multiple_of(side * half, half), half)
            value = dot(grad_t_ref[...], act_ref[skip : skip + frames, :, lanes].reshape(frames * rows, half))
            out_ref[:, tap * half : (tap + 1) * half] = value.astype(out_ref.dtype)


def input_kernel(grad_ref, w_ref, even_slope, odd_slope, feat_ref, even_ref, odd_ref, feat_out, sem):
    leaving = pltpu.make_async_copy(feat_ref, feat_out, sem)
    leaving.start()
    evens, rows, chans = even_ref.shape
    odds = odd_ref.shape[0]
    first = grad_ref[1 : evens + 1].reshape(evens * rows, chans)
    third = grad_ref[0:evens].reshape(evens * rows, chans)
    total = cols_both(first, w_ref[0]) + cols_both(third, w_ref[2])
    even_ref[...] = total.reshape(even_ref.shape) * even_slope[:evens]
    second = grad_ref[1 : odds + 1].reshape(odds * rows, chans)
    odd_ref[...] = cols_both(second, w_ref[1]).reshape(odd_ref.shape) * odd_slope[:odds]
    leaving.wait()


def backward_kernel(
    frames0,
    taps,
    valid_ref,
    pre0,
    mean_ref,
    inv_ref,
    patch_ref,
    even_ref,
    odd_ref,
    gain_ref,
    mine_ref,
    send1,
    send2,
    send3,
    dpre0,
    spread,
    out_ref,
    quarters,
):
    groups, rows, depth = patch_ref.shape
    chans = gain_ref.shape[1]
    stride = taps // 2
    width = dpre0.shape[2] // GROUP
    full_groups = frames0 // GROUP
    free_groups = min(((MIN_SAMPLES - taps) // stride + 1) // GROUP, full_groups)
    rest = frames0 - full_groups * GROUP
    patches = patch_ref[...].reshape(groups * rows, depth)
    for block in range(chans // width):
        lanes = slice(block * width, (block + 1) * width)

        def frame(g, f):
            return pre0[g, :, f * chans + block * width : f * chans + (block + 1) * width]

        def lift(g, f):
            return (odd_ref if f % 2 else even_ref)[g * (GROUP // 2) + f // 2, :, lanes]

        def sums(g, f, carry):
            bias_sum, gain_sum = carry
            return bias_sum + lift(g, f), gain_sum + lift(g, f) * frame(g, f)

        def add(g, carry):
            for f in range(GROUP):
                carry = sums(g, f, carry)
            return carry

        zero = jnp.zeros((rows, width), F32)
        carry = lax.fori_loop(0, full_groups, add, (zero, zero))
        for f in range(rest):
            carry = sums(full_groups, f, carry)
        bias_sum, gain_sum = carry
        mean, inv = mean_ref[:, lanes], inv_ref[:, lanes]
        gain_sum = (gain_sum - mean * bias_sum) * inv
        out_ref[taps : taps + 1, lanes] = jnp.sum(gain_sum, axis=0, keepdims=True)
        out_ref[taps + 1 : taps + 2, lanes] = jnp.sum(bias_sum, axis=0, keepdims=True)
        valid = jnp.broadcast_to(valid_ref[:, :1], (rows, width))
        count = valid.astype(F32)
        scale = inv * gain_ref[:, lanes]
        slant = scale * inv * gain_sum / count
        level = scale * bias_sum / count - mean * slant

        def finish(g, f, masked):
            value = scale * lift(g, f) - frame(g, f) * slant - level
            if masked:
                value = jnp.where(valid > g * GROUP + f, value, 0.0)
            dpre0[g, :, f * width : (f + 1) * width] = value.astype(BF16)

        def whole(masked, g, carry):
            for f in range(GROUP):
                finish(g, f, masked)
            return carry

        lax.fori_loop(0, free_groups, functools.partial(whole, False), 0)
        lax.fori_loop(free_groups, full_groups, functools.partial(whole, True), 0)
        for f in range(rest):
            finish(full_groups, f, True)
        if full_groups < groups:
            dpre0[full_groups, :, rest * width :] = jnp.zeros((rows, (GROUP - rest) * width), BF16)
        spread[...] = rows_first(patches, dpre0[...].reshape(groups * rows, GROUP * width))
        total = jnp.zeros((taps, width), F32)
        for f in range(GROUP):
            total += spread[stride * f : stride * f + taps, f * width : (f + 1) * width]
        out_ref[:taps, lanes] = total
    size = chans // lax.axis_size("dev")
    for place in range(4):
        columns = [slice(first, first + size) for first in range(place * size, chans, 4 * size)]
        quarters[place] = jnp.concatenate([out_ref[:, part] for part in columns], axis=1)
    place = lax.rem(lax.axis_index("dev"), 4)
    for offset, ref in enumerate((mine_ref, send1, send2, send3)):
        ref[...] = quarters[jnp.bitwise_xor(place, offset)]


def plane_kernel(*refs):
    keeps, others, outs = refs[:2], refs[2:4], refs[5:]
    size = outs[0].shape[0]
    edge = keeps[0].shape[1]
    place = lax.rem(lax.axis_index("dev"), 4)
    for offset, out_ref in enumerate(outs):
        lines = pl.ds(pl.multiple_of(jnp.bitwise_xor(place, offset) * size, size), size)
        for lanes, keep_ref, got_ref in zip((slice(0, edge), slice(edge, None)), keeps, others):
            out_ref[:, lanes] = (keep_ref[lines, :] + got_ref[lines, :].astype(F32)).astype(out_ref.dtype)


def part_kernel(own_ref, got1, got2, small_ref, sum_ref, total_ref):
    sum_ref[...] = own_ref[...] + (got1[...].astype(F32) + got2[...].astype(F32))
    total_ref[...] = small_ref[...]


def packed(size, wide):
    return size + 16, wide - 128


def write_packed(ref, value, small):
    size, lanes = ref.shape[0] - 16, ref.shape[1]
    ref[:size] = value[:, :lanes].astype(ref.dtype)
    used = size // 16
    for block in range(used):
        piece = value[block * 16 : (block + 1) * 16, lanes:]
        ref[size:, block * 128 : (block + 1) * 128] = piece.astype(ref.dtype)
    for first in range(used * 128, lanes - 128, 128):
        ref[size:, first : first + 128] = jnp.zeros((16, 128), ref.dtype)
    ref[size:, lanes - 128 :] = small.astype(ref.dtype)


def read_packed(ref, first, count):
    size = ref.shape[0] - 16
    whole = ref[pl.ds(pl.multiple_of(first, 16), count), :].astype(F32)
    pieces = [
        ref[size:, pl.ds(pl.multiple_of(first * 8 + block * 128, 128), 128)].astype(F32) for block in range(count // 16)
    ]
    return jnp.concatenate([whole, jnp.concatenate(pieces, axis=0)], axis=1)


def gather_kernel(bit, own_ref, got3, small0, small1, small2, small3, keep_ref, send_ref):
    half = own_ref.shape[0] // 2
    side = lax.rem(lax.shift_right_logical(lax.axis_index("dev"), bit), 2)
    total = (small0[...] + small1[...]) + (small2[...] + small3[...])
    for index, ref in ((1 - side, send_ref), (side, keep_ref)):
        lines = pl.ds(pl.multiple_of(index * half, half), half)
        write_packed(ref, own_ref[lines, :] + got3[lines, :].astype(F32), total)


def halve_kernel(bit, keep_ref, got_ref, next_ref, send_ref):
    half = (keep_ref.shape[0] - 16) // 2
    side = lax.rem(lax.shift_right_logical(lax.axis_index("dev"), bit), 2)
    small = keep_ref[2 * half :, -128:] + got_ref[2 * half :, -128:].astype(F32)
    for index, ref in ((1 - side, send_ref), (side, next_ref)):
        first = index * half
        write_packed(ref, read_packed(keep_ref, first, half) + read_packed(got_ref, first, half), small)


def add_kernel(mine_ref, got_ref, out_ref):
    out_ref[...] = (mine_ref[...].astype(F32) + got_ref[...].astype(F32)).astype(out_ref.dtype)


def join_kernel(taps, own_ref, other_ref, out_ref, first_ref, gain_ref, bias_ref):
    second, size, chans = out_ref.shape
    half = chans // 2
    core = lax.rem(lax.axis_index("grp"), 2)
    for ref, side in ((own_ref, core), (other_ref, 1 - core)):
        value = read_packed(ref, 0, size)
        for tap in range(second):
            lanes = pl.ds(pl.multiple_of(side * half, half), half)
            out_ref[tap, :, lanes] = value[:, tap * half : (tap + 1) * half]
    total = own_ref[size:, -128:] + other_ref[size:, -128:]
    value = total[:, :size]
    for place in range(1, 128 // size):
        mine = lax.axis_index("dev") // 4 == place
        value = jnp.where(mine, total[:, place * size : (place + 1) * size], value)
    first_ref[...] = value[:taps]
    gain_ref[...] = value[taps : taps + 1]
    bias_ref[...] = value[taps + 1 : taps + 2]


def call(kernel, outs, args, scratch=(), limit=24, flops=0, touched=0, outside=()):
    vmem = pl.BlockSpec(memory_space=pltpu.VMEM)
    args = [pltpu.with_memory_space_constraint(arg, pltpu.HBM) if i in outside else arg for i, arg in enumerate(args)]
    return pl.pallas_call(
        kernel,
        out_shape=[
            jax.ShapeDtypeStruct(out[0], out[1]) if len(out) > 2 else pltpu.VMEM(out[0], out[1]) for out in outs
        ],
        in_specs=[pl.BlockSpec(memory_space=pltpu.HBM) if i in outside else vmem for i in range(len(args))],
        out_specs=[pl.BlockSpec(memory_space=pl.ANY) if out[-1] == "hbm" else vmem for out in outs],
        scratch_shapes=[pltpu.VMEM(*entry) if isinstance(entry, tuple) else entry for entry in scratch],
        compiler_params=pltpu.CompilerParams(vmem_limit_bytes=limit * MIB),
        cost_estimate=pl.CostEstimate(flops=flops, bytes_accessed=touched, transcendentals=0),
    )(*args)


def swap(value, axis, offset):
    size = lax.axis_size(axis)
    return lax.ppermute(value, axis, [(i, i ^ offset) for i in range(size)])


def shards(wave, lengths, order, w_first, norm_gain, norm_bias, w_second, cot):
    members = lax.axis_size("dev")
    groups_of = lax.axis_size("grp")
    rows, samp = wave.shape
    taps, chans = w_first.shape
    taps_second = w_second.shape[0]
    stride = taps // 2
    frames0 = (samp - taps) // stride + 1
    frames1 = (frames0 - taps_second) // 2 + 1
    groups = -(-frames0 // GROUP)
    depth = 128
    width = LANES
    dev_bits = members.bit_length() - 1
    grp_bits = groups_of.bit_length() - 1

    offsets = [0, 1, 2, 3]
    waves = [wave] + [swap(wave, "dev", offset) for offset in offsets[1:]]
    for bit in range(2, dev_bits - 1):
        offsets += [offset | (1 << bit) for offset in offsets]
        waves += [swap(held, "dev", 1 << bit) for held in waves]
    lens = lengths.reshape(1, members * rows)
    every = members * rows
    valid, band, near_sel, far_sel, own_wave = call(
        functools.partial(setup_kernel, members),
        [
            ((rows, 128), jnp.int32),
            ((depth, GROUP * chans), BF16),
            ((rows // 2, every), BF16),
            ((rows // 2, every), BF16),
            ((rows, samp), BF16),
        ],
        [order, lens, w_first, wave],
        scratch=[
            (order.shape, order.dtype),
            (lens.shape, lens.dtype),
            (w_first.shape, BF16),
            pltpu.SemaphoreType.DMA((4,)),
        ],
        outside=(0, 1, 2, 3),
    )
    near, send = call(
        functools.partial(pick_kernel, offsets),
        [((rows // 2, samp), BF16), ((rows // 2, samp), BF16)],
        [near_sel, far_sel, own_wave, *waves[1:]],
        scratch=[((every, samp), BF16)],
    )
    far = swap(send, "dev", members // 2)
    gain = norm_gain.reshape(1, chans)
    bias = norm_bias.reshape(1, chans)
    cot_t = cot.transpose(1, 0, 2)
    pad_frames = -(-frames1 // 4) * 4
    places = [0] * members
    for dev in range(members):
        places[dev % 4 * (members // 4) + dev // 4] = dev
    feat, even, odd, pre0, even_slope, odd_slope, mean, inv, patch, grad, grad_t, gain_in, w_in = call(
        functools.partial(forward_kernel, frames0, frames1, taps, places),
        [
            ((frames1, rows, chans), BF16),
            ((pad_frames + 1, rows, chans), BF16),
            ((pad_frames, rows, chans), BF16),
            ((groups, rows, GROUP * chans), F32),
            ((pad_frames, rows, chans), F32),
            ((pad_frames, rows, chans), F32),
            ((rows, chans), F32),
            ((rows, chans), F32),
            ((groups, rows, depth), BF16),
            ((frames1 + 2, rows, chans), BF16),
            ((chans, pad_frames * rows), BF16),
            ((1, chans), F32),
            (w_second.shape, BF16),
        ],
        [near, far, valid, band, gain, bias, w_second, cot_t],
        scratch=[
            ((GROUP, rows, chans), BF16),
            ((GROUP // 2, rows, chans), F32),
            ((GROUP // 2, rows, chans), F32),
            ((rows, chans), F32),
            ((rows, chans), F32),
            (bias.shape, F32),
            (cot_t.shape, BF16),
            pltpu.SemaphoreType.DMA((4,)),
        ],
        outside=(4, 5, 6, 7),
    )
    half = chans // 2
    wide = taps_second * half
    keeps, others = [], []
    for acts, skips in (((even, odd), (0, 0)), ((even,), (1,))):
        shape = (chans, len(acts) * half)
        keep, send = call(
            functools.partial(outer_kernel, skips), [(shape, F32), (shape, BF16)], [*acts, grad_t], flops=len(acts) << 29
        )
        keeps.append(keep)
        others.append(swap(send, "grp", 1))
    evens, odds = (frames0 + 1) // 2, frames0 // 2
    lift_even, lift_odd, features = call(
        input_kernel,
        [((evens, rows, chans), F32), ((odds, rows, chans), F32), ((frames1, rows, chans), BF16, "hbm")],
        [grad, w_in, even_slope, odd_slope, feat],
        scratch=[pltpu.SemaphoreType.DMA],
        flops=1 << 30,
    )
    quarter = chans // 4
    own, *sends = call(
        plane_kernel,
        [((quarter, wide), F32)] + [((quarter, wide), BF16)] * 3,
        [*keeps, *others, lift_odd],
    )
    gots = [swap(part, "dev", offset) for offset, part in enumerate(sends, 1)]
    small, *smalls = call(
        functools.partial(backward_kernel, frames0, taps),
        [((16, quarter), F32)] * 4,
        [valid, pre0, mean, inv, patch, lift_even, lift_odd, gain_in],
        scratch=[
            ((groups, rows, GROUP * width), BF16),
            ((depth, GROUP * width), F32),
            ((16, chans), F32),
            ((4, 16, quarter), F32),
        ],
        flops=1 << 32,
    )
    small3, small2 = swap(smalls[2], "dev", 3), swap(smalls[1], "dev", 2)
    own, first = call(
        part_kernel, [((quarter, wide), F32), (small.shape, F32)], [own, gots[0], gots[1], smalls[0]]
    )
    small1 = swap(first, "dev", 1)
    size = quarter // 2
    keep, send = call(
        functools.partial(gather_kernel, dev_bits - 1),
        [(packed(size, wide), F32), (packed(size, wide), BF16)],
        [own, gots[2], small, small1, small2, small3],
    )
    for bit in range(dev_bits - 1, 2, -1):
        size //= 2
        keep, send = call(
            functools.partial(halve_kernel, bit - 1),
            [(packed(size, wide), F32), (packed(size, wide), BF16)],
            [keep, swap(send, "dev", 1 << bit)],
        )
    send = call(add_kernel, [(packed(size, wide), BF16)], [keep, swap(send, "dev", 4)])[0]
    for bit in range(1, grp_bits):
        kind = F32 if bit == grp_bits - 1 else BF16
        send = call(add_kernel, [(packed(size, wide), kind)], [send, swap(send, "grp", 1 << bit)])[0]
    grad_second, grad_first, grad_gain, grad_bias = call(
        functools.partial(join_kernel, taps),
        [
            ((taps_second, size, chans), F32, "out"),
            ((taps, size), F32, "out"),
            ((1, size), F32, "out"),
            ((1, size), F32, "out"),
        ],
        [send, swap(send, "grp", 1)],
    )
    return (
        features.transpose(1, 0, 2),
        grad_second.transpose(0, 2, 1),
        grad_first,
        grad_gain.reshape(size),
        grad_bias.reshape(size),
    )


def solution(mesh):
    placed = (
        P(("grp", "dev"), None),
        P("grp"),
        P("grp", None),
        P(),
        P(),
        P(),
        P(),
        P(("grp", "dev"), None, None),
    )
    return jax.shard_map(
        shards,
        mesh=mesh,
        in_specs=placed,
        out_specs=(
            P(("grp", "dev"), None, None),
            P(None, None, "dev"),
            P(None, "dev"),
            P("dev"),
            P("dev"),
        ),
        check_vma=False,
    )
```

```python
import functools

import jax
import jax.numpy as jnp
from jax import lax
from jax.experimental import pallas as pl
from jax.experimental.pallas import tpu as pltpu
from jax.sharding import PartitionSpec as P

F32 = jnp.float32
BF16 = jnp.bfloat16
GROUP = 8
LANES = 256
MIN_SAMPLES = 288
MIB = 1 << 20


def gelu_and_slope(value):
    bell = jnp.exp2(value * value * (-0.5 * 1.4426950408889634))
    phi = 0.5 + 0.5 * lax.erf(value * 0.7071067811865476)
    return value * phi, phi + value * bell * 0.3989422804014327


def rows_first(a, b):
    return lax.dot_general(a, b, (((0,), (0,)), ((), ())), preferred_element_type=F32)


def cols_both(a, b):
    return lax.dot_general(a, b, (((1,), (1,)), ((), ())), preferred_element_type=F32)


def dot(a, b):
    return jnp.dot(a, b, preferred_element_type=F32)


def iota(shape, dim):
    return lax.broadcasted_iota(jnp.int32, shape, dim)


def onehot(mask):
    return mask.astype(F32).astype(BF16)


def copies(sources, targets, sems):
    started = [pltpu.make_async_copy(source, target, sems.at[i]) for i, (source, target) in enumerate(zip(sources, targets))]
    for copy in started:
        copy.start()
    return started


def setup_kernel(
    members,
    order_hbm,
    len_hbm,
    w_hbm,
    wave_hbm,
    valid_ref,
    band_ref,
    near_ref,
    far_ref,
    own_ref,
    order_ref,
    len_ref,
    w_ref,
    sems,
):
    for copy in copies((order_hbm, len_hbm, w_hbm, wave_hbm), (order_ref, len_ref, w_ref, own_ref), sems):
        copy.wait()
    rows = order_ref.shape[1]
    share = rows // members
    taps, chans = w_ref.shape
    stride = taps // 2
    owner = onehot(iota((rows, members), 0) // share == iota((rows, members), 1))
    order_of = dot(owner, order_ref[...].astype(F32).astype(BF16))
    slot = iota((rows, rows), 1) - lax.rem(iota((rows, rows), 0), share) * members
    owner_first = iota((rows, 1), 0) // share * rows
    column = iota((rows, members * rows), 1)
    member = lax.axis_index("dev")
    low_half = member < members // 2
    for target, out_ref in ((member, near_ref), (jnp.bitwise_xor(member, members // 2), far_ref)):
        local = jnp.sum(jnp.where(slot == target, order_of, 0.0), axis=1, keepdims=True).astype(jnp.int32)
        picked = column == owner_first + local
        picks = picked.astype(F32)
        out_ref[...] = jnp.where(low_half, picks[: rows // 2], picks[rows // 2 :]).astype(BF16)
        if out_ref is near_ref:
            lens = jnp.sum(jnp.where(picked, len_ref[...], 0), axis=1, keepdims=True)
    valid = (lens - taps) // stride + 1
    valid_ref[...] = jnp.broadcast_to(valid, valid_ref.shape)
    depth = band_ref.shape[0]
    for f in range(GROUP):
        spread = onehot(iota((depth, taps), 0) == iota((depth, taps), 1) + stride * f)
        band_ref[:, f * chans : (f + 1) * chans] = dot(spread, w_ref[...]).astype(BF16)


def pick_kernel(offsets, near_ref, far_ref, *refs):
    waves, (mine_ref, send_ref, all_ref) = refs[:-3], refs[-3:]
    rows = waves[0].shape[0]
    all_ref[...] = jnp.zeros(all_ref.shape, BF16)
    for offset, wave_ref in zip(offsets, waves):
        first = pl.multiple_of(jnp.bitwise_xor(lax.axis_index("dev"), offset) * rows, rows)
        all_ref[pl.ds(first, rows), :] = wave_ref[...]
    mine_ref[...] = dot(near_ref[...], all_ref[...]).astype(BF16)
    send_ref[...] = dot(far_ref[...], all_ref[...]).astype(BF16)


def forward_kernel(
    frames0,
    frames1,
    taps,
    places,
    near_ref,
    far_ref,
    valid_ref,
    band_ref,
    gain_hbm,
    bias_hbm,
    w_hbm,
    cot_hbm,
    feat_ref,
    even_ref,
    odd_ref,
    pre0,
    even_slope,
    odd_slope,
    mean_ref,
    inv_ref,
    patch_ref,
    grad_ref,
    grad_t_ref,
    gain_ref,
    w_ref,
    stage,
    fresh,
    pre1,
    scale_ref,
    shift_ref,
    bias_ref,
    cot_ref,
    sems,
):
    waiting = copies((gain_hbm, bias_hbm, w_hbm, cot_hbm), (gain_ref, bias_ref, w_ref, cot_ref), sems)
    rows, samp = valid_ref.shape[0], near_ref.shape[1]
    chans = gain_ref.shape[1]
    stride = taps // 2
    depth = band_ref.shape[0]
    groups = pre0.shape[0]
    width = LANES
    parts = [slice(first, first + width) for first in range(0, chans, width)]
    min_valid = (MIN_SAMPLES - taps) // stride + 1
    full_groups = frames0 // GROUP
    free_groups = min(min_valid // GROUP, full_groups)
    low_half = lax.axis_index("dev") < lax.axis_size("dev") // 2
    near, far = near_ref[...].astype(F32), far_ref[...].astype(F32)
    wave = jnp.concatenate([jnp.where(low_half, near, far), jnp.where(low_half, far, near)], axis=0).astype(BF16)
    for g in range(groups):
        pick = onehot(iota((samp, depth), 0) == iota((samp, depth), 1) + GROUP * stride * g)
        patch_ref[g] = dot(wave, pick).astype(BF16)
    patches = patch_ref[...].reshape(groups * rows, depth)
    for f in range(GROUP):
        cols = slice(f * chans, (f + 1) * chans)
        pre0[:, :, cols] = dot(patches, band_ref[:, cols]).reshape(groups, rows, chans)

    valid = jnp.broadcast_to(valid_ref[:, :1], (rows, width))
    count = valid.astype(F32)

    def frame(g, f, lanes):
        return pre0[g, :, f * chans + lanes.start : f * chans + lanes.stop]

    def masked_to(value, t, masked):
        return jnp.where(valid > t, value, 0.0) if masked else value

    for lanes in parts:

        def over_frames(body):
            def step(masked, g, total):
                for f in range(GROUP):
                    total = total + body(g, f, masked)
                return total

            total = lax.fori_loop(0, free_groups, functools.partial(step, False), jnp.zeros((rows, width), F32))
            total = lax.fori_loop(free_groups, full_groups, functools.partial(step, True), total)
            for f in range(frames0 - full_groups * GROUP):
                total = total + body(full_groups, f, True)
            return total

        mean = over_frames(lambda g, f, masked: masked_to(frame(g, f, lanes), g * GROUP + f, masked)) / count

        def square(g, f, masked):
            centred = masked_to(frame(g, f, lanes) - mean, g * GROUP + f, masked)
            return centred * centred

        inv = lax.rsqrt(over_frames(square) / count + 1e-05)
        mean_ref[:, lanes] = mean
        inv_ref[:, lanes] = inv
        if lanes.start == 0:
            waiting[0].wait()
            waiting[1].wait()
        scale = inv * gain_ref[:, lanes]
        scale_ref[:, lanes] = scale
        shift_ref[:, lanes] = bias_ref[:, lanes] - mean * scale

    half = GROUP // 2
    span = half * rows
    frames_of = even_ref.shape[0] - 1
    even_ref[frames_of:] = jnp.zeros((1,) + even_ref.shape[1:], BF16)
    grad_ref[0] = jnp.zeros(grad_ref.shape[1:], BF16)
    grad_ref[frames1 + 1] = jnp.zeros(grad_ref.shape[1:], BF16)
    grad_t_ref[:, frames1 // half * span :] = jnp.zeros((chans, grad_t_ref.shape[1] - frames1 // half * span), BF16)
    min_valid1 = (min_valid - 3) // 2 + 1
    valid1 = lax.shift_right_arithmetic(valid - 3, 1) + 1
    slab = chans // len(places)

    def unstage(g):
        for f in range(GROUP):
            (odd_ref if f % 2 else even_ref)[g * half + f // 2] = stage[f]

    def activate0(g, masked, used=GROUP):
        for f in range(used):
            for lanes in parts:
                gelu, slope = gelu_and_slope(frame(g, f, lanes) * scale_ref[:, lanes] + shift_ref[:, lanes])
                t = g * GROUP + f
                slope_ref = odd_slope if f % 2 else even_slope
                slope_ref[g * half + f // 2, :, lanes] = masked_to(slope, t, masked)
                stage[f, :, lanes] = masked_to(gelu, t, masked).astype(BF16)

    def convolve(h, used):
        first = h * half
        for lanes in parts:
            total = dot(even_ref[pl.ds(first, used)].reshape(used * rows, chans), w_ref[0, :, lanes])
            total += dot(odd_ref[pl.ds(first, used)].reshape(used * rows, chans), w_ref[1, :, lanes])
            total += dot(even_ref[pl.ds(first + 1, used)].reshape(used * rows, chans), w_ref[2, :, lanes])
            fresh[:used, :, lanes] = total.reshape(used, rows, width)

    def activate1(h, used, masked):
        for j in range(used):
            u = h * half + j
            for lanes in parts:
                gelu, slope = gelu_and_slope(pre1[j, :, lanes])
                grad = cot_ref[u, :, lanes].astype(F32) * slope
                if masked:
                    gelu, grad = jnp.where(valid1 > u, gelu, 0.0), jnp.where(valid1 > u, grad, 0.0)
                feat_ref[u, :, lanes] = gelu.astype(BF16)
                grad_ref[u + 1, :, lanes] = grad.astype(BF16)

    def turn(h, used):
        turned = grad_ref[pl.ds(h * half + 1, used)].reshape(used * rows, chans).T
        start = h * span
        cols = pl.ds(start if isinstance(start, int) else pl.multiple_of(start, span), used * rows)
        for place, source in enumerate(places):
            grad_t_ref[place * slab : (place + 1) * slab, cols] = turned[source * slab : (source + 1) * slab]

    def fill(g, carry):
        unstage(jnp.maximum(g - 1, 0))
        activate0(g, False)
        return carry

    def steady(masked, g, carry, used=GROUP):
        unstage(g - 1)
        pre1[...] = fresh[...]
        convolve(g - 2, half)
        activate1(g - 3, half, masked)
        activate0(g, masked, used)
        turn(g - 3, half)
        return carry

    stage[...] = jnp.zeros(stage.shape, BF16)
    lax.fori_loop(0, 3, fill, 0)
    waiting[2].wait()
    waiting[3].wait()
    convolve(0, half)
    lax.fori_loop(3, free_groups, functools.partial(steady, False), 0)
    lax.fori_loop(free_groups, full_groups, functools.partial(steady, True), 0)
    rest = frames0 - full_groups * GROUP
    if rest:
        steady(True, full_groups, 0, rest)
        stage[rest:] = jnp.zeros((GROUP - rest,) + stage.shape[1:], BF16)
    unstage(groups - 1)
    last = frames1 // half
    for h in range(groups - 2, last + 1):
        pre1[...] = fresh[...]
        convolve(h, min(half, frames1 - h * half))
        activate1(h - 1, half, True)
        turn(h - 1, half)
    pre1[...] = fresh[...]
    activate1(last, frames1 - last * half, True)
    turn(last, frames1 - last * half)


def outer_kernel(skips, *refs):
    acts, (grad_t_ref, keep_ref, send_ref) = refs[:-3], refs[-3:]
    rows, chans = acts[0].shape[1:]
    frames = grad_t_ref.shape[1] // rows
    half = chans // 2
    core = lax.rem(lax.axis_index("grp"), 2)
    for tap, (act_ref, skip) in enumerate(zip(acts, skips)):
        for side, out_ref in ((1 - core, send_ref), (core, keep_ref)):
            lanes = pl.ds(pl.multiple_of(side * half, half), half)
            value = dot(grad_t_ref[...], act_ref[skip : skip + frames, :, lanes].reshape(frames * rows, half))
            out_ref[:, tap * half : (tap + 1) * half] = value.astype(out_ref.dtype)


def input_kernel(grad_ref, w_ref, even_slope, odd_slope, after_ref, feat_ref, even_ref, odd_ref, feat_out, sem):
    leaving = pltpu.make_async_copy(feat_ref, feat_out, sem)
    leaving.start()
    evens, rows, chans = even_ref.shape
    odds = odd_ref.shape[0]
    first = grad_ref[1 : evens + 1].reshape(evens * rows, chans)
    third = grad_ref[0:evens].reshape(evens * rows, chans)
    total = cols_both(first, w_ref[0]) + cols_both(third, w_ref[2])
    even_ref[...] = total.reshape(even_ref.shape) * even_slope[:evens]
    second = grad_ref[1 : odds + 1].reshape(odds * rows, chans)
    odd_ref[...] = cols_both(second, w_ref[1]).reshape(odd_ref.shape) * odd_slope[:odds]
    leaving.wait()


def backward_kernel(
    frames0,
    taps,
    valid_ref,
    pre0,
    mean_ref,
    inv_ref,
    patch_ref,
    even_ref,
    odd_ref,
    gain_ref,
    small_ref,
    dpre0,
    spread,
    out_ref,
    quarters,
):
    groups, rows, depth = patch_ref.shape
    chans = gain_ref.shape[1]
    stride = taps // 2
    width = dpre0.shape[2] // GROUP
    full_groups = frames0 // GROUP
    free_groups = min(((MIN_SAMPLES - taps) // stride + 1) // GROUP, full_groups)
    rest = frames0 - full_groups * GROUP
    patches = patch_ref[...].reshape(groups * rows, depth)
    for block in range(chans // width):
        lanes = slice(block * width, (block + 1) * width)

        def frame(g, f):
            return pre0[g, :, f * chans + block * width : f * chans + (block + 1) * width]

        def lift(g, f):
            return (odd_ref if f % 2 else even_ref)[g * (GROUP // 2) + f // 2, :, lanes]

        def sums(g, f, carry):
            bias_sum, gain_sum = carry
            return bias_sum + lift(g, f), gain_sum + lift(g, f) * frame(g, f)

        def add(g, carry):
            for f in range(GROUP):
                carry = sums(g, f, carry)
            return carry

        zero = jnp.zeros((rows, width), F32)
        carry = lax.fori_loop(0, full_groups, add, (zero, zero))
        for f in range(rest):
            carry = sums(full_groups, f, carry)
        bias_sum, gain_sum = carry
        mean, inv = mean_ref[:, lanes], inv_ref[:, lanes]
        gain_sum = (gain_sum - mean * bias_sum) * inv
        out_ref[taps : taps + 1, lanes] = jnp.sum(gain_sum, axis=0, keepdims=True)
        out_ref[taps + 1 : taps + 2, lanes] = jnp.sum(bias_sum, axis=0, keepdims=True)
        valid = jnp.broadcast_to(valid_ref[:, :1], (rows, width))
        count = valid.astype(F32)
        scale = inv * gain_ref[:, lanes]
        slant = scale * inv * gain_sum / count
        level = scale * bias_sum / count - mean * slant

        def finish(g, f, masked):
            value = scale * lift(g, f) - frame(g, f) * slant - level
            if masked:
                value = jnp.where(valid > g * GROUP + f, value, 0.0)
            dpre0[g, :, f * width : (f + 1) * width] = value.astype(BF16)

        def whole(masked, g, carry):
            for f in range(GROUP):
                finish(g, f, masked)
            return carry

        lax.fori_loop(0, free_groups, functools.partial(whole, False), 0)
        lax.fori_loop(free_groups, full_groups, functools.partial(whole, True), 0)
        for f in range(rest):
            finish(full_groups, f, True)
        if full_groups < groups:
            dpre0[full_groups, :, rest * width :] = jnp.zeros((rows, (GROUP - rest) * width), BF16)
        spread[...] = rows_first(patches, dpre0[...].reshape(groups * rows, GROUP * width))
        total = jnp.zeros((taps, width), F32)
        for f in range(GROUP):
            total += spread[stride * f : stride * f + taps, f * width : (f + 1) * width]
        out_ref[:taps, lanes] = total
    size = chans // lax.axis_size("dev")
    for place in range(4):
        columns = [slice(first, first + size) for first in range(place * size, chans, 4 * size)]
        quarters[place] = jnp.concatenate([out_ref[:, part] for part in columns], axis=1)
    place = lax.rem(lax.axis_index("dev"), 4)
    for offset in range(4):
        small_ref[offset * 16 : (offset + 1) * 16] = quarters[jnp.bitwise_xor(place, offset)]


def plane_kernel(keep_ref, got_ref, *refs):
    small_ref, outs = (None, refs) if len(refs) == 4 else (refs[0], refs[2:])
    size = outs[0].shape[0]
    place = lax.rem(lax.axis_index("dev"), 4)
    for offset, out_ref in enumerate(outs):
        lines = pl.ds(pl.multiple_of(jnp.bitwise_xor(place, offset) * size, size), size)
        out_ref[:size] = (keep_ref[lines, :] + got_ref[lines, :].astype(F32)).astype(out_ref.dtype)
        if small_ref is not None and offset:
            value = small_ref[offset * 16 : (offset + 1) * 16]
            high = value.astype(BF16)
            out_ref[size:, :128] = high
            out_ref[size:, 128:] = (value - high.astype(F32)).astype(BF16)


def packed(size, wide):
    return size + 16, wide - 128


def write_packed(ref, value, small):
    size, lanes = ref.shape[0] - 16, ref.shape[1]
    ref[:size] = value[:, :lanes].astype(ref.dtype)
    used = size // 16
    for block in range(used):
        piece = value[block * 16 : (block + 1) * 16, lanes:]
        ref[size:, block * 128 : (block + 1) * 128] = piece.astype(ref.dtype)
    for first in range(used * 128, lanes - 128, 128):
        ref[size:, first : first + 128] = jnp.zeros((16, 128), ref.dtype)
    ref[size:, lanes - 128 :] = small.astype(ref.dtype)


def read_packed(ref, first, count):
    size = ref.shape[0] - 16
    whole = ref[pl.ds(pl.multiple_of(first, 16), count), :].astype(F32)
    pieces = [
        ref[size:, pl.ds(pl.multiple_of(first * 8 + block * 128, 128), 128)].astype(F32) for block in range(count // 16)
    ]
    return jnp.concatenate([whole, jnp.concatenate(pieces, axis=0)], axis=1)


def sum_kernel(own_ref, got1, got2, got3, sum_ref):
    sum_ref[...] = own_ref[...] + (got1[...].astype(F32) + got2[...].astype(F32) + got3[...].astype(F32))


def gather_kernel(bit, sum_ref, own_ref, got1, got2, got3, small_ref, keep_ref, send_ref):
    size, edge = sum_ref.shape
    half = size // 2
    side = lax.rem(lax.shift_right_logical(lax.axis_index("dev"), bit), 2)
    small = small_ref[:16]
    for ref in (got1, got2, got3):
        small += ref[size:, :128].astype(F32) + ref[size:, 128:].astype(F32)
    for index, ref in ((1 - side, send_ref), (side, keep_ref)):
        lines = pl.ds(pl.multiple_of(index * half, half), half)
        late = got1[lines, :].astype(F32) + got2[lines, :].astype(F32) + got3[lines, :].astype(F32)
        write_packed(ref, jnp.concatenate([sum_ref[lines, :], own_ref[lines, :] + late], axis=1), small)


def halve_kernel(bit, keep_ref, got_ref, next_ref, send_ref):
    half = (keep_ref.shape[0] - 16) // 2
    side = lax.rem(lax.shift_right_logical(lax.axis_index("dev"), bit), 2)
    small = keep_ref[2 * half :, -128:] + got_ref[2 * half :, -128:].astype(F32)
    for index, ref in ((1 - side, send_ref), (side, next_ref)):
        first = index * half
        write_packed(ref, read_packed(keep_ref, first, half) + read_packed(got_ref, first, half), small)


def add_kernel(mine_ref, got_ref, out_ref):
    out_ref[...] = (mine_ref[...].astype(F32) + got_ref[...].astype(F32)).astype(out_ref.dtype)


def join_kernel(taps, own_ref, other_ref, out_ref, first_ref, gain_ref, bias_ref):
    second, size, chans = out_ref.shape
    half = chans // 2
    core = lax.rem(lax.axis_index("grp"), 2)
    for ref, side in ((own_ref, core), (other_ref, 1 - core)):
        value = read_packed(ref, 0, size)
        for tap in range(second):
            lanes = pl.ds(pl.multiple_of(side * half, half), half)
            out_ref[tap, :, lanes] = value[:, tap * half : (tap + 1) * half]
    total = own_ref[size:, -128:] + other_ref[size:, -128:]
    value = total[:, :size]
    for place in range(1, 128 // size):
        mine = lax.axis_index("dev") // 4 == place
        value = jnp.where(mine, total[:, place * size : (place + 1) * size], value)
    first_ref[...] = value[:taps]
    gain_ref[...] = value[taps : taps + 1]
    bias_ref[...] = value[taps + 1 : taps + 2]


def call(kernel, outs, args, scratch=(), limit=24, flops=0, touched=0, outside=()):
    vmem = pl.BlockSpec(memory_space=pltpu.VMEM)
    args = [pltpu.with_memory_space_constraint(arg, pltpu.HBM) if i in outside else arg for i, arg in enumerate(args)]
    return pl.pallas_call(
        kernel,
        out_shape=[
            jax.ShapeDtypeStruct(out[0], out[1]) if len(out) > 2 else pltpu.VMEM(out[0], out[1]) for out in outs
        ],
        in_specs=[pl.BlockSpec(memory_space=pltpu.HBM) if i in outside else vmem for i in range(len(args))],
        out_specs=[pl.BlockSpec(memory_space=pl.ANY) if out[-1] == "hbm" else vmem for out in outs],
        scratch_shapes=[pltpu.VMEM(*entry) if isinstance(entry, tuple) else entry for entry in scratch],
        compiler_params=pltpu.CompilerParams(vmem_limit_bytes=limit * MIB),
        cost_estimate=pl.CostEstimate(flops=flops, bytes_accessed=touched, transcendentals=0),
    )(*args)


def swap(value, axis, offset):
    size = lax.axis_size(axis)
    return lax.ppermute(value, axis, [(i, i ^ offset) for i in range(size)])


def shards(wave, lengths, order, w_first, norm_gain, norm_bias, w_second, cot):
    members = lax.axis_size("dev")
    groups_of = lax.axis_size("grp")
    rows, samp = wave.shape
    taps, chans = w_first.shape
    taps_second = w_second.shape[0]
    stride = taps // 2
    frames0 = (samp - taps) // stride + 1
    frames1 = (frames0 - taps_second) // 2 + 1
    groups = -(-frames0 // GROUP)
    depth = 128
    width = LANES
    dev_bits = members.bit_length() - 1
    grp_bits = groups_of.bit_length() - 1

    offsets = [0, 1, 2, 3]
    waves = [wave] + [swap(wave, "dev", offset) for offset in offsets[1:]]
    for bit in range(2, dev_bits - 1):
        offsets += [offset | (1 << bit) for offset in offsets]
        waves += [swap(held, "dev", 1 << bit) for held in waves]
    lens = lengths.reshape(1, members * rows)
    every = members * rows
    valid, band, near_sel, far_sel, own_wave = call(
        functools.partial(setup_kernel, members),
        [
            ((rows, 128), jnp.int32),
            ((depth, GROUP * chans), BF16),
            ((rows // 2, every), BF16),
            ((rows // 2, every), BF16),
            ((rows, samp), BF16),
        ],
        [order, lens, w_first, wave],
        scratch=[
            (order.shape, order.dtype),
            (lens.shape, lens.dtype),
            (w_first.shape, BF16),
            pltpu.SemaphoreType.DMA((4,)),
        ],
        outside=(0, 1, 2, 3),
    )
    near, send = call(
        functools.partial(pick_kernel, offsets),
        [((rows // 2, samp), BF16), ((rows // 2, samp), BF16)],
        [near_sel, far_sel, own_wave, *waves[1:]],
        scratch=[((every, samp), BF16)],
    )
    far = swap(send, "dev", members // 2)
    gain = norm_gain.reshape(1, chans)
    bias = norm_bias.reshape(1, chans)
    cot_t = cot.transpose(1, 0, 2)
    pad_frames = -(-frames1 // 4) * 4
    places = [0] * members
    for dev in range(members):
        places[dev % 4 * (members // 4) + dev // 4] = dev
    feat, even, odd, pre0, even_slope, odd_slope, mean, inv, patch, grad, grad_t, gain_in, w_in = call(
        functools.partial(forward_kernel, frames0, frames1, taps, places),
        [
            ((frames1, rows, chans), BF16),
            ((pad_frames + 1, rows, chans), BF16),
            ((pad_frames, rows, chans), BF16),
            ((groups, rows, GROUP * chans), F32),
            ((pad_frames, rows, chans), F32),
            ((pad_frames, rows, chans), F32),
            ((rows, chans), F32),
            ((rows, chans), F32),
            ((groups, rows, depth), BF16),
            ((frames1 + 2, rows, chans), BF16),
            ((chans, pad_frames * rows), BF16),
            ((1, chans), F32),
            (w_second.shape, BF16),
        ],
        [near, far, valid, band, gain, bias, w_second, cot_t],
        scratch=[
            ((GROUP, rows, chans), BF16),
            ((GROUP // 2, rows, chans), F32),
            ((GROUP // 2, rows, chans), F32),
            ((rows, chans), F32),
            ((rows, chans), F32),
            (bias.shape, F32),
            (cot_t.shape, BF16),
            pltpu.SemaphoreType.DMA((4,)),
        ],
        outside=(4, 5, 6, 7),
    )
    half = chans // 2
    wide = taps_second * half
    keeps, others = [], []
    for acts, skips in (((even, odd), (0, 0)), ((even,), (1,))):
        shape = (chans, len(acts) * half)
        keep, send = call(
            functools.partial(outer_kernel, skips), [(shape, F32), (shape, BF16)], [*acts, grad_t], flops=len(acts) << 29
        )
        keeps.append(keep)
        others.append(swap(send, "grp", 1))
    quarter = chans // 4
    shape = (quarter, 2 * half)
    own0, *sends = call(plane_kernel, [(shape, F32)] + [(shape, BF16)] * 3, [keeps[0], others[0]])
    gots0 = [swap(part, "dev", offset) for offset, part in enumerate(sends, 1)]
    evens, odds = (frames0 + 1) // 2, frames0 // 2
    lift_even, lift_odd, features = call(
        input_kernel,
        [((evens, rows, chans), F32), ((odds, rows, chans), F32), ((frames1, rows, chans), BF16, "hbm")],
        [grad, w_in, even_slope, odd_slope, own0, feat],
        scratch=[pltpu.SemaphoreType.DMA],
        flops=1 << 30,
    )
    small = call(
        functools.partial(backward_kernel, frames0, taps),
        [((64, quarter), F32)],
        [valid, pre0, mean, inv, patch, lift_even, lift_odd, gain_in],
        scratch=[
            ((groups, rows, GROUP * width), BF16),
            ((depth, GROUP * width), F32),
            ((16, chans), F32),
            ((4, 16, quarter), F32),
        ],
        flops=1 << 32,
    )[0]
    sum0 = call(sum_kernel, [(shape, F32)], [own0, *gots0])[0]
    own1, *sends = call(
        plane_kernel,
        [((quarter, half), F32)] + [((quarter + 16, half), BF16)] * 3,
        [keeps[1], others[1], small, sum0],
    )
    gots1 = [swap(part, "dev", offset) for offset, part in enumerate(sends, 1)]
    size = quarter // 2
    keep, send = call(
        functools.partial(gather_kernel, dev_bits - 1),
        [(packed(size, wide), F32), (packed(size, wide), BF16)],
        [sum0, own1, *gots1, small],
    )
    for bit in range(dev_bits - 1, 2, -1):
        size //= 2
        keep, send = call(
            functools.partial(halve_kernel, bit - 1),
            [(packed(size, wide), F32), (packed(size, wide), BF16)],
            [keep, swap(send, "dev", 1 << bit)],
        )
    send = call(add_kernel, [(packed(size, wide), BF16)], [keep, swap(send, "dev", 4)])[0]
    for bit in range(1, grp_bits):
        kind = F32 if bit == grp_bits - 1 else BF16
        send = call(add_kernel, [(packed(size, wide), kind)], [send, swap(send, "grp", 1 << bit)])[0]
    grad_second, grad_first, grad_gain, grad_bias = call(
        functools.partial(join_kernel, taps),
        [
            ((taps_second, size, chans), F32, "out"),
            ((taps, size), F32, "out"),
            ((1, size), F32, "out"),
            ((1, size), F32, "out"),
        ],
        [send, swap(send, "grp", 1)],
    )
    return (
        features.transpose(1, 0, 2),
        grad_second.transpose(0, 2, 1),
        grad_first,
        grad_gain.reshape(size),
        grad_bias.reshape(size),
    )


def solution(mesh):
    placed = (
        P(("grp", "dev"), None),
        P("grp"),
        P("grp", None),
        P(),
        P(),
        P(),
        P(),
        P(("grp", "dev"), None, None),
    )
    return jax.shard_map(
        shards,
        mesh=mesh,
        in_specs=placed,
        out_specs=(
            P(("grp", "dev"), None, None),
            P(None, None, "dev"),
            P(None, "dev"),
            P("dev"),
            P("dev"),
        ),
        check_vma=False,
    )
```

```python
import functools

import jax
import jax.numpy as jnp
from jax import lax
from jax.experimental import pallas as pl
from jax.experimental.pallas import tpu as pltpu
from jax.sharding import PartitionSpec as P

F32 = jnp.float32
BF16 = jnp.bfloat16
GROUP = 8
LANES = 256
MIN_SAMPLES = 288
MIB = 1 << 20


def gelu_and_slope(value):
    bell = jnp.exp2(value * value * (-0.5 * 1.4426950408889634))
    phi = 0.5 + 0.5 * lax.erf(value * 0.7071067811865476)
    return value * phi, phi + value * bell * 0.3989422804014327


def rows_first(a, b):
    return lax.dot_general(a, b, (((0,), (0,)), ((), ())), preferred_element_type=F32)


def cols_both(a, b):
    return lax.dot_general(a, b, (((1,), (1,)), ((), ())), preferred_element_type=F32)


def dot(a, b):
    return jnp.dot(a, b, preferred_element_type=F32)


def iota(shape, dim):
    return lax.broadcasted_iota(jnp.int32, shape, dim)


def onehot(mask):
    return mask.astype(F32).astype(BF16)


def copies(sources, targets, sems):
    started = [pltpu.make_async_copy(source, target, sems.at[i]) for i, (source, target) in enumerate(zip(sources, targets))]
    for copy in started:
        copy.start()
    return started


def setup_kernel(
    members,
    order_hbm,
    len_hbm,
    w_hbm,
    wave_hbm,
    valid_ref,
    band_ref,
    near_ref,
    far_ref,
    own_ref,
    order_ref,
    len_ref,
    w_ref,
    sems,
):
    for copy in copies((order_hbm, len_hbm, w_hbm, wave_hbm), (order_ref, len_ref, w_ref, own_ref), sems):
        copy.wait()
    rows = order_ref.shape[1]
    share = rows // members
    taps, chans = w_ref.shape
    stride = taps // 2
    owner = onehot(iota((rows, members), 0) // share == iota((rows, members), 1))
    order_of = dot(owner, order_ref[...].astype(F32).astype(BF16))
    slot = iota((rows, rows), 1) - lax.rem(iota((rows, rows), 0), share) * members
    owner_first = iota((rows, 1), 0) // share * rows
    column = iota((rows, members * rows), 1)
    member = lax.axis_index("dev")
    low_half = member < members // 2
    for target, out_ref in ((member, near_ref), (jnp.bitwise_xor(member, members // 2), far_ref)):
        local = jnp.sum(jnp.where(slot == target, order_of, 0.0), axis=1, keepdims=True).astype(jnp.int32)
        picked = column == owner_first + local
        picks = picked.astype(F32)
        out_ref[...] = jnp.where(low_half, picks[: rows // 2], picks[rows // 2 :]).astype(BF16)
        if out_ref is near_ref:
            lens = jnp.sum(jnp.where(picked, len_ref[...], 0), axis=1, keepdims=True)
    valid = (lens - taps) // stride + 1
    valid_ref[...] = jnp.broadcast_to(valid, valid_ref.shape)
    depth = band_ref.shape[0]
    for f in range(GROUP):
        spread = onehot(iota((depth, taps), 0) == iota((depth, taps), 1) + stride * f)
        band_ref[:, f * chans : (f + 1) * chans] = dot(spread, w_ref[...]).astype(BF16)


def pick_kernel(offsets, near_ref, far_ref, *refs):
    waves, (mine_ref, send_ref, all_ref) = refs[:-3], refs[-3:]
    rows = waves[0].shape[0]
    all_ref[...] = jnp.zeros(all_ref.shape, BF16)
    for offset, wave_ref in zip(offsets, waves):
        first = pl.multiple_of(jnp.bitwise_xor(lax.axis_index("dev"), offset) * rows, rows)
        all_ref[pl.ds(first, rows), :] = wave_ref[...]
    mine_ref[...] = dot(near_ref[...], all_ref[...]).astype(BF16)
    send_ref[...] = dot(far_ref[...], all_ref[...]).astype(BF16)


def forward_kernel(
    frames0,
    frames1,
    taps,
    places,
    near_ref,
    far_ref,
    valid_ref,
    band_ref,
    gain_hbm,
    bias_hbm,
    w_hbm,
    cot_hbm,
    feat_ref,
    even_ref,
    odd_ref,
    pre0,
    even_slope,
    odd_slope,
    mean_ref,
    inv_ref,
    patch_ref,
    grad_ref,
    grad_t_ref,
    gain_ref,
    w_ref,
    fresh0,
    fresh1,
    scale_ref,
    shift_ref,
    bias_ref,
    cot_ref,
    sems,
):
    waiting = copies((gain_hbm, bias_hbm, w_hbm, cot_hbm), (gain_ref, bias_ref, w_ref, cot_ref), sems)
    rows, samp = valid_ref.shape[0], near_ref.shape[1]
    chans = gain_ref.shape[1]
    stride = taps // 2
    depth = band_ref.shape[0]
    groups = pre0.shape[0]
    width = LANES
    parts = [slice(first, first + width) for first in range(0, chans, width)]
    min_valid = (MIN_SAMPLES - taps) // stride + 1
    full_groups = frames0 // GROUP
    free_groups = min(min_valid // GROUP, full_groups)
    low_half = lax.axis_index("dev") < lax.axis_size("dev") // 2
    near, far = near_ref[...].astype(F32), far_ref[...].astype(F32)
    wave = jnp.concatenate([jnp.where(low_half, near, far), jnp.where(low_half, far, near)], axis=0).astype(BF16)
    for g in range(groups):
        pick = onehot(iota((samp, depth), 0) == iota((samp, depth), 1) + GROUP * stride * g)
        patch_ref[g] = dot(wave, pick).astype(BF16)
    patches = patch_ref[...].reshape(groups * rows, depth)
    for f in range(GROUP):
        cols = slice(f * chans, (f + 1) * chans)
        pre0[:, :, cols] = dot(patches, band_ref[:, cols]).reshape(groups, rows, chans)

    valid = jnp.broadcast_to(valid_ref[:, :1], (rows, width))
    count = valid.astype(F32)

    def frame(g, f, lanes):
        return pre0[g, :, f * chans + lanes.start : f * chans + lanes.stop]

    def masked_to(value, t, masked):
        return jnp.where(valid > t, value, 0.0) if masked else value

    for lanes in parts:

        def over_frames(body):
            def step(masked, g, total):
                for f in range(GROUP):
                    total = total + body(g, f, masked)
                return total

            total = lax.fori_loop(0, free_groups, functools.partial(step, False), jnp.zeros((rows, width), F32))
            total = lax.fori_loop(free_groups, full_groups, functools.partial(step, True), total)
            for f in range(frames0 - full_groups * GROUP):
                total = total + body(full_groups, f, True)
            return total

        mean = over_frames(lambda g, f, masked: masked_to(frame(g, f, lanes), g * GROUP + f, masked)) / count

        def square(g, f, masked):
            centred = masked_to(frame(g, f, lanes) - mean, g * GROUP + f, masked)
            return centred * centred

        inv = lax.rsqrt(over_frames(square) / count + 1e-05)
        mean_ref[:, lanes] = mean
        inv_ref[:, lanes] = inv
        if lanes.start == 0:
            waiting[0].wait()
            waiting[1].wait()
        scale = inv * gain_ref[:, lanes]
        scale_ref[:, lanes] = scale
        shift_ref[:, lanes] = bias_ref[:, lanes] - mean * scale

    half = GROUP
    evens, odds = (frames0 + 1) // 2, frames0 // 2
    min_valid1 = (min_valid - 3) // 2 + 1
    valid1 = lax.shift_right_arithmetic(valid - 3, 1) + 1
    slab = chans // len(places)
    steps = -(-frames1 // half)

    def used_in(step):
        return min(half, frames1 - step * half)

    def activate0(step):
        for t in range(step * 2 * half, min((step + 1) * 2 * half, frames0)):
            for lanes in parts:
                gelu, slope = gelu_and_slope(
                    frame(t // GROUP, t % GROUP, lanes) * scale_ref[:, lanes] + shift_ref[:, lanes]
                )
                act_ref, slope_ref = (odd_ref, odd_slope) if t % 2 else (even_ref, even_slope)
                slope_ref[t // 2, :, lanes] = masked_to(slope, t, t >= min_valid)
                act_ref[t // 2, :, lanes] = masked_to(gelu, t, t >= min_valid).astype(BF16)

    def convolve(step, out_ref):
        first, used = step * half, used_in(step)
        for lanes in parts:
            total = dot(even_ref[first : first + used].reshape(used * rows, chans), w_ref[0, :, lanes])
            total += dot(odd_ref[first : first + used].reshape(used * rows, chans), w_ref[1, :, lanes])
            total += dot(even_ref[first + 1 : first + used + 1].reshape(used * rows, chans), w_ref[2, :, lanes])
            out_ref[:used, :, lanes] = total.reshape(used, rows, width)

    def activate1(step, in_ref):
        for j in range(used_in(step)):
            u = step * half + j
            for lanes in parts:
                gelu, slope = gelu_and_slope(in_ref[j, :, lanes])
                grad = cot_ref[u, :, lanes].astype(F32) * slope
                if u >= min_valid1:
                    gelu, grad = jnp.where(valid1 > u, gelu, 0.0), jnp.where(valid1 > u, grad, 0.0)
                feat_ref[u, :, lanes] = gelu.astype(BF16)
                grad_ref[u + 1, :, lanes] = grad.astype(BF16)

    def turn(step):
        first, size = step * half, used_in(step) * rows
        turned = grad_ref[first + 1 : first + 1 + used_in(step)].reshape(size, chans).T
        for place, source in enumerate(places):
            grad_t_ref[place * slab : (place + 1) * slab, first * rows : first * rows + size] = turned[
                source * slab : (source + 1) * slab
            ]

    for ref, used in ((even_ref, evens), (odd_ref, odds)):
        ref[used:] = jnp.zeros((ref.shape[0] - used,) + ref.shape[1:], BF16)
    grad_ref[0] = jnp.zeros(grad_ref.shape[1:], BF16)
    grad_ref[frames1 + 1] = jnp.zeros(grad_ref.shape[1:], BF16)
    full = frames1 * rows // 128 * 128
    grad_t_ref[:, full:] = jnp.zeros((chans, grad_t_ref.shape[1] - full), BF16)
    fresh = (fresh0, fresh1)
    for step in range(steps + 3):
        if step == 2:
            waiting[2].wait()
            waiting[3].wait()
        if 0 <= step - 2 < steps:
            convolve(step - 2, fresh[step % 2])
        if 0 <= step - 3 < steps:
            activate1(step - 3, fresh[(step - 1) % 2])
        if step < -(-frames0 // (2 * half)):
            activate0(step)
        if 0 <= step - 3 < steps:
            turn(step - 3)


def outer_kernel(skips, *refs):
    acts, (grad_t_ref, keep_ref, send_ref) = refs[:-3], refs[-3:]
    rows, chans = acts[0].shape[1:]
    frames = grad_t_ref.shape[1] // rows
    half = chans // 2
    core = lax.rem(lax.axis_index("grp"), 2)
    for tap, (act_ref, skip) in enumerate(zip(acts, skips)):
        for side, out_ref in ((1 - core, send_ref), (core, keep_ref)):
            lanes = pl.ds(pl.multiple_of(side * half, half), half)
            value = dot(grad_t_ref[...], act_ref[skip : skip + frames, :, lanes].reshape(frames * rows, half))
            out_ref[:, tap * half : (tap + 1) * half] = value.astype(out_ref.dtype)


def input_kernel(grad_ref, w_ref, even_slope, odd_slope, feat_ref, even_ref, odd_ref, feat_out, sem):
    leaving = pltpu.make_async_copy(feat_ref, feat_out, sem)
    leaving.start()
    evens, rows, chans = even_ref.shape
    odds = odd_ref.shape[0]
    first = grad_ref[1 : evens + 1].reshape(evens * rows, chans)
    third = grad_ref[0:evens].reshape(evens * rows, chans)
    total = cols_both(first, w_ref[0]) + cols_both(third, w_ref[2])
    even_ref[...] = total.reshape(even_ref.shape) * even_slope[:evens]
    second = grad_ref[1 : odds + 1].reshape(odds * rows, chans)
    odd_ref[...] = cols_both(second, w_ref[1]).reshape(odd_ref.shape) * odd_slope[:odds]
    leaving.wait()


def backward_kernel(
    frames0,
    taps,
    valid_ref,
    pre0,
    mean_ref,
    inv_ref,
    patch_ref,
    even_ref,
    odd_ref,
    gain_ref,
    mine_ref,
    send1,
    send2,
    send3,
    dpre0,
    spread,
    out_ref,
    quarters,
):
    groups, rows, depth = patch_ref.shape
    chans = gain_ref.shape[1]
    stride = taps // 2
    width = dpre0.shape[2] // GROUP
    full_groups = frames0 // GROUP
    free_groups = min(((MIN_SAMPLES - taps) // stride + 1) // GROUP, full_groups)
    rest = frames0 - full_groups * GROUP
    patches = patch_ref[...].reshape(groups * rows, depth)
    for block in range(chans // width):
        lanes = slice(block * width, (block + 1) * width)

        def frame(g, f):
            return pre0[g, :, f * chans + block * width : f * chans + (block + 1) * width]

        def lift(g, f):
            return (odd_ref if f % 2 else even_ref)[g * (GROUP // 2) + f // 2, :, lanes]

        def sums(g, f, carry):
            bias_sum, gain_sum = carry
            return bias_sum + lift(g, f), gain_sum + lift(g, f) * frame(g, f)

        def add(g, carry):
            for f in range(GROUP):
                carry = sums(g, f, carry)
            return carry

        zero = jnp.zeros((rows, width), F32)
        carry = lax.fori_loop(0, full_groups, add, (zero, zero))
        for f in range(rest):
            carry = sums(full_groups, f, carry)
        bias_sum, gain_sum = carry
        mean, inv = mean_ref[:, lanes], inv_ref[:, lanes]
        gain_sum = (gain_sum - mean * bias_sum) * inv
        out_ref[taps : taps + 1, lanes] = jnp.sum(gain_sum, axis=0, keepdims=True)
        out_ref[taps + 1 : taps + 2, lanes] = jnp.sum(bias_sum, axis=0, keepdims=True)
        valid = jnp.broadcast_to(valid_ref[:, :1], (rows, width))
        count = valid.astype(F32)
        scale = inv * gain_ref[:, lanes]
        slant = scale * inv * gain_sum / count
        level = scale * bias_sum / count - mean * slant

        def finish(g, f, masked):
            value = scale * lift(g, f) - frame(g, f) * slant - level
            if masked:
                value = jnp.where(valid > g * GROUP + f, value, 0.0)
            dpre0[g, :, f * width : (f + 1) * width] = value.astype(BF16)

        def whole(masked, g, carry):
            for f in range(GROUP):
                finish(g, f, masked)
            return carry

        lax.fori_loop(0, free_groups, functools.partial(whole, False), 0)
        lax.fori_loop(free_groups, full_groups, functools.partial(whole, True), 0)
        for f in range(rest):
            finish(full_groups, f, True)
        if full_groups < groups:
            dpre0[full_groups, :, rest * width :] = jnp.zeros((rows, (GROUP - rest) * width), BF16)
        spread[...] = rows_first(patches, dpre0[...].reshape(groups * rows, GROUP * width))
        total = jnp.zeros((taps, width), F32)
        for f in range(GROUP):
            total += spread[stride * f : stride * f + taps, f * width : (f + 1) * width]
        out_ref[:taps, lanes] = total
    size = chans // lax.axis_size("dev")
    for place in range(4):
        columns = [slice(first, first + size) for first in range(place * size, chans, 4 * size)]
        quarters[place] = jnp.concatenate([out_ref[:, part] for part in columns], axis=1)
    place = lax.rem(lax.axis_index("dev"), 4)
    for offset, ref in enumerate((mine_ref, send1, send2, send3)):
        ref[...] = quarters[jnp.bitwise_xor(place, offset)]


def plane_kernel(*refs):
    keeps, others, outs = refs[:2], refs[2:4], refs[5:]
    size = outs[0].shape[0]
    edge = keeps[0].shape[1]
    place = lax.rem(lax.axis_index("dev"), 4)
    for offset, out_ref in enumerate(outs):
        lines = pl.ds(pl.multiple_of(jnp.bitwise_xor(place, offset) * size, size), size)
        for lanes, keep_ref, got_ref in zip((slice(0, edge), slice(edge, None)), keeps, others):
            out_ref[:, lanes] = (keep_ref[lines, :] + got_ref[lines, :].astype(F32)).astype(out_ref.dtype)


def part_kernel(own_ref, got1, got2, small_ref, sum_ref, total_ref):
    sum_ref[...] = own_ref[...] + (got1[...].astype(F32) + got2[...].astype(F32))
    total_ref[...] = small_ref[...]


def packed(size, wide):
    return size + 16, wide - 128


def write_packed(ref, value, small):
    size, lanes = ref.shape[0] - 16, ref.shape[1]
    ref[:size] = value[:, :lanes].astype(ref.dtype)
    used = size // 16
    for block in range(used):
        piece = value[block * 16 : (block + 1) * 16, lanes:]
        ref[size:, block * 128 : (block + 1) * 128] = piece.astype(ref.dtype)
    for first in range(used * 128, lanes - 128, 128):
        ref[size:, first : first + 128] = jnp.zeros((16, 128), ref.dtype)
    ref[size:, lanes - 128 :] = small.astype(ref.dtype)


def read_packed(ref, first, count):
    size = ref.shape[0] - 16
    whole = ref[pl.ds(pl.multiple_of(first, 16), count), :].astype(F32)
    pieces = [
        ref[size:, pl.ds(pl.multiple_of(first * 8 + block * 128, 128), 128)].astype(F32) for block in range(count // 16)
    ]
    return jnp.concatenate([whole, jnp.concatenate(pieces, axis=0)], axis=1)


def gather_kernel(bit, own_ref, got3, small0, small1, small2, small3, keep_ref, send_ref):
    half = own_ref.shape[0] // 2
    side = lax.rem(lax.shift_right_logical(lax.axis_index("dev"), bit), 2)
    total = (small0[...] + small1[...]) + (small2[...] + small3[...])
    for index, ref in ((1 - side, send_ref), (side, keep_ref)):
        lines = pl.ds(pl.multiple_of(index * half, half), half)
        write_packed(ref, own_ref[lines, :] + got3[lines, :].astype(F32), total)


def halve_kernel(bit, keep_ref, got_ref, next_ref, send_ref):
    half = (keep_ref.shape[0] - 16) // 2
    side = lax.rem(lax.shift_right_logical(lax.axis_index("dev"), bit), 2)
    small = keep_ref[2 * half :, -128:] + got_ref[2 * half :, -128:].astype(F32)
    for index, ref in ((1 - side, send_ref), (side, next_ref)):
        first = index * half
        write_packed(ref, read_packed(keep_ref, first, half) + read_packed(got_ref, first, half), small)


def add_kernel(mine_ref, got_ref, out_ref):
    out_ref[...] = (mine_ref[...].astype(F32) + got_ref[...].astype(F32)).astype(out_ref.dtype)


def join_kernel(taps, own_ref, other_ref, out_ref, first_ref, gain_ref, bias_ref):
    second, size, chans = out_ref.shape
    half = chans // 2
    core = lax.rem(lax.axis_index("grp"), 2)
    for ref, side in ((own_ref, core), (other_ref, 1 - core)):
        value = read_packed(ref, 0, size)
        for tap in range(second):
            lanes = pl.ds(pl.multiple_of(side * half, half), half)
            out_ref[tap, :, lanes] = value[:, tap * half : (tap + 1) * half]
    total = own_ref[size:, -128:] + other_ref[size:, -128:]
    value = total[:, :size]
    for place in range(1, 128 // size):
        mine = lax.axis_index("dev") // 4 == place
        value = jnp.where(mine, total[:, place * size : (place + 1) * size], value)
    first_ref[...] = value[:taps]
    gain_ref[...] = value[taps : taps + 1]
    bias_ref[...] = value[taps + 1 : taps + 2]


def call(kernel, outs, args, scratch=(), limit=24, flops=0, touched=0, outside=()):
    vmem = pl.BlockSpec(memory_space=pltpu.VMEM)
    args = [pltpu.with_memory_space_constraint(arg, pltpu.HBM) if i in outside else arg for i, arg in enumerate(args)]
    return pl.pallas_call(
        kernel,
        out_shape=[
            jax.ShapeDtypeStruct(out[0], out[1]) if len(out) > 2 else pltpu.VMEM(out[0], out[1]) for out in outs
        ],
        in_specs=[pl.BlockSpec(memory_space=pltpu.HBM) if i in outside else vmem for i in range(len(args))],
        out_specs=[pl.BlockSpec(memory_space=pl.ANY) if out[-1] == "hbm" else vmem for out in outs],
        scratch_shapes=[pltpu.VMEM(*entry) if isinstance(entry, tuple) else entry for entry in scratch],
        compiler_params=pltpu.CompilerParams(vmem_limit_bytes=limit * MIB),
        cost_estimate=pl.CostEstimate(flops=flops, bytes_accessed=touched, transcendentals=0),
    )(*args)


def swap(value, axis, offset):
    size = lax.axis_size(axis)
    return lax.ppermute(value, axis, [(i, i ^ offset) for i in range(size)])


def shards(wave, lengths, order, w_first, norm_gain, norm_bias, w_second, cot):
    members = lax.axis_size("dev")
    groups_of = lax.axis_size("grp")
    rows, samp = wave.shape
    taps, chans = w_first.shape
    taps_second = w_second.shape[0]
    stride = taps // 2
    frames0 = (samp - taps) // stride + 1
    frames1 = (frames0 - taps_second) // 2 + 1
    groups = -(-frames0 // GROUP)
    depth = 128
    width = LANES
    dev_bits = members.bit_length() - 1
    grp_bits = groups_of.bit_length() - 1

    offsets = [0, 1, 2, 3]
    waves = [wave] + [swap(wave, "dev", offset) for offset in offsets[1:]]
    for bit in range(2, dev_bits - 1):
        offsets += [offset | (1 << bit) for offset in offsets]
        waves += [swap(held, "dev", 1 << bit) for held in waves]
    lens = lengths.reshape(1, members * rows)
    every = members * rows
    valid, band, near_sel, far_sel, own_wave = call(
        functools.partial(setup_kernel, members),
        [
            ((rows, 128), jnp.int32),
            ((depth, GROUP * chans), BF16),
            ((rows // 2, every), BF16),
            ((rows // 2, every), BF16),
            ((rows, samp), BF16),
        ],
        [order, lens, w_first, wave],
        scratch=[
            (order.shape, order.dtype),
            (lens.shape, lens.dtype),
            (w_first.shape, BF16),
            pltpu.SemaphoreType.DMA((4,)),
        ],
        outside=(0, 1, 2, 3),
    )
    near, send = call(
        functools.partial(pick_kernel, offsets),
        [((rows // 2, samp), BF16), ((rows // 2, samp), BF16)],
        [near_sel, far_sel, own_wave, *waves[1:]],
        scratch=[((every, samp), BF16)],
    )
    far = swap(send, "dev", members // 2)
    gain = norm_gain.reshape(1, chans)
    bias = norm_bias.reshape(1, chans)
    cot_t = cot.transpose(1, 0, 2)
    pad_frames = -(-frames1 // 4) * 4
    places = [0] * members
    for dev in range(members):
        places[dev % 4 * (members // 4) + dev // 4] = dev
    feat, even, odd, pre0, even_slope, odd_slope, mean, inv, patch, grad, grad_t, gain_in, w_in = call(
        functools.partial(forward_kernel, frames0, frames1, taps, places),
        [
            ((frames1, rows, chans), BF16),
            ((pad_frames + 1, rows, chans), BF16),
            ((pad_frames, rows, chans), BF16),
            ((groups, rows, GROUP * chans), F32),
            ((pad_frames, rows, chans), F32),
            ((pad_frames, rows, chans), F32),
            ((rows, chans), F32),
            ((rows, chans), F32),
            ((groups, rows, depth), BF16),
            ((frames1 + 2, rows, chans), BF16),
            ((chans, pad_frames * rows), BF16),
            ((1, chans), F32),
            (w_second.shape, BF16),
        ],
        [near, far, valid, band, gain, bias, w_second, cot_t],
        scratch=[
            ((GROUP, rows, chans), F32),
            ((GROUP, rows, chans), F32),
            ((rows, chans), F32),
            ((rows, chans), F32),
            (bias.shape, F32),
            (cot_t.shape, BF16),
            pltpu.SemaphoreType.DMA((4,)),
        ],
        outside=(4, 5, 6, 7),
    )
    half = chans // 2
    wide = taps_second * half
    keeps, others = [], []
    for acts, skips in (((even, odd), (0, 0)), ((even,), (1,))):
        shape = (chans, len(acts) * half)
        keep, send = call(
            functools.partial(outer_kernel, skips), [(shape, F32), (shape, BF16)], [*acts, grad_t], flops=len(acts) << 29
        )
        keeps.append(keep)
        others.append(swap(send, "grp", 1))
    evens, odds = (frames0 + 1) // 2, frames0 // 2
    lift_even, lift_odd, features = call(
        input_kernel,
        [((evens, rows, chans), F32), ((odds, rows, chans), F32), ((frames1, rows, chans), BF16, "hbm")],
        [grad, w_in, even_slope, odd_slope, feat],
        scratch=[pltpu.SemaphoreType.DMA],
        flops=1 << 30,
    )
    quarter = chans // 4
    own, *sends = call(
        plane_kernel,
        [((quarter, wide), F32)] + [((quarter, wide), BF16)] * 3,
        [*keeps, *others, lift_odd],
    )
    gots = [swap(part, "dev", offset) for offset, part in enumerate(sends, 1)]
    small, *smalls = call(
        functools.partial(backward_kernel, frames0, taps),
        [((16, quarter), F32)] * 4,
        [valid, pre0, mean, inv, patch, lift_even, lift_odd, gain_in],
        scratch=[
            ((groups, rows, GROUP * width), BF16),
            ((depth, GROUP * width), F32),
            ((16, chans), F32),
            ((4, 16, quarter), F32),
        ],
        flops=1 << 32,
    )
    small3, small2 = swap(smalls[2], "dev", 3), swap(smalls[1], "dev", 2)
    own, first = call(
        part_kernel, [((quarter, wide), F32), (small.shape, F32)], [own, gots[0], gots[1], smalls[0]]
    )
    small1 = swap(first, "dev", 1)
    size = quarter // 2
    keep, send = call(
        functools.partial(gather_kernel, dev_bits - 1),
        [(packed(size, wide), F32), (packed(size, wide), BF16)],
        [own, gots[2], small, small1, small2, small3],
    )
    for bit in range(dev_bits - 1, 2, -1):
        size //= 2
        keep, send = call(
            functools.partial(halve_kernel, bit - 1),
            [(packed(size, wide), F32), (packed(size, wide), BF16)],
            [keep, swap(send, "dev", 1 << bit)],
        )
    send = call(add_kernel, [(packed(size, wide), BF16)], [keep, swap(send, "dev", 4)])[0]
    for bit in range(1, grp_bits):
        kind = F32 if bit == grp_bits - 1 else BF16
        send = call(add_kernel, [(packed(size, wide), kind)], [send, swap(send, "grp", 1 << bit)])[0]
    grad_second, grad_first, grad_gain, grad_bias = call(
        functools.partial(join_kernel, taps),
        [
            ((taps_second, size, chans), F32, "out"),
            ((taps, size), F32, "out"),
            ((1, size), F32, "out"),
            ((1, size), F32, "out"),
        ],
        [send, swap(send, "grp", 1)],
    )
    return (
        features.transpose(1, 0, 2),
        grad_second.transpose(0, 2, 1),
        grad_first,
        grad_gain.reshape(size),
        grad_bias.reshape(size),
    )


def solution(mesh):
    placed = (
        P(("grp", "dev"), None),
        P("grp"),
        P("grp", None),
        P(),
        P(),
        P(),
        P(),
        P(("grp", "dev"), None, None),
    )
    return jax.shard_map(
        shards,
        mesh=mesh,
        in_specs=placed,
        out_specs=(
            P(("grp", "dev"), None, None),
            P(None, None, "dev"),
            P(None, "dev"),
            P("dev"),
            P("dev"),
        ),
        check_vma=False,
    )
```

```python
import functools

import jax
import jax.numpy as jnp
from jax import lax
from jax.experimental import pallas as pl
from jax.experimental.pallas import tpu as pltpu
from jax.sharding import PartitionSpec as P

F32 = jnp.float32
BF16 = jnp.bfloat16
GROUP = 8
LANES = 256
MIN_SAMPLES = 288
MIB = 1 << 20


def gelu_and_slope(value):
    bell = jnp.exp2(value * value * (-0.5 * 1.4426950408889634))
    phi = 0.5 + 0.5 * lax.erf(value * 0.7071067811865476)
    return value * phi, phi + value * bell * 0.3989422804014327


def cols_both(a, b):
    return lax.dot_general(a, b, (((1,), (1,)), ((), ())), preferred_element_type=F32)


def dot(a, b):
    return jnp.dot(a, b, preferred_element_type=F32)


def iota(shape, dim):
    return lax.broadcasted_iota(jnp.int32, shape, dim)


def onehot(mask):
    return mask.astype(F32).astype(BF16)


def copies(sources, targets, sems):
    started = [pltpu.make_async_copy(source, target, sems.at[i]) for i, (source, target) in enumerate(zip(sources, targets))]
    for copy in started:
        copy.start()
    return started


def setup_kernel(
    members,
    order_hbm,
    len_hbm,
    w_hbm,
    wave_hbm,
    valid_ref,
    band_ref,
    near_ref,
    far_ref,
    own_ref,
    order_ref,
    len_ref,
    w_ref,
    sems,
):
    for copy in copies((order_hbm, len_hbm, w_hbm, wave_hbm), (order_ref, len_ref, w_ref, own_ref), sems):
        copy.wait()
    rows = order_ref.shape[1]
    share = rows // members
    taps, chans = w_ref.shape
    stride = taps // 2
    owner = onehot(iota((rows, members), 0) // share == iota((rows, members), 1))
    order_of = dot(owner, order_ref[...].astype(F32).astype(BF16))
    slot = iota((rows, rows), 1) - lax.rem(iota((rows, rows), 0), share) * members
    owner_first = iota((rows, 1), 0) // share * rows
    column = iota((rows, members * rows), 1)
    member = lax.axis_index("dev")
    low_half = member < members // 2
    for target, out_ref in ((member, near_ref), (jnp.bitwise_xor(member, members // 2), far_ref)):
        local = jnp.sum(jnp.where(slot == target, order_of, 0.0), axis=1, keepdims=True).astype(jnp.int32)
        picked = column == owner_first + local
        picks = picked.astype(F32)
        out_ref[...] = jnp.where(low_half, picks[: rows // 2], picks[rows // 2 :]).astype(BF16)
        if out_ref is near_ref:
            lens = jnp.sum(jnp.where(picked, len_ref[...], 0), axis=1, keepdims=True)
    valid = (lens - taps) // stride + 1
    valid_ref[...] = jnp.broadcast_to(valid, valid_ref.shape)
    depth = band_ref.shape[0]
    for f in range(GROUP):
        spread = onehot(iota((depth, taps), 0) == iota((depth, taps), 1) + stride * f)
        band_ref[:, f * chans : (f + 1) * chans] = dot(spread, w_ref[...]).astype(BF16)


def pick_kernel(offsets, near_ref, far_ref, *refs):
    waves, (mine_ref, send_ref, all_ref) = refs[:-3], refs[-3:]
    rows = waves[0].shape[0]
    all_ref[...] = jnp.zeros(all_ref.shape, BF16)
    for offset, wave_ref in zip(offsets, waves):
        first = pl.multiple_of(jnp.bitwise_xor(lax.axis_index("dev"), offset) * rows, rows)
        all_ref[pl.ds(first, rows), :] = wave_ref[...]
    mine_ref[...] = dot(near_ref[...], all_ref[...]).astype(BF16)
    send_ref[...] = dot(far_ref[...], all_ref[...]).astype(BF16)


def forward_kernel(
    frames0,
    frames1,
    taps,
    places,
    near_ref,
    far_ref,
    valid_ref,
    band_ref,
    gain_hbm,
    bias_hbm,
    w_hbm,
    cot_hbm,
    feat_ref,
    even_ref,
    odd_ref,
    pre0,
    even_slope,
    odd_slope,
    mean_ref,
    inv_ref,
    patch_ref,
    grad_ref,
    grad_t_ref,
    gain_ref,
    w_ref,
    fresh0,
    fresh1,
    scale_ref,
    shift_ref,
    bias_ref,
    cot_ref,
    sems,
):
    waiting = copies((gain_hbm, bias_hbm, w_hbm, cot_hbm), (gain_ref, bias_ref, w_ref, cot_ref), sems)
    rows, samp = valid_ref.shape[0], near_ref.shape[1]
    chans = gain_ref.shape[1]
    stride = taps // 2
    depth = band_ref.shape[0]
    groups = pre0.shape[0]
    width = LANES
    parts = [slice(first, first + width) for first in range(0, chans, width)]
    min_valid = (MIN_SAMPLES - taps) // stride + 1
    low_half = lax.axis_index("dev") < lax.axis_size("dev") // 2
    near, far = near_ref[...].astype(F32), far_ref[...].astype(F32)
    wave = jnp.concatenate([jnp.where(low_half, near, far), jnp.where(low_half, far, near)], axis=0).astype(BF16)
    for g in range(groups):
        pick = onehot(iota((samp, depth), 0) == iota((samp, depth), 1) + GROUP * stride * g)
        patch_ref[g] = dot(wave, pick).astype(BF16)
    patches = patch_ref[...].reshape(groups * rows, depth)

    valid = jnp.broadcast_to(valid_ref[:, :1], (rows, width))
    count = valid.astype(F32)

    def frame(g, f, lanes):
        return pre0[g, :, f * chans + lanes.start : f * chans + lanes.stop]

    def masked_to(value, t, masked):
        return jnp.where(valid > t, value, 0.0) if masked else value

    for lanes in parts:
        for f in range(GROUP):
            cols = slice(f * chans + lanes.start, f * chans + lanes.stop)
            value = dot(patches, band_ref[:, cols]).reshape(groups, rows, width)
            pre0[:, :, cols] = value
            if f == 0:
                origin = value[0]
                shift = jnp.zeros((rows, width), F32)
                square = jnp.zeros((rows, width), F32)
            for g in range(groups):
                t = g * GROUP + f
                if 0 < t < frames0:
                    away = masked_to(value[g] - origin, t, t >= min_valid)
                    shift += away
                    square += away * away
        shift = shift / count
        mean = origin + shift
        inv = lax.rsqrt(jnp.maximum(square / count - shift * shift, 0.0) + 1e-05)
        mean_ref[:, lanes] = mean
        inv_ref[:, lanes] = inv
        if lanes.start == 0:
            waiting[0].wait()
            waiting[1].wait()
        scale = inv * gain_ref[:, lanes]
        scale_ref[:, lanes] = scale
        shift_ref[:, lanes] = bias_ref[:, lanes] - mean * scale

    half = GROUP
    evens, odds = (frames0 + 1) // 2, frames0 // 2
    min_valid1 = (min_valid - 3) // 2 + 1
    valid1 = lax.shift_right_arithmetic(valid - 3, 1) + 1
    slab = chans // len(places)
    steps = -(-frames1 // half)

    def used_in(step):
        return min(half, frames1 - step * half)

    def activate0(step):
        for t in range(step * 2 * half, min((step + 1) * 2 * half, frames0)):
            for lanes in parts:
                gelu, slope = gelu_and_slope(
                    frame(t // GROUP, t % GROUP, lanes) * scale_ref[:, lanes] + shift_ref[:, lanes]
                )
                act_ref, slope_ref = (odd_ref, odd_slope) if t % 2 else (even_ref, even_slope)
                slope_ref[t // 2, :, lanes] = masked_to(slope, t, t >= min_valid)
                act_ref[t // 2, :, lanes] = masked_to(gelu, t, t >= min_valid).astype(BF16)

    def convolve(step, out_ref):
        first, used = step * half, used_in(step)
        for lanes in parts:
            total = dot(even_ref[first : first + used].reshape(used * rows, chans), w_ref[0, :, lanes])
            total += dot(odd_ref[first : first + used].reshape(used * rows, chans), w_ref[1, :, lanes])
            total += dot(even_ref[first + 1 : first + used + 1].reshape(used * rows, chans), w_ref[2, :, lanes])
            out_ref[:used, :, lanes] = total.reshape(used, rows, width)

    def activate1(step, in_ref):
        for j in range(used_in(step)):
            u = step * half + j
            for lanes in parts:
                gelu, slope = gelu_and_slope(in_ref[j, :, lanes])
                grad = cot_ref[u, :, lanes].astype(F32) * slope
                if u >= min_valid1:
                    gelu, grad = jnp.where(valid1 > u, gelu, 0.0), jnp.where(valid1 > u, grad, 0.0)
                feat_ref[u, :, lanes] = gelu.astype(BF16)
                grad_ref[u + 1, :, lanes] = grad.astype(BF16)

    def turn(step):
        first, size = step * half, used_in(step) * rows
        turned = grad_ref[first + 1 : first + 1 + used_in(step)].reshape(size, chans).T
        for place, source in enumerate(places):
            grad_t_ref[place * slab : (place + 1) * slab, first * rows : first * rows + size] = turned[
                source * slab : (source + 1) * slab
            ]

    for ref, used in ((even_ref, evens), (odd_ref, odds)):
        ref[used:] = jnp.zeros((ref.shape[0] - used,) + ref.shape[1:], BF16)
    grad_ref[0] = jnp.zeros(grad_ref.shape[1:], BF16)
    grad_ref[frames1 + 1] = jnp.zeros(grad_ref.shape[1:], BF16)
    full = frames1 * rows // 128 * 128
    grad_t_ref[:, full:] = jnp.zeros((chans, grad_t_ref.shape[1] - full), BF16)
    fresh = (fresh0, fresh1)
    for step in range(steps + 3):
        if step == 2:
            waiting[2].wait()
            waiting[3].wait()
        if 0 <= step - 2 < steps:
            convolve(step - 2, fresh[step % 2])
        if 0 <= step - 3 < steps:
            activate1(step - 3, fresh[(step - 1) % 2])
        if step < -(-frames0 // (2 * half)):
            activate0(step)
        if 0 <= step - 3 < steps:
            turn(step - 3)


def outer_kernel(skips, *refs):
    acts, (grad_t_ref, keep_ref, send_ref) = refs[:-3], refs[-3:]
    rows, chans = acts[0].shape[1:]
    frames = grad_t_ref.shape[1] // rows
    half = chans // 2
    core = lax.rem(lax.axis_index("grp"), 2)
    for tap, (act_ref, skip) in enumerate(zip(acts, skips)):
        for side, out_ref in ((1 - core, send_ref), (core, keep_ref)):
            lanes = pl.ds(pl.multiple_of(side * half, half), half)
            value = dot(grad_t_ref[...], act_ref[skip : skip + frames, :, lanes].reshape(frames * rows, half))
            out_ref[:, tap * half : (tap + 1) * half] = value.astype(out_ref.dtype)


def input_kernel(grad_ref, w_ref, even_slope, odd_slope, feat_ref, even_ref, odd_ref, feat_out, sem):
    leaving = pltpu.make_async_copy(feat_ref, feat_out, sem)
    leaving.start()
    evens, rows, chans = even_ref.shape
    odds = odd_ref.shape[0]
    first = grad_ref[1 : evens + 1].reshape(evens * rows, chans)
    third = grad_ref[0:evens].reshape(evens * rows, chans)
    total = cols_both(first, w_ref[0]) + cols_both(third, w_ref[2])
    even_ref[...] = total.reshape(even_ref.shape) * even_slope[:evens]
    second = grad_ref[1 : odds + 1].reshape(odds * rows, chans)
    odd_ref[...] = cols_both(second, w_ref[1]).reshape(odd_ref.shape) * odd_slope[:odds]
    leaving.wait()


def backward_kernel(
    frames0,
    taps,
    valid_ref,
    pre0,
    mean_ref,
    inv_ref,
    patch_ref,
    even_ref,
    odd_ref,
    gain_ref,
    mine_ref,
    send1,
    send2,
    send3,
    dpre0,
    spread,
    turned_ref,
    out_ref,
    quarters,
):
    groups, rows, depth = patch_ref.shape
    chans = gain_ref.shape[1]
    stride = taps // 2
    width = dpre0.shape[2] // GROUP
    full_groups = frames0 // GROUP
    free_groups = min(((MIN_SAMPLES - taps) // stride + 1) // GROUP, full_groups)
    rest = frames0 - full_groups * GROUP
    turned = patch_ref[...].reshape(groups * rows, depth).astype(F32).T
    turned_ref[...] = turned[: turned_ref.shape[0]].astype(BF16)
    for block in range(chans // width):
        lanes = slice(block * width, (block + 1) * width)

        def frame(g, f):
            return pre0[g, :, f * chans + block * width : f * chans + (block + 1) * width]

        def lift(g, f):
            return (odd_ref if f % 2 else even_ref)[g * (GROUP // 2) + f // 2, :, lanes]

        def sums(g, f, carry):
            bias_sum, gain_sum = carry
            return bias_sum + lift(g, f), gain_sum + lift(g, f) * frame(g, f)

        def add(g, carry):
            for f in range(GROUP):
                carry = sums(g, f, carry)
            return carry

        zero = jnp.zeros((rows, width), F32)
        carry = lax.fori_loop(0, full_groups, add, (zero, zero))
        for f in range(rest):
            carry = sums(full_groups, f, carry)
        bias_sum, gain_sum = carry
        mean, inv = mean_ref[:, lanes], inv_ref[:, lanes]
        gain_sum = (gain_sum - mean * bias_sum) * inv
        out_ref[taps : taps + 1, lanes] = jnp.sum(gain_sum, axis=0, keepdims=True)
        out_ref[taps + 1 : taps + 2, lanes] = jnp.sum(bias_sum, axis=0, keepdims=True)
        valid = jnp.broadcast_to(valid_ref[:, :1], (rows, width))
        count = valid.astype(F32)
        scale = inv * gain_ref[:, lanes]
        slant = scale * inv * gain_sum / count
        level = scale * bias_sum / count - mean * slant

        def finish(g, f, masked):
            value = scale * lift(g, f) - frame(g, f) * slant - level
            if masked:
                value = jnp.where(valid > g * GROUP + f, value, 0.0)
            dpre0[g, :, f * width : (f + 1) * width] = value.astype(BF16)

        def whole(masked, g, carry):
            for f in range(GROUP):
                finish(g, f, masked)
            return carry

        lax.fori_loop(0, free_groups, functools.partial(whole, False), 0)
        lax.fori_loop(free_groups, full_groups, functools.partial(whole, True), 0)
        for f in range(rest):
            finish(full_groups, f, True)
        if full_groups < groups:
            dpre0[full_groups, :, rest * width :] = jnp.zeros((rows, (GROUP - rest) * width), BF16)
        spread[...] = dot(turned_ref[...], dpre0[...].reshape(groups * rows, GROUP * width))
        total = jnp.zeros((taps, width), F32)
        for f in range(GROUP):
            total += spread[stride * f : stride * f + taps, f * width : (f + 1) * width]
        out_ref[:taps, lanes] = total
    size = chans // lax.axis_size("dev")
    for place in range(4):
        columns = [slice(first, first + size) for first in range(place * size, chans, 4 * size)]
        quarters[place] = jnp.concatenate([out_ref[:, part] for part in columns], axis=1)
    place = lax.rem(lax.axis_index("dev"), 4)
    for offset, ref in enumerate((mine_ref, send1, send2, send3)):
        ref[...] = quarters[jnp.bitwise_xor(place, offset)]


def plane_kernel(*refs):
    keeps, others, outs = refs[:2], refs[2:4], refs[5:]
    size = outs[0].shape[0]
    edge = keeps[0].shape[1]
    place = lax.rem(lax.axis_index("dev"), 4)
    for offset, out_ref in enumerate(outs):
        lines = pl.ds(pl.multiple_of(jnp.bitwise_xor(place, offset) * size, size), size)
        for lanes, keep_ref, got_ref in zip((slice(0, edge), slice(edge, None)), keeps, others):
            out_ref[:, lanes] = (keep_ref[lines, :] + got_ref[lines, :].astype(F32)).astype(out_ref.dtype)


def part_kernel(own_ref, got1, got2, small_ref, sum_ref, total_ref):
    sum_ref[...] = own_ref[...] + (got1[...].astype(F32) + got2[...].astype(F32))
    total_ref[...] = small_ref[...]


def packed(size, wide):
    return size + 16, wide - 128


def write_packed(ref, value, small):
    size, lanes = ref.shape[0] - 16, ref.shape[1]
    ref[:size] = value[:, :lanes].astype(ref.dtype)
    used = size // 16
    for block in range(used):
        piece = value[block * 16 : (block + 1) * 16, lanes:]
        ref[size:, block * 128 : (block + 1) * 128] = piece.astype(ref.dtype)
    for first in range(used * 128, lanes - 128, 128):
        ref[size:, first : first + 128] = jnp.zeros((16, 128), ref.dtype)
    ref[size:, lanes - 128 :] = small.astype(ref.dtype)


def read_packed(ref, first, count):
    size = ref.shape[0] - 16
    whole = ref[pl.ds(pl.multiple_of(first, 16), count), :].astype(F32)
    pieces = [
        ref[size:, pl.ds(pl.multiple_of(first * 8 + block * 128, 128), 128)].astype(F32) for block in range(count // 16)
    ]
    return jnp.concatenate([whole, jnp.concatenate(pieces, axis=0)], axis=1)


def gather_kernel(bit, own_ref, got3, small0, small1, small2, small3, keep_ref, send_ref):
    half = own_ref.shape[0] // 2
    side = lax.rem(lax.shift_right_logical(lax.axis_index("dev"), bit), 2)
    total = (small0[...] + small1[...]) + (small2[...] + small3[...])
    for index, ref in ((1 - side, send_ref), (side, keep_ref)):
        lines = pl.ds(pl.multiple_of(index * half, half), half)
        write_packed(ref, own_ref[lines, :] + got3[lines, :].astype(F32), total)


def halve_kernel(bit, keep_ref, got_ref, next_ref, send_ref):
    half = (keep_ref.shape[0] - 16) // 2
    side = lax.rem(lax.shift_right_logical(lax.axis_index("dev"), bit), 2)
    small = keep_ref[2 * half :, -128:] + got_ref[2 * half :, -128:].astype(F32)
    for index, ref in ((1 - side, send_ref), (side, next_ref)):
        first = index * half
        write_packed(ref, read_packed(keep_ref, first, half) + read_packed(got_ref, first, half), small)


def add_kernel(mine_ref, got_ref, out_ref):
    out_ref[...] = (mine_ref[...].astype(F32) + got_ref[...].astype(F32)).astype(out_ref.dtype)


def join_kernel(taps, own_ref, other_ref, out_ref, first_ref, gain_ref, bias_ref):
    second, size, chans = out_ref.shape
    half = chans // 2
    core = lax.rem(lax.axis_index("grp"), 2)
    for ref, side in ((own_ref, core), (other_ref, 1 - core)):
        value = read_packed(ref, 0, size)
        for tap in range(second):
            lanes = pl.ds(pl.multiple_of(side * half, half), half)
            out_ref[tap, :, lanes] = value[:, tap * half : (tap + 1) * half]
    total = own_ref[size:, -128:] + other_ref[size:, -128:]
    value = total[:, :size]
    for place in range(1, 128 // size):
        mine = lax.axis_index("dev") // 4 == place
        value = jnp.where(mine, total[:, place * size : (place + 1) * size], value)
    first_ref[...] = value[:taps]
    gain_ref[...] = value[taps : taps + 1]
    bias_ref[...] = value[taps + 1 : taps + 2]


def call(kernel, outs, args, scratch=(), limit=24, flops=0, touched=0, outside=()):
    vmem = pl.BlockSpec(memory_space=pltpu.VMEM)
    args = [pltpu.with_memory_space_constraint(arg, pltpu.HBM) if i in outside else arg for i, arg in enumerate(args)]
    return pl.pallas_call(
        kernel,
        out_shape=[
            jax.ShapeDtypeStruct(out[0], out[1]) if len(out) > 2 else pltpu.VMEM(out[0], out[1]) for out in outs
        ],
        in_specs=[pl.BlockSpec(memory_space=pltpu.HBM) if i in outside else vmem for i in range(len(args))],
        out_specs=[pl.BlockSpec(memory_space=pl.ANY) if out[-1] == "hbm" else vmem for out in outs],
        scratch_shapes=[pltpu.VMEM(*entry) if isinstance(entry, tuple) else entry for entry in scratch],
        compiler_params=pltpu.CompilerParams(vmem_limit_bytes=limit * MIB),
        cost_estimate=pl.CostEstimate(flops=flops, bytes_accessed=touched, transcendentals=0),
    )(*args)


def swap(value, axis, offset):
    size = lax.axis_size(axis)
    return lax.ppermute(value, axis, [(i, i ^ offset) for i in range(size)])


def shards(wave, lengths, order, w_first, norm_gain, norm_bias, w_second, cot):
    members = lax.axis_size("dev")
    groups_of = lax.axis_size("grp")
    rows, samp = wave.shape
    taps, chans = w_first.shape
    taps_second = w_second.shape[0]
    stride = taps // 2
    frames0 = (samp - taps) // stride + 1
    frames1 = (frames0 - taps_second) // 2 + 1
    groups = -(-frames0 // GROUP)
    depth = 128
    width = LANES
    dev_bits = members.bit_length() - 1
    grp_bits = groups_of.bit_length() - 1

    offsets = [0, 1, 2, 3]
    waves = [wave] + [swap(wave, "dev", offset) for offset in offsets[1:]]
    for bit in range(2, dev_bits - 1):
        offsets += [offset | (1 << bit) for offset in offsets]
        waves += [swap(held, "dev", 1 << bit) for held in waves]
    lens = lengths.reshape(1, members * rows)
    every = members * rows
    valid, band, near_sel, far_sel, own_wave = call(
        functools.partial(setup_kernel, members),
        [
            ((rows, 128), jnp.int32),
            ((depth, GROUP * chans), BF16),
            ((rows // 2, every), BF16),
            ((rows // 2, every), BF16),
            ((rows, samp), BF16),
        ],
        [order, lens, w_first, wave],
        scratch=[
            (order.shape, order.dtype),
            (lens.shape, lens.dtype),
            (w_first.shape, BF16),
            pltpu.SemaphoreType.DMA((4,)),
        ],
        outside=(0, 1, 2, 3),
    )
    near, send = call(
        functools.partial(pick_kernel, offsets),
        [((rows // 2, samp), BF16), ((rows // 2, samp), BF16)],
        [near_sel, far_sel, own_wave, *waves[1:]],
        scratch=[((every, samp), BF16)],
    )
    far = swap(send, "dev", members // 2)
    gain = norm_gain.reshape(1, chans)
    bias = norm_bias.reshape(1, chans)
    cot_t = cot.transpose(1, 0, 2)
    pad_frames = -(-frames1 // 4) * 4
    places = [0] * members
    for dev in range(members):
        places[dev % 4 * (members // 4) + dev // 4] = dev
    feat, even, odd, pre0, even_slope, odd_slope, mean, inv, patch, grad, grad_t, gain_in, w_in = call(
        functools.partial(forward_kernel, frames0, frames1, taps, places),
        [
            ((frames1, rows, chans), BF16),
            ((pad_frames + 1, rows, chans), BF16),
            ((pad_frames, rows, chans), BF16),
            ((groups, rows, GROUP * chans), F32),
            ((pad_frames, rows, chans), F32),
            ((pad_frames, rows, chans), F32),
            ((rows, chans), F32),
            ((rows, chans), F32),
            ((groups, rows, depth), BF16),
            ((frames1 + 2, rows, chans), BF16),
            ((chans, pad_frames * rows), BF16),
            ((1, chans), F32),
            (w_second.shape, BF16),
        ],
        [near, far, valid, band, gain, bias, w_second, cot_t],
        scratch=[
            ((GROUP, rows, chans), F32),
            ((GROUP, rows, chans), F32),
            ((rows, chans), F32),
            ((rows, chans), F32),
            (bias.shape, F32),
            (cot_t.shape, BF16),
            pltpu.SemaphoreType.DMA((4,)),
        ],
        outside=(4, 5, 6, 7),
    )
    half = chans // 2
    wide = taps_second * half
    keeps, others = [], []
    for acts, skips in (((even, odd), (0, 0)), ((even,), (1,))):
        shape = (chans, len(acts) * half)
        keep, send = call(
            functools.partial(outer_kernel, skips), [(shape, F32), (shape, BF16)], [*acts, grad_t], flops=len(acts) << 29
        )
        keeps.append(keep)
        others.append(swap(send, "grp", 1))
    evens, odds = (frames0 + 1) // 2, frames0 // 2
    lift_even, lift_odd, features = call(
        input_kernel,
        [((evens, rows, chans), F32), ((odds, rows, chans), F32), ((frames1, rows, chans), BF16, "hbm")],
        [grad, w_in, even_slope, odd_slope, feat],
        scratch=[pltpu.SemaphoreType.DMA],
        flops=1 << 30,
    )
    quarter = chans // 4
    own, *sends = call(
        plane_kernel,
        [((quarter, wide), F32)] + [((quarter, wide), BF16)] * 3,
        [*keeps, *others, lift_odd],
    )
    gots = [swap(part, "dev", offset) for offset, part in enumerate(sends, 1)]
    used = -(-(stride * (GROUP - 1) + taps) // 16) * 16
    small, *smalls = call(
        functools.partial(backward_kernel, frames0, taps),
        [((16, quarter), F32)] * 4,
        [valid, pre0, mean, inv, patch, lift_even, lift_odd, gain_in],
        scratch=[
            ((groups, rows, GROUP * width), BF16),
            ((used, GROUP * width), F32),
            ((used, groups * rows), BF16),
            ((16, chans), F32),
            ((4, 16, quarter), F32),
        ],
        flops=1 << 32,
    )
    small3, small2 = swap(smalls[2], "dev", 3), swap(smalls[1], "dev", 2)
    own, first = call(
        part_kernel, [((quarter, wide), F32), (small.shape, F32)], [own, gots[0], gots[1], smalls[0]]
    )
    small1 = swap(first, "dev", 1)
    size = quarter // 2
    keep, send = call(
        functools.partial(gather_kernel, dev_bits - 1),
        [(packed(size, wide), F32), (packed(size, wide), BF16)],
        [own, gots[2], small, small1, small2, small3],
    )
    for bit in range(dev_bits - 1, 2, -1):
        size //= 2
        keep, send = call(
            functools.partial(halve_kernel, bit - 1),
            [(packed(size, wide), F32), (packed(size, wide), BF16)],
            [keep, swap(send, "dev", 1 << bit)],
        )
    send = call(add_kernel, [(packed(size, wide), BF16)], [keep, swap(send, "dev", 4)])[0]
    for bit in range(1, grp_bits):
        kind = F32 if bit == grp_bits - 1 else BF16
        send = call(add_kernel, [(packed(size, wide), kind)], [send, swap(send, "grp", 1 << bit)])[0]
    grad_second, grad_first, grad_gain, grad_bias = call(
        functools.partial(join_kernel, taps),
        [
            ((taps_second, size, chans), F32, "out"),
            ((taps, size), F32, "out"),
            ((1, size), F32, "out"),
            ((1, size), F32, "out"),
        ],
        [send, swap(send, "grp", 1)],
    )
    return (
        features.transpose(1, 0, 2),
        grad_second.transpose(0, 2, 1),
        grad_first,
        grad_gain.reshape(size),
        grad_bias.reshape(size),
    )


def solution(mesh):
    placed = (
        P(("grp", "dev"), None),
        P("grp"),
        P("grp", None),
        P(),
        P(),
        P(),
        P(),
        P(("grp", "dev"), None, None),
    )
    return jax.shard_map(
        shards,
        mesh=mesh,
        in_specs=placed,
        out_specs=(
            P(("grp", "dev"), None, None),
            P(None, None, "dev"),
            P(None, "dev"),
            P("dev"),
            P("dev"),
        ),
        check_vma=False,
    )
```

```python
import functools

import jax
import jax.numpy as jnp
from jax import lax
from jax.experimental import pallas as pl
from jax.experimental.pallas import tpu as pltpu
from jax.sharding import PartitionSpec as P

F32 = jnp.float32
BF16 = jnp.bfloat16
GROUP = 8
LANES = 256
MIN_SAMPLES = 288
MIB = 1 << 20


def gelu_and_slope(value):
    bell = jnp.exp2(value * value * (-0.5 * 1.4426950408889634))
    phi = 0.5 + 0.5 * lax.erf(value * 0.7071067811865476)
    return value * phi, phi + value * bell * 0.3989422804014327


def cols_both(a, b):
    return lax.dot_general(a, b, (((1,), (1,)), ((), ())), preferred_element_type=F32)


def dot(a, b):
    return jnp.dot(a, b, preferred_element_type=F32)


def iota(shape, dim):
    return lax.broadcasted_iota(jnp.int32, shape, dim)


def onehot(mask):
    return mask.astype(F32).astype(BF16)


def copies(sources, targets, sems):
    started = [pltpu.make_async_copy(source, target, sems.at[i]) for i, (source, target) in enumerate(zip(sources, targets))]
    for copy in started:
        copy.start()
    return started


def setup_kernel(
    members,
    order_hbm,
    len_hbm,
    w_hbm,
    wave_hbm,
    valid_ref,
    band_ref,
    near_ref,
    far_ref,
    own_ref,
    order_ref,
    len_ref,
    w_ref,
    sems,
):
    for copy in copies((order_hbm, len_hbm, w_hbm, wave_hbm), (order_ref, len_ref, w_ref, own_ref), sems):
        copy.wait()
    rows = order_ref.shape[1]
    share = rows // members
    taps, chans = w_ref.shape
    stride = taps // 2
    owner = onehot(iota((rows, members), 0) // share == iota((rows, members), 1))
    order_of = dot(owner, order_ref[...].astype(F32).astype(BF16))
    slot = iota((rows, rows), 1) - lax.rem(iota((rows, rows), 0), share) * members
    owner_first = iota((rows, 1), 0) // share * rows
    column = iota((rows, members * rows), 1)
    member = lax.axis_index("dev")
    low_half = member < members // 2
    for target, out_ref in ((member, near_ref), (jnp.bitwise_xor(member, members // 2), far_ref)):
        local = jnp.sum(jnp.where(slot == target, order_of, 0.0), axis=1, keepdims=True).astype(jnp.int32)
        picked = column == owner_first + local
        picks = picked.astype(F32)
        out_ref[...] = jnp.where(low_half, picks[: rows // 2], picks[rows // 2 :]).astype(BF16)
        if out_ref is near_ref:
            lens = jnp.sum(jnp.where(picked, len_ref[...], 0), axis=1, keepdims=True)
    valid = (lens - taps) // stride + 1
    valid_ref[...] = jnp.broadcast_to(valid, valid_ref.shape)
    depth = band_ref.shape[0]
    for f in range(GROUP):
        spread = onehot(iota((depth, taps), 0) == iota((depth, taps), 1) + stride * f)
        band_ref[:, f * chans : (f + 1) * chans] = dot(spread, w_ref[...]).astype(BF16)


def pick_kernel(offsets, near_ref, far_ref, *refs):
    waves, (mine_ref, send_ref, all_ref) = refs[:-3], refs[-3:]
    rows = waves[0].shape[0]
    all_ref[...] = jnp.zeros(all_ref.shape, BF16)
    for offset, wave_ref in zip(offsets, waves):
        first = pl.multiple_of(jnp.bitwise_xor(lax.axis_index("dev"), offset) * rows, rows)
        all_ref[pl.ds(first, rows), :] = wave_ref[...]
    mine_ref[...] = dot(near_ref[...], all_ref[...]).astype(BF16)
    send_ref[...] = dot(far_ref[...], all_ref[...]).astype(BF16)


def forward_kernel(
    frames0,
    frames1,
    taps,
    places,
    near_ref,
    far_ref,
    valid_ref,
    band_ref,
    gain_hbm,
    bias_hbm,
    w_hbm,
    cot_hbm,
    feat_ref,
    even_ref,
    odd_ref,
    pre0,
    even_slope,
    odd_slope,
    mean_ref,
    inv_ref,
    patch_ref,
    grad_ref,
    grad_t_ref,
    gain_ref,
    w_ref,
    fresh0,
    fresh1,
    scale_ref,
    shift_ref,
    bias_ref,
    cot_ref,
    sems,
):
    waiting = copies((gain_hbm, bias_hbm, w_hbm, cot_hbm), (gain_ref, bias_ref, w_ref, cot_ref), sems)
    rows, samp = valid_ref.shape[0], near_ref.shape[1]
    chans = gain_ref.shape[1]
    stride = taps // 2
    depth = band_ref.shape[0]
    groups = pre0.shape[0]
    width = LANES
    parts = [slice(first, first + width) for first in range(0, chans, width)]
    min_valid = (MIN_SAMPLES - taps) // stride + 1
    low_half = lax.axis_index("dev") < lax.axis_size("dev") // 2
    near, far = near_ref[...].astype(F32), far_ref[...].astype(F32)
    wave = jnp.concatenate([jnp.where(low_half, near, far), jnp.where(low_half, far, near)], axis=0).astype(BF16)
    for g in range(groups):
        pick = onehot(iota((samp, depth), 0) == iota((samp, depth), 1) + GROUP * stride * g)
        patch_ref[g] = dot(wave, pick).astype(BF16)
    patches = patch_ref[...].reshape(groups * rows, depth)

    valid = jnp.broadcast_to(valid_ref[:, :1], (rows, width))
    count = valid.astype(F32)

    def frame(g, f, lanes):
        return pre0[g, :, f * chans + lanes.start : f * chans + lanes.stop]

    def masked_to(value, t, masked):
        return jnp.where(valid > t, value, 0.0) if masked else value

    for lanes in parts:
        for f in range(GROUP):
            cols = slice(f * chans + lanes.start, f * chans + lanes.stop)
            value = dot(patches, band_ref[:, cols]).reshape(groups, rows, width)
            pre0[:, :, cols] = value
            if f == 0:
                origin = value[0]
                shift = jnp.zeros((rows, width), F32)
                square = jnp.zeros((rows, width), F32)
            for g in range(groups):
                t = g * GROUP + f
                if 0 < t < frames0:
                    away = masked_to(value[g] - origin, t, t >= min_valid)
                    shift += away
                    square += away * away
        shift = shift / count
        mean = origin + shift
        inv = lax.rsqrt(jnp.maximum(square / count - shift * shift, 0.0) + 1e-05)
        mean_ref[:, lanes] = mean
        inv_ref[:, lanes] = inv
        if lanes.start == 0:
            waiting[0].wait()
            waiting[1].wait()
        scale = inv * gain_ref[:, lanes]
        scale_ref[:, lanes] = scale
        shift_ref[:, lanes] = bias_ref[:, lanes] - mean * scale

    half = GROUP
    evens, odds = (frames0 + 1) // 2, frames0 // 2
    min_valid1 = (min_valid - 3) // 2 + 1
    valid1 = lax.shift_right_arithmetic(valid - 3, 1) + 1
    slab = chans // len(places)
    steps = -(-frames1 // half)

    def used_in(step):
        return min(half, frames1 - step * half)

    def activate0(step):
        for t in range(step * 2 * half, min((step + 1) * 2 * half, frames0)):
            for lanes in parts:
                gelu, slope = gelu_and_slope(
                    frame(t // GROUP, t % GROUP, lanes) * scale_ref[:, lanes] + shift_ref[:, lanes]
                )
                act_ref, slope_ref = (odd_ref, odd_slope) if t % 2 else (even_ref, even_slope)
                slope_ref[t // 2, :, lanes] = masked_to(slope, t, t >= min_valid)
                act_ref[t // 2, :, lanes] = masked_to(gelu, t, t >= min_valid).astype(BF16)

    def convolve(step, out_ref):
        first, used = step * half, used_in(step)
        for lanes in parts:
            total = dot(even_ref[first : first + used].reshape(used * rows, chans), w_ref[0, :, lanes])
            total += dot(odd_ref[first : first + used].reshape(used * rows, chans), w_ref[1, :, lanes])
            total += dot(even_ref[first + 1 : first + used + 1].reshape(used * rows, chans), w_ref[2, :, lanes])
            out_ref[:used, :, lanes] = total.reshape(used, rows, width)

    def activate1(step, in_ref):
        for j in range(used_in(step)):
            u = step * half + j
            for lanes in parts:
                gelu, slope = gelu_and_slope(in_ref[j, :, lanes])
                grad = cot_ref[u, :, lanes].astype(F32) * slope
                if u >= min_valid1:
                    gelu, grad = jnp.where(valid1 > u, gelu, 0.0), jnp.where(valid1 > u, grad, 0.0)
                feat_ref[u, :, lanes] = gelu.astype(BF16)
                grad_ref[u + 1, :, lanes] = grad.astype(BF16)

    def turn(step):
        first, size = step * half, used_in(step) * rows
        turned = grad_ref[first + 1 : first + 1 + used_in(step)].reshape(size, chans).T
        for place, source in enumerate(places):
            grad_t_ref[place * slab : (place + 1) * slab, first * rows : first * rows + size] = turned[
                source * slab : (source + 1) * slab
            ]

    for ref, used in ((even_ref, evens), (odd_ref, odds)):
        ref[used:] = jnp.zeros((ref.shape[0] - used,) + ref.shape[1:], BF16)
    grad_ref[0] = jnp.zeros(grad_ref.shape[1:], BF16)
    grad_ref[frames1 + 1] = jnp.zeros(grad_ref.shape[1:], BF16)
    full = frames1 * rows // 128 * 128
    grad_t_ref[:, full:] = jnp.zeros((chans, grad_t_ref.shape[1] - full), BF16)
    fresh = (fresh0, fresh1)
    for step in range(steps + 3):
        if step == 2:
            waiting[2].wait()
            waiting[3].wait()
        if 0 <= step - 2 < steps:
            convolve(step - 2, fresh[step % 2])
        if 0 <= step - 3 < steps:
            activate1(step - 3, fresh[(step - 1) % 2])
        if step < -(-frames0 // (2 * half)):
            activate0(step)
        if 0 <= step - 3 < steps:
            turn(step - 3)


def outer_kernel(skips, *refs):
    acts, (grad_t_ref, keep_ref, send_ref) = refs[:-3], refs[-3:]
    rows, chans = acts[0].shape[1:]
    frames = grad_t_ref.shape[1] // rows
    half = chans // 2
    core = lax.rem(lax.axis_index("grp"), 2)
    for tap, (act_ref, skip) in enumerate(zip(acts, skips)):
        for side, out_ref in ((1 - core, send_ref), (core, keep_ref)):
            lanes = pl.ds(pl.multiple_of(side * half, half), half)
            value = dot(grad_t_ref[...], act_ref[skip : skip + frames, :, lanes].reshape(frames * rows, half))
            out_ref[:, tap * half : (tap + 1) * half] = value.astype(out_ref.dtype)


def odd_input_kernel(grad_ref, w_ref, slope_ref, lift_ref):
    odds, rows, chans = lift_ref.shape
    second = grad_ref[1 : odds + 1].reshape(odds * rows, chans)
    lift_ref[...] = cols_both(second, w_ref[1]).reshape(lift_ref.shape) * slope_ref[:odds]


def even_input_kernel(grad_ref, w_ref, slope_ref, after_ref, feat_ref, lift_ref, feat_out, sem):
    leaving = pltpu.make_async_copy(feat_ref, feat_out, sem)
    leaving.start()
    evens, rows, chans = lift_ref.shape
    first = grad_ref[1 : evens + 1].reshape(evens * rows, chans)
    third = grad_ref[0:evens].reshape(evens * rows, chans)
    total = cols_both(first, w_ref[0]) + cols_both(third, w_ref[2])
    lift_ref[...] = total.reshape(lift_ref.shape) * slope_ref[:evens]
    leaving.wait()


def backward_kernel(
    frames0,
    taps,
    valid_ref,
    pre0,
    mean_ref,
    inv_ref,
    patch_ref,
    even_ref,
    odd_ref,
    gain_ref,
    mine_ref,
    send1,
    send2,
    send3,
    dpre0,
    spread,
    turned_ref,
    out_ref,
    quarters,
):
    groups, rows, depth = patch_ref.shape
    chans = gain_ref.shape[1]
    stride = taps // 2
    width = dpre0.shape[3] // GROUP
    turned = patch_ref[...].reshape(groups * rows, depth).astype(F32).T
    turned_ref[...] = turned[: turned_ref.shape[0]].astype(BF16)
    valid = jnp.broadcast_to(valid_ref[:, :1], (rows, width))
    count = valid.astype(F32)
    min_valid = (MIN_SAMPLES - taps) // stride + 1
    parts = [slice(first, first + width) for first in range(0, chans, width)]

    def frame(t, lanes):
        start = t % GROUP * chans
        return pre0[t // GROUP, :, start + lanes.start : start + lanes.stop]

    def lift(t, lanes):
        return (odd_ref if t % 2 else even_ref)[t // 2, :, lanes]

    def sums(lanes):
        bias_sum = gain_sum = jnp.zeros((rows, width), F32)
        for t in range(frames0):
            bias_sum += lift(t, lanes)
            gain_sum += lift(t, lanes) * frame(t, lanes)
        mean, inv = mean_ref[:, lanes], inv_ref[:, lanes]
        gain_sum = (gain_sum - mean * bias_sum) * inv
        out_ref[taps : taps + 1, lanes] = jnp.sum(gain_sum, axis=0, keepdims=True)
        out_ref[taps + 1 : taps + 2, lanes] = jnp.sum(bias_sum, axis=0, keepdims=True)
        scale = inv * gain_ref[:, lanes]
        slant = scale * inv * gain_sum / count
        return scale, slant, scale * bias_sum / count - mean * slant

    def gradients(block, lanes, scale, slant, level):
        for t in range(frames0):
            value = scale * lift(t, lanes) - frame(t, lanes) * slant - level
            if t >= min_valid:
                value = jnp.where(valid > t, value, 0.0)
            f = t % GROUP
            dpre0[block, t // GROUP, :, f * width : (f + 1) * width] = value.astype(BF16)
        rest = frames0 - frames0 // GROUP * GROUP
        if rest:
            dpre0[block, groups - 1, :, rest * width :] = jnp.zeros((rows, (GROUP - rest) * width), BF16)

    def taps_of(block, lanes):
        spread[block] = dot(turned_ref[...], dpre0[block].reshape(groups * rows, GROUP * width))
        total = jnp.zeros((taps, width), F32)
        for f in range(GROUP):
            total += spread[block, stride * f : stride * f + taps, f * width : (f + 1) * width]
        out_ref[:taps, lanes] = total

    terms = sums(parts[0])
    for block, lanes in enumerate(parts):
        gradients(block, lanes, *terms)
        if block + 1 < len(parts):
            terms = sums(parts[block + 1])
        taps_of(block, lanes)
    size = chans // lax.axis_size("dev")
    for place in range(4):
        columns = [slice(first, first + size) for first in range(place * size, chans, 4 * size)]
        quarters[place] = jnp.concatenate([out_ref[:, part] for part in columns], axis=1)
    place = lax.rem(lax.axis_index("dev"), 4)
    for offset, ref in enumerate((mine_ref, send1, send2, send3)):
        ref[...] = quarters[jnp.bitwise_xor(place, offset)]


def plane_kernel(*refs):
    keeps, others, outs = refs[:2], refs[2:4], refs[5:]
    size = outs[0].shape[0]
    edge = keeps[0].shape[1]
    place = lax.rem(lax.axis_index("dev"), 4)
    for offset, out_ref in enumerate(outs):
        lines = pl.ds(pl.multiple_of(jnp.bitwise_xor(place, offset) * size, size), size)
        for lanes, keep_ref, got_ref in zip((slice(0, edge), slice(edge, None)), keeps, others):
            out_ref[:, lanes] = (keep_ref[lines, :] + got_ref[lines, :].astype(F32)).astype(out_ref.dtype)


def part_kernel(own_ref, got1, got2, small_ref, sum_ref, total_ref):
    sum_ref[...] = own_ref[...] + (got1[...].astype(F32) + got2[...].astype(F32))
    total_ref[...] = small_ref[...]


def packed(size, wide):
    return size + 16, wide - 128


def write_packed(ref, value, small):
    size, lanes = ref.shape[0] - 16, ref.shape[1]
    ref[:size] = value[:, :lanes].astype(ref.dtype)
    used = size // 16
    for block in range(used):
        piece = value[block * 16 : (block + 1) * 16, lanes:]
        ref[size:, block * 128 : (block + 1) * 128] = piece.astype(ref.dtype)
    for first in range(used * 128, lanes - 128, 128):
        ref[size:, first : first + 128] = jnp.zeros((16, 128), ref.dtype)
    ref[size:, lanes - 128 :] = small.astype(ref.dtype)


def read_packed(ref, first, count):
    size = ref.shape[0] - 16
    whole = ref[pl.ds(pl.multiple_of(first, 16), count), :].astype(F32)
    pieces = [
        ref[size:, pl.ds(pl.multiple_of(first * 8 + block * 128, 128), 128)].astype(F32) for block in range(count // 16)
    ]
    return jnp.concatenate([whole, jnp.concatenate(pieces, axis=0)], axis=1)


def gather_kernel(bit, own_ref, got3, small0, small1, small2, small3, keep_ref, send_ref):
    half = own_ref.shape[0] // 2
    side = lax.rem(lax.shift_right_logical(lax.axis_index("dev"), bit), 2)
    total = (small0[...] + small1[...]) + (small2[...] + small3[...])
    for index, ref in ((1 - side, send_ref), (side, keep_ref)):
        lines = pl.ds(pl.multiple_of(index * half, half), half)
        write_packed(ref, own_ref[lines, :] + got3[lines, :].astype(F32), total)


def halve_kernel(bit, keep_ref, got_ref, next_ref, send_ref):
    half = (keep_ref.shape[0] - 16) // 2
    side = lax.rem(lax.shift_right_logical(lax.axis_index("dev"), bit), 2)
    small = keep_ref[2 * half :, -128:] + got_ref[2 * half :, -128:].astype(F32)
    for index, ref in ((1 - side, send_ref), (side, next_ref)):
        first = index * half
        write_packed(ref, read_packed(keep_ref, first, half) + read_packed(got_ref, first, half), small)


def add_kernel(mine_ref, got_ref, out_ref):
    out_ref[...] = (mine_ref[...].astype(F32) + got_ref[...].astype(F32)).astype(out_ref.dtype)


def join_kernel(taps, own_ref, other_ref, out_ref, first_ref, gain_ref, bias_ref):
    second, size, chans = out_ref.shape
    half = chans // 2
    core = lax.rem(lax.axis_index("grp"), 2)
    for ref, side in ((own_ref, core), (other_ref, 1 - core)):
        value = read_packed(ref, 0, size)
        for tap in range(second):
            lanes = pl.ds(pl.multiple_of(side * half, half), half)
            out_ref[tap, :, lanes] = value[:, tap * half : (tap + 1) * half]
    total = own_ref[size:, -128:] + other_ref[size:, -128:]
    value = total[:, :size]
    for place in range(1, 128 // size):
        mine = lax.axis_index("dev") // 4 == place
        value = jnp.where(mine, total[:, place * size : (place + 1) * size], value)
    first_ref[...] = value[:taps]
    gain_ref[...] = value[taps : taps + 1]
    bias_ref[...] = value[taps + 1 : taps + 2]


def call(kernel, outs, args, scratch=(), limit=24, flops=0, touched=0, outside=()):
    vmem = pl.BlockSpec(memory_space=pltpu.VMEM)
    args = [pltpu.with_memory_space_constraint(arg, pltpu.HBM) if i in outside else arg for i, arg in enumerate(args)]
    return pl.pallas_call(
        kernel,
        out_shape=[
            jax.ShapeDtypeStruct(out[0], out[1]) if len(out) > 2 else pltpu.VMEM(out[0], out[1]) for out in outs
        ],
        in_specs=[pl.BlockSpec(memory_space=pltpu.HBM) if i in outside else vmem for i in range(len(args))],
        out_specs=[pl.BlockSpec(memory_space=pl.ANY) if out[-1] == "hbm" else vmem for out in outs],
        scratch_shapes=[pltpu.VMEM(*entry) if isinstance(entry, tuple) else entry for entry in scratch],
        compiler_params=pltpu.CompilerParams(vmem_limit_bytes=limit * MIB),
        cost_estimate=pl.CostEstimate(flops=flops, bytes_accessed=touched, transcendentals=0),
    )(*args)


def swap(value, axis, offset):
    size = lax.axis_size(axis)
    return lax.ppermute(value, axis, [(i, i ^ offset) for i in range(size)])


def shards(wave, lengths, order, w_first, norm_gain, norm_bias, w_second, cot):
    members = lax.axis_size("dev")
    groups_of = lax.axis_size("grp")
    rows, samp = wave.shape
    taps, chans = w_first.shape
    taps_second = w_second.shape[0]
    stride = taps // 2
    frames0 = (samp - taps) // stride + 1
    frames1 = (frames0 - taps_second) // 2 + 1
    groups = -(-frames0 // GROUP)
    depth = 128
    width = LANES
    dev_bits = members.bit_length() - 1
    grp_bits = groups_of.bit_length() - 1

    offsets = [0, 1, 2, 3]
    waves = [wave] + [swap(wave, "dev", offset) for offset in offsets[1:]]
    for bit in range(2, dev_bits - 1):
        offsets += [offset | (1 << bit) for offset in offsets]
        waves += [swap(held, "dev", 1 << bit) for held in waves]
    lens = lengths.reshape(1, members * rows)
    every = members * rows
    valid, band, near_sel, far_sel, own_wave = call(
        functools.partial(setup_kernel, members),
        [
            ((rows, 128), jnp.int32),
            ((depth, GROUP * chans), BF16),
            ((rows // 2, every), BF16),
            ((rows // 2, every), BF16),
            ((rows, samp), BF16),
        ],
        [order, lens, w_first, wave],
        scratch=[
            (order.shape, order.dtype),
            (lens.shape, lens.dtype),
            (w_first.shape, BF16),
            pltpu.SemaphoreType.DMA((4,)),
        ],
        outside=(0, 1, 2, 3),
    )
    near, send = call(
        functools.partial(pick_kernel, offsets),
        [((rows // 2, samp), BF16), ((rows // 2, samp), BF16)],
        [near_sel, far_sel, own_wave, *waves[1:]],
        scratch=[((every, samp), BF16)],
    )
    far = swap(send, "dev", members // 2)
    gain = norm_gain.reshape(1, chans)
    bias = norm_bias.reshape(1, chans)
    cot_t = cot.transpose(1, 0, 2)
    pad_frames = -(-frames1 // 4) * 4
    places = [0] * members
    for dev in range(members):
        places[dev % 4 * (members // 4) + dev // 4] = dev
    feat, even, odd, pre0, even_slope, odd_slope, mean, inv, patch, grad, grad_t, gain_in, w_in = call(
        functools.partial(forward_kernel, frames0, frames1, taps, places),
        [
            ((frames1, rows, chans), BF16),
            ((pad_frames + 1, rows, chans), BF16),
            ((pad_frames, rows, chans), BF16),
            ((groups, rows, GROUP * chans), F32),
            ((pad_frames, rows, chans), F32),
            ((pad_frames, rows, chans), F32),
            ((rows, chans), F32),
            ((rows, chans), F32),
            ((groups, rows, depth), BF16),
            ((frames1 + 2, rows, chans), BF16),
            ((chans, pad_frames * rows), BF16),
            ((1, chans), F32),
            (w_second.shape, BF16),
        ],
        [near, far, valid, band, gain, bias, w_second, cot_t],
        scratch=[
            ((GROUP, rows, chans), F32),
            ((GROUP, rows, chans), F32),
            ((rows, chans), F32),
            ((rows, chans), F32),
            (bias.shape, F32),
            (cot_t.shape, BF16),
            pltpu.SemaphoreType.DMA((4,)),
        ],
        outside=(4, 5, 6, 7),
    )
    half = chans // 2
    wide = taps_second * half
    keeps, others = [], []
    for acts, skips in (((even, odd), (0, 0)), ((even,), (1,))):
        shape = (chans, len(acts) * half)
        keep, send = call(
            functools.partial(outer_kernel, skips), [(shape, F32), (shape, BF16)], [*acts, grad_t], flops=len(acts) << 29
        )
        keeps.append(keep)
        others.append(swap(send, "grp", 1))
    evens, odds = (frames0 + 1) // 2, frames0 // 2
    lift_odd = call(odd_input_kernel, [((odds, rows, chans), F32)], [grad, w_in, odd_slope], flops=1 << 29)[0]
    quarter = chans // 4
    own, *sends = call(
        plane_kernel,
        [((quarter, wide), F32)] + [((quarter, wide), BF16)] * 3,
        [*keeps, *others, lift_odd],
    )
    gots = [swap(part, "dev", offset) for offset, part in enumerate(sends, 1)]
    lift_even, features = call(
        even_input_kernel,
        [((evens, rows, chans), F32), ((frames1, rows, chans), BF16, "hbm")],
        [grad, w_in, even_slope, own, feat],
        scratch=[pltpu.SemaphoreType.DMA],
        flops=1 << 30,
    )
    used = -(-(stride * (GROUP - 1) + taps) // 16) * 16
    small, *smalls = call(
        functools.partial(backward_kernel, frames0, taps),
        [((16, quarter), F32)] * 4,
        [valid, pre0, mean, inv, patch, lift_even, lift_odd, gain_in],
        scratch=[
            ((chans // width, groups, rows, GROUP * width), BF16),
            ((chans // width, used, GROUP * width), F32),
            ((used, groups * rows), BF16),
            ((16, chans), F32),
            ((4, 16, quarter), F32),
        ],
        flops=1 << 32,
    )
    small3, small2 = swap(smalls[2], "dev", 3), swap(smalls[1], "dev", 2)
    own, first = call(
        part_kernel, [((quarter, wide), F32), (small.shape, F32)], [own, gots[0], gots[1], smalls[0]]
    )
    small1 = swap(first, "dev", 1)
    size = quarter // 2
    keep, send = call(
        functools.partial(gather_kernel, dev_bits - 1),
        [(packed(size, wide), F32), (packed(size, wide), BF16)],
        [own, gots[2], small, small1, small2, small3],
    )
    for bit in range(dev_bits - 1, 2, -1):
        size //= 2
        keep, send = call(
            functools.partial(halve_kernel, bit - 1),
            [(packed(size, wide), F32), (packed(size, wide), BF16)],
            [keep, swap(send, "dev", 1 << bit)],
        )
    send = call(add_kernel, [(packed(size, wide), BF16)], [keep, swap(send, "dev", 4)])[0]
    for bit in range(1, grp_bits):
        kind = F32 if bit == grp_bits - 1 else BF16
        send = call(add_kernel, [(packed(size, wide), kind)], [send, swap(send, "grp", 1 << bit)])[0]
    grad_second, grad_first, grad_gain, grad_bias = call(
        functools.partial(join_kernel, taps),
        [
            ((taps_second, size, chans), F32, "out"),
            ((taps, size), F32, "out"),
            ((1, size), F32, "out"),
            ((1, size), F32, "out"),
        ],
        [send, swap(send, "grp", 1)],
    )
    return (
        features.transpose(1, 0, 2),
        grad_second.transpose(0, 2, 1),
        grad_first,
        grad_gain.reshape(size),
        grad_bias.reshape(size),
    )


def solution(mesh):
    placed = (
        P(("grp", "dev"), None),
        P("grp"),
        P("grp", None),
        P(),
        P(),
        P(),
        P(),
        P(("grp", "dev"), None, None),
    )
    return jax.shard_map(
        shards,
        mesh=mesh,
        in_specs=placed,
        out_specs=(
            P(("grp", "dev"), None, None),
            P(None, None, "dev"),
            P(None, "dev"),
            P("dev"),
            P("dev"),
        ),
        check_vma=False,
    )
```

```python
import functools

import jax
import jax.numpy as jnp
from jax import lax
from jax.experimental import pallas as pl
from jax.experimental.pallas import tpu as pltpu
from jax.sharding import PartitionSpec as P

F32 = jnp.float32
BF16 = jnp.bfloat16
GROUP = 8
LANES = 256
MIN_SAMPLES = 288
MIB = 1 << 20


def gelu_and_slope(value):
    bell = jnp.exp2(value * value * (-0.5 * 1.4426950408889634))
    phi = 0.5 + 0.5 * lax.erf(value * 0.7071067811865476)
    return value * phi, phi + value * bell * 0.3989422804014327


def cols_both(a, b):
    return lax.dot_general(a, b, (((1,), (1,)), ((), ())), preferred_element_type=F32)


def dot(a, b):
    return jnp.dot(a, b, preferred_element_type=F32)


def iota(shape, dim):
    return lax.broadcasted_iota(jnp.int32, shape, dim)


def onehot(mask):
    return mask.astype(F32).astype(BF16)


def copies(sources, targets, sems):
    started = [pltpu.make_async_copy(source, target, sems.at[i]) for i, (source, target) in enumerate(zip(sources, targets))]
    for copy in started:
        copy.start()
    return started


def setup_kernel(
    members,
    order_hbm,
    len_hbm,
    w_hbm,
    wave_hbm,
    valid_ref,
    band_ref,
    near_ref,
    far_ref,
    own_ref,
    spread_ref,
    order_ref,
    len_ref,
    w_ref,
    sems,
):
    for copy in copies((order_hbm, len_hbm, w_hbm, wave_hbm), (order_ref, len_ref, w_ref, own_ref), sems):
        copy.wait()
    rows = order_ref.shape[1]
    share = rows // members
    taps, chans = w_ref.shape
    stride = taps // 2
    owner = onehot(iota((rows, members), 0) // share == iota((rows, members), 1))
    order_of = dot(owner, order_ref[...].astype(F32).astype(BF16))
    slot = iota((rows, rows), 1) - lax.rem(iota((rows, rows), 0), share) * members
    owner_first = iota((rows, 1), 0) // share * rows
    column = iota((rows, members * rows), 1)
    member = lax.axis_index("dev")
    low_half = member < members // 2
    for target, out_ref in ((member, near_ref), (jnp.bitwise_xor(member, members // 2), far_ref)):
        local = jnp.sum(jnp.where(slot == target, order_of, 0.0), axis=1, keepdims=True).astype(jnp.int32)
        picked = column == owner_first + local
        picks = picked.astype(F32)
        out_ref[...] = jnp.where(low_half, picks[: rows // 2], picks[rows // 2 :]).astype(BF16)
        if out_ref is near_ref:
            lens = jnp.sum(jnp.where(picked, len_ref[...], 0), axis=1, keepdims=True)
    valid = (lens - taps) // stride + 1
    valid_ref[...] = jnp.broadcast_to(valid, valid_ref.shape)
    depth = band_ref.shape[0]
    for f in range(GROUP):
        spread = onehot(iota((depth, taps), 0) == iota((depth, taps), 1) + stride * f)
        band_ref[:, f * chans : (f + 1) * chans] = dot(spread, w_ref[...]).astype(BF16)
    samp = spread_ref.shape[0]
    for first in range(0, spread_ref.shape[1], depth):
        group = first // depth
        picked = iota((samp, depth), 0) == iota((samp, depth), 1) + GROUP * stride * group
        spread_ref[:, first : first + depth] = onehot(picked)


def pick_kernel(offsets, near_ref, far_ref, *refs):
    waves, (mine_ref, send_ref, all_ref) = refs[:-3], refs[-3:]
    rows = waves[0].shape[0]
    all_ref[...] = jnp.zeros(all_ref.shape, BF16)
    for offset, wave_ref in zip(offsets, waves):
        first = pl.multiple_of(jnp.bitwise_xor(lax.axis_index("dev"), offset) * rows, rows)
        all_ref[pl.ds(first, rows), :] = wave_ref[...]
    mine_ref[...] = dot(near_ref[...], all_ref[...]).astype(BF16)
    send_ref[...] = dot(far_ref[...], all_ref[...]).astype(BF16)


def forward_kernel(
    frames0,
    frames1,
    taps,
    places,
    near_ref,
    far_ref,
    valid_ref,
    band_ref,
    spread_ref,
    gain_hbm,
    bias_hbm,
    w_hbm,
    cot_hbm,
    feat_ref,
    even_ref,
    odd_ref,
    pre0,
    even_slope,
    odd_slope,
    mean_ref,
    inv_ref,
    patch_ref,
    grad_ref,
    grad_t_ref,
    gain_ref,
    w_ref,
    fresh0,
    fresh1,
    scale_ref,
    shift_ref,
    bias_ref,
    cot_ref,
    sems,
):
    waiting = copies((gain_hbm, bias_hbm, w_hbm, cot_hbm), (gain_ref, bias_ref, w_ref, cot_ref), sems)
    rows, samp = valid_ref.shape[0], near_ref.shape[1]
    chans = gain_ref.shape[1]
    stride = taps // 2
    depth = band_ref.shape[0]
    groups = pre0.shape[0]
    width = LANES
    parts = [slice(first, first + width) for first in range(0, chans, width)]
    min_valid = (MIN_SAMPLES - taps) // stride + 1
    low_half = lax.axis_index("dev") < lax.axis_size("dev") // 2
    near, far = near_ref[...].astype(F32), far_ref[...].astype(F32)
    wave = jnp.concatenate([jnp.where(low_half, near, far), jnp.where(low_half, far, near)], axis=0).astype(BF16)
    spread_out = dot(wave, spread_ref[...]).astype(BF16)
    for g in range(groups):
        patch_ref[g] = spread_out[:, g * depth : (g + 1) * depth]
    patches = patch_ref[...].reshape(groups * rows, depth)

    valid = jnp.broadcast_to(valid_ref[:, :1], (rows, width))
    count = valid.astype(F32)

    def frame(g, f, lanes):
        return pre0[g, :, f * chans + lanes.start : f * chans + lanes.stop]

    def masked_to(value, t, masked):
        return jnp.where(valid > t, value, 0.0) if masked else value

    for lanes in parts:
        for f in range(GROUP):
            cols = slice(f * chans + lanes.start, f * chans + lanes.stop)
            value = dot(patches, band_ref[:, cols]).reshape(groups, rows, width)
            pre0[:, :, cols] = value
            if f == 0:
                origin = value[0]
                shift = jnp.zeros((rows, width), F32)
                square = jnp.zeros((rows, width), F32)
            for g in range(groups):
                t = g * GROUP + f
                if 0 < t < frames0:
                    away = masked_to(value[g] - origin, t, t >= min_valid)
                    shift += away
                    square += away * away
        shift = shift / count
        mean = origin + shift
        inv = lax.rsqrt(jnp.maximum(square / count - shift * shift, 0.0) + 1e-05)
        mean_ref[:, lanes] = mean
        inv_ref[:, lanes] = inv
        if lanes.start == 0:
            waiting[0].wait()
            waiting[1].wait()
        scale = inv * gain_ref[:, lanes]
        scale_ref[:, lanes] = scale
        shift_ref[:, lanes] = bias_ref[:, lanes] - mean * scale

    half = GROUP
    evens, odds = (frames0 + 1) // 2, frames0 // 2
    min_valid1 = (min_valid - 3) // 2 + 1
    valid1 = lax.shift_right_arithmetic(valid - 3, 1) + 1
    slab = chans // len(places)
    steps = -(-frames1 // half)

    def used_in(step):
        return min(half, frames1 - step * half)

    def activate0(step):
        for t in range(step * 2 * half, min((step + 1) * 2 * half, frames0)):
            for lanes in parts:
                gelu, slope = gelu_and_slope(
                    frame(t // GROUP, t % GROUP, lanes) * scale_ref[:, lanes] + shift_ref[:, lanes]
                )
                act_ref, slope_ref = (odd_ref, odd_slope) if t % 2 else (even_ref, even_slope)
                slope_ref[t // 2, :, lanes] = masked_to(slope, t, t >= min_valid)
                act_ref[t // 2, :, lanes] = masked_to(gelu, t, t >= min_valid).astype(BF16)

    def convolve(step, out_ref):
        first, used = step * half, used_in(step)
        for lanes in parts:
            total = dot(even_ref[first : first + used].reshape(used * rows, chans), w_ref[0, :, lanes])
            total += dot(odd_ref[first : first + used].reshape(used * rows, chans), w_ref[1, :, lanes])
            total += dot(even_ref[first + 1 : first + used + 1].reshape(used * rows, chans), w_ref[2, :, lanes])
            out_ref[:used, :, lanes] = total.reshape(used, rows, width)

    def activate1(step, in_ref):
        for j in range(used_in(step)):
            u = step * half + j
            for lanes in parts:
                gelu, slope = gelu_and_slope(in_ref[j, :, lanes])
                grad = cot_ref[u, :, lanes].astype(F32) * slope
                if u >= min_valid1:
                    gelu, grad = jnp.where(valid1 > u, gelu, 0.0), jnp.where(valid1 > u, grad, 0.0)
                feat_ref[u, :, lanes] = gelu.astype(BF16)
                grad_ref[u + 1, :, lanes] = grad.astype(BF16)

    def turn(step):
        first, size = step * half, used_in(step) * rows
        turned = grad_ref[first + 1 : first + 1 + used_in(step)].reshape(size, chans).T
        for place, source in enumerate(places):
            grad_t_ref[place * slab : (place + 1) * slab, first * rows : first * rows + size] = turned[
                source * slab : (source + 1) * slab
            ]

    for ref, used in ((even_ref, evens), (odd_ref, odds)):
        ref[used:] = jnp.zeros((ref.shape[0] - used,) + ref.shape[1:], BF16)
    grad_ref[0] = jnp.zeros(grad_ref.shape[1:], BF16)
    grad_ref[frames1 + 1] = jnp.zeros(grad_ref.shape[1:], BF16)
    full = frames1 * rows // 128 * 128
    grad_t_ref[:, full:] = jnp.zeros((chans, grad_t_ref.shape[1] - full), BF16)
    fresh = (fresh0, fresh1)
    for step in range(steps + 3):
        if step == 2:
            waiting[2].wait()
            waiting[3].wait()
        if 0 <= step - 2 < steps:
            convolve(step - 2, fresh[step % 2])
        if 0 <= step - 3 < steps:
            activate1(step - 3, fresh[(step - 1) % 2])
        if step < -(-frames0 // (2 * half)):
            activate0(step)
        if 0 <= step - 3 < steps:
            turn(step - 3)


def outer_kernel(skips, *refs):
    acts, (grad_t_ref, keep_ref, send_ref) = refs[:-3], refs[-3:]
    rows, chans = acts[0].shape[1:]
    frames = grad_t_ref.shape[1] // rows
    half = chans // 2
    core = lax.rem(lax.axis_index("grp"), 2)
    for tap, (act_ref, skip) in enumerate(zip(acts, skips)):
        for side, out_ref in ((1 - core, send_ref), (core, keep_ref)):
            lanes = pl.ds(pl.multiple_of(side * half, half), half)
            value = dot(grad_t_ref[...], act_ref[skip : skip + frames, :, lanes].reshape(frames * rows, half))
            out_ref[:, tap * half : (tap + 1) * half] = value.astype(out_ref.dtype)


def input_kernel(grad_ref, w_ref, even_slope, odd_slope, feat_ref, even_ref, odd_ref, feat_out, sem):
    leaving = pltpu.make_async_copy(feat_ref, feat_out, sem)
    leaving.start()
    evens, rows, chans = even_ref.shape
    odds = odd_ref.shape[0]
    first = grad_ref[1 : evens + 1].reshape(evens * rows, chans)
    third = grad_ref[0:evens].reshape(evens * rows, chans)
    total = cols_both(first, w_ref[0]) + cols_both(third, w_ref[2])
    even_ref[...] = total.reshape(even_ref.shape) * even_slope[:evens]
    second = grad_ref[1 : odds + 1].reshape(odds * rows, chans)
    odd_ref[...] = cols_both(second, w_ref[1]).reshape(odd_ref.shape) * odd_slope[:odds]
    leaving.wait()


def backward_kernel(
    frames0,
    taps,
    valid_ref,
    pre0,
    mean_ref,
    inv_ref,
    patch_ref,
    even_ref,
    odd_ref,
    gain_ref,
    mine_ref,
    send1,
    send2,
    send3,
    dpre0,
    spread,
    turned_ref,
    out_ref,
    quarters,
):
    groups, rows, depth = patch_ref.shape
    chans = gain_ref.shape[1]
    stride = taps // 2
    width = dpre0.shape[3] // GROUP
    turned = patch_ref[...].reshape(groups * rows, depth).astype(F32).T
    turned_ref[...] = turned[: turned_ref.shape[0]].astype(BF16)
    valid = jnp.broadcast_to(valid_ref[:, :1], (rows, width))
    count = valid.astype(F32)
    min_valid = (MIN_SAMPLES - taps) // stride + 1
    parts = [slice(first, first + width) for first in range(0, chans, width)]

    def frame(t, lanes):
        start = t % GROUP * chans
        return pre0[t // GROUP, :, start + lanes.start : start + lanes.stop]

    def lift(t, lanes):
        return (odd_ref if t % 2 else even_ref)[t // 2, :, lanes]

    def sums(lanes):
        bias_sum = gain_sum = jnp.zeros((rows, width), F32)
        for t in range(frames0):
            bias_sum += lift(t, lanes)
            gain_sum += lift(t, lanes) * frame(t, lanes)
        mean, inv = mean_ref[:, lanes], inv_ref[:, lanes]
        gain_sum = (gain_sum - mean * bias_sum) * inv
        out_ref[taps : taps + 1, lanes] = jnp.sum(gain_sum, axis=0, keepdims=True)
        out_ref[taps + 1 : taps + 2, lanes] = jnp.sum(bias_sum, axis=0, keepdims=True)
        scale = inv * gain_ref[:, lanes]
        slant = scale * inv * gain_sum / count
        return scale, slant, scale * bias_sum / count - mean * slant

    def gradients(block, lanes, scale, slant, level):
        for t in range(frames0):
            value = scale * lift(t, lanes) - frame(t, lanes) * slant - level
            if t >= min_valid:
                value = jnp.where(valid > t, value, 0.0)
            f = t % GROUP
            dpre0[block, t // GROUP, :, f * width : (f + 1) * width] = value.astype(BF16)
        rest = frames0 - frames0 // GROUP * GROUP
        if rest:
            dpre0[block, groups - 1, :, rest * width :] = jnp.zeros((rows, (GROUP - rest) * width), BF16)

    def taps_of(block, lanes):
        spread[block] = dot(turned_ref[...], dpre0[block].reshape(groups * rows, GROUP * width))
        total = jnp.zeros((taps, width), F32)
        for f in range(GROUP):
            total += spread[block, stride * f : stride * f + taps, f * width : (f + 1) * width]
        out_ref[:taps, lanes] = total

    terms = sums(parts[0])
    for block, lanes in enumerate(parts):
        gradients(block, lanes, *terms)
        if block + 1 < len(parts):
            terms = sums(parts[block + 1])
        taps_of(block, lanes)
    size = chans // lax.axis_size("dev")
    for place in range(4):
        columns = [slice(first, first + size) for first in range(place * size, chans, 4 * size)]
        quarters[place] = jnp.concatenate([out_ref[:, part] for part in columns], axis=1)
    place = lax.rem(lax.axis_index("dev"), 4)
    for offset, ref in enumerate((mine_ref, send1, send2, send3)):
        ref[...] = quarters[jnp.bitwise_xor(place, offset)]


def plane_kernel(*refs):
    keeps, others, outs = refs[:2], refs[2:4], refs[5:]
    size = outs[0].shape[0]
    edge = keeps[0].shape[1]
    place = lax.rem(lax.axis_index("dev"), 4)
    for offset, out_ref in enumerate(outs):
        lines = pl.ds(pl.multiple_of(jnp.bitwise_xor(place, offset) * size, size), size)
        for lanes, keep_ref, got_ref in zip((slice(0, edge), slice(edge, None)), keeps, others):
            out_ref[:, lanes] = (keep_ref[lines, :] + got_ref[lines, :].astype(F32)).astype(out_ref.dtype)


def part_kernel(own_ref, got1, got2, small_ref, sum_ref, total_ref):
    sum_ref[...] = own_ref[...] + (got1[...].astype(F32) + got2[...].astype(F32))
    total_ref[...] = small_ref[...]


def packed(size, wide):
    return size + 16, wide - 128


def write_packed(ref, value, small):
    size, lanes = ref.shape[0] - 16, ref.shape[1]
    ref[:size] = value[:, :lanes].astype(ref.dtype)
    used = size // 16
    for block in range(used):
        piece = value[block * 16 : (block + 1) * 16, lanes:]
        ref[size:, block * 128 : (block + 1) * 128] = piece.astype(ref.dtype)
    for first in range(used * 128, lanes - 128, 128):
        ref[size:, first : first + 128] = jnp.zeros((16, 128), ref.dtype)
    ref[size:, lanes - 128 :] = small.astype(ref.dtype)


def read_packed(ref, first, count):
    size = ref.shape[0] - 16
    whole = ref[pl.ds(pl.multiple_of(first, 16), count), :].astype(F32)
    pieces = [
        ref[size:, pl.ds(pl.multiple_of(first * 8 + block * 128, 128), 128)].astype(F32) for block in range(count // 16)
    ]
    return jnp.concatenate([whole, jnp.concatenate(pieces, axis=0)], axis=1)


def gather_kernel(bit, own_ref, got3, small0, small1, small2, small3, keep_ref, send_ref):
    half = own_ref.shape[0] // 2
    side = lax.rem(lax.shift_right_logical(lax.axis_index("dev"), bit), 2)
    total = (small0[...] + small1[...]) + (small2[...] + small3[...])
    for index, ref in ((1 - side, send_ref), (side, keep_ref)):
        lines = pl.ds(pl.multiple_of(index * half, half), half)
        write_packed(ref, own_ref[lines, :] + got3[lines, :].astype(F32), total)


def halve_kernel(bit, keep_ref, got_ref, next_ref, send_ref):
    half = (keep_ref.shape[0] - 16) // 2
    side = lax.rem(lax.shift_right_logical(lax.axis_index("dev"), bit), 2)
    small = keep_ref[2 * half :, -128:] + got_ref[2 * half :, -128:].astype(F32)
    for index, ref in ((1 - side, send_ref), (side, next_ref)):
        first = index * half
        write_packed(ref, read_packed(keep_ref, first, half) + read_packed(got_ref, first, half), small)


def add_kernel(mine_ref, got_ref, out_ref):
    out_ref[...] = (mine_ref[...].astype(F32) + got_ref[...].astype(F32)).astype(out_ref.dtype)


def join_kernel(taps, own_ref, other_ref, out_ref, first_ref, gain_ref, bias_ref):
    second, size, chans = out_ref.shape
    half = chans // 2
    core = lax.rem(lax.axis_index("grp"), 2)
    for ref, side in ((own_ref, core), (other_ref, 1 - core)):
        value = read_packed(ref, 0, size)
        for tap in range(second):
            lanes = pl.ds(pl.multiple_of(side * half, half), half)
            out_ref[tap, :, lanes] = value[:, tap * half : (tap + 1) * half]
    total = own_ref[size:, -128:] + other_ref[size:, -128:]
    value = total[:, :size]
    for place in range(1, 128 // size):
        mine = lax.axis_index("dev") // 4 == place
        value = jnp.where(mine, total[:, place * size : (place + 1) * size], value)
    first_ref[...] = value[:taps]
    gain_ref[...] = value[taps : taps + 1]
    bias_ref[...] = value[taps + 1 : taps + 2]


def call(kernel, outs, args, scratch=(), limit=24, flops=0, touched=0, outside=()):
    vmem = pl.BlockSpec(memory_space=pltpu.VMEM)
    args = [pltpu.with_memory_space_constraint(arg, pltpu.HBM) if i in outside else arg for i, arg in enumerate(args)]
    return pl.pallas_call(
        kernel,
        out_shape=[
            jax.ShapeDtypeStruct(out[0], out[1]) if len(out) > 2 else pltpu.VMEM(out[0], out[1]) for out in outs
        ],
        in_specs=[pl.BlockSpec(memory_space=pltpu.HBM) if i in outside else vmem for i in range(len(args))],
        out_specs=[pl.BlockSpec(memory_space=pl.ANY) if out[-1] == "hbm" else vmem for out in outs],
        scratch_shapes=[pltpu.VMEM(*entry) if isinstance(entry, tuple) else entry for entry in scratch],
        compiler_params=pltpu.CompilerParams(vmem_limit_bytes=limit * MIB),
        cost_estimate=pl.CostEstimate(flops=flops, bytes_accessed=touched, transcendentals=0),
    )(*args)


def swap(value, axis, offset):
    size = lax.axis_size(axis)
    return lax.ppermute(value, axis, [(i, i ^ offset) for i in range(size)])


def shards(wave, lengths, order, w_first, norm_gain, norm_bias, w_second, cot):
    members = lax.axis_size("dev")
    groups_of = lax.axis_size("grp")
    rows, samp = wave.shape
    taps, chans = w_first.shape
    taps_second = w_second.shape[0]
    stride = taps // 2
    frames0 = (samp - taps) // stride + 1
    frames1 = (frames0 - taps_second) // 2 + 1
    groups = -(-frames0 // GROUP)
    depth = 128
    width = LANES
    dev_bits = members.bit_length() - 1
    grp_bits = groups_of.bit_length() - 1

    offsets = [0, 1, 2, 3]
    waves = [wave] + [swap(wave, "dev", offset) for offset in offsets[1:]]
    for bit in range(2, dev_bits - 1):
        offsets += [offset | (1 << bit) for offset in offsets]
        waves += [swap(held, "dev", 1 << bit) for held in waves]
    lens = lengths.reshape(1, members * rows)
    every = members * rows
    valid, band, near_sel, far_sel, own_wave, spread = call(
        functools.partial(setup_kernel, members),
        [
            ((rows, 128), jnp.int32),
            ((depth, GROUP * chans), BF16),
            ((rows // 2, every), BF16),
            ((rows // 2, every), BF16),
            ((rows, samp), BF16),
            ((samp, groups * depth), BF16),
        ],
        [order, lens, w_first, wave],
        scratch=[
            (order.shape, order.dtype),
            (lens.shape, lens.dtype),
            (w_first.shape, BF16),
            pltpu.SemaphoreType.DMA((4,)),
        ],
        outside=(0, 1, 2, 3),
    )
    near, send = call(
        functools.partial(pick_kernel, offsets),
        [((rows // 2, samp), BF16), ((rows // 2, samp), BF16)],
        [near_sel, far_sel, own_wave, *waves[1:]],
        scratch=[((every, samp), BF16)],
    )
    far = swap(send, "dev", members // 2)
    gain = norm_gain.reshape(1, chans)
    bias = norm_bias.reshape(1, chans)
    cot_t = cot.transpose(1, 0, 2)
    pad_frames = -(-frames1 // 4) * 4
    places = [0] * members
    for dev in range(members):
        places[dev % 4 * (members // 4) + dev // 4] = dev
    feat, even, odd, pre0, even_slope, odd_slope, mean, inv, patch, grad, grad_t, gain_in, w_in = call(
        functools.partial(forward_kernel, frames0, frames1, taps, places),
        [
            ((frames1, rows, chans), BF16),
            ((pad_frames + 1, rows, chans), BF16),
            ((pad_frames, rows, chans), BF16),
            ((groups, rows, GROUP * chans), F32),
            ((pad_frames, rows, chans), F32),
            ((pad_frames, rows, chans), F32),
            ((rows, chans), F32),
            ((rows, chans), F32),
            ((groups, rows, depth), BF16),
            ((frames1 + 2, rows, chans), BF16),
            ((chans, pad_frames * rows), BF16),
            ((1, chans), F32),
            (w_second.shape, BF16),
        ],
        [near, far, valid, band, spread, gain, bias, w_second, cot_t],
        scratch=[
            ((GROUP, rows, chans), F32),
            ((GROUP, rows, chans), F32),
            ((rows, chans), F32),
            ((rows, chans), F32),
            (bias.shape, F32),
            (cot_t.shape, BF16),
            pltpu.SemaphoreType.DMA((4,)),
        ],
        outside=(5, 6, 7, 8),
    )
    half = chans // 2
    wide = taps_second * half
    keeps, others = [], []
    for acts, skips in (((even, odd), (0, 0)), ((even,), (1,))):
        shape = (chans, len(acts) * half)
        keep, send = call(
            functools.partial(outer_kernel, skips), [(shape, F32), (shape, BF16)], [*acts, grad_t], flops=len(acts) << 29
        )
        keeps.append(keep)
        others.append(swap(send, "grp", 1))
    evens, odds = (frames0 + 1) // 2, frames0 // 2
    lift_even, lift_odd, features = call(
        input_kernel,
        [((evens, rows, chans), F32), ((odds, rows, chans), F32), ((frames1, rows, chans), BF16, "hbm")],
        [grad, w_in, even_slope, odd_slope, feat],
        scratch=[pltpu.SemaphoreType.DMA],
        flops=1 << 30,
    )
    quarter = chans // 4
    own, *sends = call(
        plane_kernel,
        [((quarter, wide), F32)] + [((quarter, wide), BF16)] * 3,
        [*keeps, *others, lift_odd],
    )
    gots = [swap(part, "dev", offset) for offset, part in enumerate(sends, 1)]
    used = -(-(stride * (GROUP - 1) + taps) // 16) * 16
    small, *smalls = call(
        functools.partial(backward_kernel, frames0, taps),
        [((16, quarter), F32)] * 4,
        [valid, pre0, mean, inv, patch, lift_even, lift_odd, gain_in],
        scratch=[
            ((chans // width, groups, rows, GROUP * width), BF16),
            ((chans // width, used, GROUP * width), F32),
            ((used, groups * rows), BF16),
            ((16, chans), F32),
            ((4, 16, quarter), F32),
        ],
        flops=1 << 32,
    )
    small3, small2 = swap(smalls[2], "dev", 3), swap(smalls[1], "dev", 2)
    own, first = call(
        part_kernel, [((quarter, wide), F32), (small.shape, F32)], [own, gots[0], gots[1], smalls[0]]
    )
    small1 = swap(first, "dev", 1)
    size = quarter // 2
    keep, send = call(
        functools.partial(gather_kernel, dev_bits - 1),
        [(packed(size, wide), F32), (packed(size, wide), BF16)],
        [own, gots[2], small, small1, small2, small3],
    )
    for bit in range(dev_bits - 1, 2, -1):
        size //= 2
        keep, send = call(
            functools.partial(halve_kernel, bit - 1),
            [(packed(size, wide), F32), (packed(size, wide), BF16)],
            [keep, swap(send, "dev", 1 << bit)],
        )
    send = call(add_kernel, [(packed(size, wide), BF16)], [keep, swap(send, "dev", 4)])[0]
    for bit in range(1, grp_bits):
        kind = F32 if bit == grp_bits - 1 else BF16
        send = call(add_kernel, [(packed(size, wide), kind)], [send, swap(send, "grp", 1 << bit)])[0]
    grad_second, grad_first, grad_gain, grad_bias = call(
        functools.partial(join_kernel, taps),
        [
            ((taps_second, size, chans), F32, "out"),
            ((taps, size), F32, "out"),
            ((1, size), F32, "out"),
            ((1, size), F32, "out"),
        ],
        [send, swap(send, "grp", 1)],
    )
    return (
        features.transpose(1, 0, 2),
        grad_second.transpose(0, 2, 1),
        grad_first,
        grad_gain.reshape(size),
        grad_bias.reshape(size),
    )


def solution(mesh):
    placed = (
        P(("grp", "dev"), None),
        P("grp"),
        P("grp", None),
        P(),
        P(),
        P(),
        P(),
        P(("grp", "dev"), None, None),
    )
    return jax.shard_map(
        shards,
        mesh=mesh,
        in_specs=placed,
        out_specs=(
            P(("grp", "dev"), None, None),
            P(None, None, "dev"),
            P(None, "dev"),
            P("dev"),
            P("dev"),
        ),
        check_vma=False,
    )
```

```python
import functools

import jax
import jax.numpy as jnp
from jax import lax
from jax.experimental import pallas as pl
from jax.experimental.pallas import tpu as pltpu
from jax.sharding import PartitionSpec as P

F32 = jnp.float32
BF16 = jnp.bfloat16
GROUP = 8
LANES = 256
MIN_SAMPLES = 288
MIB = 1 << 20


def gelu_and_slope(value):
    bell = jnp.exp2(value * value * (-0.5 * 1.4426950408889634))
    phi = 0.5 + 0.5 * lax.erf(value * 0.7071067811865476)
    return value * phi, phi + value * bell * 0.3989422804014327


def cols_both(a, b):
    return lax.dot_general(a, b, (((1,), (1,)), ((), ())), preferred_element_type=F32)


def dot(a, b):
    return jnp.dot(a, b, preferred_element_type=F32)


def iota(shape, dim):
    return lax.broadcasted_iota(jnp.int32, shape, dim)


def onehot(mask):
    return mask.astype(F32).astype(BF16)


def copies(sources, targets, sems):
    started = [pltpu.make_async_copy(source, target, sems.at[i]) for i, (source, target) in enumerate(zip(sources, targets))]
    for copy in started:
        copy.start()
    return started


def setup_kernel(
    members,
    order_hbm,
    len_hbm,
    w_hbm,
    wave_hbm,
    valid_ref,
    band_ref,
    near_ref,
    far_ref,
    own_ref,
    order_ref,
    len_ref,
    w_ref,
    sems,
):
    for copy in copies((order_hbm, len_hbm, w_hbm, wave_hbm), (order_ref, len_ref, w_ref, own_ref), sems):
        copy.wait()
    rows = order_ref.shape[1]
    share = rows // members
    taps, chans = w_ref.shape
    stride = taps // 2
    owner = onehot(iota((rows, members), 0) // share == iota((rows, members), 1))
    order_of = dot(owner, order_ref[...].astype(F32).astype(BF16))
    slot = iota((rows, rows), 1) - lax.rem(iota((rows, rows), 0), share) * members
    owner_first = iota((rows, 1), 0) // share * rows
    column = iota((rows, members * rows), 1)
    member = lax.axis_index("dev")
    low_half = member < members // 2
    for target, out_ref in ((member, near_ref), (jnp.bitwise_xor(member, members // 2), far_ref)):
        local = jnp.sum(jnp.where(slot == target, order_of, 0.0), axis=1, keepdims=True).astype(jnp.int32)
        picked = column == owner_first + local
        picks = picked.astype(F32)
        out_ref[...] = jnp.where(low_half, picks[: rows // 2], picks[rows // 2 :]).astype(BF16)
        if out_ref is near_ref:
            lens = jnp.sum(jnp.where(picked, len_ref[...], 0), axis=1, keepdims=True)
    valid = (lens - taps) // stride + 1
    valid_ref[...] = jnp.broadcast_to(valid, valid_ref.shape)
    depth = band_ref.shape[0]
    for f in range(GROUP):
        spread = onehot(iota((depth, taps), 0) == iota((depth, taps), 1) + stride * f)
        band_ref[:, f * chans : (f + 1) * chans] = dot(spread, w_ref[...]).astype(BF16)


def pick_kernel(offsets, near_ref, far_ref, *refs):
    waves, (mine_ref, send_ref, all_ref) = refs[:-3], refs[-3:]
    rows = waves[0].shape[0]
    all_ref[...] = jnp.zeros(all_ref.shape, BF16)
    for offset, wave_ref in zip(offsets, waves):
        first = pl.multiple_of(jnp.bitwise_xor(lax.axis_index("dev"), offset) * rows, rows)
        all_ref[pl.ds(first, rows), :] = wave_ref[...]
    mine_ref[...] = dot(near_ref[...], all_ref[...]).astype(BF16)
    send_ref[...] = dot(far_ref[...], all_ref[...]).astype(BF16)


def forward_kernel(
    frames0,
    frames1,
    taps,
    places,
    near_ref,
    far_ref,
    valid_ref,
    band_ref,
    gain_hbm,
    bias_hbm,
    w_hbm,
    cot_hbm,
    feat_ref,
    even_ref,
    odd_ref,
    pre0,
    even_slope,
    odd_slope,
    mean_ref,
    inv_ref,
    patch_ref,
    grad_ref,
    grad_t_ref,
    gain_ref,
    w_ref,
    fresh0,
    fresh1,
    scale_ref,
    shift_ref,
    bias_ref,
    cot_ref,
    sems,
):
    waiting = copies((gain_hbm, bias_hbm, w_hbm, cot_hbm), (gain_ref, bias_ref, w_ref, cot_ref), sems)
    rows, samp = valid_ref.shape[0], near_ref.shape[1]
    chans = gain_ref.shape[1]
    stride = taps // 2
    depth = band_ref.shape[0]
    groups = pre0.shape[0]
    width = LANES
    parts = [slice(first, first + width) for first in range(0, chans, width)]
    min_valid = (MIN_SAMPLES - taps) // stride + 1
    low_half = lax.axis_index("dev") < lax.axis_size("dev") // 2
    near, far = near_ref[...].astype(F32), far_ref[...].astype(F32)
    wave = jnp.concatenate([jnp.where(low_half, near, far), jnp.where(low_half, far, near)], axis=0).astype(BF16)
    for g in range(groups):
        pick = onehot(iota((samp, depth), 0) == iota((samp, depth), 1) + GROUP * stride * g)
        patch_ref[g] = dot(wave, pick).astype(BF16)
    patches = patch_ref[...].reshape(groups * rows, depth)

    valid = jnp.broadcast_to(valid_ref[:, :1], (rows, width))
    count = valid.astype(F32)

    def frame(g, f, lanes):
        return pre0[g, :, f * chans + lanes.start : f * chans + lanes.stop]

    def masked_to(value, t, masked):
        return jnp.where(valid > t, value, 0.0) if masked else value

    for lanes in parts:
        for f in range(GROUP):
            cols = slice(f * chans + lanes.start, f * chans + lanes.stop)
            value = dot(patches, band_ref[:, cols]).reshape(groups, rows, width)
            pre0[:, :, cols] = value
            if f == 0:
                origin = value[0]
                shift = jnp.zeros((rows, width), F32)
                square = jnp.zeros((rows, width), F32)
            for g in range(groups):
                t = g * GROUP + f
                if 0 < t < frames0:
                    away = masked_to(value[g] - origin, t, t >= min_valid)
                    shift += away
                    square += away * away
        shift = shift / count
        mean = origin + shift
        inv = lax.rsqrt(jnp.maximum(square / count - shift * shift, 0.0) + 1e-05)
        mean_ref[:, lanes] = mean
        inv_ref[:, lanes] = inv
        if lanes.start == 0:
            waiting[0].wait()
            waiting[1].wait()
        scale = inv * gain_ref[:, lanes]
        scale_ref[:, lanes] = scale
        shift_ref[:, lanes] = bias_ref[:, lanes] - mean * scale

    half = GROUP
    evens, odds = (frames0 + 1) // 2, frames0 // 2
    min_valid1 = (min_valid - 3) // 2 + 1
    valid1 = lax.shift_right_arithmetic(valid - 3, 1) + 1
    slab = chans // len(places)
    steps = -(-frames1 // half)

    def used_in(step):
        return min(half, frames1 - step * half)

    def activate0(step):
        for t in range(step * 2 * half, min((step + 1) * 2 * half, frames0)):
            for lanes in parts:
                gelu, slope = gelu_and_slope(
                    frame(t // GROUP, t % GROUP, lanes) * scale_ref[:, lanes] + shift_ref[:, lanes]
                )
                act_ref, slope_ref = (odd_ref, odd_slope) if t % 2 else (even_ref, even_slope)
                slope_ref[t // 2, :, lanes] = masked_to(slope, t, t >= min_valid)
                act_ref[t // 2, :, lanes] = masked_to(gelu, t, t >= min_valid).astype(BF16)

    def convolve(step, out_ref):
        first, used = step * half, used_in(step)
        for lanes in parts:
            total = dot(even_ref[first : first + used].reshape(used * rows, chans), w_ref[0, :, lanes])
            total += dot(odd_ref[first : first + used].reshape(used * rows, chans), w_ref[1, :, lanes])
            total += dot(even_ref[first + 1 : first + used + 1].reshape(used * rows, chans), w_ref[2, :, lanes])
            out_ref[:used, :, lanes] = total.reshape(used, rows, width)

    def activate1(step, in_ref):
        for j in range(used_in(step)):
            u = step * half + j
            for lanes in parts:
                gelu, slope = gelu_and_slope(in_ref[j, :, lanes])
                grad = cot_ref[u, :, lanes].astype(F32) * slope
                if u >= min_valid1:
                    gelu, grad = jnp.where(valid1 > u, gelu, 0.0), jnp.where(valid1 > u, grad, 0.0)
                feat_ref[u, :, lanes] = gelu.astype(BF16)
                grad_ref[u + 1, :, lanes] = grad.astype(BF16)

    def turn(step):
        first, size = step * half, used_in(step) * rows
        turned = grad_ref[first + 1 : first + 1 + used_in(step)].reshape(size, chans).T
        for place, source in enumerate(places):
            grad_t_ref[place * slab : (place + 1) * slab, first * rows : first * rows + size] = turned[
                source * slab : (source + 1) * slab
            ]

    for ref, used in ((even_ref, evens), (odd_ref, odds)):
        ref[used:] = jnp.zeros((ref.shape[0] - used,) + ref.shape[1:], BF16)
    grad_ref[0] = jnp.zeros(grad_ref.shape[1:], BF16)
    grad_ref[frames1 + 1] = jnp.zeros(grad_ref.shape[1:], BF16)
    full = frames1 * rows // 128 * 128
    grad_t_ref[:, full:] = jnp.zeros((chans, grad_t_ref.shape[1] - full), BF16)
    fresh = (fresh0, fresh1)
    for step in range(steps + 3):
        if step == 2:
            waiting[2].wait()
            waiting[3].wait()
        if 0 <= step - 2 < steps:
            convolve(step - 2, fresh[step % 2])
        if 0 <= step - 3 < steps:
            activate1(step - 3, fresh[(step - 1) % 2])
        if step < -(-frames0 // (2 * half)):
            activate0(step)
        if 0 <= step - 3 < steps:
            turn(step - 3)


def outer_kernel(skips, *refs):
    acts, (grad_t_ref, keep_ref, send_ref) = refs[:-3], refs[-3:]
    rows, chans = acts[0].shape[1:]
    frames = grad_t_ref.shape[1] // rows
    half = chans // 2
    core = lax.rem(lax.axis_index("grp"), 2)
    for tap, (act_ref, skip) in enumerate(zip(acts, skips)):
        for side, out_ref in ((1 - core, send_ref), (core, keep_ref)):
            lanes = pl.ds(pl.multiple_of(side * half, half), half)
            value = dot(grad_t_ref[...], act_ref[skip : skip + frames, :, lanes].reshape(frames * rows, half))
            out_ref[:, tap * half : (tap + 1) * half] = value.astype(out_ref.dtype)


def input_kernel(grad_ref, w_ref, even_slope, odd_slope, feat_ref, even_ref, odd_ref, feat_out, sem):
    leaving = pltpu.make_async_copy(feat_ref, feat_out, sem)
    leaving.start()
    evens, rows, chans = even_ref.shape
    odds = odd_ref.shape[0]
    first = grad_ref[1 : evens + 1].reshape(evens * rows, chans)
    third = grad_ref[0:evens].reshape(evens * rows, chans)
    total = cols_both(first, w_ref[0]) + cols_both(third, w_ref[2])
    even_ref[...] = total.reshape(even_ref.shape) * even_slope[:evens]
    second = grad_ref[1 : odds + 1].reshape(odds * rows, chans)
    odd_ref[...] = cols_both(second, w_ref[1]).reshape(odd_ref.shape) * odd_slope[:odds]
    leaving.wait()


def backward_kernel(
    frames0,
    taps,
    valid_ref,
    pre0,
    mean_ref,
    inv_ref,
    patch_ref,
    even_ref,
    odd_ref,
    gain_ref,
    mine_ref,
    send1,
    send2,
    send3,
    dpre0,
    spread,
    turned_ref,
    out_ref,
    quarters,
):
    groups, rows, depth = patch_ref.shape
    chans = gain_ref.shape[1]
    stride = taps // 2
    width = dpre0.shape[3] // GROUP
    turned = patch_ref[...].reshape(groups * rows, depth).astype(F32).T
    turned_ref[...] = turned[: turned_ref.shape[0]].astype(BF16)
    valid = jnp.broadcast_to(valid_ref[:, :1], (rows, width))
    count = valid.astype(F32)
    min_valid = (MIN_SAMPLES - taps) // stride + 1
    parts = [slice(first, first + width) for first in range(0, chans, width)]

    def frame(t, lanes):
        start = t % GROUP * chans
        return pre0[t // GROUP, :, start + lanes.start : start + lanes.stop]

    def lift(t, lanes):
        return (odd_ref if t % 2 else even_ref)[t // 2, :, lanes]

    def sums(lanes):
        bias_sum = gain_sum = jnp.zeros((rows, width), F32)
        for t in range(frames0):
            bias_sum += lift(t, lanes)
            gain_sum += lift(t, lanes) * frame(t, lanes)
        mean, inv = mean_ref[:, lanes], inv_ref[:, lanes]
        gain_sum = (gain_sum - mean * bias_sum) * inv
        out_ref[taps : taps + 1, lanes] = jnp.sum(gain_sum, axis=0, keepdims=True)
        out_ref[taps + 1 : taps + 2, lanes] = jnp.sum(bias_sum, axis=0, keepdims=True)
        scale = inv * gain_ref[:, lanes]
        slant = scale * inv * gain_sum / count
        return scale, slant, scale * bias_sum / count - mean * slant

    def gradients(block, lanes, scale, slant, level):
        for t in range(frames0):
            value = scale * lift(t, lanes) - frame(t, lanes) * slant - level
            if t >= min_valid:
                value = jnp.where(valid > t, value, 0.0)
            f = t % GROUP
            dpre0[block, t // GROUP, :, f * width : (f + 1) * width] = value.astype(BF16)
        rest = frames0 - frames0 // GROUP * GROUP
        if rest:
            dpre0[block, groups - 1, :, rest * width :] = jnp.zeros((rows, (GROUP - rest) * width), BF16)

    def taps_of(block, lanes):
        spread[block] = dot(turned_ref[...], dpre0[block].reshape(groups * rows, GROUP * width))
        total = jnp.zeros((taps, width), F32)
        for f in range(GROUP):
            total += spread[block, stride * f : stride * f + taps, f * width : (f + 1) * width]
        out_ref[:taps, lanes] = total

    terms = sums(parts[0])
    for block, lanes in enumerate(parts):
        gradients(block, lanes, *terms)
        if block + 1 < len(parts):
            terms = sums(parts[block + 1])
        taps_of(block, lanes)
    size = chans // lax.axis_size("dev")
    for place in range(4):
        columns = [slice(first, first + size) for first in range(place * size, chans, 4 * size)]
        quarters[place] = jnp.concatenate([out_ref[:, part] for part in columns], axis=1)
    place = lax.rem(lax.axis_index("dev"), 4)
    for offset, ref in enumerate((mine_ref, send1, send2, send3)):
        ref[...] = quarters[jnp.bitwise_xor(place, offset)]


def plane_kernel(*refs):
    keeps, others, outs = refs[:2], refs[2:4], refs[5:]
    size = outs[0].shape[0]
    edge = keeps[0].shape[1]
    place = lax.rem(lax.axis_index("dev"), 4)
    for offset, out_ref in enumerate(outs):
        lines = pl.ds(pl.multiple_of(jnp.bitwise_xor(place, offset) * size, size), size)
        for lanes, keep_ref, got_ref in zip((slice(0, edge), slice(edge, None)), keeps, others):
            out_ref[:, lanes] = (keep_ref[lines, :] + got_ref[lines, :].astype(F32)).astype(out_ref.dtype)


def part_kernel(own_ref, got1, got2, small_ref, sum_ref, total_ref):
    sum_ref[...] = own_ref[...] + (got1[...].astype(F32) + got2[...].astype(F32))
    total_ref[...] = small_ref[...]


def packed(size, wide):
    return size + 16, wide - 128


def write_packed(ref, value, small):
    size, lanes = ref.shape[0] - 16, ref.shape[1]
    ref[:size] = value[:, :lanes].astype(ref.dtype)
    used = size // 16
    for block in range(used):
        piece = value[block * 16 : (block + 1) * 16, lanes:]
        ref[size:, block * 128 : (block + 1) * 128] = piece.astype(ref.dtype)
    for first in range(used * 128, lanes - 128, 128):
        ref[size:, first : first + 128] = jnp.zeros((16, 128), ref.dtype)
    ref[size:, lanes - 128 :] = small.astype(ref.dtype)


def read_packed(ref, first, count):
    size = ref.shape[0] - 16
    whole = ref[pl.ds(pl.multiple_of(first, 16), count), :].astype(F32)
    pieces = [
        ref[size:, pl.ds(pl.multiple_of(first * 8 + block * 128, 128), 128)].astype(F32) for block in range(count // 16)
    ]
    return jnp.concatenate([whole, jnp.concatenate(pieces, axis=0)], axis=1)


def gather_kernel(bit, own_ref, got3, small0, small1, small2, small3, keep_ref, send_ref):
    half = own_ref.shape[0] // 2
    side = lax.rem(lax.shift_right_logical(lax.axis_index("dev"), bit), 2)
    total = (small0[...] + small1[...]) + (small2[...] + small3[...])
    for index, ref in ((1 - side, send_ref), (side, keep_ref)):
        lines = pl.ds(pl.multiple_of(index * half, half), half)
        write_packed(ref, own_ref[lines, :] + got3[lines, :].astype(F32), total)


def halve_kernel(bit, keep_ref, got_ref, next_ref, send_ref):
    half = (keep_ref.shape[0] - 16) // 2
    side = lax.rem(lax.shift_right_logical(lax.axis_index("dev"), bit), 2)
    small = keep_ref[2 * half :, -128:] + got_ref[2 * half :, -128:].astype(F32)
    for index, ref in ((1 - side, send_ref), (side, next_ref)):
        first = index * half
        write_packed(ref, read_packed(keep_ref, first, half) + read_packed(got_ref, first, half), small)


def add_kernel(mine_ref, got_ref, out_ref):
    out_ref[...] = (mine_ref[...].astype(F32) + got_ref[...].astype(F32)).astype(out_ref.dtype)


def join_kernel(taps, own_ref, other_ref, out_ref, first_ref, gain_ref, bias_ref):
    second, size, chans = out_ref.shape
    half = chans // 2
    core = lax.rem(lax.axis_index("grp"), 2)
    for ref, side in ((own_ref, core), (other_ref, 1 - core)):
        value = read_packed(ref, 0, size)
        for tap in range(second):
            lanes = pl.ds(pl.multiple_of(side * half, half), half)
            out_ref[tap, :, lanes] = value[:, tap * half : (tap + 1) * half]
    total = own_ref[size:, -128:] + other_ref[size:, -128:]
    value = total[:, :size]
    for place in range(1, 128 // size):
        mine = lax.axis_index("dev") // 4 == place
        value = jnp.where(mine, total[:, place * size : (place + 1) * size], value)
    first_ref[...] = value[:taps]
    gain_ref[...] = value[taps : taps + 1]
    bias_ref[...] = value[taps + 1 : taps + 2]


def call(kernel, outs, args, scratch=(), limit=24, flops=0, touched=0, outside=()):
    vmem = pl.BlockSpec(memory_space=pltpu.VMEM)
    args = [pltpu.with_memory_space_constraint(arg, pltpu.HBM) if i in outside else arg for i, arg in enumerate(args)]
    return pl.pallas_call(
        kernel,
        out_shape=[
            jax.ShapeDtypeStruct(out[0], out[1]) if len(out) > 2 else pltpu.VMEM(out[0], out[1]) for out in outs
        ],
        in_specs=[pl.BlockSpec(memory_space=pltpu.HBM) if i in outside else vmem for i in range(len(args))],
        out_specs=[pl.BlockSpec(memory_space=pl.ANY) if out[-1] == "hbm" else vmem for out in outs],
        scratch_shapes=[pltpu.VMEM(*entry) if isinstance(entry, tuple) else entry for entry in scratch],
        compiler_params=pltpu.CompilerParams(vmem_limit_bytes=limit * MIB),
        cost_estimate=pl.CostEstimate(flops=flops, bytes_accessed=touched, transcendentals=0),
    )(*args)


def swap(value, axis, offset):
    size = lax.axis_size(axis)
    return lax.ppermute(value, axis, [(i, i ^ offset) for i in range(size)])


def shards(wave, lengths, order, w_first, norm_gain, norm_bias, w_second, cot):
    members = lax.axis_size("dev")
    groups_of = lax.axis_size("grp")
    rows, samp = wave.shape
    taps, chans = w_first.shape
    taps_second = w_second.shape[0]
    stride = taps // 2
    frames0 = (samp - taps) // stride + 1
    frames1 = (frames0 - taps_second) // 2 + 1
    groups = -(-frames0 // GROUP)
    depth = 128
    width = LANES
    dev_bits = members.bit_length() - 1
    grp_bits = groups_of.bit_length() - 1

    offsets = [0, 1, 2, 3]
    waves = [wave] + [swap(wave, "dev", offset) for offset in offsets[1:]]
    for bit in range(2, dev_bits - 1):
        offsets += [offset | (1 << bit) for offset in offsets]
        waves += [swap(held, "dev", 1 << bit) for held in waves]
    lens = lengths.reshape(1, members * rows)
    every = members * rows
    valid, band, near_sel, far_sel, own_wave = call(
        functools.partial(setup_kernel, members),
        [
            ((rows, 128), jnp.int32),
            ((depth, GROUP * chans), BF16),
            ((rows // 2, every), BF16),
            ((rows // 2, every), BF16),
            ((rows, samp), BF16),
        ],
        [order, lens, w_first, wave],
        scratch=[
            (order.shape, order.dtype),
            (lens.shape, lens.dtype),
            (w_first.shape, BF16),
            pltpu.SemaphoreType.DMA((4,)),
        ],
        outside=(0, 1, 2, 3),
    )
    near, send = call(
        functools.partial(pick_kernel, offsets),
        [((rows // 2, samp), BF16), ((rows // 2, samp), BF16)],
        [near_sel, far_sel, own_wave, *waves[1:]],
        scratch=[((every, samp), BF16)],
    )
    far = swap(send, "dev", members // 2)
    gain = norm_gain.reshape(1, chans)
    bias = norm_bias.reshape(1, chans)
    cot_t = cot.transpose(1, 0, 2)
    pad_frames = -(-frames1 // 4) * 4
    places = [0] * members
    for dev in range(members):
        places[dev % 4 * (members // 4) + dev // 4] = dev
    feat, even, odd, pre0, even_slope, odd_slope, mean, inv, patch, grad, grad_t, gain_in, w_in = call(
        functools.partial(forward_kernel, frames0, frames1, taps, places),
        [
            ((frames1, rows, chans), BF16),
            ((pad_frames + 1, rows, chans), BF16),
            ((pad_frames, rows, chans), BF16),
            ((groups, rows, GROUP * chans), F32),
            ((pad_frames, rows, chans), F32),
            ((pad_frames, rows, chans), F32),
            ((rows, chans), F32),
            ((rows, chans), F32),
            ((groups, rows, depth), BF16),
            ((frames1 + 2, rows, chans), BF16),
            ((chans, pad_frames * rows), BF16),
            ((1, chans), F32),
            (w_second.shape, BF16),
        ],
        [near, far, valid, band, gain, bias, w_second, cot_t],
        scratch=[
            ((GROUP, rows, chans), F32),
            ((GROUP, rows, chans), F32),
            ((rows, chans), F32),
            ((rows, chans), F32),
            (bias.shape, F32),
            (cot_t.shape, BF16),
            pltpu.SemaphoreType.DMA((4,)),
        ],
        outside=(4, 5, 6, 7),
    )
    half = chans // 2
    wide = taps_second * half
    keeps, others = [], []
    for acts, skips in (((even, odd), (0, 0)), ((even,), (1,))):
        shape = (chans, len(acts) * half)
        keep, send = call(
            functools.partial(outer_kernel, skips), [(shape, F32), (shape, BF16)], [*acts, grad_t], flops=len(acts) << 29
        )
        keeps.append(keep)
        others.append(swap(send, "grp", 1))
    evens, odds = (frames0 + 1) // 2, frames0 // 2
    lift_even, lift_odd, features = call(
        input_kernel,
        [((evens, rows, chans), F32), ((odds, rows, chans), F32), ((frames1, rows, chans), BF16, "hbm")],
        [grad, w_in, even_slope, odd_slope, feat],
        scratch=[pltpu.SemaphoreType.DMA],
        flops=1 << 30,
    )
    quarter = chans // 4
    own, *sends = call(
        plane_kernel,
        [((quarter, wide), F32)] + [((quarter, wide), BF16)] * 3,
        [*keeps, *others, lift_odd],
    )
    gots = [swap(part, "dev", offset) for offset, part in enumerate(sends, 1)]
    used = -(-(stride * (GROUP - 1) + taps) // 16) * 16
    small, *smalls = call(
        functools.partial(backward_kernel, frames0, taps),
        [((16, quarter), F32)] * 4,
        [valid, pre0, mean, inv, patch, lift_even, lift_odd, gain_in],
        scratch=[
            ((chans // width, groups, rows, GROUP * width), BF16),
            ((chans // width, used, GROUP * width), F32),
            ((used, groups * rows), BF16),
            ((16, chans), F32),
            ((4, 16, quarter), F32),
        ],
        flops=1 << 32,
    )
    small3, small2 = swap(smalls[2], "dev", 3), swap(smalls[1], "dev", 2)
    own, first = call(
        part_kernel, [((quarter, wide), F32), (small.shape, F32)], [own, gots[0], gots[1], smalls[0]]
    )
    small1 = swap(first, "dev", 1)
    size = quarter // 2
    keep, send = call(
        functools.partial(gather_kernel, dev_bits - 1),
        [(packed(size, wide), F32), (packed(size, wide), BF16)],
        [own, gots[2], small, small1, small2, small3],
    )
    for bit in range(dev_bits - 1, 2, -1):
        size //= 2
        keep, send = call(
            functools.partial(halve_kernel, bit - 1),
            [(packed(size, wide), F32), (packed(size, wide), BF16)],
            [keep, swap(send, "dev", 1 << bit)],
        )
    send = call(add_kernel, [(packed(size, wide), BF16)], [keep, swap(send, "dev", 4)])[0]
    for bit in range(1, grp_bits):
        kind = F32 if bit == grp_bits - 1 else BF16
        send = call(add_kernel, [(packed(size, wide), kind)], [send, swap(send, "grp", 1 << bit)])[0]
    grad_second, grad_first, grad_gain, grad_bias = call(
        functools.partial(join_kernel, taps),
        [
            ((taps_second, size, chans), F32, "out"),
            ((taps, size), F32, "out"),
            ((1, size), F32, "out"),
            ((1, size), F32, "out"),
        ],
        [send, swap(send, "grp", 1)],
    )
    return (
        features.transpose(1, 0, 2),
        grad_second.transpose(0, 2, 1),
        grad_first,
        grad_gain.reshape(size),
        grad_bias.reshape(size),
    )


def solution(mesh):
    placed = (
        P(("grp", "dev"), None),
        P("grp"),
        P("grp", None),
        P(),
        P(),
        P(),
        P(),
        P(("grp", "dev"), None, None),
    )
    return jax.shard_map(
        shards,
        mesh=mesh,
        in_specs=placed,
        out_specs=(
            P(("grp", "dev"), None, None),
            P(None, None, "dev"),
            P(None, "dev"),
            P("dev"),
            P("dev"),
        ),
        check_vma=False,
    )
```
